32 devices in a mesh: dp: 4 (over y, x), fsdp: 8 (over z, core).
Axes of the slice: x: 2, y: 2, z: 4, core: 2. Of those that a mesh axis runs over, the one named last changes fastest.
Arguments:
- tokens: bfloat16 [2, 2048, 2048], P(None, ('dp', 'fsdp')), may hold values from -6 to 6
- embedding: bfloat16 [2, 64, 2048], P(None, 'dp'), may hold values from -6 to 6
- image_slot: int32 [2, 2048], P(None, ('dp', 'fsdp')), may hold values from 0 to 1, as said below
- token_mask: int32 [2, 2048], P(None, ('dp', 'fsdp')), may hold values from 0 to 1, as said below
- cotangent: bfloat16 [2, 2048, 2048], P(None, ('dp', 'fsdp')), may hold values from -6 to 6
- qkv_weight: float32 [2048, 3, 2048], P('dp', None, 'fsdp'), may hold values from -0.26516504 to 0.26516504
- out_weight: float32 [2048, 2048], P('dp', 'fsdp'), may hold values from -0.4375 to 0.4375
- up_weight: float32 [2048, 8192], P('dp', 'fsdp'), may hold values from -0.22097087 to 0.22097087
- down_weight: float32 [2048, 8192], P('dp', 'fsdp'), may hold values from -0.077339804 to 0.077339804
- ada_weight: float32 [2048, 6, 2048], P('dp', None, 'fsdp'), may hold values from -0.15467961 to 0.15467961
- qkv_first: float32 [2048, 3, 2048], P('dp', None, 'fsdp'), may hold values from -7.6293945e-05 to 7.6293945e-05
- out_first: float32 [2048, 2048], P('dp', 'fsdp'), may hold values from -7.6293945e-05 to 7.6293945e-05
- up_first: float32 [2048, 8192], P('dp', 'fsdp'), may hold values from -7.6293945e-05 to 7.6293945e-05
- down_first: float32 [2048, 8192], P('dp', 'fsdp'), may hold values from -7.6293945e-05 to 7.6293945e-05
- ada_first: float32 [2048, 6, 2048], P('dp', None, 'fsdp'), may hold values from -7.6293945e-05 to 7.6293945e-05
- qkv_second: float32 [2048, 3, 2048], P('dp', None, 'fsdp'), may hold values from 6.6227384e-12 to 1.05963814e-10
- out_second: float32 [2048, 2048], P('dp', 'fsdp'), may hold values from 6.6227384e-12 to 1.05963814e-10
- up_second: float32 [2048, 8192], P('dp', 'fsdp'), may hold values from 3.973643e-12 to 1.5894572e-11
- down_second: float32 [2048, 8192], P('dp', 'fsdp'), may hold values from 6.6227384e-12 to 1.05963814e-10
- ada_second: float32 [2048, 6, 2048], P('dp', None, 'fsdp'), may hold values from 6.6227384e-12 to 1.05963814e-10
Outputs:
- block_out: bfloat16 [2, 2048, 2048], P(None, ('dp', 'fsdp'))
- input_grad: float32 [2, 2048, 2048], P(None, ('dp', 'fsdp'))
- qkv_master: float32 [2048, 3, 2048], P('dp', None, 'fsdp')
- qkv_copy: bfloat16 [2048, 3, 2048], P('dp', None, 'fsdp')
- qkv_moment: float32 [2048, 3, 2048], P('dp', None, 'fsdp')
- qkv_square: float32 [2048, 3, 2048], P('dp', None, 'fsdp')
- out_master: float32 [2048, 2048], P('dp', 'fsdp')
- out_copy: bfloat16 [2048, 2048], P('dp', 'fsdp')
- out_moment: float32 [2048, 2048], P('dp', 'fsdp')
- out_square: float32 [2048, 2048], P('dp', 'fsdp')
- up_master: float32 [2048, 8192], P('dp', 'fsdp')
- up_copy: bfloat16 [2048, 8192], P('dp', 'fsdp')
- up_moment: float32 [2048, 8192], P('dp', 'fsdp')
- up_square: float32 [2048, 8192], P('dp', 'fsdp')
- down_master: float32 [2048, 8192], P('dp', 'fsdp')
- down_copy: bfloat16 [2048, 8192], P('dp', 'fsdp')
- down_moment: float32 [2048, 8192], P('dp', 'fsdp')
- down_square: float32 [2048, 8192], P('dp', 'fsdp')
- ada_master: float32 [2048, 6, 2048], P('dp', None, 'fsdp')
- ada_copy: bfloat16 [2048, 6, 2048], P('dp', None, 'fsdp')
- ada_moment: float32 [2048, 6, 2048], P('dp', None, 'fsdp')
- ada_square: float32 [2048, 6, 2048], P('dp', None, 'fsdp')
- grad_norm: float32 [], replicated
The draws below stay inside these ranges and needn't reach their ends.
Inputs may be any that keep to these rules, and one draw needn't show every extreme that they name: Within each device's block of 64 slots image_slot never falls, and padding slots carry the largest value. `token_mask`: within each device's block of 64 slots the ones form a leading run of a quarter of the block or more; some blocks are full.
All inputs are finite; a program needn't handle non-finite values.
Results may differ from the reference program's by a relative error of at most 0.023.
The reference program's roundings to bfloat16 on the way count: a program that leaves them out, or rounds other values in their place, can miss the bound.
Values may be sent and summed in bfloat16 or wider, within the bound.
A program may use at most 256 MiB of HBM per device.

```python
import math
import jax
import jax.numpy as jnp
from jax import lax

HEADS = 16
HEAD = 128
D = 2048
FF = 8192
EMB = 2048
TOK_DEV = 64
IMG_DEV = 2
MICRO = 2
STEP = 10
TOKENS = 2048
IMAGES = 64
PARAMS = 75497472
N_FSDP = 8


def ramped_normal(key, shape, fan_in, low_end):
    standard = jax.random.truncated_normal(key, -4.0, 4.0, shape, jnp.float32)
    position_share = jnp.arange(shape[-1], dtype=jnp.float32) / max(shape[-1] - 1, 1)
    return standard * (low_end + position_share) / fan_in ** 0.5


def shared_columns(key, shape, fan_in):
    return jax.random.truncated_normal(key, -3.0, 3.0, shape, jnp.float32) / fan_in ** 0.5


def slot_layout(key):
    devices = TOKENS // TOK_DEV
    key_length, key_wide, key_cut = jax.random.split(key, 3)
    lengths = jax.random.randint(key_length, (MICRO, devices), TOK_DEV // 4, TOK_DEV + 1)
    wide = jax.random.randint(key_wide, (MICRO, devices), 0, 8) == 0
    lengths = jnp.where(wide, TOK_DEV, lengths)
    picks = jax.random.randint(key_cut, (MICRO, devices, IMG_DEV - 1), 0, TOK_DEV)
    cuts = 1 + picks * lengths[:, :, None] // TOK_DEV
    places = jnp.arange(TOK_DEV)
    slots = jnp.sum((places[None, None, :, None] >= cuts[:, :, None, :]).astype(jnp.int32), axis=-1)
    live = (places[None, None, :] < lengths[:, :, None]).astype(jnp.int32)
    return (slots.reshape(MICRO, TOKENS).astype(jnp.int32), live.reshape(MICRO, TOKENS).astype(jnp.int32))


def draw_image_slot(key, part):
    return slot_layout(key)[0]


def draw_token_mask(key, part):
    return slot_layout(key)[1]


def draw_qkv_weight(key, part):
    key = jax.random.fold_in(key, 11)
    noise = ramped_normal(key, (D, 3, D), D, 0.5)
    which = jnp.array([0.0, 0.0, 1.5], jnp.float32)
    common = shared_columns(jax.random.fold_in(key, 21), (3, D), D) * which[:, None]
    return noise + common[None, :, :]


def draw_out_weight(key, part):
    key = jax.random.fold_in(key, 12)
    return ramped_normal(key, (D, D), D // 8, 0.5)


def draw_up_weight(key, part):
    key = jax.random.fold_in(key, 13)
    noise = ramped_normal(key, (D, FF), D, 0.5)
    common = shared_columns(jax.random.fold_in(key, 23), (FF,), D)
    return noise + common[None, :]


def draw_down_weight(key, part):
    key = jax.random.fold_in(key, 14)
    return ramped_normal(key, (D, FF), FF, 0.5)


def draw_ada_weight(key, part):
    key = jax.random.fold_in(key, 15)
    return ramped_normal(key, (EMB, 6, D), EMB, 0.5)


def level_of(key, dims, shards, least, high):
    level, own = 1.0, jax.random.fold_in(key, 6)
    for axis_at, parts in shards:
        heights = jnp.exp(jax.random.uniform(jax.random.fold_in(own, axis_at), (parts,), jnp.float32, least / len(shards), high / len(shards)))
        level = level * jnp.repeat(heights, dims[axis_at] // parts).reshape([-1 if axis == axis_at else 1 for axis in range(len(dims))])
    return level


def scatter_about(stream_key, extent, scale, reach, cuts=(), kind=jnp.bfloat16):
    values = scale * jax.random.normal(stream_key, extent, jnp.float32)
    if cuts:
        values = values * level_of(stream_key, extent, cuts, -0.22, 0.18)
    return jnp.clip(values, -reach, reach).astype(kind)


def setup_inputs(seed: int = 0) -> dict:
    arg_keys = jax.random.split(jax.random.key(seed), 21)
    tokens = scatter_about(arg_keys[0], (MICRO, TOKENS, D), 1.0, 6.0, ((1, 32),))
    embedding = scatter_about(arg_keys[1], (MICRO, IMAGES, EMB), 1.0, 6.0, ((1, 4),))
    image_slot = draw_image_slot(jax.random.fold_in(arg_keys[20], 71), 0)
    token_mask = draw_token_mask(jax.random.fold_in(arg_keys[20], 71), 0)
    cotangent = scatter_about(arg_keys[4], (MICRO, TOKENS, D), 1.0, 6.0, ((1, 32),))
    qkv_weight = draw_qkv_weight(jax.random.fold_in(arg_keys[20], 71), 0)
    out_weight = draw_out_weight(jax.random.fold_in(arg_keys[20], 71), 0)
    up_weight = draw_up_weight(jax.random.fold_in(arg_keys[20], 71), 0)
    down_weight = draw_down_weight(jax.random.fold_in(arg_keys[20], 71), 0)
    ada_weight = draw_ada_weight(jax.random.fold_in(arg_keys[20], 71), 0)
    qkv_first = scatter_about(arg_keys[10], (D, 3, D), (0.11 / PARAMS ** 0.5), 7.62939453125e-05, ((0, 4), (2, 8)), jnp.float32)
    out_first = scatter_about(arg_keys[11], (D, D), (0.11 / PARAMS ** 0.5), 7.62939453125e-05, ((0, 4), (1, 8)), jnp.float32)
    up_first = scatter_about(arg_keys[12], (D, FF), (0.11 / PARAMS ** 0.5), 7.62939453125e-05, ((0, 4), (1, 8)), jnp.float32)
    down_first = scatter_about(arg_keys[13], (D, FF), (0.11 / PARAMS ** 0.5), 7.62939453125e-05, ((0, 4), (1, 8)), jnp.float32)
    ada_first = scatter_about(arg_keys[14], (EMB, 6, D), (0.11 / PARAMS ** 0.5), 7.62939453125e-05, ((0, 4), (2, 8)), jnp.float32)
    qkv_second = jnp.clip(jnp.exp(math.log(1.0596381411209777e-10) - 2.7725887 * jax.random.uniform(arg_keys[15], (D, 3, D), jnp.float32) ** level_of(arg_keys[15], (D, 3, D), ((0, 4), (2, 8)), -0.2, 0.2)), 6.62273838200611e-12, 1.0596381411209777e-10)
    out_second = jnp.clip(jnp.exp(math.log(1.0596381411209777e-10) - 2.7725887 * jax.random.uniform(arg_keys[16], (D, D), jnp.float32) ** level_of(arg_keys[16], (D, D), ((0, 4), (1, 8)), -0.2, 0.2)), 6.62273838200611e-12, 1.0596381411209777e-10)
    up_second = jnp.clip(jnp.exp(math.log(1.5894572116814665e-11) - 1.3862944 * jax.random.uniform(arg_keys[17], (D, FF), jnp.float32) ** level_of(arg_keys[17], (D, FF), ((0, 4), (1, 8)), -0.2, 0.2)), 3.973643029203666e-12, 1.5894572116814665e-11)
    down_second = jnp.clip(jnp.exp(math.log(1.0596381411209777e-10) - 2.7725887 * jax.random.uniform(arg_keys[18], (D, FF), jnp.float32) ** level_of(arg_keys[18], (D, FF), ((0, 4), (1, 8)), -0.2, 0.2)), 6.62273838200611e-12, 1.0596381411209777e-10)
    ada_second = jnp.clip(jnp.exp(math.log(1.0596381411209777e-10) - 2.7725887 * jax.random.uniform(arg_keys[19], (EMB, 6, D), jnp.float32) ** level_of(arg_keys[19], (EMB, 6, D), ((0, 4), (2, 8)), -0.2, 0.2)), 6.62273838200611e-12, 1.0596381411209777e-10)
    return {"tokens": tokens, "embedding": embedding, "image_slot": image_slot, "token_mask": token_mask, "cotangent": cotangent, "qkv_weight": qkv_weight, "out_weight": out_weight, "up_weight": up_weight, "down_weight": down_weight, "ada_weight": ada_weight, "qkv_first": qkv_first, "out_first": out_first, "up_first": up_first, "down_first": down_first, "ada_first": ada_first, "qkv_second": qkv_second, "out_second": out_second, "up_second": up_second, "down_second": down_second, "ada_second": ada_second}


@jax.custom_vjp
def low(v):
    return lax.optimization_barrier(v.astype(jnp.bfloat16)).astype(jnp.float32)

@jax.custom_vjp
def low_back(v):
    return v

def low_keep(v):
    return (low(v), None)

def low_pass(kept, grad):
    return (grad,)

def back_keep(v):
    return (v, None)

def back_low(kept, grad):
    return (low(grad),)
low.defvjp(low_keep, low_pass)
low_back.defvjp(back_keep, back_low)
HIGHEST_PRECISION = lax.Precision.HIGHEST
NORM_EPS = 1e-06
CLIP_AT = 1.0
BETA_ONE = 0.9
BETA_TWO = 0.999
LEARN_RATE = 0.05
WEIGHT_DECAY = 0.1
ADAM_EPS = 1e-08
block_target = 512

def normalize(values):
    average = lax.optimization_barrier(jnp.mean(values, axis=-1, keepdims=True))
    centred = values - average
    return centred * lax.rsqrt(lax.optimization_barrier(jnp.mean(centred * centred, axis=-1, keepdims=True)) + NORM_EPS)

def block_rows():
    limit = max(1, min(N_FSDP, block_target // TOK_DEV))
    return TOK_DEV * (1 << limit.bit_length() - 1)

def attend(pieces):
    queries, keys_part, values_part, image_ids, usable = pieces
    count = queries.shape[0]
    scores = jnp.einsum('qhe,khe->hqk', queries, keys_part, precision=HIGHEST_PRECISION) * HEAD ** (-0.5)
    scores = low_back(scores)
    allowed = (image_ids[:, None] == image_ids[None, :]) & (usable[None, :] == 1) | jnp.eye(count, dtype=bool)
    scores = jnp.where(allowed[None], scores, -1e+30)
    attn_probs = low(jax.nn.softmax(scores, axis=-1))
    return jnp.einsum('hqk,khe->qhe', attn_probs, values_part, precision=HIGHEST_PRECISION)

def forward(inputs, weights, condition, image_ids, usable):
    qkv_w, out_w, up_w, down_w, ada_w = weights
    modulation = low_back(jnp.einsum('ie,ejd->ijd', condition, ada_w, precision=HIGHEST_PRECISION))
    picked = jnp.take(modulation, image_ids, axis=0)
    shift1, scale1, gate1 = (picked[:, 0], picked[:, 1], picked[:, 2])
    shift2, scale2, gate2 = (picked[:, 3], picked[:, 4], picked[:, 5])
    hidden1 = low(normalize(inputs) * (1.0 + scale1) + shift1)
    qkv = low(low_back(jnp.einsum('td,djf->tjf', hidden1, qkv_w, precision=HIGHEST_PRECISION)))
    count = inputs.shape[0]
    rows = block_rows()
    blocks = count // rows
    queries = qkv[:, 0].reshape(blocks, rows, HEADS, HEAD)
    keys_all = qkv[:, 1].reshape(blocks, rows, HEADS, HEAD)
    values_all = qkv[:, 2].reshape(blocks, rows, HEADS, HEAD)
    attended = lax.map(jax.checkpoint(attend), (queries, keys_all, values_all, image_ids.reshape(blocks, rows), usable.reshape(blocks, rows)))
    attended = low(low_back(attended.reshape(count, D)))
    attn_branch = low_back(jnp.dot(attended, out_w.T, precision=HIGHEST_PRECISION))
    mid = inputs + gate1 * attn_branch
    hidden2 = low(normalize(mid) * (1.0 + scale2) + shift2)
    upper = low_back(jnp.dot(hidden2, up_w, precision=HIGHEST_PRECISION))
    activ = low(jax.nn.gelu(upper))
    mlp_branch = low_back(jnp.dot(activ, down_w.T, precision=HIGHEST_PRECISION))
    return mid + gate2 * mlp_branch

def reference(tokens, embedding, image_slot, token_mask, cotangent, qkv_weight, out_weight, up_weight, down_weight, ada_weight, qkv_first, out_first, up_first, down_first, ada_first, qkv_second, out_second, up_second, down_second, ada_second):
    masters = (qkv_weight, out_weight, up_weight, down_weight, ada_weight)
    firsts = (qkv_first, out_first, up_first, down_first, ada_first)
    seconds = (qkv_second, out_second, up_second, down_second, ada_second)
    rounded = tuple((master.astype(jnp.bfloat16).astype(jnp.float32) for master in masters))
    totals = tuple((jnp.zeros(master.shape, jnp.float32) for master in masters))
    block_outs = []
    input_grads = []
    positions = (jnp.arange(TOKENS) // TOK_DEV * IMG_DEV).astype(jnp.int32)
    for batch_index in range(MICRO):
        image_ids = (positions + image_slot[batch_index]).astype(jnp.int32)
        usable = token_mask[batch_index]
        condition = low(jax.nn.silu(embedding[batch_index].astype(jnp.float32)))
        inputs = tokens[batch_index].astype(jnp.float32)

        def run(values, *weights):
            return forward(values, weights, condition, image_ids, usable)
        result, pull = jax.vjp(run, inputs, *rounded)
        grad_y = cotangent[batch_index].astype(jnp.float32) * usable[:, None].astype(jnp.float32)
        pulled = pull(grad_y)
        block_outs.append(result.astype(jnp.bfloat16))
        input_grads.append(pulled[0])
        totals = tuple((total + part for total, part in zip(totals, pulled[1:])))
    squares = jnp.float32(0.0)
    for total in totals:
        squares = squares + jnp.sum(total * total)
    grad_norm = jnp.sqrt(squares)
    factor = jnp.minimum(1.0, CLIP_AT / grad_norm)
    results = []
    for master, first, second, total in zip(masters, firsts, seconds, totals):
        clipped = total * factor
        moment = BETA_ONE * first + (1.0 - BETA_ONE) * clipped
        square = BETA_TWO * second + (1.0 - BETA_TWO) * clipped * clipped
        ratio = moment / (1.0 - BETA_ONE ** STEP) / (jnp.sqrt(square / (1.0 - BETA_TWO ** STEP)) + ADAM_EPS)
        new_master = master - LEARN_RATE * (ratio + WEIGHT_DECAY * master)
        results.extend([new_master, new_master.astype(jnp.bfloat16), moment, square])
    return (jnp.stack(block_outs), jnp.stack(input_grads), results[0], results[1], results[2], results[3], results[4], results[5], results[6], results[7], results[8], results[9], results[10], results[11], results[12], results[13], results[14], results[15], results[16], results[17], results[18], results[19], grad_norm)
```

```python
import functools

import jax
import jax.numpy as jnp
from jax import lax
from jax.experimental import pallas as pl
from jax.experimental.pallas import tpu as pltpu
from jax.sharding import PartitionSpec as P

HEAD = 128
STEP = 10
MODS = 6

NORM_EPS = 1e-06
CLIP_AT = 1.0
BETA_ONE = 0.9
BETA_TWO = 0.999
LEARN_RATE = 0.05
WEIGHT_DECAY = 0.1
ADAM_EPS = 1e-08

MESH = pl.DeviceIdType.MESH
VMEM_LIMIT = 48 * 1024 * 1024
ROW_STEP = 16


class Place:
    def __init__(self, n_dp, n_fsdp):
        self.n_dp, self.n_fsdp = n_dp, n_fsdp
        self.chips = n_fsdp // 2
        self.grid_a = 2
        self.grid_b = n_dp // 2
        self.dp = lax.axis_index("dp")
        self.f = lax.axis_index("fsdp")
        self.p = self.f // 2
        self.c = self.f % 2
        self.a = self.dp // self.grid_b
        self.b = self.dp % self.grid_b

    def at_chip(self, chip):
        return (self.dp, chip * 2 + self.c)

    def sibling(self):
        return (self.dp, self.p * 2 + 1 - self.c)

    def at_dp(self, dp):
        return (dp, self.f)

    def b_peer(self, i):
        return (self.b + i) % self.grid_b

    def a_peer(self, i):
        return (self.a + i) % self.grid_a


def enter(place, line=False, grid=False):
    barrier = pltpu.get_barrier_semaphore()
    devices = []
    if line:
        devices.append(place.at_chip((place.p + 1) % place.chips))
        devices.append(place.at_chip((place.p + place.chips - 1) % place.chips))
        devices.append(place.sibling())
    if grid:
        for i in range(1, place.n_dp):
            devices.append(place.at_dp((place.dp + i) % place.n_dp))
    for device in devices:
        pl.semaphore_signal(barrier, inc=1, device_id=device, device_id_type=MESH)
    pl.semaphore_wait(barrier, len(devices))


def remote(src, dst, send, recv, device):
    return pltpu.make_async_remote_copy(
        src_ref=src, dst_ref=dst, send_sem=send, recv_sem=recv, device_id=device, device_id_type=MESH
    )


class LineGather:
    @staticmethod
    def scratch(n_fsdp):
        chips = n_fsdp // 2
        return [
            pltpu.SemaphoreType.DMA((2, chips)),
            pltpu.SemaphoreType.DMA((2, chips)),
            pltpu.SemaphoreType.DMA((chips,)),
            pltpu.SemaphoreType.DMA((chips,)),
            pltpu.SemaphoreType.DMA,
        ]

    def __init__(self, place, src, out, sems):
        self.place, self.src, self.out = place, src, out
        self.send, self.recv, self.csend, self.crecv, self.local = sems

    def _block(self, chip):
        return self.out.at[chip * 2 + self.place.c]

    def _hop(self, way, step, first):
        pc = self.place
        chip = pc.p - step if way == 0 else pc.p + step
        target = pc.p + 1 if way == 0 else pc.p - 1
        src = self.src if first else self._block(chip)
        return remote(src, self._block(chip), self.send.at[way, step], self.recv.at[way, step], pc.at_chip(target))

    def _side(self, chip, first=False):
        src = self.src if first else self._block(chip)
        return remote(src, self._block(chip), self.csend.at[chip], self.crecv.at[chip], self.place.sibling())

    def _sends(self, way, step):
        pc = self.place
        if way == 0:
            return (pc.p < pc.chips - 1) & (pc.p >= step)
        return (pc.p > 0) & (pc.p + step <= pc.chips - 1)

    def start(self):
        pc = self.place
        for way in range(2):
            @pl.when(self._sends(way, 0))
            def _():
                self._hop(way, 0, True).start()
        self._side(pc.p, True).start()
        pltpu.make_async_copy(self.src, self._block(pc.p), self.local).start()

    def step(self, step):
        pc = self.place
        for way in range(2):
            chip = pc.p - step if way == 0 else pc.p + step
            here = (chip >= 0) if way == 0 else (chip <= pc.chips - 1)

            @pl.when(here)
            def _():
                remote(
                    self._block(chip), self._block(chip), self.send.at[way, step - 1], self.recv.at[way, step - 1],
                    pc.sibling(),
                ).wait_recv()
                if step < pc.chips - 1:
                    @pl.when(self._sends(way, step))
                    def _():
                        self._hop(way, step, False).start()
                self._side(chip).start()

    def finish(self):
        pc = self.place
        pltpu.make_async_copy(self.src, self._block(pc.p), self.local).wait()
        for chip in range(pc.chips):
            remote(
                self.out.at[chip * 2 + 1 - pc.c], self.out.at[chip * 2 + 1 - pc.c], self.csend.at[chip],
                self.crecv.at[chip], pc.sibling(),
            ).wait_recv()
            self._side(chip).wait_send()
        for way in range(2):
            for step in range(pc.chips - 1):
                @pl.when(self._sends(way, step))
                def _():
                    self._hop(way, step, False).wait_send()

    def steps(self):
        return [self.start] + [functools.partial(self.step, s) for s in range(1, self.place.chips)] + [self.finish]


def row_loop(rows, body):
    def run(i, carry):
        body(pl.ds(pl.multiple_of(i * ROW_STEP, ROW_STEP), ROW_STEP))
        return carry

    lax.fori_loop(0, rows // ROW_STEP, run, 0)


class LineScatter:
    @staticmethod
    def scratch(n_fsdp, rows, width):
        chips = n_fsdp // 2
        return [
            pltpu.VMEM((chips, rows, width), jnp.bfloat16),
            pltpu.VMEM((chips, rows, width), jnp.bfloat16),
            pltpu.VMEM((2, chips, rows, width), jnp.bfloat16),
            pltpu.SemaphoreType.DMA((chips,)),
            pltpu.SemaphoreType.DMA((chips,)),
            pltpu.SemaphoreType.DMA((2, chips)),
            pltpu.SemaphoreType.DMA((2, chips)),
        ]

    def __init__(self, place, part, out, scratch):
        self.place, self.part, self.out = place, part, out
        self.side, self.total, self.inbox, self.csend, self.crecv, self.send, self.recv = scratch
        self.rows = out.shape[0]

    def _side(self, chip):
        pc = self.place
        return remote(
            self.part.at[chip * 2 + 1 - pc.c], self.side.at[chip], self.csend.at[chip], self.crecv.at[chip], pc.sibling()
        )

    def _hop(self, way, chip):
        pc = self.place
        target = pc.p + 1 if way == 0 else pc.p - 1
        return remote(
            self.total.at[chip], self.inbox.at[way, chip], self.send.at[way, chip], self.recv.at[way, chip],
            pc.at_chip(target),
        )

    def _order(self):
        chips = self.place.chips
        order = []
        for k in range(chips):
            for chip in (chips - 1 - k, k):
                if chip not in order:
                    order.append(chip)
        return order

    def start(self):
        for chip in self._order():
            self._side(chip).start()

    def _travel(self, way, chip):
        pc = self.place
        going = (chip > pc.p) if way == 0 else (chip < pc.p)
        first = (pc.p == 0) if way == 0 else (pc.p == pc.chips - 1)

        @pl.when(going)
        def _():
            self._side(chip).wait_recv()

            @pl.when(first)
            def _():
                def add(rows):
                    mine = self.part[chip * 2 + pc.c, rows, :].astype(jnp.float32)
                    other = self.side[chip, rows, :].astype(jnp.float32)
                    self.total[chip, rows, :] = (mine + other).astype(jnp.bfloat16)

                row_loop(self.rows, add)

            @pl.when(jnp.logical_not(first))
            def _():
                self._hop(way, chip).wait_recv()

                def add(rows):
                    mine = self.part[chip * 2 + pc.c, rows, :].astype(jnp.float32)
                    other = self.side[chip, rows, :].astype(jnp.float32)
                    came = self.inbox[way, chip, rows, :].astype(jnp.float32)
                    self.total[chip, rows, :] = (mine + other + came).astype(jnp.bfloat16)

                row_loop(self.rows, add)

            self._hop(way, chip).start()

    def step(self, k):
        chips = self.place.chips
        self._travel(0, chips - 1 - k)
        self._travel(1, k)

    def finish(self):
        pc = self.place
        chips = pc.chips
        self._side(pc.p).wait_recv()

        def own(rows):
            mine = self.part[pc.p * 2 + pc.c, rows, :].astype(jnp.float32)
            other = self.side[pc.p, rows, :].astype(jnp.float32)
            self.out[rows, :] = mine + other

        row_loop(self.rows, own)
        for way in range(2):
            last = (pc.p > 0) if way == 0 else (pc.p < chips - 1)

            @pl.when(last)
            def _():
                self._hop(way, pc.p).wait_recv()

                def add(rows):
                    self.out[rows, :] = self.out[rows, :] + self.inbox[way, pc.p, rows, :].astype(jnp.float32)

                row_loop(self.rows, add)

        for chip in range(chips):
            self._side(chip).wait_send()

            @pl.when(chip > pc.p)
            def _():
                self._hop(0, chip).wait_send()

            @pl.when(chip < pc.p)
            def _():
                self._hop(1, chip).wait_send()

    def steps(self):
        return [self.start] + [functools.partial(self.step, k) for k in range(self.place.chips)] + [self.finish]


class GridGather:
    @staticmethod
    def scratch(n_dp):
        na, nb = 2, n_dp // 2
        return [
            pltpu.SemaphoreType.DMA((2, max(nb - 1, 1))),
            pltpu.SemaphoreType.DMA((2, max(nb - 1, 1))),
            pltpu.SemaphoreType.DMA((2, na - 1)),
            pltpu.SemaphoreType.DMA((2, na - 1)),
            pltpu.SemaphoreType.DMA((2, max(nb - 1, 1), na - 1)),
            pltpu.SemaphoreType.DMA((2, max(nb - 1, 1), na - 1)),
            pltpu.SemaphoreType.DMA,
        ]

    def __init__(self, place, src, out, sems):
        self.place, self.src, self.out = place, src, out
        self.bsend, self.brecv, self.asend, self.arecv, self.fsend, self.frecv, self.local = sems
        self.half = src.shape[0] // 2

    def _rows(self, ref, h):
        return ref.at[pl.ds(h * self.half, self.half)]

    def _block(self, a, b, h):
        return self._rows(self.out.at[a * self.place.grid_b + b], h)

    def _b_copy(self, i, h, coming):
        pc = self.place
        b = pc.b_peer(pc.grid_b - i) if coming else pc.b
        return remote(
            self._rows(self.src, h), self._block(pc.a, b, h), self.bsend.at[h, i - 1], self.brecv.at[h, i - 1],
            pc.at_dp(pc.a * pc.grid_b + pc.b_peer(i)),
        )

    def _a_copy(self, i, h, coming):
        pc = self.place
        a = pc.a_peer(pc.grid_a - i) if coming else pc.a
        return remote(
            self._rows(self.src, h), self._block(a, pc.b, h), self.asend.at[h, i - 1], self.arecv.at[h, i - 1],
            pc.at_dp(pc.a_peer(i) * pc.grid_b + pc.b),
        )

    def _on(self, h, ib, ia, coming):
        pc = self.place
        if h == 0:
            b = pc.b_peer(pc.grid_b - ib)
            a = pc.a_peer(pc.grid_a - ia) if coming else pc.a
            target = pc.at_dp(pc.a_peer(ia) * pc.grid_b + pc.b)
        else:
            a = pc.a_peer(pc.grid_a - ia)
            b = pc.b_peer(pc.grid_b - ib) if coming else pc.b
            target = pc.at_dp(pc.a * pc.grid_b + pc.b_peer(ib))
        block = self._block(a, b, h)
        return remote(block, block, self.fsend.at[h, ib - 1, ia - 1], self.frecv.at[h, ib - 1, ia - 1], target)

    def start(self):
        pc = self.place
        for h in range(2):
            for i in range(1, pc.grid_b):
                self._b_copy(i, h, False).start()
            for i in range(1, pc.grid_a):
                self._a_copy(i, 1 - h, False).start()
        pltpu.make_async_copy(self.src, self.out.at[pc.dp], self.local).start()

    def step(self):
        pc = self.place
        for ib in range(1, pc.grid_b):
            self._b_copy(ib, 0, True).wait_recv()
            for ia in range(1, pc.grid_a):
                self._on(0, ib, ia, False).start()
        for ia in range(1, pc.grid_a):
            self._a_copy(ia, 1, True).wait_recv()
            for ib in range(1, pc.grid_b):
                self._on(1, ib, ia, False).start()

    def finish(self):
        pc = self.place
        pltpu.make_async_copy(self.src, self.out.at[pc.dp], self.local).wait()
        for ib in range(1, pc.grid_b):
            self._b_copy(ib, 1, True).wait_recv()
        for ia in range(1, pc.grid_a):
            self._a_copy(ia, 0, True).wait_recv()
        for h in range(2):
            for ib in range(1, pc.grid_b):
                for ia in range(1, pc.grid_a):
                    self._on(h, ib, ia, True).wait_recv()
                    self._on(h, ib, ia, False).wait_send()
        for h in range(2):
            for ib in range(1, pc.grid_b):
                self._b_copy(ib, h, False).wait_send()
            for ia in range(1, pc.grid_a):
                self._a_copy(ia, h, False).wait_send()

    def steps(self):
        return [self.start, self.step, self.finish]


class GridScatter:
    @staticmethod
    def scratch(n_dp, rows, width):
        na, nb = 2, n_dp // 2
        half = rows // 2
        most = max(nb - 1, 1)
        return [
            pltpu.VMEM((most, na, half, width), jnp.bfloat16),
            pltpu.VMEM((na - 1, nb, half, width), jnp.bfloat16),
            pltpu.VMEM((na, half, width), jnp.bfloat16),
            pltpu.VMEM((nb, half, width), jnp.bfloat16),
            pltpu.VMEM((na - 1, half, width), jnp.bfloat16),
            pltpu.VMEM((most, half, width), jnp.bfloat16),
            pltpu.SemaphoreType.DMA((most, na)),
            pltpu.SemaphoreType.DMA((most, na)),
            pltpu.SemaphoreType.DMA((na - 1, nb)),
            pltpu.SemaphoreType.DMA((na - 1, nb)),
            pltpu.SemaphoreType.DMA((na - 1,)),
            pltpu.SemaphoreType.DMA((na - 1,)),
            pltpu.SemaphoreType.DMA((most,)),
            pltpu.SemaphoreType.DMA((most,)),
        ]

    def __init__(self, place, part, out, scratch):
        self.place, self.part, self.out = place, part, out
        self.box_b, self.box_a, self.sum_b, self.sum_a, self.end_a, self.end_b = scratch[:6]
        self.bs, self.br, self.as_, self.ar, self.eas, self.ear, self.ebs, self.ebr = scratch[6:]
        self.half = out.shape[0] // 2

    def _part(self, a, b, h):
        return self.part.at[a * self.place.grid_b + b, pl.ds(h * self.half, self.half)]

    def _first_b(self, i, j):
        pc = self.place
        return remote(
            self._part(pc.a_peer(j), pc.b_peer(i), 0), self.box_b.at[i - 1, j], self.bs.at[i - 1, j],
            self.br.at[i - 1, j], pc.at_dp(pc.a * pc.grid_b + pc.b_peer(i)),
        )

    def _first_a(self, i, j):
        pc = self.place
        return remote(
            self._part(pc.a_peer(i), pc.b_peer(j), 1), self.box_a.at[i - 1, j], self.as_.at[i - 1, j],
            self.ar.at[i - 1, j], pc.at_dp(pc.a_peer(i) * pc.grid_b + pc.b),
        )

    def _second_a(self, i):
        pc = self.place
        return remote(
            self.sum_b.at[i], self.end_a.at[i - 1], self.eas.at[i - 1], self.ear.at[i - 1],
            pc.at_dp(pc.a_peer(i) * pc.grid_b + pc.b),
        )

    def _second_b(self, i):
        pc = self.place
        return remote(
            self.sum_a.at[i], self.end_b.at[i - 1], self.ebs.at[i - 1], self.ebr.at[i - 1],
            pc.at_dp(pc.a * pc.grid_b + pc.b_peer(i)),
        )

    def _firsts_b(self):
        pc = self.place
        return [(i, j) for j in list(range(1, pc.grid_a)) + [0] for i in range(1, pc.grid_b)]

    def _firsts_a(self):
        pc = self.place
        return [(i, j) for j in list(range(1, pc.grid_b)) + [0] for i in range(1, pc.grid_a)]

    def start(self):
        for i, j in self._firsts_b():
            self._first_b(i, j).start()
        for i, j in self._firsts_a():
            self._first_a(i, j).start()

    def _sum_b(self, j):
        pc = self.place
        for i in range(1, pc.grid_b):
            self._first_b(i, j).wait_recv()
        mine = self._part(pc.a_peer(j), pc.b, 0)

        def add(rows):
            total = mine[rows, :].astype(jnp.float32)
            for i in range(1, pc.grid_b):
                total = total + self.box_b[i - 1, j, rows, :].astype(jnp.float32)
            if j == 0:
                self.out[rows, :] = total
            else:
                self.sum_b[j, rows, :] = total.astype(jnp.bfloat16)

        row_loop(self.half, add)
        if j:
            self._second_a(j).start()

    def _sum_a(self, j):
        pc = self.place
        for i in range(1, pc.grid_a):
            self._first_a(i, j).wait_recv()
        mine = self._part(pc.a, pc.b_peer(j), 1)

        def add(rows):
            total = mine[rows, :].astype(jnp.float32)
            for i in range(1, pc.grid_a):
                total = total + self.box_a[i - 1, j, rows, :].astype(jnp.float32)
            if j == 0:
                self.out[pl.ds(pl.multiple_of(self.half + rows.start, ROW_STEP), ROW_STEP), :] = total
            else:
                self.sum_a[j, rows, :] = total.astype(jnp.bfloat16)

        row_loop(self.half, add)
        if j:
            self._second_b(j).start()

    def step(self):
        pc = self.place
        for j in range(1, pc.grid_a):
            self._sum_b(j)
        for j in range(1, pc.grid_b):
            self._sum_a(j)

    def step_own(self):
        self._sum_b(0)
        self._sum_a(0)

    def finish(self):
        pc = self.place
        for i in range(1, pc.grid_a):
            self._second_a(i).wait_recv()
        for i in range(1, pc.grid_b):
            self._second_b(i).wait_recv()

        def add(rows):
            total = self.out[rows, :]
            for i in range(1, pc.grid_a):
                total = total + self.end_a[i - 1, rows, :].astype(jnp.float32)
            self.out[rows, :] = total
            low = pl.ds(pl.multiple_of(self.half + rows.start, ROW_STEP), ROW_STEP)
            total = self.out[low, :]
            for i in range(1, pc.grid_b):
                total = total + self.end_b[i - 1, rows, :].astype(jnp.float32)
            self.out[low, :] = total

        row_loop(self.half, add)
        for i, j in self._firsts_b():
            self._first_b(i, j).wait_send()
        for i, j in self._firsts_a():
            self._first_a(i, j).wait_send()
        for i in range(1, pc.grid_a):
            self._second_a(i).wait_send()
        for i in range(1, pc.grid_b):
            self._second_b(i).wait_send()

    def steps(self):
        return [self.start, self.step, self.step_own, self.finish]


class Direct:
    @staticmethod
    def scratch(n):
        return [pltpu.SemaphoreType.DMA((n - 1,)), pltpu.SemaphoreType.DMA((n - 1,))]

    def __init__(self, place, src, out, sems, whole=False, axis="dp"):
        self.place, self.src, self.out, self.whole = place, src, out, whole
        self.send, self.recv = sems
        self.n = place.n_dp if axis == "dp" else place.n_fsdp
        self.me = place.dp if axis == "dp" else place.f
        self.axis = axis

    def _device(self, other):
        return self.place.at_dp(other) if self.axis == "dp" else (self.place.dp, other)

    def _copy(self, i, coming=False):
        other = (self.me + i) % self.n
        origin = (self.me + self.n - i) % self.n if coming else self.me
        src = self.src if self.whole else self.src.at[other]
        return remote(src, self.out.at[origin], self.send.at[i - 1], self.recv.at[i - 1], self._device(other))

    def start(self):
        for i in range(1, self.n):
            self._copy(i).start()

    def finish(self):
        for i in range(1, self.n):
            self._copy(i, True).wait_recv()
            self._copy(i).wait_send()


def split_refs(refs, counts):
    out, at = [], 0
    for count in counts:
        out.append(refs[at : at + count])
        at += count
    return out


HBM = pl.BlockSpec(memory_space=pl.ANY)
WHOLE = pl.BlockSpec(memory_space=pltpu.VMEM)


def transfer(collective_id, n_dp, n_fsdp, kinds, order=None):
    in_specs, out_specs, out_shape, scratch, counts = [], [], [], [], []
    for kind, array in kinds:
        if kind is LineGather:
            out_shape.append(jax.ShapeDtypeStruct((n_fsdp, *array.shape), array.dtype))
            spec, got = HBM, kind.scratch(n_fsdp)
        elif kind is GridGather:
            out_shape.append(jax.ShapeDtypeStruct((n_dp, *array.shape), array.dtype))
            spec, got = HBM, kind.scratch(n_dp)
        elif kind is LineScatter:
            out_shape.append(jax.ShapeDtypeStruct(array.shape[1:], jnp.float32))
            spec, got = WHOLE, kind.scratch(n_fsdp, *array.shape[1:])
        else:
            out_shape.append(jax.ShapeDtypeStruct(array.shape[1:], jnp.float32))
            spec, got = WHOLE, kind.scratch(n_dp, *array.shape[1:])
        in_specs.append(spec)
        out_specs.append(spec)
        scratch += got
        counts.append(len(got))
    has_line = any(kind in (LineGather, LineScatter) for kind, _ in kinds)
    has_grid = any(kind in (GridGather, GridScatter) for kind, _ in kinds)

    def kernel(*refs):
        count = len(kinds)
        ins, outs, rest = refs[:count], refs[count : 2 * count], refs[2 * count :]
        place = Place(n_dp, n_fsdp)
        enter(place, has_line, has_grid)
        work = [
            kind(place, ins[i], outs[i], got).steps()
            for i, ((kind, _), got) in enumerate(zip(kinds, split_refs(rest, counts)))
        ]
        for at in range(max(len(steps) for steps in work)):
            for steps in work:
                if at < len(steps) - 1:
                    steps[at]()
        for steps in work:
            steps[-1]()

    return pl.pallas_call(
        kernel,
        out_shape=out_shape,
        in_specs=in_specs,
        out_specs=out_specs,
        scratch_shapes=scratch,
        compiler_params=pltpu.CompilerParams(
            collective_id=collective_id, has_side_effects=True, vmem_limit_bytes=VMEM_LIMIT
        ),
    )(*[array for _, array in kinds])


def modulation_kernel(n_dp, n_fsdp, tokens, codes, condition, ada, qkv, out_w):
    images, deep = condition.shape[1:]
    wide = ada.shape[1]
    line = LineGather.scratch(n_fsdp)
    grid = GridGather.scratch(n_dp)
    direct = Direct.scratch(n_dp)
    counts = [len(line)] * 3 + [len(grid)] * 2 + [len(direct)] * 2

    def kernel(tok, cod, cond, ada_ref, qkv_ref, out_ref, tok_g, cod_g, mods_g, cond_g, qkv_g, out_g, *rest):
        parts, boxes, mods = rest[:3]
        sems = split_refs(rest[3:], counts)
        place = Place(n_dp, n_fsdp)
        enter(place, True, True)
        conds = Direct(place, cond, cond_g, sems[5])
        conds.start()
        lines = [LineGather(place, tok, tok_g, sems[0]), LineGather(place, cod, cod_g, sems[1])]
        grids = [GridGather(place, qkv_ref, qkv_g, sems[3]), GridGather(place, out_ref, out_g, sems[4])]
        grids[0].start()
        for gather in lines:
            gather.start()
        cond_g[place.dp] = cond[place.dp]
        conds.finish()
        for d in range(n_dp):
            parts[d] = jnp.dot(cond_g[d], ada_ref[...], preferred_element_type=jnp.float32)
        sums = Direct(place, parts, boxes, sems[6])
        sums.start()
        for gather in lines:
            gather.step(1)
        grids[0].step()
        grids[1].start()
        sums.finish()
        total = parts[place.dp]
        for i in range(1, n_dp):
            total = total + boxes[(place.dp + i) % n_dp]
        mods[...] = total
        last = LineGather(place, mods, mods_g, sems[2])
        last.start()
        for step in range(2, place.chips):
            for gather in lines:
                gather.step(step)
            last.step(step - 1)
        last.step(place.chips - 1)
        grids[1].step()
        for gather in lines + [last] + grids:
            gather.finish()

    return pl.pallas_call(
        kernel,
        out_shape=[
            jax.ShapeDtypeStruct((n_fsdp, *tokens.shape), tokens.dtype),
            jax.ShapeDtypeStruct((n_fsdp, *codes.shape), codes.dtype),
            jax.ShapeDtypeStruct((n_fsdp, images, wide), jnp.float32),
            jax.ShapeDtypeStruct(condition.shape, condition.dtype),
            jax.ShapeDtypeStruct((n_dp, *qkv.shape), qkv.dtype),
            jax.ShapeDtypeStruct((n_dp, *out_w.shape), out_w.dtype),
        ],
        in_specs=[HBM, HBM, WHOLE, WHOLE, HBM, HBM],
        out_specs=[HBM, HBM, HBM, WHOLE, HBM, HBM],
        scratch_shapes=[
            pltpu.VMEM((n_dp, images, wide), jnp.float32),
            pltpu.VMEM((n_dp, images, wide), jnp.float32),
            pltpu.VMEM((images, wide), jnp.float32),
            *line, *line, *line, *grid, *grid, *direct, *direct,
        ],
        compiler_params=pltpu.CompilerParams(
            collective_id=0, has_side_effects=True, vmem_limit_bytes=VMEM_LIMIT
        ),
    )(tokens, codes, condition, ada, qkv, out_w)


def modulation_grad_kernel(n_dp, n_fsdp, grad_mods):
    rows = grad_mods.shape[1]

    def kernel(src, out, ss, rs, ds, dr):
        place = Place(n_dp, n_fsdp)
        barrier = pltpu.get_barrier_semaphore()
        for i in range(1, n_dp):
            pl.semaphore_signal(
                barrier, inc=1, device_id=place.at_dp((place.dp + i) % n_dp), device_id_type=MESH
            )
        for i in range(1, n_fsdp):
            pl.semaphore_signal(
                barrier, inc=1, device_id=(place.dp, (place.f + i) % n_fsdp), device_id_type=MESH
            )
        pl.semaphore_wait(barrier, n_dp + n_fsdp - 2)
        mine = out.at[place.dp]
        inner = Direct(place, src, mine, (ss, rs), axis="fsdp")
        inner.start()
        mine[place.f] = src[place.f]
        inner.finish()
        outer = Direct(place, mine, out, (ds, dr), whole=True)
        outer.start()
        outer.finish()

    return pl.pallas_call(
        kernel,
        out_shape=jax.ShapeDtypeStruct((n_dp, n_fsdp, rows, 128), grad_mods.dtype),
        in_specs=[WHOLE],
        out_specs=WHOLE,
        scratch_shapes=Direct.scratch(n_fsdp) + Direct.scratch(n_dp),
        compiler_params=pltpu.CompilerParams(
            collective_id=1, has_side_effects=True, vmem_limit_bytes=VMEM_LIMIT
        ),
    )(grad_mods)


def normalize(values):
    average = jnp.mean(values, axis=-1, keepdims=True)
    centred = values - average
    inv_std = lax.rsqrt(jnp.mean(centred * centred, axis=-1, keepdims=True) + NORM_EPS)
    return (centred * inv_std, inv_std)


def normalize_back(grad, normed, inv_std):
    return inv_std * (
        grad
        - jnp.mean(grad, axis=-1, keepdims=True)
        - normed * jnp.mean(grad * normed, axis=-1, keepdims=True)
    )


def split_heads(qkv_low, tok_rows):
    heads_here = qkv_low.shape[1] // (3 * HEAD)
    split = qkv_low.reshape(-1, tok_rows, 3, heads_here, HEAD)
    return split[:, :, 0], split[:, :, 1], split[:, :, 2]


def masked_scores(queries, keys_part, allowed):
    scores = jnp.einsum(
        "bqhe,bkhe->bhqk", queries, keys_part, preferred_element_type=jnp.float32
    ) * HEAD ** (-0.5)
    return jnp.where(allowed[:, None], scores, -1e30)


def attention_forward(qkv_low, allowed, tok_rows):
    queries, keys_part, values_part = split_heads(qkv_low, tok_rows)
    scores = masked_scores(queries, keys_part, allowed)
    row_max = jnp.max(scores, axis=-1, keepdims=True)
    raw_exp = jnp.exp(scores - row_max)
    attn_probs = raw_exp / jnp.sum(raw_exp, axis=-1, keepdims=True)
    probs_low = attn_probs.astype(jnp.bfloat16)
    attended = jnp.einsum(
        "bhqk,bkhe->bqhe", probs_low, values_part, preferred_element_type=jnp.float32
    )
    return attended.reshape(qkv_low.shape[0], -1).astype(jnp.bfloat16), attn_probs


def attention_backward(qkv_low, attn_probs, tok_rows, grad_heads):
    queries, keys_part, values_part = split_heads(qkv_low, tok_rows)
    probs_low = attn_probs.astype(jnp.bfloat16)
    grad_out = grad_heads.reshape(queries.shape)
    grad_p = jnp.einsum(
        "bqhe,bkhe->bhqk", grad_out, values_part, preferred_element_type=jnp.float32
    )
    row_delta = jnp.sum(attn_probs * grad_p, axis=-1, keepdims=True)
    grad_scores = (attn_probs * (grad_p - row_delta)).astype(jnp.bfloat16)
    scale = HEAD ** (-0.5)
    grad_query = (
        jnp.einsum("bhqk,bkhe->bqhe", grad_scores, keys_part, preferred_element_type=jnp.float32)
        * scale
    )
    grad_key = (
        jnp.einsum("bhqk,bqhe->bkhe", grad_scores, queries, preferred_element_type=jnp.float32)
        * scale
    )
    grad_value = jnp.einsum(
        "bhqk,bqhe->bkhe", probs_low, grad_out, preferred_element_type=jnp.float32
    )
    stacked = jnp.stack([grad_query, grad_key, grad_value], axis=2)
    return stacked.reshape(qkv_low.shape).astype(jnp.bfloat16)


def contract_rows(left, right):
    return lax.dot_general(
        left, right, (((0,), (0,)), ((), ())), preferred_element_type=jnp.float32
    )


def contract_last(left, right):
    return lax.dot_general(
        left, right, (((1,), (1,)), ((), ())), preferred_element_type=jnp.float32
    )


def body(n_dp, n_fsdp, *arguments):
    tokens, embedding, image_slot, token_mask, cotangent = arguments[:5]
    masters, firsts, seconds = arguments[5:10], arguments[10:15], arguments[15:20]
    qkv_w, out_w, up_w, down_w, ada_w = masters
    low = jnp.bfloat16
    micro, tok_rows, width = tokens.shape
    own_rows = micro * tok_rows
    group_rows = own_rows * n_fsdp
    image_count = embedding.shape[1] // n_fsdp
    deep = embedding.shape[2]
    f = lax.axis_index("fsdp")

    condition = jax.nn.silu(embedding.astype(jnp.float32)).astype(low)
    condition = condition.reshape(micro, n_fsdp, image_count, deep).transpose(1, 0, 2, 3)
    images = n_fsdp * micro * image_count
    condition = condition.reshape(images, n_dp, deep // n_dp).transpose(1, 0, 2)

    own_tokens = tokens.reshape(own_rows, width)
    codes = jnp.stack([image_slot.reshape(own_rows), token_mask.reshape(own_rows)]).astype(jnp.float32)
    codes = jnp.pad(codes, ((0, 6), (0, 0)))
    qkv_low_w = qkv_w.astype(low).reshape(qkv_w.shape[0], -1)
    ada_low_w = ada_w.astype(low).reshape(ada_w.shape[0], -1)

    tok_g, codes_g, mods_g, cond_all, qkv_g, out_g = modulation_kernel(
        n_dp, n_fsdp, own_tokens, codes, condition, ada_low_w, qkv_low_w, out_w.astype(low)
    )
    qkv_g = qkv_g.reshape(width, -1)
    out_g = out_g.reshape(width, -1)

    mods = mods_g.reshape(n_fsdp, n_fsdp, micro, image_count, MODS, -1)
    mods = mods.transpose(1, 2, 3, 4, 0, 5).reshape(n_fsdp, micro, image_count, MODS, width)
    slot_g = codes_g[:, 0].reshape(n_fsdp, micro, tok_rows)
    live_g = codes_g[:, 1].reshape(n_fsdp, micro, tok_rows)

    def pick(table, slots):
        picked = table[..., 0:1, :]
        for i in range(1, image_count):
            picked = jnp.where(slots[..., None] == i, table[..., i : i + 1, :], picked)
        return picked

    mods_own = lax.dynamic_index_in_dim(mods, f, 0, keepdims=False)
    slots = image_slot.astype(jnp.float32)
    shift1, scale1, gate1, shift2, scale2, gate2 = [pick(mods_own[:, :, j], slots) for j in range(MODS)]

    normed1_g, _ = normalize(tok_g.reshape(n_fsdp, micro, tok_rows, width).astype(jnp.float32))
    hidden1_g = normed1_g * (1.0 + pick(mods[:, :, :, 1], slot_g)) + pick(mods[:, :, :, 0], slot_g)
    hidden1_g = hidden1_g.astype(low).reshape(group_rows, width)

    same = slot_g[:, :, :, None] == slot_g[:, :, None, :]
    allowed = (same & (live_g[:, :, None, :] > 0.5)) | jnp.eye(tok_rows, dtype=bool)
    allowed = allowed.reshape(-1, tok_rows, tok_rows)

    qkv_low = jnp.dot(hidden1_g, qkv_g, preferred_element_type=jnp.float32).astype(low)
    attended, attn_probs = attention_forward(qkv_low, allowed, tok_rows)
    attn_part = contract_last(attended, out_g).astype(low).reshape(n_fsdp, own_rows, width)

    attn_own, cot_g, up_g = transfer(
        2, n_dp, n_fsdp,
        [(LineScatter, attn_part), (LineGather, cotangent.reshape(own_rows, width)), (GridGather, up_w.astype(low))],
    )
    up_g = up_g.reshape(width, -1)
    attn_own = attn_own.reshape(micro, tok_rows, width)
    inputs = tokens.astype(jnp.float32)
    mid = inputs + gate1 * attn_own
    normed2, inv_std2 = normalize(mid)
    hidden2 = (normed2 * (1.0 + scale2) + shift2).astype(low)

    hidden2_g, down_g = transfer(
        3, n_dp, n_fsdp, [(LineGather, hidden2.reshape(own_rows, width)), (GridGather, down_w.astype(low))]
    )
    hidden2_g = hidden2_g.reshape(group_rows, width)
    down_g = down_g.reshape(width, -1)

    grad_mlp_g = cot_g.reshape(n_fsdp, micro, tok_rows, width).astype(jnp.float32) * live_g[..., None]
    grad_mlp_g = (grad_mlp_g * pick(mods[:, :, :, 5], slot_g)).astype(low).reshape(group_rows, width)
    upper = jnp.dot(hidden2_g, up_g, preferred_element_type=jnp.float32)
    activ_full, gelu_pull = jax.vjp(jax.nn.gelu, upper)
    activ = activ_full.astype(low)
    grad_act = jnp.dot(grad_mlp_g, down_g, preferred_element_type=jnp.float32)
    grad_upper = gelu_pull(grad_act)[0].astype(low)
    grad_h2_part = contract_last(grad_upper, up_g).astype(low).reshape(n_fsdp, own_rows, width)
    mlp_part = contract_last(activ, down_g).astype(low).reshape(n_fsdp, own_rows, width)
    grad_down = contract_rows(grad_mlp_g, activ).astype(low).reshape(n_dp, -1, activ.shape[1])
    grad_up = contract_rows(hidden2_g, grad_upper).astype(low).reshape(n_dp, -1, activ.shape[1])

    grad_h2, grad_down = transfer(4, n_dp, n_fsdp, [(LineScatter, grad_h2_part), (GridScatter, grad_down)])
    grad_h2 = grad_h2.reshape(micro, tok_rows, width)
    live = token_mask.astype(jnp.float32)[..., None]
    grad_y = cotangent.astype(jnp.float32) * live
    grad_mid = grad_y + normalize_back(grad_h2 * (1.0 + scale2), normed2, inv_std2)
    grad_attn = (grad_mid * gate1).astype(low)

    mlp_own, grad_attn_g, grad_up = transfer(
        5, n_dp, n_fsdp,
        [(LineScatter, mlp_part), (LineGather, grad_attn.reshape(own_rows, width)), (GridScatter, grad_up)],
    )
    mlp_own = mlp_own.reshape(micro, tok_rows, width)
    block_out = (mid + gate2 * mlp_own).astype(low)

    grad_attn_g = grad_attn_g.reshape(group_rows, width)
    grad_heads = jnp.dot(grad_attn_g, out_g, preferred_element_type=jnp.float32).astype(low)
    grad_out = contract_rows(grad_attn_g, attended).astype(low).reshape(n_dp, -1, attended.shape[1])
    grad_qkv = attention_backward(qkv_low, attn_probs, tok_rows, grad_heads)
    grad_h1_part = contract_last(grad_qkv, qkv_g).astype(low).reshape(n_fsdp, own_rows, width)
    grad_qkv_w = contract_rows(hidden1_g, grad_qkv).astype(low).reshape(n_dp, -1, grad_qkv.shape[1])

    grad_h1, grad_qkv_w, grad_out = transfer(
        6, n_dp, n_fsdp, [(LineScatter, grad_h1_part), (GridScatter, grad_qkv_w), (GridScatter, grad_out)]
    )
    grad_h1 = grad_h1.reshape(micro, tok_rows, width)
    normed1, inv_std1 = normalize(inputs)
    input_grad = grad_mid + normalize_back(grad_h1 * (1.0 + scale1), normed1, inv_std1)

    terms = (grad_h1, grad_h1 * normed1, grad_mid * attn_own, grad_h2, grad_h2 * normed2, grad_y * mlp_own)
    grad_mods = []
    for i in range(image_count):
        chosen = (image_slot == i).astype(jnp.float32)[..., None]
        grad_mods.append(jnp.stack([jnp.sum(term * chosen, axis=1) for term in terms], axis=1))
    grad_mods = jnp.stack(grad_mods, axis=1).astype(low).astype(jnp.float32)
    grad_mods = grad_mods.reshape(micro * image_count, MODS, n_fsdp, -1).transpose(2, 0, 1, 3)
    columns = grad_mods.shape[-1]
    all_mods = modulation_grad_kernel(n_dp, n_fsdp, grad_mods.reshape(n_fsdp, -1, 128))
    all_mods = all_mods.reshape(n_dp * images, MODS * columns).astype(low)
    grad_ada = contract_rows(cond_all.reshape(n_dp * images, -1), all_mods)

    grads = (grad_qkv_w, grad_out, grad_down, grad_up, grad_ada)
    local_squares = jnp.float32(0.0)
    for total in grads:
        local_squares = local_squares + jnp.sum(total * total)
    grad_norm = jnp.sqrt(lax.psum(local_squares, ("dp", "fsdp")))
    factor = jnp.minimum(1.0, CLIP_AT / grad_norm)
    results = []
    for master, first, second, total in zip(masters, firsts, seconds, (grad_qkv_w, grad_out, grad_up, grad_down, grad_ada)):
        clipped = total.reshape(master.shape) * factor
        moment = BETA_ONE * first + (1.0 - BETA_ONE) * clipped
        square = BETA_TWO * second + (1.0 - BETA_TWO) * clipped * clipped
        ratio = (
            moment / (1.0 - BETA_ONE**STEP) / (jnp.sqrt(square / (1.0 - BETA_TWO**STEP)) + ADAM_EPS)
        )
        new_master = master - LEARN_RATE * (ratio + WEIGHT_DECAY * master)
        results.extend([new_master, new_master.astype(low), moment, square])
    return (block_out, input_grad, *results, grad_norm)


def solution(mesh):
    n_dp, n_fsdp = mesh.shape["dp"], mesh.shape["fsdp"]
    rows = P(None, ("dp", "fsdp"), None)
    slots = P(None, ("dp", "fsdp"))
    thick = P("dp", None, "fsdp")
    flat = P("dp", "fsdp")
    weights = (thick, flat, flat, flat, thick)
    updated = tuple(spec for spec in weights for _ in range(4))
    return jax.shard_map(
        functools.partial(body, n_dp, n_fsdp),
        mesh=mesh,
        in_specs=(rows, P(None, "dp", None), slots, slots, rows, *weights, *weights, *weights),
        out_specs=(rows, rows, *updated, P()),
        check_vma=False,
    )
```

```python
import functools

import jax
import jax.numpy as jnp
from jax import lax
from jax.experimental import pallas as pl
from jax.experimental.pallas import tpu as pltpu
from jax.sharding import PartitionSpec as P

HEAD = 128
STEP = 10
MODS = 6

NORM_EPS = 1e-06
CLIP_AT = 1.0
BETA_ONE = 0.9
BETA_TWO = 0.999
LEARN_RATE = 0.05
WEIGHT_DECAY = 0.1
ADAM_EPS = 1e-08

MESH = pl.DeviceIdType.MESH
VMEM_LIMIT = 48 * 1024 * 1024
ROW_STEP = 16


class Place:
    def __init__(self, n_dp, n_fsdp):
        self.n_dp, self.n_fsdp = n_dp, n_fsdp
        self.chips = n_fsdp // 2
        self.grid_a = 2
        self.grid_b = n_dp // 2
        self.dp = lax.axis_index("dp")
        self.f = lax.axis_index("fsdp")
        self.p = self.f // 2
        self.c = self.f % 2
        self.a = self.dp // self.grid_b
        self.b = self.dp % self.grid_b

    def at_chip(self, chip):
        return (self.dp, chip * 2 + self.c)

    def sibling(self):
        return (self.dp, self.p * 2 + 1 - self.c)

    def at_dp(self, dp):
        return (dp, self.f)

    def b_peer(self, i):
        return (self.b + i) % self.grid_b

    def a_peer(self, i):
        return (self.a + i) % self.grid_a


def enter(place, line=False, grid=False):
    barrier = pltpu.get_barrier_semaphore()
    devices = []
    if line:
        devices.append(place.at_chip((place.p + 1) % place.chips))
        devices.append(place.at_chip((place.p + place.chips - 1) % place.chips))
        devices.append(place.sibling())
    if grid:
        for i in range(1, place.n_dp):
            devices.append(place.at_dp((place.dp + i) % place.n_dp))
    for device in devices:
        pl.semaphore_signal(barrier, inc=1, device_id=device, device_id_type=MESH)
    pl.semaphore_wait(barrier, len(devices))


def remote(src, dst, send, recv, device):
    return pltpu.make_async_remote_copy(
        src_ref=src, dst_ref=dst, send_sem=send, recv_sem=recv, device_id=device, device_id_type=MESH
    )


class LineGather:
    @staticmethod
    def scratch(n_fsdp):
        chips = n_fsdp // 2
        return [
            pltpu.SemaphoreType.DMA((2, chips)),
            pltpu.SemaphoreType.DMA((2, chips)),
            pltpu.SemaphoreType.DMA((chips,)),
            pltpu.SemaphoreType.DMA((chips,)),
            pltpu.SemaphoreType.DMA,
        ]

    def __init__(self, place, src, out, sems, block=None):
        self.place, self.src, self.out = place, src, out
        self.send, self.recv, self.csend, self.crecv, self.local = sems
        self.of = block or (lambda ref, d: ref.at[d])

    def _block(self, chip):
        return self.of(self.out, chip * 2 + self.place.c)

    def _hop(self, way, step, first):
        pc = self.place
        chip = pc.p - step if way == 0 else pc.p + step
        target = pc.p + 1 if way == 0 else pc.p - 1
        src = self.src if first else self._block(chip)
        return remote(src, self._block(chip), self.send.at[way, step], self.recv.at[way, step], pc.at_chip(target))

    def _side(self, chip, first=False):
        src = self.src if first else self._block(chip)
        return remote(src, self._block(chip), self.csend.at[chip], self.crecv.at[chip], self.place.sibling())

    def _sends(self, way, step):
        pc = self.place
        if way == 0:
            return (pc.p < pc.chips - 1) & (pc.p >= step)
        return (pc.p > 0) & (pc.p + step <= pc.chips - 1)

    def start(self):
        pc = self.place
        for way in range(2):
            @pl.when(self._sends(way, 0))
            def _():
                self._hop(way, 0, True).start()
        self._side(pc.p, True).start()
        pltpu.make_async_copy(self.src, self._block(pc.p), self.local).start()

    def step(self, step):
        pc = self.place
        for way in range(2):
            chip = pc.p - step if way == 0 else pc.p + step
            here = (chip >= 0) if way == 0 else (chip <= pc.chips - 1)

            @pl.when(here)
            def _():
                remote(
                    self._block(chip), self._block(chip), self.send.at[way, step - 1], self.recv.at[way, step - 1],
                    pc.sibling(),
                ).wait_recv()
                if step < pc.chips - 1:
                    @pl.when(self._sends(way, step))
                    def _():
                        self._hop(way, step, False).start()
                self._side(chip).start()

    def finish(self):
        pc = self.place
        pltpu.make_async_copy(self.src, self._block(pc.p), self.local).wait()
        for chip in range(pc.chips):
            other = self.of(self.out, chip * 2 + 1 - pc.c)
            remote(other, other, self.csend.at[chip], self.crecv.at[chip], pc.sibling()).wait_recv()
            self._side(chip).wait_send()
        for way in range(2):
            for step in range(pc.chips - 1):
                @pl.when(self._sends(way, step))
                def _():
                    self._hop(way, step, False).wait_send()

    def steps(self):
        return [self.start] + [functools.partial(self.step, s) for s in range(1, self.place.chips)] + [self.finish]


def row_loop(rows, body, first=0):
    def run(i, carry):
        body(pl.ds(pl.multiple_of(first + i * ROW_STEP, ROW_STEP), ROW_STEP))
        return carry

    lax.fori_loop(0, rows // ROW_STEP, run, 0)


class LineScatter:
    pieces = 4

    @classmethod
    def scratch(cls, n_fsdp, rows, width):
        chips = n_fsdp // 2
        return [
            pltpu.VMEM((chips, rows, width), jnp.bfloat16),
            pltpu.VMEM((chips, rows, width), jnp.bfloat16),
            pltpu.VMEM((2, chips, rows, width), jnp.bfloat16),
            pltpu.SemaphoreType.DMA((chips,)),
            pltpu.SemaphoreType.DMA((chips,)),
            pltpu.SemaphoreType.DMA((2, chips, cls.pieces)),
            pltpu.SemaphoreType.DMA((2, chips, cls.pieces)),
        ]

    def __init__(self, place, part, out, scratch):
        self.place, self.part, self.out = place, part, out
        self.side, self.total, self.inbox, self.csend, self.crecv, self.send, self.recv = scratch
        self.rows = out.shape[0]
        self.piece = self.rows // self.pieces
        self.lag = 2
        self.slots = (place.chips - 1) * self.lag + place.chips * self.pieces

    def _side(self, chip):
        pc = self.place
        return remote(
            self.part.at[chip * 2 + 1 - pc.c], self.side.at[chip], self.csend.at[chip], self.crecv.at[chip], pc.sibling()
        )

    def _hop(self, way, chip, s):
        pc = self.place
        target = pc.p + 1 if way == 0 else pc.p - 1
        rows = pl.ds(pl.multiple_of(s * self.piece, self.piece), self.piece)
        return remote(
            self.total.at[chip, rows], self.inbox.at[way, chip, rows], self.send.at[way, chip, s],
            self.recv.at[way, chip, s], pc.at_chip(target),
        )

    def start(self):
        chips = self.place.chips
        order = []
        for k in range(chips):
            for chip in (chips - 1 - k, k):
                if chip not in order:
                    order.append(chip)
        for chip in order:
            self._side(chip).start()

    def _add(self, chip, s, inboxes, store):
        pc = self.place

        def add(rows):
            total = self.part[chip * 2 + pc.c, rows, :].astype(jnp.float32)
            total = total + self.side[chip, rows, :].astype(jnp.float32)
            for way in inboxes:
                total = total + self.inbox[way, chip, rows, :].astype(jnp.float32)
            store(rows, total)

        row_loop(self.piece, add, s * self.piece)

    def _travel(self, way, t):
        pc = self.place
        chips = pc.chips
        i = t - (pc.p if way == 0 else chips - 1 - pc.p) * self.lag
        k = jnp.clip(i // self.pieces, 0, chips - 1)
        s = lax.rem(jnp.maximum(i, 0), self.pieces)
        chip = chips - 1 - k if way == 0 else k
        going = (i >= 0) & (i < chips * self.pieces) & ((chip > pc.p) if way == 0 else (chip < pc.p))
        first = (pc.p == 0) if way == 0 else (pc.p == chips - 1)

        def store(rows, total):
            self.total[chip, rows, :] = total.astype(jnp.bfloat16)

        @pl.when(going)
        def _():
            @pl.when(s == 0)
            def _():
                self._side(chip).wait_recv()

            @pl.when(first)
            def _():
                self._add(chip, s, (), store)

            @pl.when(jnp.logical_not(first))
            def _():
                self._hop(way, chip, s).wait_recv()
                self._add(chip, s, (way,), store)

            self._hop(way, chip, s).start()

    def step(self, t):
        self._travel(0, t)
        self._travel(1, t)

    def run(self, begin, end):
        def one(t, carry):
            self.step(t)
            return carry

        lax.fori_loop(begin, end, one, 0)

    def finish(self):
        pc = self.place
        chips = pc.chips
        self._side(pc.p).wait_recv()

        def store(rows, total):
            self.out[rows, :] = total

        def piece(s, carry):
            @pl.when(pc.p == 0)
            def _():
                self._hop(1, pc.p, s).wait_recv()
                self._add(pc.p, s, (1,), store)

            @pl.when(pc.p == chips - 1)
            def _():
                self._hop(0, pc.p, s).wait_recv()
                self._add(pc.p, s, (0,), store)

            @pl.when((pc.p > 0) & (pc.p < chips - 1))
            def _():
                self._hop(0, pc.p, s).wait_recv()
                self._hop(1, pc.p, s).wait_recv()
                self._add(pc.p, s, (0, 1), store)

            return carry

        lax.fori_loop(0, self.pieces, piece, 0)
        for chip in range(chips):
            self._side(chip).wait_send()

            def sent(s, carry):
                @pl.when(chip > pc.p)
                def _():
                    self._hop(0, chip, s).wait_send()

                @pl.when(chip < pc.p)
                def _():
                    self._hop(1, chip, s).wait_send()

                return carry

            lax.fori_loop(0, self.pieces, sent, 0)

    def steps(self):
        third = self.slots // 3
        cuts = [0, third, 2 * third, self.slots]
        return [self.start] + [functools.partial(self.run, a, b) for a, b in zip(cuts, cuts[1:])] + [self.finish]


class GridGather:
    @staticmethod
    def scratch(n_dp):
        na, nb = 2, n_dp // 2
        return [
            pltpu.SemaphoreType.DMA((2, max(nb - 1, 1))),
            pltpu.SemaphoreType.DMA((2, max(nb - 1, 1))),
            pltpu.SemaphoreType.DMA((2, na - 1)),
            pltpu.SemaphoreType.DMA((2, na - 1)),
            pltpu.SemaphoreType.DMA((2, max(nb - 1, 1), na - 1)),
            pltpu.SemaphoreType.DMA((2, max(nb - 1, 1), na - 1)),
            pltpu.SemaphoreType.DMA,
        ]

    def __init__(self, place, src, out, sems):
        self.place, self.src, self.out = place, src, out
        self.bsend, self.brecv, self.asend, self.arecv, self.fsend, self.frecv, self.local = sems
        self.half = src.shape[1] // 2

    def _own(self, h):
        return self.src.at[:, pl.ds(h * self.half, self.half)]

    def _block(self, a, b, h):
        return self.out.at[:, a * self.place.grid_b + b, pl.ds(h * self.half, self.half)]

    def _b_copy(self, i, h, coming):
        pc = self.place
        b = pc.b_peer(pc.grid_b - i) if coming else pc.b
        return remote(
            self._own(h), self._block(pc.a, b, h), self.bsend.at[h, i - 1], self.brecv.at[h, i - 1],
            pc.at_dp(pc.a * pc.grid_b + pc.b_peer(i)),
        )

    def _a_copy(self, i, h, coming):
        pc = self.place
        a = pc.a_peer(pc.grid_a - i) if coming else pc.a
        return remote(
            self._own(h), self._block(a, pc.b, h), self.asend.at[h, i - 1], self.arecv.at[h, i - 1],
            pc.at_dp(pc.a_peer(i) * pc.grid_b + pc.b),
        )

    def _on(self, h, ib, ia, coming):
        pc = self.place
        if h == 0:
            b = pc.b_peer(pc.grid_b - ib)
            a = pc.a_peer(pc.grid_a - ia) if coming else pc.a
            target = pc.at_dp(pc.a_peer(ia) * pc.grid_b + pc.b)
        else:
            a = pc.a_peer(pc.grid_a - ia)
            b = pc.b_peer(pc.grid_b - ib) if coming else pc.b
            target = pc.at_dp(pc.a * pc.grid_b + pc.b_peer(ib))
        block = self._block(a, b, h)
        return remote(block, block, self.fsend.at[h, ib - 1, ia - 1], self.frecv.at[h, ib - 1, ia - 1], target)

    def start(self):
        pc = self.place
        for h in range(2):
            for i in range(1, pc.grid_b):
                self._b_copy(i, h, False).start()
            for i in range(1, pc.grid_a):
                self._a_copy(i, 1 - h, False).start()
        pltpu.make_async_copy(self.src, self.out.at[:, pc.dp], self.local).start()

    def step(self):
        pc = self.place
        for ib in range(1, pc.grid_b):
            self._b_copy(ib, 0, True).wait_recv()
            for ia in range(1, pc.grid_a):
                self._on(0, ib, ia, False).start()
        for ia in range(1, pc.grid_a):
            self._a_copy(ia, 1, True).wait_recv()
            for ib in range(1, pc.grid_b):
                self._on(1, ib, ia, False).start()

    def finish(self):
        pc = self.place
        pltpu.make_async_copy(self.src, self.out.at[:, pc.dp], self.local).wait()
        for ib in range(1, pc.grid_b):
            self._b_copy(ib, 1, True).wait_recv()
        for ia in range(1, pc.grid_a):
            self._a_copy(ia, 0, True).wait_recv()
        for h in range(2):
            for ib in range(1, pc.grid_b):
                for ia in range(1, pc.grid_a):
                    self._on(h, ib, ia, True).wait_recv()
                    self._on(h, ib, ia, False).wait_send()
        for h in range(2):
            for ib in range(1, pc.grid_b):
                self._b_copy(ib, h, False).wait_send()
            for ia in range(1, pc.grid_a):
                self._a_copy(ia, h, False).wait_send()

    def steps(self):
        return [self.start, self.step, self.finish]


class GridScatter:
    @staticmethod
    def scratch(n_dp, which, rows, width):
        na, nb = 2, n_dp // 2
        half = rows // 2
        most = max(nb - 1, 1)
        return [
            pltpu.VMEM((most, na, which, half, width), jnp.bfloat16),
            pltpu.VMEM((na - 1, nb, which, half, width), jnp.bfloat16),
            pltpu.VMEM((na - 1, which, half, width), jnp.bfloat16),
            pltpu.VMEM((most, which, half, width), jnp.bfloat16),
            pltpu.VMEM((na - 1, which, half, width), jnp.bfloat16),
            pltpu.VMEM((most, which, half, width), jnp.bfloat16),
            pltpu.SemaphoreType.DMA((most, na)),
            pltpu.SemaphoreType.DMA((most, na)),
            pltpu.SemaphoreType.DMA((na - 1, nb)),
            pltpu.SemaphoreType.DMA((na - 1, nb)),
            pltpu.SemaphoreType.DMA((na - 1,)),
            pltpu.SemaphoreType.DMA((na - 1,)),
            pltpu.SemaphoreType.DMA((most,)),
            pltpu.SemaphoreType.DMA((most,)),
        ]

    def __init__(self, place, part, out, squares, scratch):
        self.place, self.part, self.out, self.squares = place, part, out, squares
        self.box_b, self.box_a, self.sum_b, self.sum_a, self.end_a, self.end_b = scratch[:6]
        self.bs, self.br, self.as_, self.ar, self.eas, self.ear, self.ebs, self.ebr = scratch[6:]
        self.which = out.shape[0]
        self.half = out.shape[1] // 2

    def _part(self, a, b, h):
        return self.part.at[:, a * self.place.grid_b + b, pl.ds(h * self.half, self.half)]

    def _first_b(self, i, j):
        pc = self.place
        return remote(
            self._part(pc.a_peer(j), pc.b_peer(i), 0), self.box_b.at[i - 1, j], self.bs.at[i - 1, j],
            self.br.at[i - 1, j], pc.at_dp(pc.a * pc.grid_b + pc.b_peer(i)),
        )

    def _first_a(self, i, j):
        pc = self.place
        return remote(
            self._part(pc.a_peer(i), pc.b_peer(j), 1), self.box_a.at[i - 1, j], self.as_.at[i - 1, j],
            self.ar.at[i - 1, j], pc.at_dp(pc.a_peer(i) * pc.grid_b + pc.b),
        )

    def _second_a(self, i):
        pc = self.place
        return remote(
            self.sum_b.at[i - 1], self.end_a.at[i - 1], self.eas.at[i - 1], self.ear.at[i - 1],
            pc.at_dp(pc.a_peer(i) * pc.grid_b + pc.b),
        )

    def _second_b(self, i):
        pc = self.place
        return remote(
            self.sum_a.at[i - 1], self.end_b.at[i - 1], self.ebs.at[i - 1], self.ebr.at[i - 1],
            pc.at_dp(pc.a * pc.grid_b + pc.b_peer(i)),
        )

    def _firsts_b(self):
        pc = self.place
        return [(i, j) for j in list(range(1, pc.grid_a)) + [0] for i in range(1, pc.grid_b)]

    def _firsts_a(self):
        pc = self.place
        return [(i, j) for j in list(range(1, pc.grid_b)) + [0] for i in range(1, pc.grid_a)]

    def start(self):
        for (ib, jb), (ia, ja) in zip(self._firsts_b(), self._firsts_a(), strict=False):
            self._first_b(ib, jb).start()
            self._first_a(ia, ja).start()
        shared = min(len(self._firsts_b()), len(self._firsts_a()))
        for i, j in self._firsts_b()[shared:]:
            self._first_b(i, j).start()
        for i, j in self._firsts_a()[shared:]:
            self._first_a(i, j).start()

    def _low(self, rows):
        return pl.ds(pl.multiple_of(self.half + rows.start, ROW_STEP), ROW_STEP)

    def _sum_b(self, j):
        pc = self.place
        for i in range(1, pc.grid_b):
            self._first_b(i, j).wait_recv()
        mine = pc.a_peer(j) * pc.grid_b + pc.b

        def add(rows):
            for w in range(self.which):
                total = self.part[w, mine, rows, :].astype(jnp.float32)
                for i in range(1, pc.grid_b):
                    total = total + self.box_b[i - 1, j, w, rows, :].astype(jnp.float32)
                if j == 0:
                    self.out[w, rows, :] = total
                else:
                    self.sum_b[j - 1, w, rows, :] = total.astype(jnp.bfloat16)

        row_loop(self.half, add)
        if j:
            self._second_a(j).start()

    def _sum_a(self, j):
        pc = self.place
        for i in range(1, pc.grid_a):
            self._first_a(i, j).wait_recv()
        mine = pc.a * pc.grid_b + pc.b_peer(j)

        def add(rows):
            for w in range(self.which):
                total = self.part[w, mine, self._low(rows), :].astype(jnp.float32)
                for i in range(1, pc.grid_a):
                    total = total + self.box_a[i - 1, j, w, rows, :].astype(jnp.float32)
                if j == 0:
                    self.out[w, self._low(rows), :] = total
                else:
                    self.sum_a[j - 1, w, rows, :] = total.astype(jnp.bfloat16)

        row_loop(self.half, add)
        if j:
            self._second_b(j).start()

    def step(self):
        pc = self.place
        for j in range(1, max(pc.grid_a, pc.grid_b)):
            if j < pc.grid_a:
                self._sum_b(j)
            if j < pc.grid_b:
                self._sum_a(j)

    def step_own(self):
        self._sum_b(0)
        self._sum_a(0)

    def finish(self):
        pc = self.place
        for i in range(1, pc.grid_a):
            self._second_a(i).wait_recv()
        for i in range(1, pc.grid_b):
            self._second_b(i).wait_recv()
        self.squares[...] = jnp.zeros_like(self.squares)

        def tile(total):
            total = total * total
            folded = total[:, :128]
            for at in range(128, total.shape[1], 128):
                folded = folded + total[:, at : at + 128]
            return folded

        def add(rows):
            low = self._low(rows)
            for w in range(self.which):
                total = self.out[w, rows, :]
                for i in range(1, pc.grid_a):
                    total = total + self.end_a[i - 1, w, rows, :].astype(jnp.float32)
                self.out[w, rows, :] = total
                self.squares[...] += tile(total)
                total = self.out[w, low, :]
                for i in range(1, pc.grid_b):
                    total = total + self.end_b[i - 1, w, rows, :].astype(jnp.float32)
                self.out[w, low, :] = total
                self.squares[...] += tile(total)

        row_loop(self.half, add)
        for i, j in self._firsts_b():
            self._first_b(i, j).wait_send()
        for i, j in self._firsts_a():
            self._first_a(i, j).wait_send()
        for i in range(1, pc.grid_a):
            self._second_a(i).wait_send()
        for i in range(1, pc.grid_b):
            self._second_b(i).wait_send()

    def steps(self):
        return [self.start, self.step, self.step_own, self.finish]


class Direct:
    @staticmethod
    def scratch(n):
        return [pltpu.SemaphoreType.DMA((n - 1,)), pltpu.SemaphoreType.DMA((n - 1,))]

    def __init__(self, place, src, out, sems, axis="dp", block=None):
        self.place, self.src, self.out = place, src, out
        self.send, self.recv = sems
        self.n = place.n_dp if axis == "dp" else place.n_fsdp
        self.me = place.dp if axis == "dp" else place.f
        self.axis = axis
        self.of = block or (lambda ref, d: ref)

    def _device(self, other):
        return self.place.at_dp(other) if self.axis == "dp" else (self.place.dp, other)

    def _copy(self, i, coming=False):
        other = (self.me + i) % self.n
        origin = (self.me + self.n - i) % self.n if coming else self.me
        return remote(
            self.of(self.src, other), self.out.at[origin], self.send.at[i - 1], self.recv.at[i - 1], self._device(other)
        )

    def start(self):
        for i in range(1, self.n):
            self._copy(i).start()

    def finish(self):
        for i in range(1, self.n):
            self._copy(i, True).wait_recv()
            self._copy(i).wait_send()


def split_refs(refs, counts):
    out, at = [], 0
    for count in counts:
        out.append(refs[at : at + count])
        at += count
    return out


HBM = pl.BlockSpec(memory_space=pl.ANY)
WHOLE = pl.BlockSpec(memory_space=pltpu.VMEM)
TILE = (ROW_STEP, 128)


def parameters(collective_id):
    return pltpu.CompilerParams(collective_id=collective_id, has_side_effects=True, vmem_limit_bytes=VMEM_LIMIT)


def transfer(collective_id, n_dp, n_fsdp, kinds):
    in_specs, out_specs, out_shape, scratch, counts, outs_of = [], [], [], [], [], []
    for kind, array in kinds:
        shapes = []
        if kind is LineGather:
            shapes.append(jax.ShapeDtypeStruct((n_fsdp, *array.shape), array.dtype))
            spec, got = HBM, kind.scratch(n_fsdp)
        elif kind is GridGather:
            shapes.append(jax.ShapeDtypeStruct((array.shape[0], n_dp, *array.shape[1:]), array.dtype))
            spec, got = HBM, kind.scratch(n_dp)
        elif kind is LineScatter:
            shapes.append(jax.ShapeDtypeStruct(array.shape[1:], jnp.float32))
            spec, got = WHOLE, kind.scratch(n_fsdp, *array.shape[1:])
        else:
            shape = (array.shape[0], *array.shape[2:])
            shapes.append(jax.ShapeDtypeStruct(shape, jnp.float32))
            shapes.append(jax.ShapeDtypeStruct(TILE, jnp.float32))
            spec, got = WHOLE, kind.scratch(n_dp, *shape)
        in_specs.append(spec)
        out_specs += [spec] * len(shapes)
        out_shape += shapes
        outs_of.append(len(shapes))
        scratch += got
        counts.append(len(got))
    has_line = any(kind in (LineGather, LineScatter) for kind, _ in kinds)
    has_grid = any(kind in (GridGather, GridScatter) for kind, _ in kinds)

    def kernel(*refs):
        count = len(kinds)
        ins, rest = refs[:count], refs[count:]
        outs = split_refs(rest[: sum(outs_of)], outs_of)
        scratches = split_refs(rest[sum(outs_of) :], counts)
        place = Place(n_dp, n_fsdp)
        enter(place, has_line, has_grid)
        work = [
            kind(place, ins[i], *outs[i], scratches[i]).steps() for i, (kind, _) in enumerate(kinds)
        ]
        for at in range(max(len(steps) for steps in work)):
            for steps in work:
                if at < len(steps) - 1:
                    steps[at]()
        for steps in work:
            steps[-1]()

    return pl.pallas_call(
        kernel,
        out_shape=out_shape,
        in_specs=in_specs,
        out_specs=out_specs,
        scratch_shapes=scratch,
        compiler_params=parameters(collective_id),
    )(*[array for _, array in kinds])


def modulation_kernel(n_dp, n_fsdp, tokens, codes, embedding, ada, qkv, out_w):
    images = embedding.shape[0]
    deep, wide = ada.shape[1:]
    line = LineGather.scratch(n_fsdp)
    grid = GridGather.scratch(n_dp)
    direct = Direct.scratch(n_dp)
    counts = [len(line)] * 3 + [len(grid)] * 2 + [len(direct)] * 2

    def kernel(tok, cod, emb, ada_ref, qkv_ref, out_ref, tok_g, cod_g, mods_g, cond_g, qkv_g, out_g, *rest):
        cond, parts, boxes, mods = rest[:4]
        sems = split_refs(rest[4:], counts)
        place = Place(n_dp, n_fsdp)
        enter(place, True, True)
        lines = [LineGather(place, tok, tok_g, sems[0]), LineGather(place, cod, cod_g, sems[1])]
        grids = [GridGather(place, qkv_ref, qkv_g, sems[3]), GridGather(place, out_ref, out_g, sems[4])]
        for gather in lines:
            gather.start()
        level = emb[...].astype(jnp.float32)
        level = (level / (1.0 + jnp.exp(-level))).astype(jnp.bfloat16)
        for d in range(n_dp):
            cond[d] = level[:, d * deep : (d + 1) * deep]
        conds = Direct(place, cond, cond_g, sems[5], block=lambda ref, d: ref.at[d])
        conds.start()
        grids[0].start()
        cond_g[place.dp] = cond[place.dp]
        conds.finish()
        for j in range(MODS):
            weight = ada_ref[j].astype(jnp.bfloat16)
            for d in range(n_dp):
                parts[d, j] = jnp.dot(cond_g[d], weight, preferred_element_type=jnp.float32)
        sums = Direct(place, parts, boxes, sems[6], block=lambda ref, d: ref.at[d])
        sums.start()
        sums.finish()
        for j in range(MODS):
            total = parts[place.dp, j]
            for i in range(1, n_dp):
                total = total + boxes[(place.dp + i) % n_dp, j]
            mods[j] = total
        last = LineGather(
            place, mods, mods_g, sems[2],
            block=lambda ref, d: ref.at[:, :, pl.ds(pl.multiple_of(d * wide, wide), wide)],
        )
        for gather in lines:
            gather.step(1)
        last.start()
        grids[0].step()
        grids[1].start()
        for step in range(2, place.chips):
            for gather in lines:
                gather.step(step)
            last.step(step - 1)
        last.step(place.chips - 1)
        grids[1].step()
        for gather in lines + [last] + grids:
            gather.finish()

    return pl.pallas_call(
        kernel,
        out_shape=[
            jax.ShapeDtypeStruct((n_fsdp, *tokens.shape), tokens.dtype),
            jax.ShapeDtypeStruct((n_fsdp, *codes.shape), codes.dtype),
            jax.ShapeDtypeStruct((MODS, images, wide * n_fsdp), jnp.float32),
            jax.ShapeDtypeStruct((n_dp, images, deep), jnp.bfloat16),
            jax.ShapeDtypeStruct((qkv.shape[0], n_dp, *qkv.shape[1:]), qkv.dtype),
            jax.ShapeDtypeStruct((out_w.shape[0], n_dp, *out_w.shape[1:]), out_w.dtype),
        ],
        in_specs=[HBM, HBM, WHOLE, WHOLE, HBM, HBM],
        out_specs=[HBM, HBM, HBM, WHOLE, HBM, HBM],
        scratch_shapes=[
            pltpu.VMEM((n_dp, images, deep), jnp.bfloat16),
            pltpu.VMEM((n_dp, MODS, images, wide), jnp.float32),
            pltpu.VMEM((n_dp, MODS, images, wide), jnp.float32),
            pltpu.VMEM((MODS, images, wide), jnp.float32),
            *line, *line, *line, *grid, *grid, *direct, *direct,
        ],
        compiler_params=parameters(0),
    )(tokens, codes, embedding, ada, qkv, out_w)


def norm_kernel(n_dp, n_fsdp, grad_mods, condition, squares):
    _, _, padded, wide = grad_mods.shape
    images, deep = condition.shape[1:]
    rows = images // n_fsdp

    def kernel(src, cond, squares_ref, grad, norm, boxes, mine, all_mods, tile, tiles, sums, sums_all, *sems):
        place = Place(n_dp, n_fsdp)
        barrier = pltpu.get_barrier_semaphore()
        for i in range(1, n_dp):
            pl.semaphore_signal(
                barrier, inc=1, device_id=place.at_dp((place.dp + i) % n_dp), device_id_type=MESH
            )
        for i in range(1, n_fsdp):
            pl.semaphore_signal(
                barrier, inc=1, device_id=(place.dp, (place.f + i) % n_fsdp), device_id_type=MESH
            )
        pl.semaphore_wait(barrier, n_dp + n_fsdp - 2)
        inner = Direct(place, src, boxes, sems[0:2], "fsdp", block=lambda ref, d: ref.at[d])
        inner.start()
        boxes[place.f] = src[place.f]
        inner.finish()
        for j in range(MODS):
            part = jnp.concatenate([boxes[f, j, :rows, :] for f in range(n_fsdp)], axis=0)
            mine[j] = part.astype(jnp.bfloat16)
        outer = Direct(place, mine, all_mods, sems[2:4])
        outer.start()
        all_mods[place.dp] = mine[...]
        outer.finish()
        total = squares_ref[...]
        for j in range(MODS):
            grad[j] = lax.dot_general(
                cond[0], all_mods[0, j], (((0,), (0,)), ((), ())), preferred_element_type=jnp.float32
            )
            for d in range(1, n_dp):
                grad[j] += lax.dot_general(
                    cond[d], all_mods[d, j], (((0,), (0,)), ((), ())), preferred_element_type=jnp.float32
                )
        tile[...] = total

        def add(at):
            for j in range(MODS):
                values = grad[j, at, :]
                values = values * values
                for lane in range(0, wide, 128):
                    tile[...] += values[:, lane : lane + 128]

        row_loop(deep, add)
        first = Direct(place, tile, tiles, sems[4:6], "fsdp")
        first.start()
        tiles[place.f] = tile[...]
        first.finish()
        total = tiles[0]
        for f in range(1, n_fsdp):
            total = total + tiles[f]
        sums[...] = total
        second = Direct(place, sums, sums_all, sems[6:8])
        second.start()
        sums_all[place.dp] = sums[...]
        second.finish()
        total = sums_all[0]
        for d in range(1, n_dp):
            total = total + sums_all[d]
        norm[0, 0] = jnp.sqrt(jnp.sum(total))

    return pl.pallas_call(
        kernel,
        out_shape=[
            jax.ShapeDtypeStruct((MODS, deep, wide), jnp.float32),
            jax.ShapeDtypeStruct((1, 1), jnp.float32),
        ],
        in_specs=[WHOLE] * 3,
        out_specs=[WHOLE, pl.BlockSpec(memory_space=pltpu.SMEM)],
        scratch_shapes=[
            pltpu.VMEM(grad_mods.shape, jnp.float32),
            pltpu.VMEM((MODS, images, wide), jnp.bfloat16),
            pltpu.VMEM((n_dp, MODS, images, wide), jnp.bfloat16),
            pltpu.VMEM(TILE, jnp.float32),
            pltpu.VMEM((n_fsdp, *TILE), jnp.float32),
            pltpu.VMEM(TILE, jnp.float32),
            pltpu.VMEM((n_dp, *TILE), jnp.float32),
            *Direct.scratch(n_fsdp), *Direct.scratch(n_dp), *Direct.scratch(n_fsdp), *Direct.scratch(n_dp),
        ],
        compiler_params=parameters(1),
    )(grad_mods, condition, squares)


def adam_kernel(factor, grad, master, first, second):
    which, rows, columns = master.shape
    step = min(rows, max(64, 131072 // columns))
    block = pl.BlockSpec((1, step, columns), lambda w, r: (w, r, 0))

    def kernel(factor_ref, grad_ref, master_ref, first_ref, second_ref, new_ref, copy_ref, moment_ref, square_ref):
        scale = factor_ref[0, 0]
        clipped = grad_ref[...] * scale
        moment = BETA_ONE * first_ref[...] + (1.0 - BETA_ONE) * clipped
        square = BETA_TWO * second_ref[...] + (1.0 - BETA_TWO) * clipped * clipped
        moment_ref[...] = moment
        square_ref[...] = square
        below = jnp.sqrt(square * (1.0 / (1.0 - BETA_TWO**STEP))) + ADAM_EPS
        ratio = moment * (1.0 / (1.0 - BETA_ONE**STEP)) / below
        old = master_ref[...]
        new = old - LEARN_RATE * (ratio + WEIGHT_DECAY * old)
        new_ref[...] = new
        copy_ref[...] = new.astype(jnp.bfloat16)

    shape = jax.ShapeDtypeStruct(master.shape, jnp.float32)
    return pl.pallas_call(
        kernel,
        grid=(which, rows // step),
        out_shape=[shape, jax.ShapeDtypeStruct(master.shape, jnp.bfloat16), shape, shape],
        in_specs=[pl.BlockSpec(memory_space=pltpu.SMEM)] + [block] * 4,
        out_specs=[block] * 4,
        compiler_params=pltpu.CompilerParams(vmem_limit_bytes=VMEM_LIMIT),
    )(factor, grad, master, first, second)


def normalize(values):
    average = jnp.mean(values, axis=-1, keepdims=True)
    centred = values - average
    inv_std = lax.rsqrt(jnp.mean(centred * centred, axis=-1, keepdims=True) + NORM_EPS)
    return (centred * inv_std, inv_std)


def normalize_back(grad, normed, inv_std):
    return inv_std * (
        grad
        - jnp.mean(grad, axis=-1, keepdims=True)
        - normed * jnp.mean(grad * normed, axis=-1, keepdims=True)
    )


def masked_scores(queries, keys_part, allowed):
    scores = jnp.einsum(
        "bqhe,bkhe->bhqk", queries, keys_part, preferred_element_type=jnp.float32
    ) * HEAD ** (-0.5)
    return jnp.where(allowed[:, None], scores, -1e30)


def attention_forward(qkv_low, allowed):
    queries, keys_part, values_part = qkv_low.reshape(3, *allowed.shape[:2], -1, HEAD)
    scores = masked_scores(queries, keys_part, allowed)
    row_max = jnp.max(scores, axis=-1, keepdims=True)
    raw_exp = jnp.exp(scores - row_max)
    attn_probs = raw_exp / jnp.sum(raw_exp, axis=-1, keepdims=True)
    probs_low = attn_probs.astype(jnp.bfloat16)
    attended = jnp.einsum(
        "bhqk,bkhe->bqhe", probs_low, values_part, preferred_element_type=jnp.float32
    )
    return attended.reshape(qkv_low.shape[1:]).astype(jnp.bfloat16), attn_probs


def attention_backward(qkv_low, attn_probs, grad_heads):
    queries, keys_part, values_part = qkv_low.reshape(3, attn_probs.shape[0], attn_probs.shape[2], -1, HEAD)
    probs_low = attn_probs.astype(jnp.bfloat16)
    grad_out = grad_heads.reshape(queries.shape)
    grad_p = jnp.einsum(
        "bqhe,bkhe->bhqk", grad_out, values_part, preferred_element_type=jnp.float32
    )
    row_delta = jnp.sum(attn_probs * grad_p, axis=-1, keepdims=True)
    grad_scores = (attn_probs * (grad_p - row_delta)).astype(jnp.bfloat16)
    scale = HEAD ** (-0.5)
    grad_query = (
        jnp.einsum("bhqk,bkhe->bqhe", grad_scores, keys_part, preferred_element_type=jnp.float32)
        * scale
    )
    grad_key = (
        jnp.einsum("bhqk,bqhe->bkhe", grad_scores, queries, preferred_element_type=jnp.float32)
        * scale
    )
    grad_value = jnp.einsum(
        "bhqk,bqhe->bkhe", probs_low, grad_out, preferred_element_type=jnp.float32
    )
    stacked = jnp.stack([grad_query, grad_key, grad_value])
    return stacked.reshape(qkv_low.shape).astype(jnp.bfloat16)


def contract_rows(left, right):
    return lax.dot_general(
        left, right, (((0,), (0,)), ((), ())), preferred_element_type=jnp.float32
    )


def contract_last(left, right):
    return lax.dot_general(
        left, right, (((1,), (1,)), ((), ())), preferred_element_type=jnp.float32
    )


def body(n_dp, n_fsdp, *arguments):
    tokens, embedding, image_slot, token_mask, cotangent = arguments[:5]
    weights = [w if w.ndim == 3 else w[:, None] for w in arguments[5:]]
    weights = [w.transpose(1, 0, 2) for w in weights]
    masters, firsts, seconds = weights[:5], weights[5:10], weights[10:]
    qkv_w, out_w, up_w, down_w, ada_w = masters
    low = jnp.bfloat16
    micro, tok_rows, width = tokens.shape
    own_rows = micro * tok_rows
    group_rows = own_rows * n_fsdp
    image_count = embedding.shape[1] // n_fsdp
    images = micro * n_fsdp * image_count
    f = lax.axis_index("fsdp")

    own_tokens = tokens.reshape(own_rows, width)
    codes = jnp.stack([image_slot.reshape(own_rows), token_mask.reshape(own_rows)]).astype(jnp.float32)
    codes = jnp.pad(codes, ((0, 6), (0, 0)))

    tok_g, codes_g, mods, cond_all, qkv_g, out_g = modulation_kernel(
        n_dp, n_fsdp, own_tokens, codes, embedding.reshape(images, -1), ada_w, qkv_w.astype(low), out_w.astype(low)
    )
    qkv_g = qkv_g.reshape(3, width, -1)
    out_g = out_g.reshape(width, -1)

    mods = mods.reshape(MODS, micro, n_fsdp, image_count, width).transpose(0, 2, 1, 3, 4)
    slot_g = codes_g[:, 0].reshape(n_fsdp, micro, tok_rows)
    live_g = codes_g[:, 1].reshape(n_fsdp, micro, tok_rows)

    def pick(table, slots):
        picked = table[..., 0:1, :]
        for i in range(1, image_count):
            picked = jnp.where(slots[..., None] == i, table[..., i : i + 1, :], picked)
        return picked

    mods_own = lax.dynamic_index_in_dim(mods, f, 1, keepdims=False)
    slots = image_slot.astype(jnp.float32)
    shift1, scale1, gate1, shift2, scale2, gate2 = [pick(mods_own[j], slots) for j in range(MODS)]

    normed1_g, _ = normalize(tok_g.reshape(n_fsdp, micro, tok_rows, width).astype(jnp.float32))
    hidden1_g = normed1_g * (1.0 + pick(mods[1], slot_g)) + pick(mods[0], slot_g)
    hidden1_g = hidden1_g.astype(low).reshape(group_rows, width)

    rows_blk = 2 * own_rows
    place_g = jnp.arange(group_rows, dtype=jnp.int32) // tok_rows
    image_ids = (place_g.astype(jnp.float32) * image_count + slot_g.reshape(-1)).reshape(-1, rows_blk)
    usable = live_g.reshape(-1, rows_blk)
    same = image_ids[:, :, None] == image_ids[:, None, :]
    allowed = (same & (usable[:, None, :] > 0.5)) | jnp.eye(rows_blk, dtype=bool)[None]

    qkv_low = jnp.einsum("td,jdf->jtf", hidden1_g, qkv_g, preferred_element_type=jnp.float32).astype(low)
    attended, attn_probs = attention_forward(qkv_low, allowed)
    attn_part = contract_last(attended, out_g).astype(low).reshape(n_fsdp, own_rows, width)

    attn_own, cot_g, up_g = transfer(
        2, n_dp, n_fsdp,
        [(LineScatter, attn_part), (LineGather, cotangent.reshape(own_rows, width)), (GridGather, up_w.astype(low))],
    )
    up_g = up_g.reshape(width, -1)
    attn_own = attn_own.reshape(micro, tok_rows, width)
    inputs = tokens.astype(jnp.float32)
    mid = inputs + gate1 * attn_own
    normed2, inv_std2 = normalize(mid)
    hidden2 = (normed2 * (1.0 + scale2) + shift2).astype(low)

    hidden2_g, down_g = transfer(
        3, n_dp, n_fsdp, [(LineGather, hidden2.reshape(own_rows, width)), (GridGather, down_w.astype(low))]
    )
    hidden2_g = hidden2_g.reshape(group_rows, width)
    down_g = down_g.reshape(width, -1)

    grad_mlp_g = cot_g.reshape(n_fsdp, micro, tok_rows, width).astype(jnp.float32) * live_g[..., None]
    grad_mlp_g = (grad_mlp_g * pick(mods[5], slot_g)).astype(low).reshape(group_rows, width)
    upper = jnp.dot(hidden2_g, up_g, preferred_element_type=jnp.float32)
    activ_full, gelu_pull = jax.vjp(jax.nn.gelu, upper)
    activ = activ_full.astype(low)
    grad_act = jnp.dot(grad_mlp_g, down_g, preferred_element_type=jnp.float32)
    grad_upper = gelu_pull(grad_act)[0].astype(low)
    grad_h2_part = contract_last(grad_upper, up_g).astype(low).reshape(n_fsdp, own_rows, width)
    mlp_part = contract_last(activ, down_g).astype(low).reshape(n_fsdp, own_rows, width)
    cut = (1, n_dp, width // n_dp, activ.shape[1])
    grad_down = contract_rows(grad_mlp_g, activ).astype(low).reshape(cut)
    grad_up = contract_rows(hidden2_g, grad_upper).astype(low).reshape(cut)

    grad_h2, grad_down, squares_down = transfer(
        4, n_dp, n_fsdp, [(LineScatter, grad_h2_part), (GridScatter, grad_down)]
    )
    grad_h2 = grad_h2.reshape(micro, tok_rows, width)
    live = token_mask.astype(jnp.float32)[..., None]
    grad_y = cotangent.astype(jnp.float32) * live
    grad_mid = grad_y + normalize_back(grad_h2 * (1.0 + scale2), normed2, inv_std2)
    grad_attn = (grad_mid * gate1).astype(low)

    mlp_own, grad_attn_g, grad_up, squares_up = transfer(
        5, n_dp, n_fsdp,
        [(LineScatter, mlp_part), (LineGather, grad_attn.reshape(own_rows, width)), (GridScatter, grad_up)],
    )
    mlp_own = mlp_own.reshape(micro, tok_rows, width)
    block_out = (mid + gate2 * mlp_own).astype(low)

    grad_attn_g = grad_attn_g.reshape(group_rows, width)
    grad_heads = jnp.dot(grad_attn_g, out_g, preferred_element_type=jnp.float32).astype(low)
    grad_out = contract_rows(grad_attn_g, attended).astype(low).reshape(1, n_dp, -1, attended.shape[1])
    grad_qkv = attention_backward(qkv_low, attn_probs, grad_heads)
    grad_h1_part = jnp.einsum("jtf,jdf->td", grad_qkv, qkv_g, preferred_element_type=jnp.float32)
    grad_h1_part = grad_h1_part.astype(low).reshape(n_fsdp, own_rows, width)
    grad_qkv_w = jnp.einsum("td,jtf->jdf", hidden1_g, grad_qkv, preferred_element_type=jnp.float32)
    grad_qkv_w = grad_qkv_w.astype(low).reshape(3, n_dp, -1, grad_qkv.shape[2])

    grad_h1, grad_qkv_w, squares_qkv, grad_out, squares_out = transfer(
        6, n_dp, n_fsdp, [(LineScatter, grad_h1_part), (GridScatter, grad_qkv_w), (GridScatter, grad_out)]
    )
    grad_h1 = grad_h1.reshape(micro, tok_rows, width)
    normed1, inv_std1 = normalize(inputs)
    input_grad = grad_mid + normalize_back(grad_h1 * (1.0 + scale1), normed1, inv_std1)

    terms = (grad_h1, grad_h1 * normed1, grad_mid * attn_own, grad_h2, grad_h2 * normed2, grad_y * mlp_own)
    grad_mods = []
    for i in range(image_count):
        chosen = (image_slot == i).astype(jnp.float32)[..., None]
        grad_mods.append(jnp.stack([jnp.sum(term * chosen, axis=1) for term in terms]))
    grad_mods = jnp.stack(grad_mods, axis=2).astype(low).astype(jnp.float32)
    own_images = micro * image_count
    grad_mods = grad_mods.reshape(MODS, own_images, n_fsdp, -1).transpose(2, 0, 1, 3)
    grad_mods = jnp.pad(grad_mods, ((0, 0), (0, 0), (0, -own_images % 8), (0, 0)))
    cond_all = cond_all.reshape(n_dp, micro, n_fsdp, image_count, -1).transpose(0, 2, 1, 3, 4)
    grad_ada, grad_norm = norm_kernel(
        n_dp, n_fsdp, grad_mods, cond_all.reshape(n_dp, images, -1),
        squares_qkv + squares_out + squares_up + squares_down,
    )

    factor = jnp.minimum(1.0, CLIP_AT / grad_norm)
    results = []
    grads = (grad_qkv_w, grad_out, grad_up, grad_down, grad_ada)
    for given, grad, master, first, second in zip(arguments[5:], grads, masters, firsts, seconds):
        for updated in adam_kernel(factor, grad, master, first, second):
            results.append(updated.transpose(1, 0, 2).reshape(given.shape))
    return (block_out, input_grad, *results, grad_norm[0, 0])


def solution(mesh):
    n_dp, n_fsdp = mesh.shape["dp"], mesh.shape["fsdp"]
    rows = P(None, ("dp", "fsdp"), None)
    slots = P(None, ("dp", "fsdp"))
    thick = P("dp", None, "fsdp")
    flat = P("dp", "fsdp")
    weights = (thick, flat, flat, flat, thick)
    updated = tuple(spec for spec in weights for _ in range(4))
    return jax.shard_map(
        functools.partial(body, n_dp, n_fsdp),
        mesh=mesh,
        in_specs=(rows, P(None, "dp", None), slots, slots, rows, *weights, *weights, *weights),
        out_specs=(rows, rows, *updated, P()),
        check_vma=False,
    )
```

```python
import functools

import jax
import jax.numpy as jnp
from jax import lax
from jax.experimental import pallas as pl
from jax.experimental.pallas import tpu as pltpu
from jax.sharding import PartitionSpec as P

HEAD = 128
STEP = 10
MODS = 6

NORM_EPS = 1e-06
CLIP_AT = 1.0
BETA_ONE = 0.9
BETA_TWO = 0.999
LEARN_RATE = 0.05
WEIGHT_DECAY = 0.1
ADAM_EPS = 1e-08

MESH = pl.DeviceIdType.MESH
VMEM_LIMIT = 62 * 1024 * 1024
ROW_STEP = 16


class Place:
    def __init__(self, n_dp, n_fsdp):
        self.n_dp, self.n_fsdp = n_dp, n_fsdp
        self.chips = n_fsdp // 2
        self.grid_a = 2
        self.grid_b = n_dp // 2
        self.dp = lax.axis_index("dp")
        self.f = lax.axis_index("fsdp")
        self.p = self.f // 2
        self.c = self.f % 2
        self.a = self.dp // self.grid_b
        self.b = self.dp % self.grid_b

    def at_chip(self, chip):
        return (self.dp, chip * 2 + self.c)

    def sibling(self):
        return (self.dp, self.p * 2 + 1 - self.c)

    def at_dp(self, dp):
        return (dp, self.f)

    def b_peer(self, i):
        return (self.b + i) % self.grid_b

    def a_peer(self, i):
        return (self.a + i) % self.grid_a


def enter(place, line=False, grid=False, group=False):
    barrier = pltpu.get_barrier_semaphore()
    devices = []
    if group:
        for i in range(1, place.n_fsdp):
            devices.append((place.dp, (place.f + i) % place.n_fsdp))
    elif line:
        devices.append(place.at_chip((place.p + 1) % place.chips))
        devices.append(place.at_chip((place.p + place.chips - 1) % place.chips))
        devices.append(place.sibling())
    if grid:
        for i in range(1, place.n_dp):
            devices.append(place.at_dp((place.dp + i) % place.n_dp))
    for device in devices:
        pl.semaphore_signal(barrier, inc=1, device_id=device, device_id_type=MESH)
    pl.semaphore_wait(barrier, len(devices))


def remote(src, dst, send, recv, device):
    return pltpu.make_async_remote_copy(
        src_ref=src, dst_ref=dst, send_sem=send, recv_sem=recv, device_id=device, device_id_type=MESH
    )


class LineGather:
    @staticmethod
    def scratch(n_fsdp):
        chips = n_fsdp // 2
        return [
            pltpu.SemaphoreType.DMA((2, chips)),
            pltpu.SemaphoreType.DMA((2, chips)),
            pltpu.SemaphoreType.DMA((chips,)),
            pltpu.SemaphoreType.DMA((chips,)),
            pltpu.SemaphoreType.DMA,
        ]

    def __init__(self, place, src, out, sems, block=None):
        self.place, self.src, self.out = place, src, out
        self.send, self.recv, self.csend, self.crecv, self.local = sems
        self.of = block or (lambda ref, d: ref.at[d])

    def _block(self, chip):
        return self.of(self.out, chip * 2 + self.place.c)

    def _hop(self, way, step, first):
        pc = self.place
        chip = pc.p - step if way == 0 else pc.p + step
        target = pc.p + 1 if way == 0 else pc.p - 1
        src = self.src if first else self._block(chip)
        return remote(src, self._block(chip), self.send.at[way, step], self.recv.at[way, step], pc.at_chip(target))

    def _side(self, chip, first=False):
        src = self.src if first else self._block(chip)
        return remote(src, self._block(chip), self.csend.at[chip], self.crecv.at[chip], self.place.sibling())

    def _sends(self, way, step):
        pc = self.place
        if way == 0:
            return (pc.p < pc.chips - 1) & (pc.p >= step)
        return (pc.p > 0) & (pc.p + step <= pc.chips - 1)

    def start_way(self, way):
        @pl.when(self._sends(way, 0))
        def _():
            self._hop(way, 0, True).start()

    def start_here(self):
        pc = self.place
        self._side(pc.p, True).start()
        pltpu.make_async_copy(self.src, self._block(pc.p), self.local).start()

    def start(self):
        self.start_way(0)
        self.start_way(1)
        self.start_here()

    def step(self, step):
        pc = self.place
        for way in range(2):
            chip = pc.p - step if way == 0 else pc.p + step
            here = (chip >= 0) if way == 0 else (chip <= pc.chips - 1)

            @pl.when(here)
            def _():
                remote(
                    self._block(chip), self._block(chip), self.send.at[way, step - 1], self.recv.at[way, step - 1],
                    pc.sibling(),
                ).wait_recv()
                if step < pc.chips - 1:
                    @pl.when(self._sends(way, step))
                    def _():
                        self._hop(way, step, False).start()
                self._side(chip).start()

    def ready(self, chip):
        pc = self.place
        other = self.of(self.out, chip * 2 + 1 - pc.c)
        remote(other, other, self.csend.at[chip], self.crecv.at[chip], pc.sibling()).wait_recv()

        @pl.when(chip == pc.p)
        def _():
            pltpu.make_async_copy(self.src, self._block(pc.p), self.local).wait()

    def drain(self):
        pc = self.place
        for chip in range(pc.chips):
            self._side(chip).wait_send()
        for way in range(2):
            for step in range(pc.chips - 1):
                @pl.when(self._sends(way, step))
                def _():
                    self._hop(way, step, False).wait_send()

    def finish(self):
        for chip in range(self.place.chips):
            self.ready(chip)
        self.drain()


def row_loop(rows, body, first=0):
    def run(i, carry):
        body(pl.ds(pl.multiple_of(first + i * ROW_STEP, ROW_STEP), ROW_STEP))
        return carry

    lax.fori_loop(0, rows // ROW_STEP, run, 0)


class LineScatter:
    pieces = 4

    @classmethod
    def scratch(cls, n_fsdp, rows, width):
        chips = n_fsdp // 2
        return [
            pltpu.VMEM((chips, rows, width), jnp.bfloat16),
            pltpu.VMEM((chips + 1, rows, width), jnp.bfloat16),
            pltpu.SemaphoreType.DMA((chips,)),
            pltpu.SemaphoreType.DMA((chips,)),
            pltpu.SemaphoreType.DMA((2, chips, cls.pieces)),
            pltpu.SemaphoreType.DMA((2, chips, cls.pieces)),
        ]

    def __init__(self, place, part, out, scratch, mine=None, lag=2):
        self.place, self.part, self.out, self.mine = place, part, out, mine
        self.side, self.inbox, self.csend, self.crecv, self.send, self.recv = scratch
        self.rows = out.shape[0]
        self.piece = self.rows // self.pieces
        self.lag = lag
        self.slots = (place.chips - 1) * self.lag + place.chips * self.pieces

    def _side(self, chip):
        pc = self.place
        return remote(
            self.part.at[chip * 2 + 1 - pc.c], self.side.at[chip], self.csend.at[chip], self.crecv.at[chip], pc.sibling()
        )

    def _hop(self, way, chip, s):
        pc = self.place
        target = pc.p + 1 if way == 0 else pc.p - 1
        rows = pl.ds(pl.multiple_of(s * self.piece, self.piece), self.piece)
        return remote(
            self.side.at[chip, rows], self.inbox.at[chip + 1 - way, rows], self.send.at[way, chip, s],
            self.recv.at[way, chip, s], pc.at_chip(target),
        )

    def start(self):
        def one(k, carry):
            self.offer(self.order(k))
            return carry

        lax.fori_loop(0, self.place.chips, one, 0)

    def offer(self, chip):
        self._side(chip).start()

    def order(self, k):
        pc = self.place
        chips = pc.chips
        after, before = chips - 1 - pc.p, pc.p
        short = jnp.minimum(after, before)
        lone = jnp.maximum(after, before) - short
        rest = jnp.maximum(k - lone, 0)
        near = short - rest // 2
        pair = jnp.where(lax.rem(rest, 2) == 0, pc.p + near, pc.p - near)
        return jnp.where(k < lone, jnp.where(after > before, chips - 1 - k, k), pair)

    def first_slot(self, k):
        pc = self.place
        chips = pc.chips
        chip = self.order(k)
        after = pc.p * self.lag + (chips - 1 - chip) * self.pieces
        before = (chips - 1 - pc.p) * self.lag + chip * self.pieces
        slot = jnp.where(chip > pc.p, after, before)
        return jnp.where((k >= chips - 1) | (chip == pc.p), self.slots, slot)

    def paced(self, compute, pace, then):
        def one(k, slot):
            chip = self.order(k)
            compute(chip)
            self.offer(chip)
            until = jnp.minimum(self.first_slot(k + 1), self.first_slot(k + 2))
            until = jnp.maximum(jnp.minimum(until, (k + 1) * pace), slot)
            self.run(slot, until)
            then(k)
            return until

        return lax.fori_loop(0, self.place.chips, one, jnp.int32(0))

    def beside(self, slot, count, work, every=1):
        def one(i, carry):
            work(i)

            @pl.when(lax.rem(i, every) == every - 1)
            def _():
                self.step(slot + i // every)

            return carry

        lax.fori_loop(0, count, one, 0)
        return slot + count // every

    def run_to(self, slot, end):
        end = jnp.maximum(slot, end)
        self.run(slot, end)
        return end

    def _add(self, chip, s, inboxes, store):
        pc = self.place

        def add(rows):
            if self.mine is None:
                total = self.part[chip * 2 + pc.c, rows, :].astype(jnp.float32)
            else:
                total = self.mine[chip, rows, :].astype(jnp.float32)
            total = total + self.side[chip, rows, :].astype(jnp.float32)
            for way in inboxes:
                total = total + self.inbox[chip + 1 - way, rows, :].astype(jnp.float32)
            store(rows, total)

        row_loop(self.piece, add, s * self.piece)

    def _travel(self, way, t):
        pc = self.place
        chips = pc.chips
        i = t - (pc.p if way == 0 else chips - 1 - pc.p) * self.lag
        k = jnp.clip(i // self.pieces, 0, chips - 1)
        s = lax.rem(jnp.maximum(i, 0), self.pieces)
        chip = chips - 1 - k if way == 0 else k
        going = (i >= 0) & (i < chips * self.pieces) & ((chip > pc.p) if way == 0 else (chip < pc.p))
        first = (pc.p == 0) if way == 0 else (pc.p == chips - 1)

        def store(rows, total):
            self.side[chip, rows, :] = total.astype(jnp.bfloat16)

        @pl.when(going)
        def _():
            @pl.when(s == 0)
            def _():
                self._side(chip).wait_recv()

            @pl.when(first)
            def _():
                self._add(chip, s, (), store)

            @pl.when(jnp.logical_not(first))
            def _():
                self._hop(way, chip, s).wait_recv()
                self._add(chip, s, (way,), store)

            self._hop(way, chip, s).start()

    def step(self, t):
        self._travel(0, t)
        self._travel(1, t)

    def run(self, begin, end):
        def one(t, carry):
            self.step(t)
            return carry

        lax.fori_loop(begin, end, one, 0)

    def finish(self):
        pc = self.place
        chips = pc.chips
        self._side(pc.p).wait_recv()

        def store(rows, total):
            self.out[rows, :] = total

        def piece(s, carry):
            @pl.when(pc.p == 0)
            def _():
                self._hop(1, pc.p, s).wait_recv()
                self._add(pc.p, s, (1,), store)

            @pl.when(pc.p == chips - 1)
            def _():
                self._hop(0, pc.p, s).wait_recv()
                self._add(pc.p, s, (0,), store)

            @pl.when((pc.p > 0) & (pc.p < chips - 1))
            def _():
                self._hop(0, pc.p, s).wait_recv()
                self._hop(1, pc.p, s).wait_recv()
                self._add(pc.p, s, (0, 1), store)

            return carry

        lax.fori_loop(0, self.pieces, piece, 0)
        for chip in range(chips):
            self._side(chip).wait_send()

            def sent(s, carry):
                @pl.when(chip > pc.p)
                def _():
                    self._hop(0, chip, s).wait_send()

                @pl.when(chip < pc.p)
                def _():
                    self._hop(1, chip, s).wait_send()

                return carry

            lax.fori_loop(0, self.pieces, sent, 0)


class GridGather:
    @staticmethod
    def scratch(n_dp):
        na, nb = 2, n_dp // 2
        return [
            pltpu.SemaphoreType.DMA((2, max(nb - 1, 1))),
            pltpu.SemaphoreType.DMA((2, max(nb - 1, 1))),
            pltpu.SemaphoreType.DMA((2, na - 1)),
            pltpu.SemaphoreType.DMA((2, na - 1)),
            pltpu.SemaphoreType.DMA((2, max(nb - 1, 1), na - 1)),
            pltpu.SemaphoreType.DMA((2, max(nb - 1, 1), na - 1)),
            pltpu.SemaphoreType.DMA,
        ]

    def __init__(self, place, src, out, sems):
        self.place, self.src, self.out = place, src, out
        self.bsend, self.brecv, self.asend, self.arecv, self.fsend, self.frecv, self.local = sems
        self.half = src.shape[1] // 2

    def _own(self, h):
        return self.src.at[:, pl.ds(h * self.half, self.half)]

    def _block(self, a, b, h):
        return self.out.at[:, a * self.place.grid_b + b, pl.ds(h * self.half, self.half)]

    def _b_copy(self, i, h, coming):
        pc = self.place
        b = pc.b_peer(pc.grid_b - i) if coming else pc.b
        return remote(
            self._own(h), self._block(pc.a, b, h), self.bsend.at[h, i - 1], self.brecv.at[h, i - 1],
            pc.at_dp(pc.a * pc.grid_b + pc.b_peer(i)),
        )

    def _a_copy(self, i, h, coming):
        pc = self.place
        a = pc.a_peer(pc.grid_a - i) if coming else pc.a
        return remote(
            self._own(h), self._block(a, pc.b, h), self.asend.at[h, i - 1], self.arecv.at[h, i - 1],
            pc.at_dp(pc.a_peer(i) * pc.grid_b + pc.b),
        )

    def _on(self, h, ib, ia, coming):
        pc = self.place
        if h == 0:
            b = pc.b_peer(pc.grid_b - ib)
            a = pc.a_peer(pc.grid_a - ia) if coming else pc.a
            target = pc.at_dp(pc.a_peer(ia) * pc.grid_b + pc.b)
        else:
            a = pc.a_peer(pc.grid_a - ia)
            b = pc.b_peer(pc.grid_b - ib) if coming else pc.b
            target = pc.at_dp(pc.a * pc.grid_b + pc.b_peer(ib))
        block = self._block(a, b, h)
        return remote(block, block, self.fsend.at[h, ib - 1, ia - 1], self.frecv.at[h, ib - 1, ia - 1], target)

    def start(self):
        pc = self.place
        for h in range(2):
            for i in range(1, pc.grid_b):
                self._b_copy(i, h, False).start()
            for i in range(1, pc.grid_a):
                self._a_copy(i, 1 - h, False).start()
        pltpu.make_async_copy(self.src, self.out.at[:, pc.dp], self.local).start()

    def step(self):
        pc = self.place
        for ib in range(1, pc.grid_b):
            self._b_copy(ib, 0, True).wait_recv()
            for ia in range(1, pc.grid_a):
                self._on(0, ib, ia, False).start()
        for ia in range(1, pc.grid_a):
            self._a_copy(ia, 1, True).wait_recv()
            for ib in range(1, pc.grid_b):
                self._on(1, ib, ia, False).start()

    def finish(self):
        pc = self.place
        pltpu.make_async_copy(self.src, self.out.at[:, pc.dp], self.local).wait()
        for ib in range(1, pc.grid_b):
            self._b_copy(ib, 1, True).wait_recv()
        for ia in range(1, pc.grid_a):
            self._a_copy(ia, 0, True).wait_recv()
        for h in range(2):
            for ib in range(1, pc.grid_b):
                for ia in range(1, pc.grid_a):
                    self._on(h, ib, ia, True).wait_recv()
                    self._on(h, ib, ia, False).wait_send()
        for h in range(2):
            for ib in range(1, pc.grid_b):
                self._b_copy(ib, h, False).wait_send()
            for ia in range(1, pc.grid_a):
                self._a_copy(ia, h, False).wait_send()


class GridScatter:
    @staticmethod
    def scratch(n_dp, which, rows, width):
        na, nb = 2, n_dp // 2
        half = rows // 2
        most = max(nb - 1, 1)
        return [
            pltpu.VMEM((most, na, which, half, width), jnp.bfloat16),
            pltpu.VMEM((na - 1, nb, which, half, width), jnp.bfloat16),
            pltpu.VMEM((na - 1, which, half, width), jnp.bfloat16),
            pltpu.VMEM((most, which, half, width), jnp.bfloat16),
            pltpu.VMEM((na - 1, which, half, width), jnp.bfloat16),
            pltpu.VMEM((most, which, half, width), jnp.bfloat16),
            pltpu.SemaphoreType.DMA((most, na)),
            pltpu.SemaphoreType.DMA((most, na)),
            pltpu.SemaphoreType.DMA((na - 1, nb)),
            pltpu.SemaphoreType.DMA((na - 1, nb)),
            pltpu.SemaphoreType.DMA((na - 1,)),
            pltpu.SemaphoreType.DMA((na - 1,)),
            pltpu.SemaphoreType.DMA((most,)),
            pltpu.SemaphoreType.DMA((most,)),
        ]

    def __init__(self, place, part, out, squares, scratch):
        self.place, self.part, self.out, self.squares = place, part, out, squares
        self.box_b, self.box_a, self.sum_b, self.sum_a, self.end_a, self.end_b = scratch[:6]
        self.bs, self.br, self.as_, self.ar, self.eas, self.ear, self.ebs, self.ebr = scratch[6:]
        self.which = out.shape[0]
        self.half = out.shape[1] // 2

    def _part(self, a, b, h):
        return self.part.at[:, a * self.place.grid_b + b, pl.ds(h * self.half, self.half)]

    def _first_b(self, i, j):
        pc = self.place
        return remote(
            self._part(pc.a_peer(j), pc.b_peer(i), 0), self.box_b.at[i - 1, j], self.bs.at[i - 1, j],
            self.br.at[i - 1, j], pc.at_dp(pc.a * pc.grid_b + pc.b_peer(i)),
        )

    def _first_a(self, i, j):
        pc = self.place
        return remote(
            self._part(pc.a_peer(i), pc.b_peer(j), 1), self.box_a.at[i - 1, j], self.as_.at[i - 1, j],
            self.ar.at[i - 1, j], pc.at_dp(pc.a_peer(i) * pc.grid_b + pc.b),
        )

    def _second_a(self, i):
        pc = self.place
        return remote(
            self.sum_b.at[i - 1], self.end_a.at[i - 1], self.eas.at[i - 1], self.ear.at[i - 1],
            pc.at_dp(pc.a_peer(i) * pc.grid_b + pc.b),
        )

    def _second_b(self, i):
        pc = self.place
        return remote(
            self.sum_a.at[i - 1], self.end_b.at[i - 1], self.ebs.at[i - 1], self.ebr.at[i - 1],
            pc.at_dp(pc.a * pc.grid_b + pc.b_peer(i)),
        )

    def _firsts_b(self):
        pc = self.place
        return [(i, j) for j in list(range(1, pc.grid_a)) + [0] for i in range(1, pc.grid_b)]

    def _firsts_a(self):
        pc = self.place
        return [(i, j) for j in list(range(1, pc.grid_b)) + [0] for i in range(1, pc.grid_a)]

    def start(self):
        for (ib, jb), (ia, ja) in zip(self._firsts_b(), self._firsts_a(), strict=False):
            self._first_b(ib, jb).start()
            self._first_a(ia, ja).start()
        shared = min(len(self._firsts_b()), len(self._firsts_a()))
        for i, j in self._firsts_b()[shared:]:
            self._first_b(i, j).start()
        for i, j in self._firsts_a()[shared:]:
            self._first_a(i, j).start()

    def _low(self, rows):
        return pl.ds(pl.multiple_of(self.half + rows.start, ROW_STEP), ROW_STEP)

    def _sum_b(self, j):
        pc = self.place
        for i in range(1, pc.grid_b):
            self._first_b(i, j).wait_recv()
        mine = pc.a_peer(j) * pc.grid_b + pc.b

        def add(rows):
            for w in range(self.which):
                total = self.part[w, mine, rows, :].astype(jnp.float32)
                for i in range(1, pc.grid_b):
                    total = total + self.box_b[i - 1, j, w, rows, :].astype(jnp.float32)
                if j == 0:
                    self.out[w, rows, :] = total
                else:
                    self.sum_b[j - 1, w, rows, :] = total.astype(jnp.bfloat16)

        row_loop(self.half, add)
        if j:
            self._second_a(j).start()

    def _sum_a(self, j):
        pc = self.place
        for i in range(1, pc.grid_a):
            self._first_a(i, j).wait_recv()
        mine = pc.a * pc.grid_b + pc.b_peer(j)

        def add(rows):
            for w in range(self.which):
                total = self.part[w, mine, self._low(rows), :].astype(jnp.float32)
                for i in range(1, pc.grid_a):
                    total = total + self.box_a[i - 1, j, w, rows, :].astype(jnp.float32)
                if j == 0:
                    self.out[w, self._low(rows), :] = total
                else:
                    self.sum_a[j - 1, w, rows, :] = total.astype(jnp.bfloat16)

        row_loop(self.half, add)
        if j:
            self._second_b(j).start()

    def step(self):
        pc = self.place
        for j in range(1, max(pc.grid_a, pc.grid_b)):
            if j < pc.grid_a:
                self._sum_b(j)
            if j < pc.grid_b:
                self._sum_a(j)

    def step_own(self):
        self._sum_b(0)
        self._sum_a(0)

    def finish(self):
        pc = self.place
        for i in range(1, pc.grid_a):
            self._second_a(i).wait_recv()
        for i in range(1, pc.grid_b):
            self._second_b(i).wait_recv()
        self.squares[...] = jnp.zeros_like(self.squares)

        def tile(total):
            total = total * total
            folded = total[:, :128]
            for at in range(128, total.shape[1], 128):
                folded = folded + total[:, at : at + 128]
            return folded

        def add(rows):
            low = self._low(rows)
            for w in range(self.which):
                total = self.out[w, rows, :]
                for i in range(1, pc.grid_a):
                    total = total + self.end_a[i - 1, w, rows, :].astype(jnp.float32)
                self.out[w, rows, :] = total
                self.squares[...] += tile(total)
                total = self.out[w, low, :]
                for i in range(1, pc.grid_b):
                    total = total + self.end_b[i - 1, w, rows, :].astype(jnp.float32)
                self.out[w, low, :] = total
                self.squares[...] += tile(total)

        row_loop(self.half, add)
        for i, j in self._firsts_b():
            self._first_b(i, j).wait_send()
        for i, j in self._firsts_a():
            self._first_a(i, j).wait_send()
        for i in range(1, pc.grid_a):
            self._second_a(i).wait_send()
        for i in range(1, pc.grid_b):
            self._second_b(i).wait_send()


class Direct:
    @staticmethod
    def scratch(n):
        return [pltpu.SemaphoreType.DMA((n - 1,)), pltpu.SemaphoreType.DMA((n - 1,))]

    def __init__(self, place, src, out, sems, axis="dp", block=None):
        self.place, self.src, self.out = place, src, out
        self.send, self.recv = sems
        self.n = place.n_dp if axis == "dp" else place.n_fsdp
        self.me = place.dp if axis == "dp" else place.f
        self.axis = axis
        self.of = block or (lambda ref, d: ref)

    def _device(self, other):
        return self.place.at_dp(other) if self.axis == "dp" else (self.place.dp, other)

    def _copy(self, i, coming=False):
        other = (self.me + i) % self.n
        origin = (self.me + self.n - i) % self.n if coming else self.me
        return remote(
            self.of(self.src, other), self.out.at[origin], self.send.at[i - 1], self.recv.at[i - 1], self._device(other)
        )

    def start(self):
        for i in range(1, self.n):
            self._copy(i).start()

    def finish(self):
        for i in range(1, self.n):
            self._copy(i, True).wait_recv()
            self._copy(i).wait_send()


def split_refs(refs, counts):
    out, at = [], 0
    for count in counts:
        out.append(refs[at : at + count])
        at += count
    return out


HBM = pl.BlockSpec(memory_space=pl.ANY)
WHOLE = pl.BlockSpec(memory_space=pltpu.VMEM)
TILE = (ROW_STEP, 128)


def parameters(collective_id):
    return pltpu.CompilerParams(collective_id=collective_id, has_side_effects=True, vmem_limit_bytes=VMEM_LIMIT)


def matmul(left, right):
    return jnp.dot(left, right, preferred_element_type=jnp.float32)


def matmul_last(left, right):
    return lax.dot_general(left, right, (((1,), (1,)), ((), ())), preferred_element_type=jnp.float32)


def matmul_first(left, right):
    return lax.dot_general(left, right, (((0,), (0,)), ((), ())), preferred_element_type=jnp.float32)


def loop(count, work):
    def one(i, carry):
        work(i)
        return carry

    lax.fori_loop(0, count, one, 0)


def span(i, size):
    return pl.ds(pl.multiple_of(i * size, size), size)


def chip_rows(ref, chip):
    pair = ref[span(chip, 2)]
    return pair.reshape(-1, pair.shape[-1])


def pair_mask(codes_ref, chip, rows):
    pair = [codes_ref[chip * 2 + i] for i in range(2)]
    query = jnp.floor(jnp.concatenate([block[:rows] for block in pair], axis=0))
    query = jnp.concatenate([query] * (2 * rows // 128), axis=1)
    key = jnp.concatenate([block[rows : rows + 1] for block in pair], axis=1)
    shape = (2 * rows, 2 * rows)
    same = lax.broadcasted_iota(jnp.int32, shape, 0) == lax.broadcasted_iota(jnp.int32, shape, 1)
    return (query == key) | same


class Rows:
    def __init__(self, place, codes, mods, micro, rows, slots_here):
        self.place, self.codes, self.mods = place, codes, mods
        self.micro, self.tok_rows, self.slots_here = micro, rows // micro, slots_here

    def tiles(self, work):
        for m in range(self.micro):
            row_loop(self.tok_rows, functools.partial(work, m), m * self.tok_rows)

    def slot_live(self, m, rows):
        column = self.codes[rows, :][:, :1]
        number = jnp.floor(column)
        first = ((self.place.f * self.micro + m) * self.slots_here).astype(jnp.float32)
        return number - first, jnp.where(column == number, 1.0, 0.0)

    def pick(self, j, m, slot):
        at = m * self.slots_here
        picked = self.mods[j, at : at + 1, :]
        for i in range(1, self.slots_here):
            picked = jnp.where(slot == i, self.mods[j, at + i : at + i + 1, :], picked)
        return picked

    def add_up(self, out, j, m, slot, values):
        for i in range(self.slots_here):
            at = m * self.slots_here + i
            chosen = jnp.where(slot == i, values, 0.0)
            out[j, at : at + 1, :] += jnp.sum(chosen, axis=0, keepdims=True)


def cast_rows(src, dst):
    for w in range(src.shape[0]):
        def tile(rows):
            dst[w, rows, :] = src[w, rows, :].astype(dst.dtype)

        row_loop(src.shape[1], tile)


def attention_probs(query, key, allowed):
    scores = jnp.where(allowed, matmul_last(query, key) * HEAD ** (-0.5), -1e30)
    raw = jnp.exp(scores - jnp.max(scores, axis=-1, keepdims=True))
    return raw / jnp.sum(raw, axis=-1, keepdims=True)


def attention_kernel(n_dp, n_fsdp, micro, tokens, cotangent, codes, embedding, ada, qkv, out_w, up, down):
    low, f32 = jnp.bfloat16, jnp.float32
    images = embedding.shape[0]
    rows, width = tokens.shape
    deep, wide = ada.shape[1:]
    which, _, head_columns = qkv.shape
    slots_here = images // (micro * n_fsdp)
    own_images = micro * slots_here
    line = LineGather.scratch(n_fsdp)
    grid = GridGather.scratch(n_dp)
    direct = Direct.scratch(n_dp)
    scatter_got = LineScatter.scratch(n_fsdp, rows, width)
    counts = [len(line)] * 3 + [len(grid)] * 3 + [len(direct)] * 3 + [len(scatter_got)]
    weights = (qkv, out_w, up, down)
    pair = 2 * rows

    def kernel(
        tok, cot, code_row, emb, ada_ref, qkv_f, out_f, up_f, down_f,
        attn_own, mid, hidden2, mods_own, cond_g, cod, cod_g, qkv_low, attended, down_low,
        hidden_out, qkv_out, out_out, up_g, gmlp_g,
        cond, parts, boxes, mail, inbox, hidden, gmlp, part, hidden_g, qkv_g, out_g,
        qkv_s, out_s, up_s, down_s, qkv_l, out_l, up_l, moves, *rest,
    ):
        sems = split_refs(rest, counts)
        place = Place(n_dp, n_fsdp)
        fetches = [
            pltpu.make_async_copy(ref, stage, moves.at[i])
            for i, (ref, stage) in enumerate(((qkv_f, qkv_s), (out_f, out_s), (up_f, up_s), (down_f, down_s)))
        ]
        for fetch in fetches:
            fetch.start()
        level = emb[...].astype(f32)
        level = (level / (1.0 + jnp.exp(-level))).astype(low)
        for d in range(n_dp):
            cond[d] = level[:, d * deep : (d + 1) * deep]
        number = code_row[0:1, :] + ((place.f * micro) * slots_here).astype(f32)
        live = code_row[1:2, :]
        cod[:rows, :] = jnp.transpose(jnp.broadcast_to(jnp.where(live > 0.5, number, number + 0.25), (rows, rows)))
        cod[rows:, :] = jnp.broadcast_to(jnp.where(live > 0.5, number, -1.0), (8, rows))
        own = Rows(place, cod, mods_own, micro, rows, slots_here)
        enter(place, True, True, True)
        conds = Direct(place, cond, cond_g, sems[6], block=lambda ref, d: ref.at[d])
        conds.start()
        code_line = LineGather(place, cod, cod_g, sems[0])
        code_line.start()
        cond_g[place.dp] = cond[place.dp]
        fetches[0].wait()
        cast_rows(qkv_s, qkv_l)
        conds.finish()
        every = cond_g[...].reshape(n_dp * images, deep)
        for j in range(MODS):
            parts[:, j] = matmul(every, ada_ref[j].astype(low)).reshape(n_dp, images, wide)
        sums = Direct(place, parts, boxes, sems[7], block=lambda ref, d: ref.at[d])
        sums.start()
        fetches[1].wait()
        cast_rows(out_s, out_l)
        fetches[2].wait()
        cast_rows(up_s, up_l)
        fetches[3].wait()
        cast_rows(down_s, down_low)
        sums.finish()
        grids = [GridGather(place, qkv_l, qkv_g, sems[3]), GridGather(place, out_l, out_g, sems[4])]
        grids[0].start()
        for j in range(MODS):
            total = parts[place.dp, j]
            for i in range(1, n_dp):
                total = total + boxes[(place.dp + i) % n_dp, j]
            for f in range(n_fsdp):
                for m in range(micro):
                    at = (m * n_fsdp + f) * slots_here
                    mail[f, j, m * slots_here : (m + 1) * slots_here, :] = total[at : at + slots_here]
        letters = Direct(place, mail, inbox, sems[8], "fsdp", block=lambda ref, d: ref.at[d])
        letters.start()
        inbox[place.f] = mail[place.f]
        letters.finish()
        for f in range(n_fsdp):
            for j in range(MODS):
                mods_own[j, :, f * wide : (f + 1) * wide] = inbox[f, j]

        def first_norm(m, at):
            slot, _ = own.slot_live(m, at)
            normed, _ = normalize(tok[at, :].astype(f32))
            hidden[at, :] = (normed * (1.0 + own.pick(1, m, slot)) + own.pick(0, m, slot)).astype(low)

        own.tiles(first_norm)
        hidden_line = LineGather(place, hidden, hidden_g, sems[1])
        hidden_line.start()

        def branch_grad(m, at):
            slot, alive = own.slot_live(m, at)
            gmlp[at, :] = (cot[at, :].astype(f32) * alive * own.pick(5, m, slot)).astype(low)

        own.tiles(branch_grad)
        gmlp_line = LineGather(place, gmlp, gmlp_g, sems[2])
        gmlp_line.start_here()
        ups = GridGather(place, up_l, up_g, sems[5])
        for step in range(1, place.chips):
            hidden_line.step(step)
            code_line.step(step)

            @pl.when(place.p + 1 == step)
            def _():
                gmlp_line.start_way(0)

            @pl.when(place.chips - place.p == step)
            def _():
                gmlp_line.start_way(1)

            if step == 1:
                grids[0].step()
                grids[1].start()
            if step == place.chips - 1:
                grids[1].step()
                ups.start()
        hidden_line.finish()
        code_line.finish()
        for gather in grids:
            gather.finish()
        leaves = [
            pltpu.make_async_copy(ref, out, moves.at[len(weights) + i])
            for i, (ref, out) in enumerate(((hidden_g, hidden_out), (qkv_g, qkv_out), (out_g, out_out)))
        ]
        for leave in leaves:
            leave.start()
        scatter = LineScatter(place, part, attn_own, sems[9])

        def compute(chip):
            at = span(chip, pair)
            values = chip_rows(hidden_g, chip)
            for w in range(which):
                weight = qkv_g[w].reshape(width, head_columns)
                qkv_low[w, at, :] = matmul(values, weight).astype(low)
            allowed = pair_mask(cod_g, chip, rows)
            for h in range(head_columns // HEAD):
                head = slice(h * HEAD, (h + 1) * HEAD)
                probs = attention_probs(qkv_low[0, at, head], qkv_low[1, at, head], allowed)
                attended[at, head] = matmul(probs.astype(low), qkv_low[2, at, head]).astype(low)
            heads = attended[at, :]
            weight_rows = out_g.shape[2]
            for d in range(n_dp):
                piece = matmul_last(heads, out_g[0, d]).astype(low).reshape(2, rows, weight_rows)
                part[span(chip, 2), :, d * weight_rows : (d + 1) * weight_rows] = piece

        def then(k):
            @pl.when(k == 1)
            def _():
                gmlp_line.step(1)

        slot = scatter.paced(compute, 2, then)
        for step in range(2, place.chips):
            gmlp_line.step(step)
            slot = scatter.run_to(slot, scatter.slots * (step + 1) // (place.chips + 1))
            if step == place.chips // 2:
                ups.step()
        scatter.run_to(slot, scatter.slots)
        scatter.finish()

        def second_norm(m, at):
            slot, _ = own.slot_live(m, at)
            values = tok[at, :].astype(f32) + own.pick(2, m, slot) * attn_own[at, :]
            mid[at, :] = values
            normed, _ = normalize(values)
            hidden2[at, :] = (normed * (1.0 + own.pick(4, m, slot)) + own.pick(3, m, slot)).astype(low)

        own.tiles(second_norm)
        gmlp_line.finish()
        ups.finish()
        for leave in leaves:
            leave.wait()

    def gathered(w):
        return jax.ShapeDtypeStruct((w.shape[0], n_dp, *w.shape[1:]), low)

    return pl.pallas_call(
        kernel,
        out_shape=[
            jax.ShapeDtypeStruct((rows, width), f32),
            jax.ShapeDtypeStruct((rows, width), f32),
            jax.ShapeDtypeStruct((rows, width), low),
            jax.ShapeDtypeStruct((MODS, own_images, width), f32),
            jax.ShapeDtypeStruct((n_dp, images, deep), low),
            jax.ShapeDtypeStruct((rows + 8, rows), f32),
            jax.ShapeDtypeStruct((n_fsdp, rows + 8, rows), f32),
            jax.ShapeDtypeStruct((which, n_fsdp * rows, head_columns), low),
            jax.ShapeDtypeStruct((n_fsdp * rows, head_columns), low),
            jax.ShapeDtypeStruct(down.shape, low),
            jax.ShapeDtypeStruct((n_fsdp, rows, width), low),
            gathered(qkv),
            gathered(out_w),
            gathered(up),
            jax.ShapeDtypeStruct((n_fsdp, rows, width), low),
        ],
        in_specs=[WHOLE] * 5 + [HBM] * 4,
        out_specs=[WHOLE] * 10 + [HBM] * 5,
        scratch_shapes=[
            pltpu.VMEM((n_dp, images, deep), low),
            pltpu.VMEM((n_dp, MODS, images, wide), f32),
            pltpu.VMEM((n_dp, MODS, images, wide), f32),
            pltpu.VMEM((n_fsdp, MODS, own_images, wide), f32),
            pltpu.VMEM((n_fsdp, MODS, own_images, wide), f32),
            pltpu.VMEM((rows, width), low),
            pltpu.VMEM((rows, width), low),
            pltpu.VMEM((n_fsdp, rows, width), low),
            pltpu.VMEM((n_fsdp, rows, width), low),
            pltpu.VMEM((which, n_dp, *qkv.shape[1:]), low),
            pltpu.VMEM((1, n_dp, *out_w.shape[1:]), low),
            *[pltpu.VMEM(w.shape, f32) for w in weights],
            *[pltpu.VMEM(w.shape, low) for w in weights[:3]],
            pltpu.SemaphoreType.DMA((len(weights) + 3,)),
            *line, *line, *line, *grid, *grid, *grid, *direct, *direct, *Direct.scratch(n_fsdp), *scatter_got,
        ],
        compiler_params=parameters(0),
    )(tokens, cotangent, codes, embedding, ada, qkv, out_w, up, down)


def gelu_parts(v):
    root = 0.7978845608028654
    square = v * v
    bent = jnp.tanh(root * (v + 0.044715 * v * square))
    value = 0.5 * v * (1.0 + bent)
    slope = 0.5 * (1.0 + bent) + (0.5 * root) * v * (1.0 - bent * bent) * (1.0 + (3.0 * 0.044715) * square)
    return value, slope


COLUMN_STEP = 256


def feed_forward_kernel(n_dp, n_fsdp, micro, hidden, mid, attn_own, cotangent, codes, mods, grad_mlp, up_g, down):
    low, f32 = jnp.bfloat16, jnp.float32
    rows, width = hidden.shape
    _, weight_rows, columns = down.shape
    tokens = n_fsdp * rows
    pair = 2 * rows
    own_images = mods.shape[1]
    line = LineGather.scratch(n_fsdp)
    grid = GridGather.scratch(n_dp)
    scatter_got = LineScatter.scratch(n_fsdp, rows, width)
    grads_got = GridScatter.scratch(n_dp, 1, weight_rows, columns)
    counts = [len(line), len(grid), len(scatter_got), len(grads_got)]
    tiles = columns // COLUMN_STEP
    row_tiles = weight_rows // COLUMN_STEP

    def kernel(
        hid, mid_ref, attn_ref, cot, cod, mods_ref, down_ref, gmlp_ref, up_ref,
        grad_mid, grad_attn, sums_own, grad_down, squares, mlp_part, grad_up,
        gmlp, up, hidden_g, down_g, upper, activ, grad_upper, part, gdown, grad_h2, stage, stage_up,
        moves, out_sem, up_sem, *rest,
    ):
        sems = split_refs(rest, counts)
        place = Place(n_dp, n_fsdp)
        fetch_up = pltpu.make_async_copy(up_ref, up, moves.at[0])
        fetch_gmlp = pltpu.make_async_copy(gmlp_ref, gmlp, moves.at[1])
        fetch_up.start()
        fetch_gmlp.start()
        enter(place, True, True)
        hidden_line = LineGather(place, hid, hidden_g, sems[0])
        downs = GridGather(place, down_ref, down_g, sems[1])
        hidden_line.start()
        downs.start()
        fetch_up.wait()

        def forward(chip):
            at = span(chip, pair)
            hidden_line.ready(chip)

            def tile(i):
                to = span(i, COLUMN_STEP)
                values = chip_rows(hidden_g, chip)
                total = jnp.zeros((pair, COLUMN_STEP), f32)
                for d in range(n_dp):
                    total = total + matmul(values[:, d * weight_rows : (d + 1) * weight_rows], up[0, d, :, to])
                upper[at, to] = total
                activ[at, to] = gelu_parts(total)[0].astype(low)

            loop(tiles, tile)

        def forward_at(distance):
            def side(i):
                chip = place.p + (1 - 2 * i) * distance

                @pl.when((chip >= 0) & (chip < place.chips))
                def _():
                    forward(chip)

            loop(2 if distance else 1, side)

        for step in range(1, place.chips):
            hidden_line.step(step)
            if step == place.chips // 2:
                downs.step()
            forward_at(step - 1)
        forward_at(place.chips - 1)
        fetch_gmlp.wait()
        downs.finish()
        scatter = LineScatter(place, part, grad_h2, sems[2])
        grads = GridScatter(place, gdown, grad_down, squares, sems[3])

        def backward(chip):
            at = span(chip, pair)

            def tile(i):
                to = span(i, COLUMN_STEP)
                values = chip_rows(gmlp, chip)
                total = jnp.zeros((pair, COLUMN_STEP), f32)
                for d in range(n_dp):
                    total = total + matmul(values[:, d * weight_rows : (d + 1) * weight_rows], down_g[0, d, :, to])
                grad_upper[at, to] = (total * gelu_parts(upper[at, to])[1]).astype(low)

            loop(tiles, tile)
            values = grad_upper[at, :]
            for d in range(n_dp):
                piece = matmul_last(values, up[0, d]).astype(low).reshape(2, rows, weight_rows)
                part[span(chip, 2), :, d * weight_rows : (d + 1) * weight_rows] = piece

        def down_tile(i):
            d, r = i // row_tiles, lax.rem(i, row_tiles)
            left = gmlp[:, :, span(i, COLUMN_STEP)].reshape(tokens, COLUMN_STEP)
            gdown[0, d, span(r, COLUMN_STEP), :] = matmul_first(left, activ[...]).astype(low)

        def then(k):
            @pl.when(k == 0)
            def _():
                loop(n_dp * row_tiles, down_tile)
                grads.start()

        slot = scatter.paced(backward, 2, then)

        def up_copy(i, d, r):
            return pltpu.make_async_copy(
                stage_up.at[lax.rem(i, 2)], grad_up.at[0, d, span(r, COLUMN_STEP)], up_sem.at[lax.rem(i, 2)]
            )

        def up_tile(i):
            d, r = i // row_tiles, lax.rem(i, row_tiles)

            @pl.when(i >= 2)
            def _():
                up_copy(i, 0, 0).wait()

            left = hidden_g[:, :, span(i, COLUMN_STEP)].reshape(tokens, COLUMN_STEP)
            stage_up[lax.rem(i, 2)] = matmul_first(left, grad_upper[...]).astype(low)
            up_copy(i, d, r).start()

        slot = scatter.beside(slot, n_dp * row_tiles, up_tile)
        up_copy(0, 0, 0).wait()
        up_copy(1, 0, 0).wait()
        grads.step()

        def mlp_copy(chip):
            to = lax.rem(chip, 2)
            return pltpu.make_async_copy(stage.at[to], mlp_part.at[span(chip, 2)], out_sem.at[to])

        def mlp_tile(chip):
            @pl.when(chip >= 2)
            def _():
                mlp_copy(chip).wait()

            values = activ[span(chip, pair), :]
            for d in range(n_dp):
                piece = matmul_last(values, down_g[0, d]).astype(low).reshape(2, rows, weight_rows)
                stage[lax.rem(chip, 2), :, :, d * weight_rows : (d + 1) * weight_rows] = piece
            mlp_copy(chip).start()

        slot = scatter.beside(slot, place.chips, mlp_tile)
        mlp_copy(0).wait()
        mlp_copy(1).wait()
        scatter.run_to(slot, scatter.slots)
        grads.step_own()
        scatter.finish()
        own = Rows(place, cod, mods_ref, micro, rows, own_images // micro)
        sums_own[...] = jnp.zeros_like(sums_own)

        def norm_grad(m, at):
            slot, alive = own.slot_live(m, at)
            normed, inv_std = normalize(mid_ref[at, :])
            grad = grad_h2[at, :]
            before = normalize_back(grad * (1.0 + own.pick(4, m, slot)), normed, inv_std)
            total = cot[at, :].astype(f32) * alive + before
            grad_mid[at, :] = total
            grad_attn[at, :] = (total * own.pick(2, m, slot)).astype(low)
            own.add_up(sums_own, 0, m, slot, total * attn_ref[at, :])
            own.add_up(sums_own, 1, m, slot, grad)
            own.add_up(sums_own, 2, m, slot, grad * normed)

        own.tiles(norm_grad)
        grads.finish()
        hidden_line.drain()

    return pl.pallas_call(
        kernel,
        out_shape=[
            jax.ShapeDtypeStruct((rows, width), f32),
            jax.ShapeDtypeStruct((rows, width), low),
            jax.ShapeDtypeStruct((3, own_images, width), f32),
            jax.ShapeDtypeStruct((1, weight_rows, columns), f32),
            jax.ShapeDtypeStruct(TILE, f32),
            jax.ShapeDtypeStruct((n_fsdp, rows, width), low),
            jax.ShapeDtypeStruct((1, n_dp, weight_rows, columns), low),
        ],
        in_specs=[WHOLE] * 6 + [HBM] * 3,
        out_specs=[WHOLE] * 5 + [HBM] * 2,
        scratch_shapes=[
            pltpu.VMEM((n_fsdp, rows, width), low),
            pltpu.VMEM((1, n_dp, weight_rows, columns), low),
            pltpu.VMEM((n_fsdp, rows, width), low),
            pltpu.VMEM((1, n_dp, weight_rows, columns), low),
            pltpu.VMEM((tokens, columns), f32),
            pltpu.VMEM((tokens, columns), low),
            pltpu.VMEM((tokens, columns), low),
            pltpu.VMEM((n_fsdp, rows, width), low),
            pltpu.VMEM((1, n_dp, weight_rows, columns), low),
            pltpu.VMEM((rows, width), f32),
            pltpu.VMEM((2, 2, rows, width), low),
            pltpu.VMEM((2, COLUMN_STEP, columns), low),
            pltpu.SemaphoreType.DMA((2,)),
            pltpu.SemaphoreType.DMA((2,)),
            pltpu.SemaphoreType.DMA((2,)),
            *line, *grid, *scatter_got, *grads_got,
        ],
        compiler_params=parameters(2),
    )(hidden, mid, attn_own, cotangent, codes, mods, down, grad_mlp, up_g)


def attention_grad_kernel(
    n_dp, n_fsdp, micro, grad_attn, tokens_own, mid, grad_mid, cotangent, codes, mods, codes_g, mlp_part, grad_up, qkv_g,
    out_g, qkv_low, attended, hidden_g,
):
    low, f32 = jnp.bfloat16, jnp.float32
    rows, width = grad_attn.shape
    which, _, weight_rows, head_columns = qkv_g.shape
    tokens = n_fsdp * rows
    pair = 2 * rows
    chips = n_fsdp // 2
    own_images = mods.shape[1]
    line = LineGather.scratch(n_fsdp)
    scatter_got = LineScatter.scratch(n_fsdp, rows, width)
    up_shape = (1, *grad_up.shape[2:])
    up_got = GridScatter.scratch(n_dp, *up_shape)
    qkv_got = GridScatter.scratch(n_dp, which, weight_rows, head_columns)
    out_got = GridScatter.scratch(n_dp, 1, weight_rows, head_columns)
    counts = [len(line), len(scatter_got), len(scatter_got), len(up_got), len(qkv_got), len(out_got)]
    row_tiles = weight_rows // COLUMN_STEP

    def kernel(
        ga, tok, mid_ref, gmid, cot, cod, mods_ref, cod_g, mlp_ref, gup_ref, qkv_wr, out_wr, qkv_lr, att_r, hid_r,
        block_out, input_grad, sums_own, grad_up_own, grad_qkv_own, grad_out_own, squares,
        ga_g, gqkv, gqkv_w, gout_w, mlp_own, grad_h1, tile_up, tile_qkv, tile_out,
        mine, gup, qkv_w, out_w, qkv_ref, att, hid_g, moves, mine_sem, *rest,
    ):
        sems = split_refs(rest, counts)
        place = Place(n_dp, n_fsdp)
        fetches = [
            pltpu.make_async_copy(ref, to, moves.at[i])
            for i, (ref, to) in enumerate(
                ((gup_ref, gup), (att_r, att), (out_wr, out_w), (qkv_lr, qkv_ref), (qkv_wr, qkv_w), (hid_r, hid_g))
            )
        ]
        terms = [
            pltpu.make_async_copy(mlp_ref.at[chip * 2 + place.c], mine.at[chip], mine_sem.at[chip])
            for chip in range(chips)
        ]
        fetches[0].start()
        for term in terms:
            term.start()
        for fetch in fetches[1:]:
            fetch.start()
        enter(place, True, True)
        ga_line = LineGather(place, ga, ga_g, sems[0])
        mlp_scatter = LineScatter(place, mlp_ref, mlp_own, sems[1], mine, LineScatter.pieces)
        ups = GridScatter(place, gup, grad_up_own, tile_up, sems[3])
        ga_line.start()
        fetches[0].wait()
        ups.start()
        mlp_scatter.start()
        for term in terms:
            term.wait()
        travel = LineScatter.pieces * (chips - 1)
        at_slot = 0
        for step in range(1, chips):
            ga_line.step(step)
            if step < chips - 1:
                to_slot = travel * step // (chips - 1)
                mlp_scatter.run(at_slot, to_slot)
                at_slot = to_slot
            if step == chips // 2:
                ups.step()
        ga_line.finish()
        for fetch in fetches[1:]:
            fetch.wait()
        scatter = LineScatter(place, ga_g, grad_h1, sems[2])
        qkvs = GridScatter(place, gqkv_w, grad_qkv_own, tile_qkv, sems[4])
        outs = GridScatter(place, gout_w, grad_out_own, tile_out, sems[5])

        def out_tile(i):
            d, r = i // row_tiles, lax.rem(i, row_tiles)
            left = ga_g[:, :, span(i, COLUMN_STEP)].reshape(tokens, COLUMN_STEP)
            gout_w[0, d, span(r, COLUMN_STEP), :] = matmul_first(left, att[...]).astype(low)

        loop(n_dp * row_tiles, out_tile)
        outs.start()

        def compute(chip):
            at = span(chip, pair)
            values = chip_rows(ga_g, chip)
            grad_heads = matmul(values, out_w[0].reshape(width, head_columns)).astype(low)
            allowed = pair_mask(cod_g, chip, rows)
            for h in range(head_columns // HEAD):
                head = slice(h * HEAD, (h + 1) * HEAD)
                query, key, value = [qkv_ref[w, at, head] for w in range(which)]
                grad_head = grad_heads[:, head]
                probs = attention_probs(query, key, allowed)
                grad_p = matmul_last(grad_head, value)
                delta = jnp.sum(probs * grad_p, axis=-1, keepdims=True)
                grad_scores = (probs * (grad_p - delta)).astype(low)
                scale = HEAD ** (-0.5)
                gqkv[0, at, head] = (matmul(grad_scores, key) * scale).astype(low)
                gqkv[1, at, head] = (matmul_first(grad_scores, query) * scale).astype(low)
                gqkv[2, at, head] = matmul_first(probs.astype(low), grad_head).astype(low)
            for d in range(n_dp):
                total = matmul_last(gqkv[0, at, :], qkv_w[0, d])
                for w in range(1, which):
                    total = total + matmul_last(gqkv[w, at, :], qkv_w[w, d])
                piece = total.astype(low).reshape(2, rows, weight_rows)
                ga_g[span(chip, 2), :, d * weight_rows : (d + 1) * weight_rows] = piece

        def then(k):
            @pl.when(k == 1)
            def _():
                mlp_scatter.run(at_slot, travel)

        slot = scatter.paced(compute, 2, then)

        def grad_tile(i):
            d, r = i // row_tiles, lax.rem(i, row_tiles)
            left = hid_g[:, :, span(i, COLUMN_STEP)].reshape(tokens, COLUMN_STEP)
            for w in range(which):
                gqkv_w[w, d, span(r, COLUMN_STEP), :] = matmul_first(left, gqkv[w]).astype(low)

        slot = scatter.beside(slot, n_dp * row_tiles, grad_tile, 4)
        qkvs.start()
        outs.step()
        slot = scatter.run_to(slot, scatter.slots * 5 // 8)
        ups.step_own()
        mlp_scatter.finish()
        ups.finish()
        own = Rows(place, cod, mods_ref, micro, rows, own_images // micro)
        sums_own[...] = jnp.zeros_like(sums_own)

        def branch_out(m, at):
            slot_of, alive = own.slot_live(m, at)
            branch = mlp_own[at, :]
            block_out[at, :] = (mid_ref[at, :] + own.pick(5, m, slot_of) * branch).astype(low)
            own.add_up(sums_own, 2, m, slot_of, cot[at, :].astype(f32) * alive * branch)

        own.tiles(branch_out)
        slot = scatter.run_to(slot, scatter.slots * 3 // 4)
        qkvs.step()
        scatter.run_to(slot, scatter.slots)
        outs.step_own()
        qkvs.step_own()
        scatter.finish()

        def norm_grad(m, at):
            slot_of, _ = own.slot_live(m, at)
            normed, inv_std = normalize(tok[at, :].astype(f32))
            grad = grad_h1[at, :]
            before = normalize_back(grad * (1.0 + own.pick(1, m, slot_of)), normed, inv_std)
            input_grad[at, :] = gmid[at, :] + before
            own.add_up(sums_own, 0, m, slot_of, grad)
            own.add_up(sums_own, 1, m, slot_of, grad * normed)

        own.tiles(norm_grad)
        outs.finish()
        qkvs.finish()
        squares[...] = tile_up[...] + tile_qkv[...] + tile_out[...]

    return pl.pallas_call(
        kernel,
        out_shape=[
            jax.ShapeDtypeStruct((rows, width), low),
            jax.ShapeDtypeStruct((rows, width), f32),
            jax.ShapeDtypeStruct((3, own_images, width), f32),
            jax.ShapeDtypeStruct(up_shape, f32),
            jax.ShapeDtypeStruct((which, weight_rows, head_columns), f32),
            jax.ShapeDtypeStruct((1, weight_rows, head_columns), f32),
            jax.ShapeDtypeStruct(TILE, f32),
        ],
        in_specs=[WHOLE] * 8 + [HBM] * 7,
        out_specs=[WHOLE] * 7,
        scratch_shapes=[
            pltpu.VMEM((n_fsdp, rows, width), low),
            pltpu.VMEM((which, tokens, head_columns), low),
            pltpu.VMEM((which, n_dp, weight_rows, head_columns), low),
            pltpu.VMEM((1, n_dp, weight_rows, head_columns), low),
            pltpu.VMEM((rows, width), f32),
            pltpu.VMEM((rows, width), f32),
            pltpu.VMEM(TILE, f32),
            pltpu.VMEM(TILE, f32),
            pltpu.VMEM(TILE, f32),
            pltpu.VMEM((chips, rows, width), low),
            *[pltpu.VMEM(a.shape, low) for a in (grad_up, qkv_g, out_g, qkv_low, attended, hidden_g)],
            pltpu.SemaphoreType.DMA((6,)),
            pltpu.SemaphoreType.DMA((chips,)),
            *line, *scatter_got, *scatter_got, *up_got, *qkv_got, *out_got,
        ],
        compiler_params=parameters(3),
    )(
        grad_attn, tokens_own, mid, grad_mid, cotangent, codes, mods, codes_g, mlp_part, grad_up, qkv_g, out_g, qkv_low,
        attended, hidden_g,
    )


def norm_kernel(n_dp, n_fsdp, micro, sums_first, sums_second, condition, squares):
    own_images, width = sums_first.shape[1:]
    wide = width // n_fsdp
    images, deep = condition.shape[1:]
    lanes = wide // 128
    slots_here = own_images // micro
    source = [(0, 0), (0, 1), (1, 0), (1, 1), (1, 2), (0, 2)]

    def kernel(
        sums_a, sums_b, cond, squares_ref, grad, norm, mail, boxes, mine, all_mods, tile, tiles, sums, sums_all, *sems
    ):
        place = Place(n_dp, n_fsdp)
        barrier = pltpu.get_barrier_semaphore()
        for i in range(1, n_dp):
            pl.semaphore_signal(
                barrier, inc=1, device_id=place.at_dp((place.dp + i) % n_dp), device_id_type=MESH
            )
        for i in range(1, n_fsdp):
            pl.semaphore_signal(
                barrier, inc=1, device_id=(place.dp, (place.f + i) % n_fsdp), device_id_type=MESH
            )
        for j, (which, row) in enumerate(source):
            values = (sums_a, sums_b)[which][row].astype(jnp.bfloat16).astype(jnp.float32)
            for f in range(n_fsdp):
                for g in range(lanes):
                    at = (j * lanes + g) * own_images
                    mail[f, at : at + own_images, :] = values[:, f * wide + g * 128 : f * wide + (g + 1) * 128]
        pl.semaphore_wait(barrier, n_dp + n_fsdp - 2)
        inner = Direct(place, mail, boxes, sems[0:2], "fsdp", block=lambda ref, d: ref.at[d])
        inner.start()
        boxes[place.f] = mail[place.f]
        inner.finish()
        for j in range(MODS):
            for g in range(lanes):
                pieces = []
                for m in range(micro):
                    at = (j * lanes + g) * own_images + m * slots_here
                    pieces += [boxes[f, at : at + slots_here, :] for f in range(n_fsdp)]
                mine[j, :, g * 128 : (g + 1) * 128] = jnp.concatenate(pieces, axis=0).astype(jnp.bfloat16)
        outer = Direct(place, mine, all_mods, sems[2:4])
        outer.start()
        all_mods[place.dp] = mine[...]
        outer.finish()
        total = squares_ref[...]
        every = cond[...].reshape(n_dp * images, deep)
        for j in range(MODS):
            grad[j] = matmul_first(every, all_mods[:, j].reshape(n_dp * images, wide))
        tile[...] = total

        def add(at):
            for j in range(MODS):
                values = grad[j, at, :]
                values = values * values
                for lane in range(0, wide, 128):
                    tile[...] += values[:, lane : lane + 128]

        row_loop(deep, add)
        first = Direct(place, tile, tiles, sems[4:6], "fsdp")
        first.start()
        tiles[place.f] = tile[...]
        first.finish()
        total = tiles[0]
        for f in range(1, n_fsdp):
            total = total + tiles[f]
        sums[...] = total
        second = Direct(place, sums, sums_all, sems[6:8])
        second.start()
        sums_all[place.dp] = sums[...]
        second.finish()
        total = sums_all[0]
        for d in range(1, n_dp):
            total = total + sums_all[d]
        norm[0, 0] = jnp.sqrt(jnp.sum(total))

    return pl.pallas_call(
        kernel,
        out_shape=[
            jax.ShapeDtypeStruct((MODS, deep, wide), jnp.float32),
            jax.ShapeDtypeStruct((1, 1), jnp.float32),
        ],
        in_specs=[WHOLE] * 4,
        out_specs=[WHOLE, pl.BlockSpec(memory_space=pltpu.SMEM)],
        scratch_shapes=[
            pltpu.VMEM((n_fsdp, MODS * lanes * own_images, 128), jnp.float32),
            pltpu.VMEM((n_fsdp, MODS * lanes * own_images, 128), jnp.float32),
            pltpu.VMEM((MODS, images, wide), jnp.bfloat16),
            pltpu.VMEM((n_dp, MODS, images, wide), jnp.bfloat16),
            pltpu.VMEM(TILE, jnp.float32),
            pltpu.VMEM((n_fsdp, *TILE), jnp.float32),
            pltpu.VMEM(TILE, jnp.float32),
            pltpu.VMEM((n_dp, *TILE), jnp.float32),
            *Direct.scratch(n_fsdp), *Direct.scratch(n_dp), *Direct.scratch(n_fsdp), *Direct.scratch(n_dp),
        ],
        compiler_params=parameters(1),
    )(sums_first, sums_second, condition, squares)


def adam_kernel(factor, grad, master, first, second):
    which, rows, columns = master.shape
    step = min(rows, max(64, 131072 // columns))
    block = pl.BlockSpec((1, step, columns), lambda w, r: (w, r, 0))

    def kernel(factor_ref, grad_ref, master_ref, first_ref, second_ref, new_ref, copy_ref, moment_ref, square_ref):
        scale = factor_ref[0, 0]
        clipped = grad_ref[...] * scale
        moment = BETA_ONE * first_ref[...] + (1.0 - BETA_ONE) * clipped
        square = BETA_TWO * second_ref[...] + (1.0 - BETA_TWO) * clipped * clipped
        moment_ref[...] = moment
        square_ref[...] = square
        below = jnp.sqrt(square * (1.0 / (1.0 - BETA_TWO**STEP))) + ADAM_EPS
        ratio = moment * (1.0 / (1.0 - BETA_ONE**STEP)) / below
        old = master_ref[...]
        new = old - LEARN_RATE * (ratio + WEIGHT_DECAY * old)
        new_ref[...] = new
        copy_ref[...] = new.astype(jnp.bfloat16)

    shape = jax.ShapeDtypeStruct(master.shape, jnp.float32)
    return pl.pallas_call(
        kernel,
        grid=(which, rows // step),
        out_shape=[shape, jax.ShapeDtypeStruct(master.shape, jnp.bfloat16), shape, shape],
        in_specs=[pl.BlockSpec(memory_space=pltpu.SMEM)] + [block] * 4,
        out_specs=[block] * 4,
        compiler_params=pltpu.CompilerParams(vmem_limit_bytes=VMEM_LIMIT),
    )(factor, grad, master, first, second)


def normalize(values):
    average = jnp.mean(values, axis=-1, keepdims=True)
    centred = values - average
    inv_std = lax.rsqrt(jnp.mean(centred * centred, axis=-1, keepdims=True) + NORM_EPS)
    return (centred * inv_std, inv_std)


def normalize_back(grad, normed, inv_std):
    return inv_std * (
        grad
        - jnp.mean(grad, axis=-1, keepdims=True)
        - normed * jnp.mean(grad * normed, axis=-1, keepdims=True)
    )


def body(n_dp, n_fsdp, *arguments):
    tokens, embedding, image_slot, token_mask, cotangent = arguments[:5]
    weights = [w if w.ndim == 3 else w[:, None] for w in arguments[5:]]
    weights = [w.transpose(1, 0, 2) for w in weights]
    masters, firsts, seconds = weights[:5], weights[5:10], weights[10:]
    qkv_w, out_w, up_w, down_w, ada_w = masters
    micro, tok_rows, width = tokens.shape
    own_rows = micro * tok_rows
    image_count = embedding.shape[1] // n_fsdp
    images = micro * n_fsdp * image_count
    images_of = jnp.arange(micro, dtype=jnp.int32)[:, None] * image_count
    codes = jnp.stack([(images_of + image_slot).reshape(own_rows), token_mask.reshape(own_rows)])
    codes = jnp.pad(codes.astype(jnp.float32), ((0, 6), (0, 0)))
    own_tokens = tokens.reshape(own_rows, width)
    own_cot = cotangent.reshape(own_rows, width)

    (
        attn_own, mid, hidden2, mods, cond_all, codes, codes_g, qkv_low, attended, down_low,
        hidden1_g, qkv_g, out_g, up_g, grad_mlp_g,
    ) = attention_kernel(
        n_dp, n_fsdp, micro, own_tokens, own_cot, codes, embedding.reshape(images, -1), ada_w, qkv_w, out_w, up_w, down_w
    )
    grad_mid, grad_attn, sums_second, grad_down, squares_down, mlp_part, grad_up = feed_forward_kernel(
        n_dp, n_fsdp, micro, hidden2, mid, attn_own, own_cot, codes, mods, grad_mlp_g, up_g, down_low
    )
    block_out, input_grad, sums_first, grad_up, grad_qkv_w, grad_out, squares = attention_grad_kernel(
        n_dp, n_fsdp, micro, grad_attn, own_tokens, mid, grad_mid, own_cot, codes, mods, codes_g, mlp_part, grad_up,
        qkv_g, out_g, qkv_low, attended, hidden1_g,
    )
    block_out = block_out.reshape(tokens.shape)
    input_grad = input_grad.reshape(tokens.shape)
    grad_ada, grad_norm = norm_kernel(
        n_dp, n_fsdp, micro, sums_first, sums_second, cond_all, squares_down + squares
    )

    factor = jnp.minimum(1.0, CLIP_AT / grad_norm)
    results = []
    grads = (grad_qkv_w, grad_out, grad_up, grad_down, grad_ada)
    for given, grad, master, first, second in zip(arguments[5:], grads, masters, firsts, seconds):
        for updated in adam_kernel(factor, grad, master, first, second):
            results.append(updated.transpose(1, 0, 2).reshape(given.shape))
    return (block_out, input_grad, *results, grad_norm[0, 0])


def solution(mesh):
    n_dp, n_fsdp = mesh.shape["dp"], mesh.shape["fsdp"]
    rows = P(None, ("dp", "fsdp"), None)
    slots = P(None, ("dp", "fsdp"))
    thick = P("dp", None, "fsdp")
    flat = P("dp", "fsdp")
    weights = (thick, flat, flat, flat, thick)
    updated = tuple(spec for spec in weights for _ in range(4))
    return jax.shard_map(
        functools.partial(body, n_dp, n_fsdp),
        mesh=mesh,
        in_specs=(rows, P(None, "dp", None), slots, slots, rows, *weights, *weights, *weights),
        out_specs=(rows, rows, *updated, P()),
        check_vma=False,
    )
```

```python
import functools

import jax
import jax.numpy as jnp
from jax import lax
from jax.experimental import pallas as pl
from jax.experimental.pallas import tpu as pltpu
from jax.sharding import PartitionSpec as P

HEAD = 128
STEP = 10
MODS = 6
FIRST_KINDS = (0, 1, 5)
OTHER_KINDS = (2, 3, 4)

NORM_EPS = 1e-06
CLIP_AT = 1.0
BETA_ONE = 0.9
BETA_TWO = 0.999
LEARN_RATE = 0.05
WEIGHT_DECAY = 0.1
ADAM_EPS = 1e-08

MESH = pl.DeviceIdType.MESH
VMEM_LIMIT = 62 * 1024 * 1024
ROW_STEP = 16


class Place:
    def __init__(self, n_dp, n_fsdp):
        self.n_dp, self.n_fsdp = n_dp, n_fsdp
        self.chips = n_fsdp // 2
        self.grid_a = 2
        self.grid_b = n_dp // 2
        self.dp = lax.axis_index("dp")
        self.f = lax.axis_index("fsdp")
        self.p = self.f // 2
        self.c = self.f % 2
        self.a = self.dp // self.grid_b
        self.b = self.dp % self.grid_b

    def at_chip(self, chip):
        return (self.dp, chip * 2 + self.c)

    def sibling(self):
        return (self.dp, self.p * 2 + 1 - self.c)

    def at_dp(self, dp):
        return (dp, self.f)

    def b_peer(self, i):
        return (self.b + i) % self.grid_b

    def a_peer(self, i):
        return (self.a + i) % self.grid_a


def announce(place, line=False, grid=False, group=False):
    barrier = pltpu.get_barrier_semaphore()
    devices = []
    if group:
        for i in range(1, place.n_fsdp):
            devices.append((place.dp, (place.f + i) % place.n_fsdp))
    elif line:
        devices.append(place.at_chip((place.p + 1) % place.chips))
        devices.append(place.at_chip((place.p + place.chips - 1) % place.chips))
        devices.append(place.sibling())
    if grid:
        for i in range(1, place.n_dp):
            devices.append(place.at_dp((place.dp + i) % place.n_dp))
    for device in devices:
        pl.semaphore_signal(barrier, inc=1, device_id=device, device_id_type=MESH)
    return len(devices)


def enter(place, line=False, grid=False, group=False):
    count = announce(place, line, grid, group)
    pl.semaphore_wait(pltpu.get_barrier_semaphore(), count)


def remote(src, dst, send, recv, device):
    return pltpu.make_async_remote_copy(
        src_ref=src, dst_ref=dst, send_sem=send, recv_sem=recv, device_id=device, device_id_type=MESH
    )


class LineGather:
    @staticmethod
    def scratch(n_fsdp):
        chips = n_fsdp // 2
        return [
            pltpu.SemaphoreType.DMA((2, chips)),
            pltpu.SemaphoreType.DMA((2, chips)),
            pltpu.SemaphoreType.DMA((chips,)),
            pltpu.SemaphoreType.DMA((chips,)),
            pltpu.SemaphoreType.DMA,
        ]

    def __init__(self, place, src, out, sems, block=None):
        self.place, self.src, self.out = place, src, out
        self.send, self.recv, self.csend, self.crecv, self.local = sems
        self.of = block or (lambda ref, d: ref.at[d])

    def _block(self, chip):
        return self.of(self.out, chip * 2 + self.place.c)

    def _hop(self, way, step, first):
        pc = self.place
        chip = pc.p - step if way == 0 else pc.p + step
        target = pc.p + 1 if way == 0 else pc.p - 1
        src = self.src if first else self._block(chip)
        return remote(src, self._block(chip), self.send.at[way, step], self.recv.at[way, step], pc.at_chip(target))

    def _side(self, chip, first=False):
        src = self.src if first else self._block(chip)
        return remote(src, self._block(chip), self.csend.at[chip], self.crecv.at[chip], self.place.sibling())

    def _sends(self, way, step):
        pc = self.place
        if way == 0:
            return (pc.p < pc.chips - 1) & (pc.p >= step)
        return (pc.p > 0) & (pc.p + step <= pc.chips - 1)

    def start_way(self, way):
        @pl.when(self._sends(way, 0))
        def _():
            self._hop(way, 0, True).start()

    def start_here(self):
        pc = self.place
        self._side(pc.p, True).start()
        pltpu.make_async_copy(self.src, self._block(pc.p), self.local).start()

    def start(self):
        self.start_way(0)
        self.start_way(1)
        self.start_here()

    def step(self, step):
        pc = self.place
        for way in range(2):
            chip = pc.p - step if way == 0 else pc.p + step
            here = (chip >= 0) if way == 0 else (chip <= pc.chips - 1)

            @pl.when(here)
            def _():
                remote(
                    self._block(chip), self._block(chip), self.send.at[way, step - 1], self.recv.at[way, step - 1],
                    pc.sibling(),
                ).wait_recv()
                if step < pc.chips - 1:
                    @pl.when(self._sends(way, step))
                    def _():
                        self._hop(way, step, False).start()
                self._side(chip).start()

    def ready(self, chip):
        pc = self.place
        other = self.of(self.out, chip * 2 + 1 - pc.c)
        remote(other, other, self.csend.at[chip], self.crecv.at[chip], pc.sibling()).wait_recv()

        @pl.when(chip == pc.p)
        def _():
            pltpu.make_async_copy(self.src, self._block(pc.p), self.local).wait()

    def drain(self):
        pc = self.place
        for chip in range(pc.chips):
            self._side(chip).wait_send()
        for way in range(2):
            for step in range(pc.chips - 1):
                @pl.when(self._sends(way, step))
                def _():
                    self._hop(way, step, False).wait_send()

    def finish(self):
        for chip in range(self.place.chips):
            self.ready(chip)
        self.drain()


class LineCast:
    @staticmethod
    def scratch(n_fsdp):
        return [pltpu.SemaphoreType.DMA((n_fsdp // 2,)) for _ in range(4)] + [pltpu.SemaphoreType.DMA]

    def __init__(self, place, src, out, sems, block):
        self.place, self.src, self.out, self.of = place, src, out, block
        self.send, self.recv, self.csend, self.crecv, self.local = sems

    def _copy(self, i, coming=False):
        pc = self.place
        chip = (pc.p + pc.chips - i) % pc.chips if coming else pc.p
        return remote(
            self.src, self.of(self.out, chip * 2 + pc.c), self.send.at[i], self.recv.at[i],
            pc.at_chip((pc.p + i) % pc.chips),
        )

    def _side(self, i, coming=False):
        pc = self.place
        chip = (pc.p + pc.chips - i) % pc.chips
        block = self.of(self.out, chip * 2 + (1 - pc.c if coming else pc.c))
        return remote(block if i else self.src, block, self.csend.at[i], self.crecv.at[i], pc.sibling())

    def start(self):
        pc = self.place
        for i in range(1, pc.chips):
            self._copy(i).start()
        self._side(0).start()
        pltpu.make_async_copy(self.src, self.of(self.out, pc.f), self.local).start()

    def step(self):
        for i in range(1, self.place.chips):
            self._copy(i, True).wait_recv()
            self._side(i).start()

    def finish(self):
        pc = self.place
        pltpu.make_async_copy(self.src, self.of(self.out, pc.f), self.local).wait()
        for i in range(pc.chips):
            self._side(i, True).wait_recv()
            self._side(i).wait_send()
        for i in range(1, pc.chips):
            self._copy(i).wait_send()


def row_loop(rows, body, first=0):
    def run(i, carry):
        body(pl.ds(pl.multiple_of(first + i * ROW_STEP, ROW_STEP), ROW_STEP))
        return carry

    lax.fori_loop(0, rows // ROW_STEP, run, 0)


class LineScatter:
    pieces = 4

    @classmethod
    def scratch(cls, n_fsdp, rows, width):
        chips = n_fsdp // 2
        return [
            pltpu.VMEM((chips, rows, width), jnp.bfloat16),
            pltpu.VMEM((chips + 1, rows, width), jnp.bfloat16),
            pltpu.SemaphoreType.DMA((chips,)),
            pltpu.SemaphoreType.DMA((chips,)),
            pltpu.SemaphoreType.DMA((2, chips, cls.pieces)),
            pltpu.SemaphoreType.DMA((2, chips, cls.pieces)),
        ]

    def __init__(self, place, part, out, scratch, mine=None, lag=2):
        self.place, self.part, self.out, self.mine = place, part, out, mine
        self.side, self.inbox, self.csend, self.crecv, self.send, self.recv = scratch
        self.rows = out.shape[0]
        self.piece = self.rows // self.pieces
        self.lag = lag
        self.slots = (place.chips - 1) * self.lag + place.chips * self.pieces

    def _side(self, chip):
        pc = self.place
        return remote(
            self.part.at[chip * 2 + 1 - pc.c], self.side.at[chip], self.csend.at[chip], self.crecv.at[chip], pc.sibling()
        )

    def _hop(self, way, chip, s):
        pc = self.place
        target = pc.p + 1 if way == 0 else pc.p - 1
        rows = pl.ds(pl.multiple_of(s * self.piece, self.piece), self.piece)
        return remote(
            self.side.at[chip, rows], self.inbox.at[chip + 1 - way, rows], self.send.at[way, chip, s],
            self.recv.at[way, chip, s], pc.at_chip(target),
        )

    def start(self):
        def one(k, carry):
            self.offer(self.order(k))
            return carry

        lax.fori_loop(0, self.place.chips, one, 0)

    def offer(self, chip):
        self._side(chip).start()

    def order(self, k):
        pc = self.place
        chips = pc.chips
        after, before = chips - 1 - pc.p, pc.p
        short = jnp.minimum(after, before)
        lone = jnp.maximum(after, before) - short
        rest = jnp.maximum(k - lone, 0)
        near = short - rest // 2
        pair = jnp.where(lax.rem(rest, 2) == 0, pc.p + near, pc.p - near)
        return jnp.where(k < lone, jnp.where(after > before, chips - 1 - k, k), pair)

    def first_slot(self, k):
        pc = self.place
        chips = pc.chips
        chip = self.order(k)
        after = pc.p * self.lag + (chips - 1 - chip) * self.pieces
        before = (chips - 1 - pc.p) * self.lag + chip * self.pieces
        slot = jnp.where(chip > pc.p, after, before)
        return jnp.where((k >= chips - 1) | (chip == pc.p), self.slots, slot)

    def paced(self, compute, pace, then):
        def one(k, slot):
            chip = self.order(k)
            compute(chip)
            self.offer(chip)
            until = jnp.minimum(self.first_slot(k + 1), self.first_slot(k + 2))
            until = jnp.maximum(jnp.minimum(until, (k + 1) * pace), slot)
            self.run(slot, until)
            then(k)
            return until

        return lax.fori_loop(0, self.place.chips, one, jnp.int32(0))

    def beside(self, slot, count, work, every=1):
        def one(i, carry):
            work(i)

            @pl.when(lax.rem(i, every) == every - 1)
            def _():
                self.step(slot + i // every)

            return carry

        lax.fori_loop(0, count, one, 0)
        return slot + count // every

    def run_to(self, slot, end):
        end = jnp.maximum(slot, end)
        self.run(slot, end)
        return end

    def _add(self, chip, s, inboxes, store):
        pc = self.place

        def add(rows):
            if self.mine is None:
                total = self.part[chip * 2 + pc.c, rows, :].astype(jnp.float32)
            else:
                total = self.mine[chip, rows, :].astype(jnp.float32)
            total = total + self.side[chip, rows, :].astype(jnp.float32)
            for way in inboxes:
                total = total + self.inbox[chip + 1 - way, rows, :].astype(jnp.float32)
            store(rows, total)

        row_loop(self.piece, add, s * self.piece)

    def _travel(self, way, t):
        pc = self.place
        chips = pc.chips
        i = t - (pc.p if way == 0 else chips - 1 - pc.p) * self.lag
        k = jnp.clip(i // self.pieces, 0, chips - 1)
        s = lax.rem(jnp.maximum(i, 0), self.pieces)
        chip = chips - 1 - k if way == 0 else k
        going = (i >= 0) & (i < chips * self.pieces) & ((chip > pc.p) if way == 0 else (chip < pc.p))
        first = (pc.p == 0) if way == 0 else (pc.p == chips - 1)

        def store(rows, total):
            self.side[chip, rows, :] = total.astype(jnp.bfloat16)

        @pl.when(going)
        def _():
            @pl.when(s == 0)
            def _():
                self._side(chip).wait_recv()

            @pl.when(first)
            def _():
                self._add(chip, s, (), store)

            @pl.when(jnp.logical_not(first))
            def _():
                self._hop(way, chip, s).wait_recv()
                self._add(chip, s, (way,), store)

            self._hop(way, chip, s).start()

    def step(self, t):
        self._travel(0, t)
        self._travel(1, t)

    def run(self, begin, end):
        def one(t, carry):
            self.step(t)
            return carry

        lax.fori_loop(begin, end, one, 0)

    def finish(self):
        pc = self.place
        chips = pc.chips
        self._side(pc.p).wait_recv()

        def store(rows, total):
            self.out[rows, :] = total

        def piece(s, carry):
            @pl.when(pc.p == 0)
            def _():
                self._hop(1, pc.p, s).wait_recv()
                self._add(pc.p, s, (1,), store)

            @pl.when(pc.p == chips - 1)
            def _():
                self._hop(0, pc.p, s).wait_recv()
                self._add(pc.p, s, (0,), store)

            @pl.when((pc.p > 0) & (pc.p < chips - 1))
            def _():
                self._hop(0, pc.p, s).wait_recv()
                self._hop(1, pc.p, s).wait_recv()
                self._add(pc.p, s, (0, 1), store)

            return carry

        lax.fori_loop(0, self.pieces, piece, 0)
        for chip in range(chips):
            self._side(chip).wait_send()

            def sent(s, carry):
                @pl.when(chip > pc.p)
                def _():
                    self._hop(0, chip, s).wait_send()

                @pl.when(chip < pc.p)
                def _():
                    self._hop(1, chip, s).wait_send()

                return carry

            lax.fori_loop(0, self.pieces, sent, 0)


class GridGather:
    @staticmethod
    def scratch(n_dp):
        na, nb = 2, n_dp // 2
        return [
            pltpu.SemaphoreType.DMA((2, max(nb - 1, 1))),
            pltpu.SemaphoreType.DMA((2, max(nb - 1, 1))),
            pltpu.SemaphoreType.DMA((2, na - 1)),
            pltpu.SemaphoreType.DMA((2, na - 1)),
            pltpu.SemaphoreType.DMA((2, max(nb - 1, 1), na - 1)),
            pltpu.SemaphoreType.DMA((2, max(nb - 1, 1), na - 1)),
            pltpu.SemaphoreType.DMA,
        ]

    def __init__(self, place, src, out, sems):
        self.place, self.src, self.out = place, src, out
        self.bsend, self.brecv, self.asend, self.arecv, self.fsend, self.frecv, self.local = sems
        self.half = src.shape[1] // 2

    def _own(self, h):
        return self.src.at[:, pl.ds(h * self.half, self.half)]

    def _block(self, a, b, h):
        return self.out.at[:, a * self.place.grid_b + b, pl.ds(h * self.half, self.half)]

    def _b_copy(self, i, h, coming):
        pc = self.place
        b = pc.b_peer(pc.grid_b - i) if coming else pc.b
        return remote(
            self._own(h), self._block(pc.a, b, h), self.bsend.at[h, i - 1], self.brecv.at[h, i - 1],
            pc.at_dp(pc.a * pc.grid_b + pc.b_peer(i)),
        )

    def _a_copy(self, i, h, coming):
        pc = self.place
        a = pc.a_peer(pc.grid_a - i) if coming else pc.a
        return remote(
            self._own(h), self._block(a, pc.b, h), self.asend.at[h, i - 1], self.arecv.at[h, i - 1],
            pc.at_dp(pc.a_peer(i) * pc.grid_b + pc.b),
        )

    def _on(self, h, ib, ia, coming):
        pc = self.place
        if h == 0:
            b = pc.b_peer(pc.grid_b - ib)
            a = pc.a_peer(pc.grid_a - ia) if coming else pc.a
            target = pc.at_dp(pc.a_peer(ia) * pc.grid_b + pc.b)
        else:
            a = pc.a_peer(pc.grid_a - ia)
            b = pc.b_peer(pc.grid_b - ib) if coming else pc.b
            target = pc.at_dp(pc.a * pc.grid_b + pc.b_peer(ib))
        block = self._block(a, b, h)
        return remote(block, block, self.fsend.at[h, ib - 1, ia - 1], self.frecv.at[h, ib - 1, ia - 1], target)

    def start(self):
        pc = self.place
        for h in range(2):
            for i in range(1, pc.grid_b):
                self._b_copy(i, h, False).start()
            for i in range(1, pc.grid_a):
                self._a_copy(i, 1 - h, False).start()
        pltpu.make_async_copy(self.src, self.out.at[:, pc.dp], self.local).start()

    def step(self):
        pc = self.place
        for ib in range(1, pc.grid_b):
            self._b_copy(ib, 0, True).wait_recv()
            for ia in range(1, pc.grid_a):
                self._on(0, ib, ia, False).start()
        for ia in range(1, pc.grid_a):
            self._a_copy(ia, 1, True).wait_recv()
            for ib in range(1, pc.grid_b):
                self._on(1, ib, ia, False).start()

    def finish(self):
        pc = self.place
        pltpu.make_async_copy(self.src, self.out.at[:, pc.dp], self.local).wait()
        for ib in range(1, pc.grid_b):
            self._b_copy(ib, 1, True).wait_recv()
        for ia in range(1, pc.grid_a):
            self._a_copy(ia, 0, True).wait_recv()
        for h in range(2):
            for ib in range(1, pc.grid_b):
                for ia in range(1, pc.grid_a):
                    self._on(h, ib, ia, True).wait_recv()
                    self._on(h, ib, ia, False).wait_send()
        for h in range(2):
            for ib in range(1, pc.grid_b):
                self._b_copy(ib, h, False).wait_send()
            for ia in range(1, pc.grid_a):
                self._a_copy(ia, h, False).wait_send()


class GridScatter:
    @staticmethod
    def scratch(n_dp, which, rows, width):
        na, nb = 2, n_dp // 2
        half = rows // 2
        most = max(nb - 1, 1)
        return [
            pltpu.VMEM((most, na, which, half, width), jnp.bfloat16),
            pltpu.VMEM((na - 1, nb, which, half, width), jnp.bfloat16),
            pltpu.VMEM((na - 1, which, half, width), jnp.bfloat16),
            pltpu.VMEM((most, which, half, width), jnp.bfloat16),
            pltpu.VMEM((na - 1, which, half, width), jnp.bfloat16),
            pltpu.VMEM((most, which, half, width), jnp.bfloat16),
            pltpu.SemaphoreType.DMA((most, na)),
            pltpu.SemaphoreType.DMA((most, na)),
            pltpu.SemaphoreType.DMA((na - 1, nb)),
            pltpu.SemaphoreType.DMA((na - 1, nb)),
            pltpu.SemaphoreType.DMA((na - 1,)),
            pltpu.SemaphoreType.DMA((na - 1,)),
            pltpu.SemaphoreType.DMA((most,)),
            pltpu.SemaphoreType.DMA((most,)),
        ]

    def __init__(self, place, part, out, squares, scratch):
        self.place, self.part, self.out, self.squares = place, part, out, squares
        self.box_b, self.box_a, self.sum_b, self.sum_a, self.end_a, self.end_b = scratch[:6]
        self.bs, self.br, self.as_, self.ar, self.eas, self.ear, self.ebs, self.ebr = scratch[6:]
        self.which = out.shape[0]
        self.half = out.shape[1] // 2

    def _part(self, a, b, h):
        return self.part.at[:, a * self.place.grid_b + b, pl.ds(h * self.half, self.half)]

    def _first_b(self, i, j):
        pc = self.place
        return remote(
            self._part(pc.a_peer(j), pc.b_peer(i), 0), self.box_b.at[i - 1, j], self.bs.at[i - 1, j],
            self.br.at[i - 1, j], pc.at_dp(pc.a * pc.grid_b + pc.b_peer(i)),
        )

    def _first_a(self, i, j):
        pc = self.place
        return remote(
            self._part(pc.a_peer(i), pc.b_peer(j), 1), self.box_a.at[i - 1, j], self.as_.at[i - 1, j],
            self.ar.at[i - 1, j], pc.at_dp(pc.a_peer(i) * pc.grid_b + pc.b),
        )

    def _second_a(self, i):
        pc = self.place
        return remote(
            self.sum_b.at[i - 1], self.end_a.at[i - 1], self.eas.at[i - 1], self.ear.at[i - 1],
            pc.at_dp(pc.a_peer(i) * pc.grid_b + pc.b),
        )

    def _second_b(self, i):
        pc = self.place
        return remote(
            self.sum_a.at[i - 1], self.end_b.at[i - 1], self.ebs.at[i - 1], self.ebr.at[i - 1],
            pc.at_dp(pc.a * pc.grid_b + pc.b_peer(i)),
        )

    def _firsts_b(self):
        pc = self.place
        return [(i, j) for j in list(range(1, pc.grid_a)) + [0] for i in range(1, pc.grid_b)]

    def _firsts_a(self):
        pc = self.place
        return [(i, j) for j in list(range(1, pc.grid_b)) + [0] for i in range(1, pc.grid_a)]

    def start(self):
        for (ib, jb), (ia, ja) in zip(self._firsts_b(), self._firsts_a(), strict=False):
            self._first_b(ib, jb).start()
            self._first_a(ia, ja).start()
        shared = min(len(self._firsts_b()), len(self._firsts_a()))
        for i, j in self._firsts_b()[shared:]:
            self._first_b(i, j).start()
        for i, j in self._firsts_a()[shared:]:
            self._first_a(i, j).start()

    def _low(self, rows):
        return pl.ds(pl.multiple_of(self.half + rows.start, ROW_STEP), ROW_STEP)

    def _sum_b(self, j):
        pc = self.place
        for i in range(1, pc.grid_b):
            self._first_b(i, j).wait_recv()
        mine = pc.a_peer(j) * pc.grid_b + pc.b

        def add(rows):
            for w in range(self.which):
                total = self.part[w, mine, rows, :].astype(jnp.float32)
                for i in range(1, pc.grid_b):
                    total = total + self.box_b[i - 1, j, w, rows, :].astype(jnp.float32)
                if j == 0:
                    self.out[w, rows, :] = total
                else:
                    self.sum_b[j - 1, w, rows, :] = total.astype(jnp.bfloat16)

        row_loop(self.half, add)
        if j:
            self._second_a(j).start()

    def _sum_a(self, j):
        pc = self.place
        for i in range(1, pc.grid_a):
            self._first_a(i, j).wait_recv()
        mine = pc.a * pc.grid_b + pc.b_peer(j)

        def add(rows):
            for w in range(self.which):
                total = self.part[w, mine, self._low(rows), :].astype(jnp.float32)
                for i in range(1, pc.grid_a):
                    total = total + self.box_a[i - 1, j, w, rows, :].astype(jnp.float32)
                if j == 0:
                    self.out[w, self._low(rows), :] = total
                else:
                    self.sum_a[j - 1, w, rows, :] = total.astype(jnp.bfloat16)

        row_loop(self.half, add)
        if j:
            self._second_b(j).start()

    def step(self):
        pc = self.place
        for j in range(1, max(pc.grid_a, pc.grid_b)):
            if j < pc.grid_a:
                self._sum_b(j)
            if j < pc.grid_b:
                self._sum_a(j)

    def step_own(self):
        self._sum_b(0)
        self._sum_a(0)

    def finish(self):
        pc = self.place
        for i in range(1, pc.grid_a):
            self._second_a(i).wait_recv()
        for i in range(1, pc.grid_b):
            self._second_b(i).wait_recv()
        self.squares[...] = jnp.zeros_like(self.squares)

        def tile(total):
            total = total * total
            folded = total[:, :128]
            for at in range(128, total.shape[1], 128):
                folded = folded + total[:, at : at + 128]
            return folded

        def add(rows):
            low = self._low(rows)
            for w in range(self.which):
                total = self.out[w, rows, :]
                for i in range(1, pc.grid_a):
                    total = total + self.end_a[i - 1, w, rows, :].astype(jnp.float32)
                self.out[w, rows, :] = total
                self.squares[...] += tile(total)
                total = self.out[w, low, :]
                for i in range(1, pc.grid_b):
                    total = total + self.end_b[i - 1, w, rows, :].astype(jnp.float32)
                self.out[w, low, :] = total
                self.squares[...] += tile(total)

        row_loop(self.half, add)
        for i, j in self._firsts_b():
            self._first_b(i, j).wait_send()
        for i, j in self._firsts_a():
            self._first_a(i, j).wait_send()
        for i in range(1, pc.grid_a):
            self._second_a(i).wait_send()
        for i in range(1, pc.grid_b):
            self._second_b(i).wait_send()


class Direct:
    @staticmethod
    def scratch(n):
        return [pltpu.SemaphoreType.DMA((n - 1,)), pltpu.SemaphoreType.DMA((n - 1,))]

    def __init__(self, place, src, out, sems, axis="dp", block=None, to=None):
        self.place, self.src, self.out = place, src, out
        self.send, self.recv = sems
        self.n = place.n_dp if axis == "dp" else place.n_fsdp
        self.me = place.dp if axis == "dp" else place.f
        self.axis = axis
        self.of = block or (lambda ref, d: ref)
        self.to = to or (lambda ref, d: ref.at[d])

    def _device(self, other):
        return self.place.at_dp(other) if self.axis == "dp" else (self.place.dp, other)

    def _copy(self, i, coming=False):
        other = (self.me + i) % self.n
        origin = (self.me + self.n - i) % self.n if coming else self.me
        return remote(
            self.of(self.src, other), self.to(self.out, origin), self.send.at[i - 1], self.recv.at[i - 1], self._device(other)
        )

    def start(self):
        for i in range(1, self.n):
            self._copy(i).start()

    def finish(self):
        for i in range(1, self.n):
            self._copy(i, True).wait_recv()
            self._copy(i).wait_send()


def split_refs(refs, counts):
    out, at = [], 0
    for count in counts:
        out.append(refs[at : at + count])
        at += count
    return out


HBM = pl.BlockSpec(memory_space=pl.ANY)
WHOLE = pl.BlockSpec(memory_space=pltpu.VMEM)
TILE = (ROW_STEP, 128)


def parameters(collective_id):
    return pltpu.CompilerParams(collective_id=collective_id, has_side_effects=True, vmem_limit_bytes=VMEM_LIMIT)


def matmul(left, right):
    return jnp.dot(left, right, preferred_element_type=jnp.float32)


def matmul_last(left, right):
    return lax.dot_general(left, right, (((1,), (1,)), ((), ())), preferred_element_type=jnp.float32)


def matmul_first(left, right):
    return lax.dot_general(left, right, (((0,), (0,)), ((), ())), preferred_element_type=jnp.float32)


def loop(count, work):
    def one(i, carry):
        work(i)
        return carry

    lax.fori_loop(0, count, one, 0)


def span(i, size):
    return pl.ds(pl.multiple_of(i * size, size), size)


def chip_rows(ref, chip):
    pair = ref[span(chip, 2)]
    return pair.reshape(-1, pair.shape[-1])


def pair_mask(codes_ref, chip, rows):
    pair = [codes_ref[chip * 2 + i] for i in range(2)]
    query = jnp.floor(jnp.concatenate([block[:rows] for block in pair], axis=0))
    query = jnp.concatenate([query] * (2 * rows // 128), axis=1)
    key = jnp.concatenate([block[rows : rows + 1] for block in pair], axis=1)
    shape = (2 * rows, 2 * rows)
    same = lax.broadcasted_iota(jnp.int32, shape, 0) == lax.broadcasted_iota(jnp.int32, shape, 1)
    return (query == key) | same


class Rows:
    def __init__(self, place, codes, mods, micro, rows, slots_here):
        self.place, self.codes, self.mods = place, codes, mods
        self.micro, self.tok_rows, self.slots_here = micro, rows // micro, slots_here

    def tiles(self, work):
        for m in range(self.micro):
            row_loop(self.tok_rows, functools.partial(work, m), m * self.tok_rows)

    def slot_live(self, m, rows):
        column = self.codes[rows, :][:, :1]
        number = jnp.floor(column)
        first = ((self.place.f * self.micro + m) * self.slots_here).astype(jnp.float32)
        return number - first, jnp.where(column == number, 1.0, 0.0)

    def pick(self, j, m, slot):
        at = m * self.slots_here
        picked = self.mods[j, at : at + 1, :]
        for i in range(1, self.slots_here):
            picked = jnp.where(slot == i, self.mods[j, at + i : at + i + 1, :], picked)
        return picked

    def add_up(self, out, j, m, slot, values):
        for i in range(self.slots_here):
            at = m * self.slots_here + i
            chosen = jnp.where(slot == i, values, 0.0)
            out[j, at : at + 1, :] += jnp.sum(chosen, axis=0, keepdims=True)


def cast_rows(src, dst):
    for w in range(src.shape[0]):
        def tile(rows):
            dst[w, rows, :] = src[w, rows, :].astype(dst.dtype)

        row_loop(src.shape[1], tile)


def attention_probs(query, key, allowed):
    scores = jnp.where(allowed, matmul_last(query, key) * HEAD ** (-0.5), -1e30)
    raw = jnp.exp(scores - jnp.max(scores, axis=-1, keepdims=True))
    return raw / jnp.sum(raw, axis=-1, keepdims=True)


def attention_kernel(n_dp, n_fsdp, micro, tokens, cotangent, codes, embedding, ada, qkv, out_w, up, down):
    low, f32 = jnp.bfloat16, jnp.float32
    images = embedding.shape[0]
    rows, width = tokens.shape
    deep, wide = ada.shape[1:]
    which, _, head_columns = qkv.shape
    slots_here = images // (micro * n_fsdp)
    own_images = micro * slots_here
    line = LineGather.scratch(n_fsdp)
    grid = GridGather.scratch(n_dp)
    direct = Direct.scratch(n_dp)
    scatter_got = LineScatter.scratch(n_fsdp, rows, width)
    counts = [len(line)] * 3 + [len(grid)] * 3 + [len(direct)] * 5 + [len(LineCast.scratch(n_fsdp)), len(scatter_got)]
    weights = (qkv, out_w, up, down, ada)
    pair = 2 * rows

    def kernel(
        tok, cot, code_row, emb, ada_f, qkv_f, out_f, up_f, down_f,
        attn_own, mid, hidden2, mods_own, cond_g, products, cod, cod_g, qkv_low, attended, down_low,
        hidden_out, qkv_out, out_out, up_g, gmlp_g,
        cond, parts, boxes, mail_first, mail, inbox, mods_g, averages, inv_stds, product, products_g, gmlp, part, hidden_g, qkv_g, out_g,
        qkv_s, out_s, up_s, down_s, ada_s, qkv_l, out_l, up_l, moves, *rest,
    ):
        sems = split_refs(rest, counts)
        place = Place(n_dp, n_fsdp)
        fetches = [
            pltpu.make_async_copy(ref, stage, moves.at[i])
            for i, (ref, stage) in enumerate(
                ((qkv_f, qkv_s), (out_f, out_s), (up_f, up_s), (down_f, down_s), (ada_f, ada_s))
            )
        ]
        for i in (0, 1, 4, 2, 3):
            fetches[i].start()
        present = announce(place, True, True, True)
        level = emb[...].astype(f32)
        level = (level / (1.0 + jnp.exp(-level))).astype(low)
        for d in range(n_dp):
            cond[d] = level[:, d * deep : (d + 1) * deep]
        number = code_row[0:1, :] + ((place.f * micro) * slots_here).astype(f32)
        live = code_row[1:2, :]
        cod[:rows, :] = jnp.transpose(jnp.broadcast_to(jnp.where(live > 0.5, number, number + 0.25), (rows, rows)))
        cod[rows:, :] = jnp.broadcast_to(jnp.where(live > 0.5, number, -1.0), (8, rows))
        own = Rows(place, cod, mods_own, micro, rows, slots_here)
        fetches[0].wait()
        cast_rows(qkv_s, qkv_l)
        fetches[1].wait()
        cast_rows(out_s, out_l)
        pl.semaphore_wait(pltpu.get_barrier_semaphore(), present)
        conds = Direct(place, cond, cond_g, sems[6], block=lambda ref, d: ref.at[d])
        conds.start()
        token_line = LineGather(place, tok, hidden_g, sems[1])
        code_line = LineGather(place, cod, cod_g, sems[0])
        token_line.start()
        code_line.start()
        grids = [GridGather(place, qkv_l, qkv_g, sems[3]), GridGather(place, out_l, out_g, sems[4])]
        cond_g[place.dp] = cond[place.dp]
        fetches[4].wait()
        conds.finish()
        every = cond_g[...].reshape(n_dp * images, deep)

        def project(kinds):
            for j, kind in kinds:
                parts[:, j] = matmul(every, ada_s[kind].astype(low)).reshape(n_dp, images, wide)

        def add_parts(kinds, letter):
            for j in kinds:
                total = parts[place.dp, j]
                for i in range(1, n_dp):
                    total = total + boxes[(place.dp + i) % n_dp, j]
                for f in range(n_fsdp):
                    for m in range(micro):
                        at = (m * n_fsdp + f) * slots_here
                        letter[f, j - kinds[0], m * slots_here : (m + 1) * slots_here, :] = total[at : at + slots_here]

        first_sums = Direct(
            place, parts, boxes, sems[7], block=lambda ref, d: ref.at[d, 0:3], to=lambda ref, d: ref.at[d, 0:3]
        )
        other_sums = Direct(
            place, parts, boxes, sems[8], block=lambda ref, d: ref.at[d, 3:MODS], to=lambda ref, d: ref.at[d, 3:MODS]
        )
        project(list(enumerate(FIRST_KINDS)))
        first_sums.start()
        for gather in grids:
            gather.start()
        project(list(enumerate(OTHER_KINDS, 3)))
        product[...] = matmul_last(every, every)

        def statistics(chip):
            token_line.ready(chip)
            for i in range(2):
                device = chip * 2 + i

                def tile(at):
                    values = hidden_g[device, at, :].astype(f32)
                    average = jnp.mean(values, axis=-1, keepdims=True)
                    centred = values - average
                    inv_std = lax.rsqrt(jnp.mean(centred * centred, axis=-1, keepdims=True) + NORM_EPS)
                    averages[device, at, :] = jnp.broadcast_to(average, (ROW_STEP, 128))
                    inv_stds[device, at, :] = jnp.broadcast_to(inv_std, (ROW_STEP, 128))

                row_loop(rows, tile)

        def statistics_at(distance):
            def side(i):
                chip = place.p + (1 - 2 * i) * distance

                @pl.when((chip >= 0) & (chip < place.chips))
                def _():
                    statistics(chip)

            loop(2 if distance else 1, side)

        statistics_at(0)
        first_sums.finish()
        add_parts((0, 1, 2), mail_first)
        mods_line = LineCast(
            place, mail_first, mods_g, sems[11],
            block=lambda ref, d: ref.at[:, :, :, pl.ds(pl.multiple_of(d * wide, wide), wide)],
        )
        mods_line.start()
        token_line.step(1)
        code_line.step(1)
        fetches[2].wait()
        cast_rows(up_s, up_l)
        fetches[3].wait()
        cast_rows(down_s, down_low)
        crosses = Direct(place, product, products_g, sems[10])
        products_g[place.dp] = product[...]
        mods_line.step()
        ups = GridGather(place, up_l, up_g, sems[5])
        letters = Direct(place, mail, inbox, sems[9], "fsdp", block=lambda ref, d: ref.at[d])
        gmlp_line = LineGather(place, gmlp, gmlp_g, sems[2])

        def branch_grad(m, at):
            slot, alive = own.slot_live(m, at)
            gmlp[at, :] = (cot[at, :].astype(f32) * alive * own.pick(5, m, slot)).astype(low)

        mods_line.finish()
        for j, kind in enumerate(FIRST_KINDS):
            mods_own[kind] = mods_g[place.f, j]
        own.tiles(branch_grad)
        gmlp_line.start_here()
        for step in range(2, place.chips + 1):
            if step < place.chips:
                token_line.step(step)
                code_line.step(step)
            if step == 2:
                for gather in grids:
                    gather.step()
            statistics_at(step - 1)

            @pl.when((place.p + 1 == step) | ((place.p + 1 < step) & (step == 2)))
            def _():
                gmlp_line.start_way(0)

            @pl.when((place.chips - place.p == step) | ((place.chips - place.p < step) & (step == 2)))
            def _():
                gmlp_line.start_way(1)

        for gather in grids:
            gather.finish()
        other_sums.start()
        crosses.start()
        ups.start()
        token_line.drain()
        code_line.finish()
        leaves = [
            pltpu.make_async_copy(ref, out, moves.at[len(weights) + i])
            for i, (ref, out) in enumerate(((qkv_g, qkv_out), (out_g, out_out), (hidden_g, hidden_out)))
        ]
        for leave in leaves[:2]:
            leave.start()
        scatter = LineScatter(place, part, attn_own, sems[12])

        def norm_block(chip):
            for i in range(2):
                device = chip * 2 + i
                for m in range(micro):
                    first = ((device * micro + m) * slots_here).astype(f32)

                    def table(j, slot):
                        at = m * slots_here
                        picked = mods_g[device, j, at : at + 1, :]
                        for k in range(1, slots_here):
                            picked = jnp.where(slot == k, mods_g[device, j, at + k : at + k + 1, :], picked)
                        return picked

                    def tile(at):
                        slot = jnp.floor(cod_g[device, at, :][:, :1]) - first
                        centred = hidden_g[device, at, :].astype(f32) - averages[device, at, :][:, :1]
                        normed = centred * inv_stds[device, at, :][:, :1]
                        hidden_g[device, at, :] = (normed * (1.0 + table(1, slot)) + table(0, slot)).astype(low)

                    row_loop(rows // micro, tile, m * (rows // micro))

        def compute(chip):
            at = span(chip, pair)
            norm_block(chip)
            values = chip_rows(hidden_g, chip)
            for w in range(which):
                weight = qkv_g[w].reshape(width, head_columns)
                qkv_low[w, at, :] = matmul(values, weight).astype(low)
            allowed = pair_mask(cod_g, chip, rows)
            for h in range(head_columns // HEAD):
                head = slice(h * HEAD, (h + 1) * HEAD)
                probs = attention_probs(qkv_low[0, at, head], qkv_low[1, at, head], allowed)
                attended[at, head] = matmul(probs.astype(low), qkv_low[2, at, head]).astype(low)
            heads = attended[at, :]
            weight_rows = out_g.shape[2]
            for d in range(n_dp):
                piece = matmul_last(heads, out_g[0, d]).astype(low).reshape(2, rows, weight_rows)
                part[span(chip, 2), :, d * weight_rows : (d + 1) * weight_rows] = piece

        def then(k):
            @pl.when(k == 1)
            def _():
                gmlp_line.step(1)

        slot = scatter.paced(compute, 2, then)
        leaves[2].start()
        for step in range(2, place.chips):
            gmlp_line.step(step)
            slot = scatter.run_to(slot, scatter.slots * (step + 1) // (place.chips + 1))
            if step == place.chips // 2:
                other_sums.finish()
                add_parts((3, 4, 5), mail)
                letters.start()
                inbox[place.f] = mail[place.f]
                ups.step()
                crosses.finish()
                total = products_g[0]
                for d in range(1, n_dp):
                    total = total + products_g[d]
                products[...] = total
        scatter.run_to(slot, scatter.slots)
        scatter.finish()
        letters.finish()
        for f in range(n_fsdp):
            for j, kind in enumerate(OTHER_KINDS):
                mods_own[kind, :, f * wide : (f + 1) * wide] = inbox[f, j]

        def second_norm(m, at):
            slot, _ = own.slot_live(m, at)
            values = tok[at, :].astype(f32) + own.pick(2, m, slot) * attn_own[at, :]
            mid[at, :] = values
            normed, _ = normalize(values)
            hidden2[at, :] = (normed * (1.0 + own.pick(4, m, slot)) + own.pick(3, m, slot)).astype(low)

        own.tiles(second_norm)
        gmlp_line.finish()
        ups.finish()
        for leave in leaves:
            leave.wait()

    def gathered(w):
        return jax.ShapeDtypeStruct((w.shape[0], n_dp, *w.shape[1:]), low)

    return pl.pallas_call(
        kernel,
        out_shape=[
            jax.ShapeDtypeStruct((rows, width), f32),
            jax.ShapeDtypeStruct((rows, width), f32),
            jax.ShapeDtypeStruct((rows, width), low),
            jax.ShapeDtypeStruct((MODS, own_images, width), f32),
            jax.ShapeDtypeStruct((n_dp, images, deep), low),
            jax.ShapeDtypeStruct((n_dp * images, n_dp * images), f32),
            jax.ShapeDtypeStruct((rows + 8, rows), f32),
            jax.ShapeDtypeStruct((n_fsdp, rows + 8, rows), f32),
            jax.ShapeDtypeStruct((which, n_fsdp * rows, head_columns), low),
            jax.ShapeDtypeStruct((n_fsdp * rows, head_columns), low),
            jax.ShapeDtypeStruct(down.shape, low),
            jax.ShapeDtypeStruct((n_fsdp, rows, width), low),
            gathered(qkv),
            gathered(out_w),
            gathered(up),
            jax.ShapeDtypeStruct((n_fsdp, rows, width), low),
        ],
        in_specs=[WHOLE] * 4 + [HBM] * 5,
        out_specs=[WHOLE] * 11 + [HBM] * 5,
        scratch_shapes=[
            pltpu.VMEM((n_dp, images, deep), low),
            pltpu.VMEM((n_dp, MODS, images, wide), f32),
            pltpu.VMEM((n_dp, MODS, images, wide), f32),
            pltpu.VMEM((n_fsdp, 3, own_images, wide), f32),
            pltpu.VMEM((n_fsdp, 3, own_images, wide), f32),
            pltpu.VMEM((n_fsdp, 3, own_images, wide), f32),
            pltpu.VMEM((n_fsdp, 3, own_images, width), f32),
            pltpu.VMEM((n_fsdp, rows, 128), f32),
            pltpu.VMEM((n_fsdp, rows, 128), f32),
            pltpu.VMEM((n_dp * images, n_dp * images), f32),
            pltpu.VMEM((n_dp, n_dp * images, n_dp * images), f32),
            pltpu.VMEM((rows, width), low),
            pltpu.VMEM((n_fsdp, rows, width), low),
            pltpu.VMEM((n_fsdp, rows, width), low),
            pltpu.VMEM((which, n_dp, *qkv.shape[1:]), low),
            pltpu.VMEM((1, n_dp, *out_w.shape[1:]), low),
            *[pltpu.VMEM(w.shape, f32) for w in weights],
            *[pltpu.VMEM(w.shape, low) for w in weights[:3]],
            pltpu.SemaphoreType.DMA((len(weights) + 3,)),
            *line, *line, *line, *grid, *grid, *grid, *direct, *direct, *direct,
            *Direct.scratch(n_fsdp), *direct, *LineCast.scratch(n_fsdp), *scatter_got,
        ],
        compiler_params=parameters(0),
    )(tokens, cotangent, codes, embedding, ada, qkv, out_w, up, down)


def gelu_parts(v):
    root = 0.7978845608028654
    square = v * v
    bent = jnp.tanh(root * (v + 0.044715 * v * square))
    value = 0.5 * v * (1.0 + bent)
    slope = 0.5 * (1.0 + bent) + (0.5 * root) * v * (1.0 - bent * bent) * (1.0 + (3.0 * 0.044715) * square)
    return value, slope


COLUMN_STEP = 256


def feed_forward_kernel(n_dp, n_fsdp, micro, hidden, mid, attn_own, cotangent, codes, mods, grad_mlp, up_g, down):
    low, f32 = jnp.bfloat16, jnp.float32
    rows, width = hidden.shape
    _, weight_rows, columns = down.shape
    tokens = n_fsdp * rows
    pair = 2 * rows
    own_images = mods.shape[1]
    line = LineGather.scratch(n_fsdp)
    grid = GridGather.scratch(n_dp)
    scatter_got = LineScatter.scratch(n_fsdp, rows, width)
    grads_got = GridScatter.scratch(n_dp, 1, weight_rows, columns)
    counts = [len(line), len(grid), len(scatter_got), len(grads_got)]
    tiles = columns // COLUMN_STEP
    row_tiles = weight_rows // COLUMN_STEP

    def kernel(
        hid, mid_ref, attn_ref, cot, cod, mods_ref, down_ref, gmlp_ref, up_ref,
        grad_mid, grad_attn, sums_own, grad_down, squares, mlp_part, grad_up,
        gmlp, up, hidden_g, down_g, upper, activ, grad_upper, part, gdown, grad_h2, stage, stage_up,
        moves, out_sem, up_sem, *rest,
    ):
        sems = split_refs(rest, counts)
        place = Place(n_dp, n_fsdp)
        fetch_up = pltpu.make_async_copy(up_ref, up, moves.at[0])
        fetch_gmlp = pltpu.make_async_copy(gmlp_ref, gmlp, moves.at[1])
        fetch_up.start()
        fetch_gmlp.start()
        enter(place, True, True)
        hidden_line = LineGather(place, hid, hidden_g, sems[0])
        downs = GridGather(place, down_ref, down_g, sems[1])
        hidden_line.start()
        downs.start()
        fetch_up.wait()

        def forward(chip):
            at = span(chip, pair)
            hidden_line.ready(chip)

            def tile(i):
                to = span(i, COLUMN_STEP)
                values = chip_rows(hidden_g, chip)
                total = jnp.zeros((pair, COLUMN_STEP), f32)
                for d in range(n_dp):
                    total = total + matmul(values[:, d * weight_rows : (d + 1) * weight_rows], up[0, d, :, to])
                upper[at, to] = total
                activ[at, to] = gelu_parts(total)[0].astype(low)

            loop(tiles, tile)

        def forward_at(distance):
            def side(i):
                chip = place.p + (1 - 2 * i) * distance

                @pl.when((chip >= 0) & (chip < place.chips))
                def _():
                    forward(chip)

            loop(2 if distance else 1, side)

        for step in range(1, place.chips):
            hidden_line.step(step)
            if step == place.chips // 2:
                downs.step()
            forward_at(step - 1)
        forward_at(place.chips - 1)
        fetch_gmlp.wait()
        downs.finish()
        scatter = LineScatter(place, part, grad_h2, sems[2])
        grads = GridScatter(place, gdown, grad_down, squares, sems[3])

        def backward(chip):
            at = span(chip, pair)

            def tile(i):
                to = span(i, COLUMN_STEP)
                values = chip_rows(gmlp, chip)
                total = jnp.zeros((pair, COLUMN_STEP), f32)
                for d in range(n_dp):
                    total = total + matmul(values[:, d * weight_rows : (d + 1) * weight_rows], down_g[0, d, :, to])
                grad_upper[at, to] = (total * gelu_parts(upper[at, to])[1]).astype(low)

            loop(tiles, tile)
            values = grad_upper[at, :]
            for d in range(n_dp):
                piece = matmul_last(values, up[0, d]).astype(low).reshape(2, rows, weight_rows)
                part[span(chip, 2), :, d * weight_rows : (d + 1) * weight_rows] = piece

        def down_tile(i):
            d, r = i // row_tiles, lax.rem(i, row_tiles)
            left = gmlp[:, :, span(i, COLUMN_STEP)].reshape(tokens, COLUMN_STEP)
            gdown[0, d, span(r, COLUMN_STEP), :] = matmul_first(left, activ[...]).astype(low)

        def then(k):
            @pl.when(k == 0)
            def _():
                loop(n_dp * row_tiles, down_tile)
                grads.start()

        slot = scatter.paced(backward, 2, then)

        def up_copy(i, d, r):
            return pltpu.make_async_copy(
                stage_up.at[lax.rem(i, 2)], grad_up.at[0, d, span(r, COLUMN_STEP)], up_sem.at[lax.rem(i, 2)]
            )

        def up_tile(i):
            d, r = i // row_tiles, lax.rem(i, row_tiles)

            @pl.when(i >= 2)
            def _():
                up_copy(i, 0, 0).wait()

            left = hidden_g[:, :, span(i, COLUMN_STEP)].reshape(tokens, COLUMN_STEP)
            stage_up[lax.rem(i, 2)] = matmul_first(left, grad_upper[...]).astype(low)
            up_copy(i, d, r).start()

        slot = scatter.beside(slot, n_dp * row_tiles, up_tile)
        up_copy(0, 0, 0).wait()
        up_copy(1, 0, 0).wait()
        grads.step()

        def mlp_copy(chip):
            to = lax.rem(chip, 2)
            return pltpu.make_async_copy(stage.at[to], mlp_part.at[span(chip, 2)], out_sem.at[to])

        def mlp_tile(chip):
            @pl.when(chip >= 2)
            def _():
                mlp_copy(chip).wait()

            values = activ[span(chip, pair), :]
            for d in range(n_dp):
                piece = matmul_last(values, down_g[0, d]).astype(low).reshape(2, rows, weight_rows)
                stage[lax.rem(chip, 2), :, :, d * weight_rows : (d + 1) * weight_rows] = piece
            mlp_copy(chip).start()

        slot = scatter.beside(slot, place.chips, mlp_tile)
        mlp_copy(0).wait()
        mlp_copy(1).wait()
        scatter.run_to(slot, scatter.slots)
        grads.step_own()
        scatter.finish()
        own = Rows(place, cod, mods_ref, micro, rows, own_images // micro)
        sums_own[...] = jnp.zeros_like(sums_own)

        def norm_grad(m, at):
            slot, alive = own.slot_live(m, at)
            normed, inv_std = normalize(mid_ref[at, :])
            grad = grad_h2[at, :]
            before = normalize_back(grad * (1.0 + own.pick(4, m, slot)), normed, inv_std)
            total = cot[at, :].astype(f32) * alive + before
            grad_mid[at, :] = total
            grad_attn[at, :] = (total * own.pick(2, m, slot)).astype(low)
            own.add_up(sums_own, 0, m, slot, total * attn_ref[at, :])
            own.add_up(sums_own, 1, m, slot, grad)
            own.add_up(sums_own, 2, m, slot, grad * normed)

        own.tiles(norm_grad)
        grads.finish()
        hidden_line.drain()

    return pl.pallas_call(
        kernel,
        out_shape=[
            jax.ShapeDtypeStruct((rows, width), f32),
            jax.ShapeDtypeStruct((rows, width), low),
            jax.ShapeDtypeStruct((3, own_images, width), f32),
            jax.ShapeDtypeStruct((1, weight_rows, columns), f32),
            jax.ShapeDtypeStruct(TILE, f32),
            jax.ShapeDtypeStruct((n_fsdp, rows, width), low),
            jax.ShapeDtypeStruct((1, n_dp, weight_rows, columns), low),
        ],
        in_specs=[WHOLE] * 6 + [HBM] * 3,
        out_specs=[WHOLE] * 5 + [HBM] * 2,
        scratch_shapes=[
            pltpu.VMEM((n_fsdp, rows, width), low),
            pltpu.VMEM((1, n_dp, weight_rows, columns), low),
            pltpu.VMEM((n_fsdp, rows, width), low),
            pltpu.VMEM((1, n_dp, weight_rows, columns), low),
            pltpu.VMEM((tokens, columns), f32),
            pltpu.VMEM((tokens, columns), low),
            pltpu.VMEM((tokens, columns), low),
            pltpu.VMEM((n_fsdp, rows, width), low),
            pltpu.VMEM((1, n_dp, weight_rows, columns), low),
            pltpu.VMEM((rows, width), f32),
            pltpu.VMEM((2, 2, rows, width), low),
            pltpu.VMEM((2, COLUMN_STEP, columns), low),
            pltpu.SemaphoreType.DMA((2,)),
            pltpu.SemaphoreType.DMA((2,)),
            pltpu.SemaphoreType.DMA((2,)),
            *line, *grid, *scatter_got, *grads_got,
        ],
        compiler_params=parameters(2),
    )(hidden, mid, attn_own, cotangent, codes, mods, down, grad_mlp, up_g)


def attention_grad_kernel(
    n_dp, n_fsdp, micro, grad_attn, tokens_own, mid, grad_mid, cotangent, codes, mods, codes_g, mlp_part, grad_up, qkv_g,
    out_g, qkv_low, attended, hidden_g,
):
    low, f32 = jnp.bfloat16, jnp.float32
    rows, width = grad_attn.shape
    which, _, weight_rows, head_columns = qkv_g.shape
    tokens = n_fsdp * rows
    pair = 2 * rows
    chips = n_fsdp // 2
    own_images = mods.shape[1]
    line = LineGather.scratch(n_fsdp)
    scatter_got = LineScatter.scratch(n_fsdp, rows, width)
    up_shape = (1, *grad_up.shape[2:])
    up_got = GridScatter.scratch(n_dp, *up_shape)
    qkv_got = GridScatter.scratch(n_dp, which, weight_rows, head_columns)
    out_got = GridScatter.scratch(n_dp, 1, weight_rows, head_columns)
    counts = [len(line), len(scatter_got), len(scatter_got), len(up_got), len(qkv_got), len(out_got)]
    row_tiles = weight_rows // COLUMN_STEP

    def kernel(
        ga, tok, mid_ref, gmid, cot, cod, mods_ref, cod_g, mlp_ref, gup_ref, qkv_wr, out_wr, qkv_lr, att_r, hid_r,
        block_out, input_grad, sums_own, grad_up_own, grad_qkv_own, grad_out_own, squares,
        ga_g, gqkv, gqkv_w, gout_w, mlp_own, grad_h1, tile_up, tile_qkv, tile_out,
        mine, gup, qkv_w, out_w, qkv_ref, att, hid_g, moves, mine_sem, *rest,
    ):
        sems = split_refs(rest, counts)
        place = Place(n_dp, n_fsdp)
        fetches = [
            pltpu.make_async_copy(ref, to, moves.at[i])
            for i, (ref, to) in enumerate(
                ((gup_ref, gup), (att_r, att), (out_wr, out_w), (qkv_lr, qkv_ref), (qkv_wr, qkv_w), (hid_r, hid_g))
            )
        ]
        terms = [
            pltpu.make_async_copy(mlp_ref.at[chip * 2 + place.c], mine.at[chip], mine_sem.at[chip])
            for chip in range(chips)
        ]
        fetches[0].start()
        for term in terms:
            term.start()
        for fetch in fetches[1:]:
            fetch.start()
        enter(place, True, True)
        ga_line = LineGather(place, ga, ga_g, sems[0])
        mlp_scatter = LineScatter(place, mlp_ref, mlp_own, sems[1], mine, LineScatter.pieces)
        ups = GridScatter(place, gup, grad_up_own, tile_up, sems[3])
        ga_line.start()
        fetches[0].wait()
        ups.start()
        mlp_scatter.start()
        for term in terms:
            term.wait()
        travel = LineScatter.pieces * (chips - 1)
        at_slot = 0

        def backward(chip):
            at = span(chip, pair)
            ga_line.ready(chip)
            values = chip_rows(ga_g, chip)
            grad_heads = matmul(values, out_w[0].reshape(width, head_columns)).astype(low)
            allowed = pair_mask(cod_g, chip, rows)
            for h in range(head_columns // HEAD):
                head = slice(h * HEAD, (h + 1) * HEAD)
                query, key, value = [qkv_ref[w, at, head] for w in range(which)]
                grad_head = grad_heads[:, head]
                probs = attention_probs(query, key, allowed)
                grad_p = matmul_last(grad_head, value)
                delta = jnp.sum(probs * grad_p, axis=-1, keepdims=True)
                grad_scores = (probs * (grad_p - delta)).astype(low)
                scale = HEAD ** (-0.5)
                gqkv[0, at, head] = (matmul(grad_scores, key) * scale).astype(low)
                gqkv[1, at, head] = (matmul_first(grad_scores, query) * scale).astype(low)
                gqkv[2, at, head] = matmul_first(probs.astype(low), grad_head).astype(low)

        def backward_at(distance):
            def side(i):
                chip = place.p + (1 - 2 * i) * distance

                @pl.when((chip >= 0) & (chip < place.chips))
                def _():
                    backward(chip)

            loop(2 if distance else 1, side)

        for step in range(1, chips):
            ga_line.step(step)
            if step < chips - 1:
                to_slot = travel * step // (chips - 1)
                mlp_scatter.run(at_slot, to_slot)
                at_slot = to_slot
            if step == 1:
                for fetch in fetches[1:]:
                    fetch.wait()
            backward_at(step - 1)
            if step == chips // 2:
                ups.step()
        backward_at(chips - 1)
        ga_line.drain()
        scatter = LineScatter(place, ga_g, grad_h1, sems[2])
        qkvs = GridScatter(place, gqkv_w, grad_qkv_own, tile_qkv, sems[4])
        outs = GridScatter(place, gout_w, grad_out_own, tile_out, sems[5])

        def out_tile(i):
            d, r = i // row_tiles, lax.rem(i, row_tiles)
            left = ga_g[:, :, span(i, COLUMN_STEP)].reshape(tokens, COLUMN_STEP)
            gout_w[0, d, span(r, COLUMN_STEP), :] = matmul_first(left, att[...]).astype(low)

        loop(n_dp * row_tiles, out_tile)
        outs.start()

        def compute(chip):
            at = span(chip, pair)
            for d in range(n_dp):
                total = matmul_last(gqkv[0, at, :], qkv_w[0, d])
                for w in range(1, which):
                    total = total + matmul_last(gqkv[w, at, :], qkv_w[w, d])
                piece = total.astype(low).reshape(2, rows, weight_rows)
                ga_g[span(chip, 2), :, d * weight_rows : (d + 1) * weight_rows] = piece

        def grad_tile(i):
            d, r = i // row_tiles, lax.rem(i, row_tiles)
            left = hid_g[:, :, span(i, COLUMN_STEP)].reshape(tokens, COLUMN_STEP)
            for w in range(which):
                gqkv_w[w, d, span(r, COLUMN_STEP), :] = matmul_first(left, gqkv[w]).astype(low)

        def then(k):
            @pl.when(k == 0)
            def _():
                loop(n_dp * row_tiles, grad_tile)
                qkvs.start()

            @pl.when(k == 1)
            def _():
                mlp_scatter.run(at_slot, travel)

        slot = scatter.paced(compute, 2, then)
        outs.step()
        slot = scatter.run_to(slot, scatter.slots // 2)
        qkvs.step()
        slot = scatter.run_to(slot, scatter.slots * 5 // 8)
        ups.step_own()
        mlp_scatter.finish()
        ups.finish()
        own = Rows(place, cod, mods_ref, micro, rows, own_images // micro)
        sums_own[...] = jnp.zeros_like(sums_own)

        def branch_out(m, at):
            slot_of, alive = own.slot_live(m, at)
            branch = mlp_own[at, :]
            block_out[at, :] = (mid_ref[at, :] + own.pick(5, m, slot_of) * branch).astype(low)
            own.add_up(sums_own, 2, m, slot_of, cot[at, :].astype(f32) * alive * branch)

        own.tiles(branch_out)
        scatter.run_to(slot, scatter.slots)
        outs.step_own()
        qkvs.step_own()
        scatter.finish()

        def norm_grad(m, at):
            slot_of, _ = own.slot_live(m, at)
            normed, inv_std = normalize(tok[at, :].astype(f32))
            grad = grad_h1[at, :]
            before = normalize_back(grad * (1.0 + own.pick(1, m, slot_of)), normed, inv_std)
            input_grad[at, :] = gmid[at, :] + before
            own.add_up(sums_own, 0, m, slot_of, grad)
            own.add_up(sums_own, 1, m, slot_of, grad * normed)

        own.tiles(norm_grad)
        outs.finish()
        qkvs.finish()
        squares[...] = tile_up[...] + tile_qkv[...] + tile_out[...]

    return pl.pallas_call(
        kernel,
        out_shape=[
            jax.ShapeDtypeStruct((rows, width), low),
            jax.ShapeDtypeStruct((rows, width), f32),
            jax.ShapeDtypeStruct((3, own_images, width), f32),
            jax.ShapeDtypeStruct(up_shape, f32),
            jax.ShapeDtypeStruct((which, weight_rows, head_columns), f32),
            jax.ShapeDtypeStruct((1, weight_rows, head_columns), f32),
            jax.ShapeDtypeStruct(TILE, f32),
        ],
        in_specs=[WHOLE] * 8 + [HBM] * 7,
        out_specs=[WHOLE] * 7,
        scratch_shapes=[
            pltpu.VMEM((n_fsdp, rows, width), low),
            pltpu.VMEM((which, tokens, head_columns), low),
            pltpu.VMEM((which, n_dp, weight_rows, head_columns), low),
            pltpu.VMEM((1, n_dp, weight_rows, head_columns), low),
            pltpu.VMEM((rows, width), f32),
            pltpu.VMEM((rows, width), f32),
            pltpu.VMEM(TILE, f32),
            pltpu.VMEM(TILE, f32),
            pltpu.VMEM(TILE, f32),
            pltpu.VMEM((chips, rows, width), low),
            *[pltpu.VMEM(a.shape, low) for a in (grad_up, qkv_g, out_g, qkv_low, attended, hidden_g)],
            pltpu.SemaphoreType.DMA((6,)),
            pltpu.SemaphoreType.DMA((chips,)),
            *line, *scatter_got, *scatter_got, *up_got, *qkv_got, *out_got,
        ],
        compiler_params=parameters(3),
    )(
        grad_attn, tokens_own, mid, grad_mid, cotangent, codes, mods, codes_g, mlp_part, grad_up, qkv_g, out_g, qkv_low,
        attended, hidden_g,
    )


def norm_kernel(n_dp, n_fsdp, micro, sums_first, sums_second, condition, products, squares):
    own_images, width = sums_first.shape[1:]
    wide = width // n_fsdp
    images, deep = condition.shape[1:]
    lanes = wide // 128
    slots_here = own_images // micro
    source = [(0, 0), (0, 1), (1, 0), (1, 1), (1, 2), (0, 2)]

    def kernel(
        sums_a, sums_b, cond, product, squares_ref, grad, norm, mail, boxes, mine, all_mods, columns, tile, tiles, *sems
    ):
        place = Place(n_dp, n_fsdp)
        barrier = pltpu.get_barrier_semaphore()
        for i in range(1, n_dp):
            pl.semaphore_signal(
                barrier, inc=1, device_id=place.at_dp((place.dp + i) % n_dp), device_id_type=MESH
            )
        for i in range(1, n_fsdp):
            pl.semaphore_signal(
                barrier, inc=1, device_id=(place.dp, (place.f + i) % n_fsdp), device_id_type=MESH
            )
        for j, (which, row) in enumerate(source):
            values = (sums_a, sums_b)[which][row].astype(jnp.bfloat16).astype(jnp.float32)
            for f in range(n_fsdp):
                for g in range(lanes):
                    at = (j * lanes + g) * own_images
                    mail[f, at : at + own_images, :] = values[:, f * wide + g * 128 : f * wide + (g + 1) * 128]
        pl.semaphore_wait(barrier, n_dp + n_fsdp - 2)
        inner = Direct(place, mail, boxes, sems[0:2], "fsdp", block=lambda ref, d: ref.at[d])
        inner.start()
        boxes[place.f] = mail[place.f]
        inner.finish()
        for j in range(MODS):
            for g in range(lanes):
                pieces = []
                for m in range(micro):
                    at = (j * lanes + g) * own_images + m * slots_here
                    pieces += [boxes[f, at : at + slots_here, :] for f in range(n_fsdp)]
                mine[j, :, g * 128 : (g + 1) * 128] = jnp.concatenate(pieces, axis=0).astype(jnp.bfloat16)
        outer = Direct(place, mine, all_mods, sems[2:4])
        beside = Direct(place, squares_ref, columns, sems[4:6])
        outer.start()
        beside.start()
        all_mods[place.dp] = mine[...]
        columns[place.dp] = squares_ref[...]
        high = product[...].astype(jnp.bfloat16)
        rest = (product[...] - high.astype(jnp.float32)).astype(jnp.bfloat16)
        outer.finish()
        beside.finish()
        total = columns[0]
        for d in range(1, n_dp):
            total = total + columns[d]
        for j in range(MODS):
            values = all_mods[:, j].reshape(n_dp * images, wide)
            both = (matmul(high, values) + matmul(rest, values)) * values.astype(jnp.float32)
            for at in range(0, n_dp * images, ROW_STEP):
                for lane in range(0, wide, 128):
                    total = total + both[at : at + ROW_STEP, lane : lane + 128]
        tile[...] = total
        first = Direct(place, tile, tiles, sems[6:8], "fsdp")
        first.start()
        tiles[place.f] = tile[...]
        every = cond[...].reshape(n_dp * images, deep)
        for j in range(MODS):
            grad[j] = matmul_first(every, all_mods[:, j].reshape(n_dp * images, wide))
        first.finish()
        total = tiles[0]
        for f in range(1, n_fsdp):
            total = total + tiles[f]
        norm[0, 0] = jnp.sqrt(jnp.sum(total))

    return pl.pallas_call(
        kernel,
        out_shape=[
            jax.ShapeDtypeStruct((MODS, deep, wide), jnp.float32),
            jax.ShapeDtypeStruct((1, 1), jnp.float32),
        ],
        in_specs=[WHOLE] * 5,
        out_specs=[WHOLE, pl.BlockSpec(memory_space=pltpu.SMEM)],
        scratch_shapes=[
            pltpu.VMEM((n_fsdp, MODS * lanes * own_images, 128), jnp.float32),
            pltpu.VMEM((n_fsdp, MODS * lanes * own_images, 128), jnp.float32),
            pltpu.VMEM((MODS, images, wide), jnp.bfloat16),
            pltpu.VMEM((n_dp, MODS, images, wide), jnp.bfloat16),
            pltpu.VMEM((n_dp, *TILE), jnp.float32),
            pltpu.VMEM(TILE, jnp.float32),
            pltpu.VMEM((n_fsdp, *TILE), jnp.float32),
            *Direct.scratch(n_fsdp), *Direct.scratch(n_dp), *Direct.scratch(n_dp), *Direct.scratch(n_fsdp),
        ],
        compiler_params=parameters(1),
    )(sums_first, sums_second, condition, products, squares)


def adam_kernel(factor, grad, master, first, second):
    which, rows, columns = master.shape
    step = min(rows, max(64, 131072 // columns))
    block = pl.BlockSpec((1, step, columns), lambda w, r: (w, r, 0))

    def kernel(factor_ref, grad_ref, master_ref, first_ref, second_ref, new_ref, copy_ref, moment_ref, square_ref):
        scale = factor_ref[0, 0]
        clipped = grad_ref[...] * scale
        moment = BETA_ONE * first_ref[...] + (1.0 - BETA_ONE) * clipped
        square = BETA_TWO * second_ref[...] + (1.0 - BETA_TWO) * clipped * clipped
        moment_ref[...] = moment
        square_ref[...] = square
        below = jnp.sqrt(square * (1.0 / (1.0 - BETA_TWO**STEP))) + ADAM_EPS
        ratio = moment * (1.0 / (1.0 - BETA_ONE**STEP)) / below
        old = master_ref[...]
        new = old - LEARN_RATE * (ratio + WEIGHT_DECAY * old)
        new_ref[...] = new
        copy_ref[...] = new.astype(jnp.bfloat16)

    shape = jax.ShapeDtypeStruct(master.shape, jnp.float32)
    return pl.pallas_call(
        kernel,
        grid=(which, rows // step),
        out_shape=[shape, jax.ShapeDtypeStruct(master.shape, jnp.bfloat16), shape, shape],
        in_specs=[pl.BlockSpec(memory_space=pltpu.SMEM)] + [block] * 4,
        out_specs=[block] * 4,
        compiler_params=pltpu.CompilerParams(vmem_limit_bytes=VMEM_LIMIT),
    )(factor, grad, master, first, second)


def normalize(values):
    average = jnp.mean(values, axis=-1, keepdims=True)
    centred = values - average
    inv_std = lax.rsqrt(jnp.mean(centred * centred, axis=-1, keepdims=True) + NORM_EPS)
    return (centred * inv_std, inv_std)


def normalize_back(grad, normed, inv_std):
    return inv_std * (
        grad
        - jnp.mean(grad, axis=-1, keepdims=True)
        - normed * jnp.mean(grad * normed, axis=-1, keepdims=True)
    )


def body(n_dp, n_fsdp, *arguments):
    tokens, embedding, image_slot, token_mask, cotangent = arguments[:5]
    weights = [w if w.ndim == 3 else w[:, None] for w in arguments[5:]]
    weights = [w.transpose(1, 0, 2) for w in weights]
    masters, firsts, seconds = weights[:5], weights[5:10], weights[10:]
    qkv_w, out_w, up_w, down_w, ada_w = masters
    micro, tok_rows, width = tokens.shape
    own_rows = micro * tok_rows
    image_count = embedding.shape[1] // n_fsdp
    images = micro * n_fsdp * image_count
    images_of = jnp.arange(micro, dtype=jnp.int32)[:, None] * image_count
    codes = jnp.stack([(images_of + image_slot).reshape(own_rows), token_mask.reshape(own_rows)])
    codes = jnp.pad(codes.astype(jnp.float32), ((0, 6), (0, 0)))
    own_tokens = tokens.reshape(own_rows, width)
    own_cot = cotangent.reshape(own_rows, width)

    (
        attn_own, mid, hidden2, mods, cond_all, products, codes, codes_g, qkv_low, attended, down_low,
        hidden1_g, qkv_g, out_g, up_g, grad_mlp_g,
    ) = attention_kernel(
        n_dp, n_fsdp, micro, own_tokens, own_cot, codes, embedding.reshape(images, -1), ada_w, qkv_w, out_w, up_w, down_w
    )
    grad_mid, grad_attn, sums_second, grad_down, squares_down, mlp_part, grad_up = feed_forward_kernel(
        n_dp, n_fsdp, micro, hidden2, mid, attn_own, own_cot, codes, mods, grad_mlp_g, up_g, down_low
    )
    block_out, input_grad, sums_first, grad_up, grad_qkv_w, grad_out, squares = attention_grad_kernel(
        n_dp, n_fsdp, micro, grad_attn, own_tokens, mid, grad_mid, own_cot, codes, mods, codes_g, mlp_part, grad_up,
        qkv_g, out_g, qkv_low, attended, hidden1_g,
    )
    block_out = block_out.reshape(tokens.shape)
    input_grad = input_grad.reshape(tokens.shape)
    grad_ada, grad_norm = norm_kernel(
        n_dp, n_fsdp, micro, sums_first, sums_second, cond_all, products, squares_down + squares
    )

    factor = jnp.minimum(1.0, CLIP_AT / grad_norm)
    results = []
    grads = (grad_qkv_w, grad_out, grad_up, grad_down, grad_ada)
    for given, grad, master, first, second in zip(arguments[5:], grads, masters, firsts, seconds):
        for updated in adam_kernel(factor, grad, master, first, second):
            results.append(updated.transpose(1, 0, 2).reshape(given.shape))
    return (block_out, input_grad, *results, grad_norm[0, 0])


def solution(mesh):
    n_dp, n_fsdp = mesh.shape["dp"], mesh.shape["fsdp"]
    rows = P(None, ("dp", "fsdp"), None)
    slots = P(None, ("dp", "fsdp"))
    thick = P("dp", None, "fsdp")
    flat = P("dp", "fsdp")
    weights = (thick, flat, flat, flat, thick)
    updated = tuple(spec for spec in weights for _ in range(4))
    return jax.shard_map(
        functools.partial(body, n_dp, n_fsdp),
        mesh=mesh,
        in_specs=(rows, P(None, "dp", None), slots, slots, rows, *weights, *weights, *weights),
        out_specs=(rows, rows, *updated, P()),
        check_vma=False,
    )
```

```python
import functools

import jax
import jax.numpy as jnp
from jax import lax
from jax.experimental import pallas as pl
from jax.experimental.pallas import tpu as pltpu
from jax.sharding import PartitionSpec as P

HEAD = 128
STEP = 10
MODS = 6
FIRST_KINDS = (0, 1, 5)
OTHER_KINDS = (2, 3, 4)

NORM_EPS = 1e-06
CLIP_AT = 1.0
BETA_ONE = 0.9
BETA_TWO = 0.999
LEARN_RATE = 0.05
WEIGHT_DECAY = 0.1
ADAM_EPS = 1e-08

MESH = pl.DeviceIdType.MESH
VMEM_LIMIT = 62 * 1024 * 1024
SMALL_LIMIT = 16 * 1024 * 1024
NORM_LIMIT = 24 * 1024 * 1024
ROW_STEP = 16


class Place:
    def __init__(self, n_dp, n_fsdp):
        self.n_dp, self.n_fsdp = n_dp, n_fsdp
        self.chips = n_fsdp // 2
        self.grid_a = 2
        self.grid_b = n_dp // 2
        self.dp = lax.axis_index("dp")
        self.f = lax.axis_index("fsdp")
        self.p = self.f // 2
        self.c = self.f % 2
        self.a = self.dp // self.grid_b
        self.b = self.dp % self.grid_b

    def at_chip(self, chip):
        return (self.dp, chip * 2 + self.c)

    def sibling(self):
        return (self.dp, self.p * 2 + 1 - self.c)

    def at_dp(self, dp):
        return (dp, self.f)

    def b_peer(self, i):
        return (self.b + i) % self.grid_b

    def a_peer(self, i):
        return (self.a + i) % self.grid_a


def announce(place, line=False, grid=False, group=False):
    barrier = pltpu.get_barrier_semaphore()
    devices = []
    if group:
        for i in range(1, place.n_fsdp):
            devices.append((place.dp, (place.f + i) % place.n_fsdp))
    elif line:
        devices.append(place.at_chip((place.p + 1) % place.chips))
        devices.append(place.at_chip((place.p + place.chips - 1) % place.chips))
        devices.append(place.sibling())
    if grid:
        for i in range(1, place.n_dp):
            devices.append(place.at_dp((place.dp + i) % place.n_dp))
    for device in devices:
        pl.semaphore_signal(barrier, inc=1, device_id=device, device_id_type=MESH)
    return len(devices)


def enter(place, line=False, grid=False, group=False):
    count = announce(place, line, grid, group)
    pl.semaphore_wait(pltpu.get_barrier_semaphore(), count)


def remote(src, dst, send, recv, device):
    return pltpu.make_async_remote_copy(
        src_ref=src, dst_ref=dst, send_sem=send, recv_sem=recv, device_id=device, device_id_type=MESH
    )


class LineGather:
    @staticmethod
    def scratch(n_fsdp):
        chips = n_fsdp // 2
        return [
            pltpu.SemaphoreType.DMA((2, chips)),
            pltpu.SemaphoreType.DMA((2, chips)),
            pltpu.SemaphoreType.DMA((chips,)),
            pltpu.SemaphoreType.DMA((chips,)),
            pltpu.SemaphoreType.DMA,
        ]

    def __init__(self, place, src, out, sems, block=None):
        self.place, self.src, self.out = place, src, out
        self.send, self.recv, self.csend, self.crecv, self.local = sems
        self.of = block or (lambda ref, d: ref.at[d])

    def _block(self, chip):
        return self.of(self.out, chip * 2 + self.place.c)

    def _hop(self, way, step, first):
        pc = self.place
        chip = pc.p - step if way == 0 else pc.p + step
        target = pc.p + 1 if way == 0 else pc.p - 1
        src = self.src if first else self._block(chip)
        return remote(src, self._block(chip), self.send.at[way, step], self.recv.at[way, step], pc.at_chip(target))

    def _side(self, chip, first=False):
        src = self.src if first else self._block(chip)
        return remote(src, self._block(chip), self.csend.at[chip], self.crecv.at[chip], self.place.sibling())

    def _sends(self, way, step):
        pc = self.place
        if way == 0:
            return (pc.p < pc.chips - 1) & (pc.p >= step)
        return (pc.p > 0) & (pc.p + step <= pc.chips - 1)

    def start_way(self, way):
        @pl.when(self._sends(way, 0))
        def _():
            self._hop(way, 0, True).start()

    def start_here(self):
        pc = self.place
        self._side(pc.p, True).start()
        pltpu.make_async_copy(self.src, self._block(pc.p), self.local).start()

    def start(self):
        self.start_way(0)
        self.start_way(1)
        self.start_here()

    def step(self, step):
        pc = self.place
        for way in range(2):
            chip = pc.p - step if way == 0 else pc.p + step
            here = (chip >= 0) if way == 0 else (chip <= pc.chips - 1)

            @pl.when(here)
            def _():
                remote(
                    self._block(chip), self._block(chip), self.send.at[way, step - 1], self.recv.at[way, step - 1],
                    pc.sibling(),
                ).wait_recv()
                if step < pc.chips - 1:
                    @pl.when(self._sends(way, step))
                    def _():
                        self._hop(way, step, False).start()
                self._side(chip).start()

    def ready(self, chip):
        pc = self.place
        other = self.of(self.out, chip * 2 + 1 - pc.c)
        remote(other, other, self.csend.at[chip], self.crecv.at[chip], pc.sibling()).wait_recv()

        @pl.when(chip == pc.p)
        def _():
            pltpu.make_async_copy(self.src, self._block(pc.p), self.local).wait()

    def drain(self):
        pc = self.place
        for chip in range(pc.chips):
            self._side(chip).wait_send()
        for way in range(2):
            for step in range(pc.chips - 1):
                @pl.when(self._sends(way, step))
                def _():
                    self._hop(way, step, False).wait_send()

    def finish(self):
        for chip in range(self.place.chips):
            self.ready(chip)
        self.drain()


class LineCast:
    @staticmethod
    def scratch(n_fsdp):
        return [pltpu.SemaphoreType.DMA((n_fsdp // 2,)) for _ in range(4)] + [pltpu.SemaphoreType.DMA]

    def __init__(self, place, src, out, sems, block):
        self.place, self.src, self.out, self.of = place, src, out, block
        self.send, self.recv, self.csend, self.crecv, self.local = sems

    def _copy(self, i, coming=False):
        pc = self.place
        chip = (pc.p + pc.chips - i) % pc.chips if coming else pc.p
        return remote(
            self.src, self.of(self.out, chip * 2 + pc.c), self.send.at[i], self.recv.at[i],
            pc.at_chip((pc.p + i) % pc.chips),
        )

    def _side(self, i, coming=False):
        pc = self.place
        chip = (pc.p + pc.chips - i) % pc.chips
        block = self.of(self.out, chip * 2 + (1 - pc.c if coming else pc.c))
        return remote(block if i else self.src, block, self.csend.at[i], self.crecv.at[i], pc.sibling())

    def start(self):
        pc = self.place
        for i in range(1, pc.chips):
            self._copy(i).start()
        self._side(0).start()
        pltpu.make_async_copy(self.src, self.of(self.out, pc.f), self.local).start()

    def step(self):
        for i in range(1, self.place.chips):
            self._copy(i, True).wait_recv()
            self._side(i).start()

    def finish(self):
        pc = self.place
        pltpu.make_async_copy(self.src, self.of(self.out, pc.f), self.local).wait()
        for i in range(pc.chips):
            self._side(i, True).wait_recv()
            self._side(i).wait_send()
        for i in range(1, pc.chips):
            self._copy(i).wait_send()


def row_loop(rows, body, first=0):
    def run(i, carry):
        body(pl.ds(pl.multiple_of(first + i * ROW_STEP, ROW_STEP), ROW_STEP))
        return carry

    lax.fori_loop(0, rows // ROW_STEP, run, 0)


class LineScatter:
    pieces = 4

    @classmethod
    def scratch(cls, n_fsdp, rows, width):
        chips = n_fsdp // 2
        return [
            pltpu.VMEM((chips, rows, width), jnp.bfloat16),
            pltpu.VMEM((chips + 1, rows, width), jnp.bfloat16),
            pltpu.SemaphoreType.DMA((chips,)),
            pltpu.SemaphoreType.DMA((chips,)),
            pltpu.SemaphoreType.DMA((2, chips, cls.pieces)),
            pltpu.SemaphoreType.DMA((2, chips, cls.pieces)),
        ]

    def __init__(self, place, part, out, scratch, mine=None, lag=2):
        self.place, self.part, self.out, self.mine = place, part, out, mine
        self.side, self.inbox, self.csend, self.crecv, self.send, self.recv = scratch
        self.rows = out.shape[0]
        self.piece = self.rows // self.pieces
        self.lag = lag
        self.slots = (place.chips - 1) * self.lag + place.chips * self.pieces

    def _side(self, chip):
        pc = self.place
        return remote(
            self.part.at[chip * 2 + 1 - pc.c], self.side.at[chip], self.csend.at[chip], self.crecv.at[chip], pc.sibling()
        )

    def _hop(self, way, chip, s):
        pc = self.place
        target = pc.p + 1 if way == 0 else pc.p - 1
        rows = pl.ds(pl.multiple_of(s * self.piece, self.piece), self.piece)
        return remote(
            self.side.at[chip, rows], self.inbox.at[chip + 1 - way, rows], self.send.at[way, chip, s],
            self.recv.at[way, chip, s], pc.at_chip(target),
        )

    def start(self):
        def one(k, carry):
            self.offer(self.order(k))
            return carry

        lax.fori_loop(0, self.place.chips, one, 0)

    def offer(self, chip):
        self._side(chip).start()

    def order(self, k):
        pc = self.place
        chips = pc.chips
        after, before = chips - 1 - pc.p, pc.p
        short = jnp.minimum(after, before)
        lone = jnp.maximum(after, before) - short
        rest = jnp.maximum(k - lone, 0)
        near = short - rest // 2
        pair = jnp.where(lax.rem(rest, 2) == 0, pc.p + near, pc.p - near)
        return jnp.where(k < lone, jnp.where(after > before, chips - 1 - k, k), pair)

    def first_slot(self, k):
        pc = self.place
        chips = pc.chips
        chip = self.order(k)
        after = pc.p * self.lag + (chips - 1 - chip) * self.pieces
        before = (chips - 1 - pc.p) * self.lag + chip * self.pieces
        slot = jnp.where(chip > pc.p, after, before)
        return jnp.where((k >= chips - 1) | (chip == pc.p), self.slots, slot)

    def paced(self, compute, pace, then):
        def one(k, slot):
            chip = self.order(k)
            compute(chip)
            self.offer(chip)
            until = jnp.minimum(self.first_slot(k + 1), self.first_slot(k + 2))
            until = jnp.maximum(jnp.minimum(until, (k + 1) * pace), slot)
            self.run(slot, until)
            then(k)
            return until

        return lax.fori_loop(0, self.place.chips, one, jnp.int32(0))

    def beside(self, slot, count, work, every=1):
        def one(i, carry):
            work(i)

            @pl.when(lax.rem(i, every) == every - 1)
            def _():
                self.step(slot + i // every)

            return carry

        lax.fori_loop(0, count, one, 0)
        return slot + count // every

    def run_to(self, slot, end):
        end = jnp.maximum(slot, end)
        self.run(slot, end)
        return end

    def _add(self, chip, s, inboxes, store):
        pc = self.place

        def add(rows):
            if self.mine is None:
                total = self.part[chip * 2 + pc.c, rows, :].astype(jnp.float32)
            else:
                total = self.mine[chip, rows, :].astype(jnp.float32)
            total = total + self.side[chip, rows, :].astype(jnp.float32)
            for way in inboxes:
                total = total + self.inbox[chip + 1 - way, rows, :].astype(jnp.float32)
            store(rows, total)

        row_loop(self.piece, add, s * self.piece)

    def _travel(self, way, t):
        pc = self.place
        chips = pc.chips
        i = t - (pc.p if way == 0 else chips - 1 - pc.p) * self.lag
        k = jnp.clip(i // self.pieces, 0, chips - 1)
        s = lax.rem(jnp.maximum(i, 0), self.pieces)
        chip = chips - 1 - k if way == 0 else k
        going = (i >= 0) & (i < chips * self.pieces) & ((chip > pc.p) if way == 0 else (chip < pc.p))
        first = (pc.p == 0) if way == 0 else (pc.p == chips - 1)

        def store(rows, total):
            self.side[chip, rows, :] = total.astype(jnp.bfloat16)

        @pl.when(going)
        def _():
            @pl.when(s == 0)
            def _():
                self._side(chip).wait_recv()

            @pl.when(first)
            def _():
                self._add(chip, s, (), store)

            @pl.when(jnp.logical_not(first))
            def _():
                self._hop(way, chip, s).wait_recv()
                self._add(chip, s, (way,), store)

            self._hop(way, chip, s).start()

    def step(self, t):
        self._travel(0, t)
        self._travel(1, t)

    def run(self, begin, end):
        def one(t, carry):
            self.step(t)
            return carry

        lax.fori_loop(begin, end, one, 0)

    def finish(self):
        pc = self.place
        chips = pc.chips
        self._side(pc.p).wait_recv()

        def store(rows, total):
            self.out[rows, :] = total

        def piece(s, carry):
            @pl.when(pc.p == 0)
            def _():
                self._hop(1, pc.p, s).wait_recv()
                self._add(pc.p, s, (1,), store)

            @pl.when(pc.p == chips - 1)
            def _():
                self._hop(0, pc.p, s).wait_recv()
                self._add(pc.p, s, (0,), store)

            @pl.when((pc.p > 0) & (pc.p < chips - 1))
            def _():
                self._hop(0, pc.p, s).wait_recv()
                self._hop(1, pc.p, s).wait_recv()
                self._add(pc.p, s, (0, 1), store)

            return carry

        lax.fori_loop(0, self.pieces, piece, 0)
        for chip in range(chips):
            self._side(chip).wait_send()

            def sent(s, carry):
                @pl.when(chip > pc.p)
                def _():
                    self._hop(0, chip, s).wait_send()

                @pl.when(chip < pc.p)
                def _():
                    self._hop(1, chip, s).wait_send()

                return carry

            lax.fori_loop(0, self.pieces, sent, 0)


class GridGather:
    @staticmethod
    def scratch(n_dp):
        na, nb = 2, n_dp // 2
        return [
            pltpu.SemaphoreType.DMA((2, max(nb - 1, 1))),
            pltpu.SemaphoreType.DMA((2, max(nb - 1, 1))),
            pltpu.SemaphoreType.DMA((2, na - 1)),
            pltpu.SemaphoreType.DMA((2, na - 1)),
            pltpu.SemaphoreType.DMA((2, max(nb - 1, 1), na - 1)),
            pltpu.SemaphoreType.DMA((2, max(nb - 1, 1), na - 1)),
            pltpu.SemaphoreType.DMA,
        ]

    def __init__(self, place, src, out, sems):
        self.place, self.src, self.out = place, src, out
        self.bsend, self.brecv, self.asend, self.arecv, self.fsend, self.frecv, self.local = sems
        self.half = src.shape[1] // 2

    def _own(self, h):
        return self.src.at[:, pl.ds(h * self.half, self.half)]

    def _block(self, a, b, h):
        return self.out.at[:, a * self.place.grid_b + b, pl.ds(h * self.half, self.half)]

    def _b_copy(self, i, h, coming):
        pc = self.place
        b = pc.b_peer(pc.grid_b - i) if coming else pc.b
        return remote(
            self._own(h), self._block(pc.a, b, h), self.bsend.at[h, i - 1], self.brecv.at[h, i - 1],
            pc.at_dp(pc.a * pc.grid_b + pc.b_peer(i)),
        )

    def _a_copy(self, i, h, coming):
        pc = self.place
        a = pc.a_peer(pc.grid_a - i) if coming else pc.a
        return remote(
            self._own(h), self._block(a, pc.b, h), self.asend.at[h, i - 1], self.arecv.at[h, i - 1],
            pc.at_dp(pc.a_peer(i) * pc.grid_b + pc.b),
        )

    def _on(self, h, ib, ia, coming):
        pc = self.place
        if h == 0:
            b = pc.b_peer(pc.grid_b - ib)
            a = pc.a_peer(pc.grid_a - ia) if coming else pc.a
            target = pc.at_dp(pc.a_peer(ia) * pc.grid_b + pc.b)
        else:
            a = pc.a_peer(pc.grid_a - ia)
            b = pc.b_peer(pc.grid_b - ib) if coming else pc.b
            target = pc.at_dp(pc.a * pc.grid_b + pc.b_peer(ib))
        block = self._block(a, b, h)
        return remote(block, block, self.fsend.at[h, ib - 1, ia - 1], self.frecv.at[h, ib - 1, ia - 1], target)

    def start(self):
        pc = self.place
        for h in range(2):
            for i in range(1, pc.grid_b):
                self._b_copy(i, h, False).start()
            for i in range(1, pc.grid_a):
                self._a_copy(i, 1 - h, False).start()
        pltpu.make_async_copy(self.src, self.out.at[:, pc.dp], self.local).start()

    def step(self):
        pc = self.place
        for ib in range(1, pc.grid_b):
            self._b_copy(ib, 0, True).wait_recv()
            for ia in range(1, pc.grid_a):
                self._on(0, ib, ia, False).start()
        for ia in range(1, pc.grid_a):
            self._a_copy(ia, 1, True).wait_recv()
            for ib in range(1, pc.grid_b):
                self._on(1, ib, ia, False).start()

    def finish(self):
        pc = self.place
        pltpu.make_async_copy(self.src, self.out.at[:, pc.dp], self.local).wait()
        for ib in range(1, pc.grid_b):
            self._b_copy(ib, 1, True).wait_recv()
        for ia in range(1, pc.grid_a):
            self._a_copy(ia, 0, True).wait_recv()
        for h in range(2):
            for ib in range(1, pc.grid_b):
                for ia in range(1, pc.grid_a):
                    self._on(h, ib, ia, True).wait_recv()
                    self._on(h, ib, ia, False).wait_send()
        for h in range(2):
            for ib in range(1, pc.grid_b):
                self._b_copy(ib, h, False).wait_send()
            for ia in range(1, pc.grid_a):
                self._a_copy(ia, h, False).wait_send()


class GridScatter:
    @staticmethod
    def scratch(n_dp, which, rows, width):
        na, nb = 2, n_dp // 2
        half = rows // 2
        most = max(nb - 1, 1)
        return [
            pltpu.VMEM((most, na, which, half, width), jnp.bfloat16),
            pltpu.VMEM((na - 1, nb, which, half, width), jnp.bfloat16),
            pltpu.VMEM((na - 1, which, half, width), jnp.bfloat16),
            pltpu.VMEM((most, which, half, width), jnp.bfloat16),
            pltpu.VMEM((na - 1, which, half, width), jnp.bfloat16),
            pltpu.VMEM((most, which, half, width), jnp.bfloat16),
            pltpu.SemaphoreType.DMA((most, na)),
            pltpu.SemaphoreType.DMA((most, na)),
            pltpu.SemaphoreType.DMA((na - 1, nb)),
            pltpu.SemaphoreType.DMA((na - 1, nb)),
            pltpu.SemaphoreType.DMA((na - 1,)),
            pltpu.SemaphoreType.DMA((na - 1,)),
            pltpu.SemaphoreType.DMA((most,)),
            pltpu.SemaphoreType.DMA((most,)),
        ]

    def __init__(self, place, part, out, squares, scratch):
        self.place, self.part, self.out, self.squares = place, part, out, squares
        self.box_b, self.box_a, self.sum_b, self.sum_a, self.end_a, self.end_b = scratch[:6]
        self.bs, self.br, self.as_, self.ar, self.eas, self.ear, self.ebs, self.ebr = scratch[6:]
        self.which = out.shape[0]
        self.half = out.shape[1] // 2

    def _part(self, a, b, h):
        return self.part.at[:, a * self.place.grid_b + b, pl.ds(h * self.half, self.half)]

    def _first_b(self, i, j):
        pc = self.place
        return remote(
            self._part(pc.a_peer(j), pc.b_peer(i), 0), self.box_b.at[i - 1, j], self.bs.at[i - 1, j],
            self.br.at[i - 1, j], pc.at_dp(pc.a * pc.grid_b + pc.b_peer(i)),
        )

    def _first_a(self, i, j):
        pc = self.place
        return remote(
            self._part(pc.a_peer(i), pc.b_peer(j), 1), self.box_a.at[i - 1, j], self.as_.at[i - 1, j],
            self.ar.at[i - 1, j], pc.at_dp(pc.a_peer(i) * pc.grid_b + pc.b),
        )

    def _second_a(self, i):
        pc = self.place
        return remote(
            self.sum_b.at[i - 1], self.end_a.at[i - 1], self.eas.at[i - 1], self.ear.at[i - 1],
            pc.at_dp(pc.a_peer(i) * pc.grid_b + pc.b),
        )

    def _second_b(self, i):
        pc = self.place
        return remote(
            self.sum_a.at[i - 1], self.end_b.at[i - 1], self.ebs.at[i - 1], self.ebr.at[i - 1],
            pc.at_dp(pc.a * pc.grid_b + pc.b_peer(i)),
        )

    def _firsts_b(self):
        pc = self.place
        return [(i, j) for j in list(range(1, pc.grid_a)) + [0] for i in range(1, pc.grid_b)]

    def _firsts_a(self):
        pc = self.place
        return [(i, j) for j in list(range(1, pc.grid_b)) + [0] for i in range(1, pc.grid_a)]

    def start(self):
        for (ib, jb), (ia, ja) in zip(self._firsts_b(), self._firsts_a(), strict=False):
            self._first_b(ib, jb).start()
            self._first_a(ia, ja).start()
        shared = min(len(self._firsts_b()), len(self._firsts_a()))
        for i, j in self._firsts_b()[shared:]:
            self._first_b(i, j).start()
        for i, j in self._firsts_a()[shared:]:
            self._first_a(i, j).start()

    def _low(self, rows):
        return pl.ds(pl.multiple_of(self.half + rows.start, ROW_STEP), ROW_STEP)

    def _sum_b(self, j):
        pc = self.place
        for i in range(1, pc.grid_b):
            self._first_b(i, j).wait_recv()
        mine = pc.a_peer(j) * pc.grid_b + pc.b

        def add(rows):
            for w in range(self.which):
                total = self.part[w, mine, rows, :].astype(jnp.float32)
                for i in range(1, pc.grid_b):
                    total = total + self.box_b[i - 1, j, w, rows, :].astype(jnp.float32)
                if j == 0:
                    self.out[w, rows, :] = total
                else:
                    self.sum_b[j - 1, w, rows, :] = total.astype(jnp.bfloat16)

        row_loop(self.half, add)
        if j:
            self._second_a(j).start()

    def _sum_a(self, j):
        pc = self.place
        for i in range(1, pc.grid_a):
            self._first_a(i, j).wait_recv()
        mine = pc.a * pc.grid_b + pc.b_peer(j)

        def add(rows):
            for w in range(self.which):
                total = self.part[w, mine, self._low(rows), :].astype(jnp.float32)
                for i in range(1, pc.grid_a):
                    total = total + self.box_a[i - 1, j, w, rows, :].astype(jnp.float32)
                if j == 0:
                    self.out[w, self._low(rows), :] = total
                else:
                    self.sum_a[j - 1, w, rows, :] = total.astype(jnp.bfloat16)

        row_loop(self.half, add)
        if j:
            self._second_b(j).start()

    def step(self):
        pc = self.place
        for j in range(1, max(pc.grid_a, pc.grid_b)):
            if j < pc.grid_a:
                self._sum_b(j)
            if j < pc.grid_b:
                self._sum_a(j)

    def step_own(self):
        self._sum_b(0)
        self._sum_a(0)

    def finish(self):
        pc = self.place
        for i in range(1, pc.grid_a):
            self._second_a(i).wait_recv()
        for i in range(1, pc.grid_b):
            self._second_b(i).wait_recv()
        self.squares[...] = jnp.zeros_like(self.squares)

        def tile(total):
            total = total * total
            folded = total[:, :128]
            for at in range(128, total.shape[1], 128):
                folded = folded + total[:, at : at + 128]
            return folded

        def add(rows):
            low = self._low(rows)
            for w in range(self.which):
                total = self.out[w, rows, :]
                for i in range(1, pc.grid_a):
                    total = total + self.end_a[i - 1, w, rows, :].astype(jnp.float32)
                self.out[w, rows, :] = total
                self.squares[...] += tile(total)
                total = self.out[w, low, :]
                for i in range(1, pc.grid_b):
                    total = total + self.end_b[i - 1, w, rows, :].astype(jnp.float32)
                self.out[w, low, :] = total
                self.squares[...] += tile(total)

        row_loop(self.half, add)
        for i, j in self._firsts_b():
            self._first_b(i, j).wait_send()
        for i, j in self._firsts_a():
            self._first_a(i, j).wait_send()
        for i in range(1, pc.grid_a):
            self._second_a(i).wait_send()
        for i in range(1, pc.grid_b):
            self._second_b(i).wait_send()


class Direct:
    @staticmethod
    def scratch(n):
        return [pltpu.SemaphoreType.DMA((n - 1,)), pltpu.SemaphoreType.DMA((n - 1,))]

    def __init__(self, place, src, out, sems, axis="dp", block=None, to=None):
        self.place, self.src, self.out = place, src, out
        self.send, self.recv = sems
        self.n = place.n_dp if axis == "dp" else place.n_fsdp
        self.me = place.dp if axis == "dp" else place.f
        self.axis = axis
        self.of = block or (lambda ref, d: ref)
        self.to = to or (lambda ref, d: ref.at[d])

    def _device(self, other):
        return self.place.at_dp(other) if self.axis == "dp" else (self.place.dp, other)

    def _copy(self, i, coming=False):
        other = (self.me + i) % self.n
        origin = (self.me + self.n - i) % self.n if coming else self.me
        return remote(
            self.of(self.src, other), self.to(self.out, origin), self.send.at[i - 1], self.recv.at[i - 1], self._device(other)
        )

    def start(self):
        for i in range(1, self.n):
            self._copy(i).start()

    def finish(self):
        for i in range(1, self.n):
            self._copy(i, True).wait_recv()
            self._copy(i).wait_send()


def split_refs(refs, counts):
    out, at = [], 0
    for count in counts:
        out.append(refs[at : at + count])
        at += count
    return out


HBM = pl.BlockSpec(memory_space=pl.ANY)
WHOLE = pl.BlockSpec(memory_space=pltpu.VMEM)
TILE = (ROW_STEP, 128)


def parameters(collective_id, limit=VMEM_LIMIT):
    return pltpu.CompilerParams(collective_id=collective_id, has_side_effects=True, vmem_limit_bytes=limit)


def matmul(left, right):
    return jnp.dot(left, right, preferred_element_type=jnp.float32)


def matmul_last(left, right):
    return lax.dot_general(left, right, (((1,), (1,)), ((), ())), preferred_element_type=jnp.float32)


def matmul_first(left, right):
    return lax.dot_general(left, right, (((0,), (0,)), ((), ())), preferred_element_type=jnp.float32)


def loop(count, work):
    def one(i, carry):
        work(i)
        return carry

    lax.fori_loop(0, count, one, 0)


def span(i, size):
    return pl.ds(pl.multiple_of(i * size, size), size)


def chip_rows(ref, chip):
    pair = ref[span(chip, 2)]
    return pair.reshape(-1, pair.shape[-1])


def pair_mask(codes_ref, chip, rows):
    pair = [codes_ref[chip * 2 + i] for i in range(2)]
    query = jnp.floor(jnp.concatenate([block[:rows] for block in pair], axis=0))
    query = jnp.concatenate([query] * (2 * rows // 128), axis=1)
    key = jnp.concatenate([block[rows : rows + 1] for block in pair], axis=1)
    shape = (2 * rows, 2 * rows)
    same = lax.broadcasted_iota(jnp.int32, shape, 0) == lax.broadcasted_iota(jnp.int32, shape, 1)
    return (query == key) | same


class Rows:
    def __init__(self, place, codes, mods, micro, rows, slots_here):
        self.place, self.codes, self.mods = place, codes, mods
        self.micro, self.tok_rows, self.slots_here = micro, rows // micro, slots_here

    def tiles(self, work):
        for m in range(self.micro):
            row_loop(self.tok_rows, functools.partial(work, m), m * self.tok_rows)

    def slot_live(self, m, rows):
        column = self.codes[rows, :][:, :1]
        number = jnp.floor(column)
        first = ((self.place.f * self.micro + m) * self.slots_here).astype(jnp.float32)
        return number - first, jnp.where(column == number, 1.0, 0.0)

    def pick(self, j, m, slot):
        at = m * self.slots_here
        picked = self.mods[j, at : at + 1, :]
        for i in range(1, self.slots_here):
            picked = jnp.where(slot == i, self.mods[j, at + i : at + i + 1, :], picked)
        return picked

    def add_up(self, out, j, m, slot, values):
        for i in range(self.slots_here):
            at = m * self.slots_here + i
            chosen = jnp.where(slot == i, values, 0.0)
            out[j, at : at + 1, :] += jnp.sum(chosen, axis=0, keepdims=True)


def cast_rows(src, dst):
    for w in range(src.shape[0]):
        def tile(rows):
            dst[w, rows, :] = src[w, rows, :].astype(dst.dtype)

        row_loop(src.shape[1], tile)


def attention_probs(query, key, allowed):
    scores = jnp.where(allowed, matmul_last(query, key) * HEAD ** (-0.5), -1e30)
    raw = jnp.exp(scores - jnp.max(scores, axis=-1, keepdims=True))
    return raw / jnp.sum(raw, axis=-1, keepdims=True)


def attention_kernel(n_dp, n_fsdp, micro, tokens, cotangent, codes, embedding, ada, qkv, out_w, up, down):
    low, f32 = jnp.bfloat16, jnp.float32
    images = embedding.shape[0]
    rows, width = tokens.shape
    deep, wide = ada.shape[1:]
    which, _, head_columns = qkv.shape
    slots_here = images // (micro * n_fsdp)
    own_images = micro * slots_here
    line = LineGather.scratch(n_fsdp)
    grid = GridGather.scratch(n_dp)
    direct = Direct.scratch(n_dp)
    scatter_got = LineScatter.scratch(n_fsdp, rows, width)
    counts = [len(line)] * 3 + [len(grid)] * 3 + [len(direct)] * 5 + [len(LineCast.scratch(n_fsdp)), len(scatter_got)]
    weights = (qkv, out_w, up, down, ada)
    pair = 2 * rows

    def kernel(
        tok, cot, code_row, emb, ada_f, qkv_f, out_f, up_f, down_f,
        attn_own, mid, hidden2, mods_own, cond_g, products, cod, cod_g, qkv_low, attended, down_low,
        hidden_out, qkv_out, out_out, up_g, gmlp_g,
        cond, parts, boxes, mail_first, mail, inbox, mods_g, averages, inv_stds, product, products_g, gmlp, part, hidden_g, qkv_g, out_g,
        qkv_s, out_s, up_s, down_s, ada_s, qkv_l, out_l, up_l, moves, *rest,
    ):
        sems = split_refs(rest, counts)
        place = Place(n_dp, n_fsdp)
        fetches = [
            pltpu.make_async_copy(ref, stage, moves.at[i])
            for i, (ref, stage) in enumerate(
                ((qkv_f, qkv_s), (out_f, out_s), (up_f, up_s), (down_f, down_s), (ada_f, ada_s))
            )
        ]
        for i in (0, 1, 4, 2, 3):
            fetches[i].start()
        present = announce(place, True, True, True)
        level = emb[...].astype(f32)
        level = (level / (1.0 + jnp.exp(-level))).astype(low)
        for d in range(n_dp):
            cond[d] = level[:, d * deep : (d + 1) * deep]
        number = code_row[0:1, :] + ((place.f * micro) * slots_here).astype(f32)
        live = code_row[1:2, :]
        cod[:rows, :] = jnp.transpose(jnp.broadcast_to(jnp.where(live > 0.5, number, number + 0.25), (rows, rows)))
        cod[rows:, :] = jnp.broadcast_to(jnp.where(live > 0.5, number, -1.0), (8, rows))
        own = Rows(place, cod, mods_own, micro, rows, slots_here)
        fetches[0].wait()
        cast_rows(qkv_s, qkv_l)
        fetches[1].wait()
        cast_rows(out_s, out_l)
        pl.semaphore_wait(pltpu.get_barrier_semaphore(), present)
        conds = Direct(place, cond, cond_g, sems[6], block=lambda ref, d: ref.at[d])
        conds.start()
        token_line = LineGather(place, tok, hidden_g, sems[1])
        code_line = LineGather(place, cod, cod_g, sems[0])
        token_line.start()
        code_line.start()
        grids = [GridGather(place, qkv_l, qkv_g, sems[3]), GridGather(place, out_l, out_g, sems[4])]
        cond_g[place.dp] = cond[place.dp]
        fetches[4].wait()
        conds.finish()
        every = cond_g[...].reshape(n_dp * images, deep)

        def project(kinds):
            for j, kind in kinds:
                parts[:, j] = matmul(every, ada_s[kind].astype(low)).reshape(n_dp, images, wide)

        def add_parts(kinds, letter):
            for j in kinds:
                total = parts[place.dp, j]
                for i in range(1, n_dp):
                    total = total + boxes[(place.dp + i) % n_dp, j]
                for f in range(n_fsdp):
                    for m in range(micro):
                        at = (m * n_fsdp + f) * slots_here
                        letter[f, j - kinds[0], m * slots_here : (m + 1) * slots_here, :] = total[at : at + slots_here]

        first_sums = Direct(
            place, parts, boxes, sems[7], block=lambda ref, d: ref.at[d, 0:3], to=lambda ref, d: ref.at[d, 0:3]
        )
        other_sums = Direct(
            place, parts, boxes, sems[8], block=lambda ref, d: ref.at[d, 3:MODS], to=lambda ref, d: ref.at[d, 3:MODS]
        )
        project(list(enumerate(FIRST_KINDS)))
        first_sums.start()
        for gather in grids:
            gather.start()
        project(list(enumerate(OTHER_KINDS, 3)))
        product[...] = matmul_last(every, every)

        def statistics(chip):
            token_line.ready(chip)
            for i in range(2):
                device = chip * 2 + i

                def tile(at):
                    values = hidden_g[device, at, :].astype(f32)
                    average = jnp.mean(values, axis=-1, keepdims=True)
                    centred = values - average
                    inv_std = lax.rsqrt(jnp.mean(centred * centred, axis=-1, keepdims=True) + NORM_EPS)
                    averages[device, at, :] = jnp.broadcast_to(average, (ROW_STEP, 128))
                    inv_stds[device, at, :] = jnp.broadcast_to(inv_std, (ROW_STEP, 128))

                row_loop(rows, tile)

        def statistics_at(distance):
            def side(i):
                chip = place.p + (1 - 2 * i) * distance

                @pl.when((chip >= 0) & (chip < place.chips))
                def _():
                    statistics(chip)

            loop(2 if distance else 1, side)

        statistics_at(0)
        first_sums.finish()
        add_parts((0, 1, 2), mail_first)
        mods_line = LineCast(
            place, mail_first, mods_g, sems[11],
            block=lambda ref, d: ref.at[:, :, :, pl.ds(pl.multiple_of(d * wide, wide), wide)],
        )
        mods_line.start()
        token_line.step(1)
        code_line.step(1)
        fetches[2].wait()
        cast_rows(up_s, up_l)
        fetches[3].wait()
        cast_rows(down_s, down_low)
        crosses = Direct(place, product, products_g, sems[10])
        products_g[place.dp] = product[...]
        mods_line.step()
        ups = GridGather(place, up_l, up_g, sems[5])
        letters = Direct(place, mail, inbox, sems[9], "fsdp", block=lambda ref, d: ref.at[d])
        gmlp_line = LineGather(place, gmlp, gmlp_g, sems[2])

        def branch_grad(m, at):
            slot, alive = own.slot_live(m, at)
            gmlp[at, :] = (cot[at, :].astype(f32) * alive * own.pick(5, m, slot)).astype(low)

        mods_line.finish()
        for j, kind in enumerate(FIRST_KINDS):
            mods_own[kind] = mods_g[place.f, j]
        own.tiles(branch_grad)
        gmlp_line.start_here()
        for step in range(2, place.chips + 1):
            if step < place.chips:
                token_line.step(step)
                code_line.step(step)
            if step == 2:
                for gather in grids:
                    gather.step()
            statistics_at(step - 1)

            @pl.when((place.p + 1 == step) | ((place.p + 1 < step) & (step == 2)))
            def _():
                gmlp_line.start_way(0)

            @pl.when((place.chips - place.p == step) | ((place.chips - place.p < step) & (step == 2)))
            def _():
                gmlp_line.start_way(1)

        for gather in grids:
            gather.finish()
        other_sums.start()
        crosses.start()
        ups.start()
        token_line.drain()
        code_line.finish()
        leaves = [
            pltpu.make_async_copy(ref, out, moves.at[len(weights) + i])
            for i, (ref, out) in enumerate(((qkv_g, qkv_out), (out_g, out_out), (hidden_g, hidden_out)))
        ]
        for leave in leaves[:2]:
            leave.start()
        scatter = LineScatter(place, part, attn_own, sems[12])

        def norm_block(chip):
            for i in range(2):
                device = chip * 2 + i
                for m in range(micro):
                    first = ((device * micro + m) * slots_here).astype(f32)

                    def table(j, slot):
                        at = m * slots_here
                        picked = mods_g[device, j, at : at + 1, :]
                        for k in range(1, slots_here):
                            picked = jnp.where(slot == k, mods_g[device, j, at + k : at + k + 1, :], picked)
                        return picked

                    def tile(at):
                        slot = jnp.floor(cod_g[device, at, :][:, :1]) - first
                        centred = hidden_g[device, at, :].astype(f32) - averages[device, at, :][:, :1]
                        normed = centred * inv_stds[device, at, :][:, :1]
                        hidden_g[device, at, :] = (normed * (1.0 + table(1, slot)) + table(0, slot)).astype(low)

                    row_loop(rows // micro, tile, m * (rows // micro))

        def compute(chip):
            at = span(chip, pair)
            norm_block(chip)
            values = chip_rows(hidden_g, chip)
            for w in range(which):
                weight = qkv_g[w].reshape(width, head_columns)
                qkv_low[w, at, :] = matmul(values, weight).astype(low)
            allowed = pair_mask(cod_g, chip, rows)
            for h in range(head_columns // HEAD):
                head = slice(h * HEAD, (h + 1) * HEAD)
                probs = attention_probs(qkv_low[0, at, head], qkv_low[1, at, head], allowed)
                attended[at, head] = matmul(probs.astype(low), qkv_low[2, at, head]).astype(low)
            heads = attended[at, :]
            weight_rows = out_g.shape[2]
            for d in range(n_dp):
                piece = matmul_last(heads, out_g[0, d]).astype(low).reshape(2, rows, weight_rows)
                part[span(chip, 2), :, d * weight_rows : (d + 1) * weight_rows] = piece

        def then(k):
            @pl.when(k == 1)
            def _():
                gmlp_line.step(1)

        slot = scatter.paced(compute, 1, then)
        leaves[2].start()
        for step in range(2, place.chips):
            gmlp_line.step(step)
            slot = scatter.run_to(slot, scatter.slots * (step + 1) // (place.chips + 1))
            if step == place.chips // 2:
                other_sums.finish()
                add_parts((3, 4, 5), mail)
                letters.start()
                inbox[place.f] = mail[place.f]
                ups.step()
                crosses.finish()
                total = products_g[0]
                for d in range(1, n_dp):
                    total = total + products_g[d]
                products[...] = total
        scatter.run_to(slot, scatter.slots)
        scatter.finish()
        letters.finish()
        for f in range(n_fsdp):
            for j, kind in enumerate(OTHER_KINDS):
                mods_own[kind, :, f * wide : (f + 1) * wide] = inbox[f, j]

        def second_norm(m, at):
            slot, _ = own.slot_live(m, at)
            values = tok[at, :].astype(f32) + own.pick(2, m, slot) * attn_own[at, :]
            mid[at, :] = values
            normed, _ = normalize(values)
            hidden2[at, :] = (normed * (1.0 + own.pick(4, m, slot)) + own.pick(3, m, slot)).astype(low)

        own.tiles(second_norm)
        gmlp_line.finish()
        ups.finish()
        for leave in leaves:
            leave.wait()

    def gathered(w):
        return jax.ShapeDtypeStruct((w.shape[0], n_dp, *w.shape[1:]), low)

    return pl.pallas_call(
        kernel,
        out_shape=[
            jax.ShapeDtypeStruct((rows, width), f32),
            jax.ShapeDtypeStruct((rows, width), f32),
            jax.ShapeDtypeStruct((rows, width), low),
            jax.ShapeDtypeStruct((MODS, own_images, width), f32),
            jax.ShapeDtypeStruct((n_dp, images, deep), low),
            jax.ShapeDtypeStruct((n_dp * images, n_dp * images), f32),
            jax.ShapeDtypeStruct((rows + 8, rows), f32),
            jax.ShapeDtypeStruct((n_fsdp, rows + 8, rows), f32),
            jax.ShapeDtypeStruct((which, n_fsdp * rows, head_columns), low),
            jax.ShapeDtypeStruct((n_fsdp * rows, head_columns), low),
            jax.ShapeDtypeStruct(down.shape, low),
            jax.ShapeDtypeStruct((n_fsdp, rows, width), low),
            gathered(qkv),
            gathered(out_w),
            gathered(up),
            jax.ShapeDtypeStruct((n_fsdp, rows, width), low),
        ],
        in_specs=[WHOLE] * 4 + [HBM] * 5,
        out_specs=[WHOLE] * 11 + [HBM] * 5,
        scratch_shapes=[
            pltpu.VMEM((n_dp, images, deep), low),
            pltpu.VMEM((n_dp, MODS, images, wide), f32),
            pltpu.VMEM((n_dp, MODS, images, wide), f32),
            pltpu.VMEM((n_fsdp, 3, own_images, wide), f32),
            pltpu.VMEM((n_fsdp, 3, own_images, wide), f32),
            pltpu.VMEM((n_fsdp, 3, own_images, wide), f32),
            pltpu.VMEM((n_fsdp, 3, own_images, width), f32),
            pltpu.VMEM((n_fsdp, rows, 128), f32),
            pltpu.VMEM((n_fsdp, rows, 128), f32),
            pltpu.VMEM((n_dp * images, n_dp * images), f32),
            pltpu.VMEM((n_dp, n_dp * images, n_dp * images), f32),
            pltpu.VMEM((rows, width), low),
            pltpu.VMEM((n_fsdp, rows, width), low),
            pltpu.VMEM((n_fsdp, rows, width), low),
            pltpu.VMEM((which, n_dp, *qkv.shape[1:]), low),
            pltpu.VMEM((1, n_dp, *out_w.shape[1:]), low),
            *[pltpu.VMEM(w.shape, f32) for w in weights],
            *[pltpu.VMEM(w.shape, low) for w in weights[:3]],
            pltpu.SemaphoreType.DMA((len(weights) + 3,)),
            *line, *line, *line, *grid, *grid, *grid, *direct, *direct, *direct,
            *Direct.scratch(n_fsdp), *direct, *LineCast.scratch(n_fsdp), *scatter_got,
        ],
        compiler_params=parameters(0),
    )(tokens, cotangent, codes, embedding, ada, qkv, out_w, up, down)


def gelu_parts(v):
    root = 0.7978845608028654
    square = v * v
    bent = jnp.tanh(root * (v + 0.044715 * v * square))
    value = 0.5 * v * (1.0 + bent)
    slope = 0.5 * (1.0 + bent) + (0.5 * root) * v * (1.0 - bent * bent) * (1.0 + (3.0 * 0.044715) * square)
    return value, slope


COLUMN_STEP = 256


def feed_forward_kernel(n_dp, n_fsdp, micro, hidden, mid, attn_own, cotangent, codes, mods, grad_mlp, up_g, down):
    low, f32 = jnp.bfloat16, jnp.float32
    rows, width = hidden.shape
    _, weight_rows, columns = down.shape
    tokens = n_fsdp * rows
    pair = 2 * rows
    own_images = mods.shape[1]
    line = LineGather.scratch(n_fsdp)
    grid = GridGather.scratch(n_dp)
    scatter_got = LineScatter.scratch(n_fsdp, rows, width)
    grads_got = GridScatter.scratch(n_dp, 1, weight_rows, columns)
    counts = [len(line), len(grid), len(scatter_got), len(grads_got)]
    tiles = columns // COLUMN_STEP
    row_tiles = weight_rows // COLUMN_STEP

    def kernel(
        hid, mid_ref, attn_ref, cot, cod, mods_ref, down_ref, gmlp_ref, up_ref,
        grad_mid, grad_attn, sums_own, grad_down, squares, mlp_part, grad_up,
        gmlp, up, hidden_g, down_g, upper, activ, grad_upper, part, gdown, grad_h2, stage, stage_up,
        moves, out_sem, up_sem, *rest,
    ):
        sems = split_refs(rest, counts)
        place = Place(n_dp, n_fsdp)
        fetch_up = pltpu.make_async_copy(up_ref, up, moves.at[0])
        fetch_gmlp = pltpu.make_async_copy(gmlp_ref, gmlp, moves.at[1])
        fetch_up.start()
        fetch_gmlp.start()
        enter(place, True, True)
        hidden_line = LineGather(place, hid, hidden_g, sems[0])
        downs = GridGather(place, down_ref, down_g, sems[1])
        hidden_line.start()
        downs.start()
        fetch_up.wait()

        def forward(chip):
            at = span(chip, pair)
            hidden_line.ready(chip)

            def tile(i):
                to = span(i, COLUMN_STEP)
                values = chip_rows(hidden_g, chip)
                total = jnp.zeros((pair, COLUMN_STEP), f32)
                for d in range(n_dp):
                    total = total + matmul(values[:, d * weight_rows : (d + 1) * weight_rows], up[0, d, :, to])
                upper[at, to] = total
                activ[at, to] = gelu_parts(total)[0].astype(low)

            loop(tiles, tile)

        def forward_at(distance):
            def side(i):
                chip = place.p + (1 - 2 * i) * distance

                @pl.when((chip >= 0) & (chip < place.chips))
                def _():
                    forward(chip)

            loop(2 if distance else 1, side)

        for step in range(1, place.chips):
            hidden_line.step(step)
            if step == place.chips // 2:
                downs.step()
            forward_at(step - 1)
        forward_at(place.chips - 1)
        fetch_gmlp.wait()
        downs.finish()
        scatter = LineScatter(place, part, grad_h2, sems[2])
        grads = GridScatter(place, gdown, grad_down, squares, sems[3])

        def backward(chip):
            at = span(chip, pair)

            def tile(i):
                to = span(i, COLUMN_STEP)
                values = chip_rows(gmlp, chip)
                total = jnp.zeros((pair, COLUMN_STEP), f32)
                for d in range(n_dp):
                    total = total + matmul(values[:, d * weight_rows : (d + 1) * weight_rows], down_g[0, d, :, to])
                grad_upper[at, to] = (total * gelu_parts(upper[at, to])[1]).astype(low)

            loop(tiles, tile)
            values = grad_upper[at, :]
            for d in range(n_dp):
                piece = matmul_last(values, up[0, d]).astype(low).reshape(2, rows, weight_rows)
                part[span(chip, 2), :, d * weight_rows : (d + 1) * weight_rows] = piece

        def down_tile(i):
            d, r = i // row_tiles, lax.rem(i, row_tiles)
            left = gmlp[:, :, span(i, COLUMN_STEP)].reshape(tokens, COLUMN_STEP)
            gdown[0, d, span(r, COLUMN_STEP), :] = matmul_first(left, activ[...]).astype(low)

        def then(k):
            @pl.when(k == 0)
            def _():
                loop(n_dp * row_tiles, down_tile)
                grads.start()

        slot = scatter.paced(backward, 2, then)

        def up_copy(i, d, r):
            return pltpu.make_async_copy(
                stage_up.at[lax.rem(i, 2)], grad_up.at[0, d, span(r, COLUMN_STEP)], up_sem.at[lax.rem(i, 2)]
            )

        def up_tile(i):
            d, r = i // row_tiles, lax.rem(i, row_tiles)

            @pl.when(i >= 2)
            def _():
                up_copy(i, 0, 0).wait()

            left = hidden_g[:, :, span(i, COLUMN_STEP)].reshape(tokens, COLUMN_STEP)
            stage_up[lax.rem(i, 2)] = matmul_first(left, grad_upper[...]).astype(low)
            up_copy(i, d, r).start()

        slot = scatter.beside(slot, n_dp * row_tiles, up_tile)
        up_copy(0, 0, 0).wait()
        up_copy(1, 0, 0).wait()
        grads.step()

        def mlp_copy(chip):
            to = lax.rem(chip, 2)
            return pltpu.make_async_copy(stage.at[to], mlp_part.at[span(chip, 2)], out_sem.at[to])

        def mlp_tile(chip):
            @pl.when(chip >= 2)
            def _():
                mlp_copy(chip).wait()

            values = activ[span(chip, pair), :]
            for d in range(n_dp):
                piece = matmul_last(values, down_g[0, d]).astype(low).reshape(2, rows, weight_rows)
                stage[lax.rem(chip, 2), :, :, d * weight_rows : (d + 1) * weight_rows] = piece
            mlp_copy(chip).start()

        slot = scatter.beside(slot, place.chips, mlp_tile)
        mlp_copy(0).wait()
        mlp_copy(1).wait()
        scatter.run_to(slot, scatter.slots)
        grads.step_own()
        scatter.finish()
        own = Rows(place, cod, mods_ref, micro, rows, own_images // micro)
        sums_own[...] = jnp.zeros_like(sums_own)

        def norm_grad(m, at):
            slot, alive = own.slot_live(m, at)
            normed, inv_std = normalize(mid_ref[at, :])
            grad = grad_h2[at, :]
            before = normalize_back(grad * (1.0 + own.pick(4, m, slot)), normed, inv_std)
            total = cot[at, :].astype(f32) * alive + before
            grad_mid[at, :] = total
            grad_attn[at, :] = (total * own.pick(2, m, slot)).astype(low)
            own.add_up(sums_own, 0, m, slot, total * attn_ref[at, :])
            own.add_up(sums_own, 1, m, slot, grad)
            own.add_up(sums_own, 2, m, slot, grad * normed)

        own.tiles(norm_grad)
        grads.finish()
        hidden_line.drain()

    return pl.pallas_call(
        kernel,
        out_shape=[
            jax.ShapeDtypeStruct((rows, width), f32),
            jax.ShapeDtypeStruct((rows, width), low),
            jax.ShapeDtypeStruct((3, own_images, width), f32),
            jax.ShapeDtypeStruct((1, weight_rows, columns), f32),
            jax.ShapeDtypeStruct(TILE, f32),
            jax.ShapeDtypeStruct((n_fsdp, rows, width), low),
            jax.ShapeDtypeStruct((1, n_dp, weight_rows, columns), low),
        ],
        in_specs=[WHOLE] * 6 + [HBM] * 3,
        out_specs=[WHOLE] * 5 + [HBM] * 2,
        scratch_shapes=[
            pltpu.VMEM((n_fsdp, rows, width), low),
            pltpu.VMEM((1, n_dp, weight_rows, columns), low),
            pltpu.VMEM((n_fsdp, rows, width), low),
            pltpu.VMEM((1, n_dp, weight_rows, columns), low),
            pltpu.VMEM((tokens, columns), f32),
            pltpu.VMEM((tokens, columns), low),
            pltpu.VMEM((tokens, columns), low),
            pltpu.VMEM((n_fsdp, rows, width), low),
            pltpu.VMEM((1, n_dp, weight_rows, columns), low),
            pltpu.VMEM((rows, width), f32),
            pltpu.VMEM((2, 2, rows, width), low),
            pltpu.VMEM((2, COLUMN_STEP, columns), low),
            pltpu.SemaphoreType.DMA((2,)),
            pltpu.SemaphoreType.DMA((2,)),
            pltpu.SemaphoreType.DMA((2,)),
            *line, *grid, *scatter_got, *grads_got,
        ],
        compiler_params=parameters(2),
    )(hidden, mid, attn_own, cotangent, codes, mods, down, grad_mlp, up_g)


def attention_grad_kernel(
    n_dp, n_fsdp, micro, grad_attn, tokens_own, mid, grad_mid, cotangent, codes, mods, codes_g, mlp_part, grad_up, qkv_g,
    out_g, qkv_low, attended, hidden_g,
):
    low, f32 = jnp.bfloat16, jnp.float32
    rows, width = grad_attn.shape
    which, _, weight_rows, head_columns = qkv_g.shape
    tokens = n_fsdp * rows
    pair = 2 * rows
    chips = n_fsdp // 2
    own_images = mods.shape[1]
    line = LineGather.scratch(n_fsdp)
    scatter_got = LineScatter.scratch(n_fsdp, rows, width)
    up_shape = (1, *grad_up.shape[2:])
    up_got = GridScatter.scratch(n_dp, *up_shape)
    qkv_got = GridScatter.scratch(n_dp, which, weight_rows, head_columns)
    out_got = GridScatter.scratch(n_dp, 1, weight_rows, head_columns)
    counts = [len(line), len(scatter_got), len(scatter_got), len(up_got), len(qkv_got), len(out_got)]
    row_tiles = weight_rows // COLUMN_STEP

    def kernel(
        ga, tok, mid_ref, gmid, cot, cod, mods_ref, cod_g, mlp_ref, gup_ref, qkv_wr, out_wr, qkv_lr, att_r, hid_r,
        block_out, input_grad, sums_own, grad_up_own, grad_qkv_own, grad_out_own, squares,
        ga_g, gqkv, gqkv_w, gout_w, mlp_own, grad_h1, tile_up, tile_qkv, tile_out,
        mine, gup, qkv_w, out_w, qkv_ref, att, hid_g, moves, mine_sem, *rest,
    ):
        sems = split_refs(rest, counts)
        place = Place(n_dp, n_fsdp)
        fetches = [
            pltpu.make_async_copy(ref, to, moves.at[i])
            for i, (ref, to) in enumerate(
                ((gup_ref, gup), (att_r, att), (out_wr, out_w), (qkv_lr, qkv_ref), (qkv_wr, qkv_w), (hid_r, hid_g))
            )
        ]
        terms = [
            pltpu.make_async_copy(mlp_ref.at[chip * 2 + place.c], mine.at[chip], mine_sem.at[chip])
            for chip in range(chips)
        ]
        fetches[0].start()
        for term in terms:
            term.start()
        for fetch in fetches[1:]:
            fetch.start()
        enter(place, True, True)
        ga_line = LineGather(place, ga, ga_g, sems[0])
        mlp_scatter = LineScatter(place, mlp_ref, mlp_own, sems[1], mine, LineScatter.pieces)
        ups = GridScatter(place, gup, grad_up_own, tile_up, sems[3])
        ga_line.start()
        fetches[0].wait()
        ups.start()
        mlp_scatter.start()
        for term in terms:
            term.wait()
        travel = LineScatter.pieces * (chips - 1)
        at_slot = 0

        def backward(chip):
            at = span(chip, pair)
            ga_line.ready(chip)
            values = chip_rows(ga_g, chip)
            grad_heads = matmul(values, out_w[0].reshape(width, head_columns)).astype(low)
            allowed = pair_mask(cod_g, chip, rows)
            for h in range(head_columns // HEAD):
                head = slice(h * HEAD, (h + 1) * HEAD)
                query, key, value = [qkv_ref[w, at, head] for w in range(which)]
                grad_head = grad_heads[:, head]
                probs = attention_probs(query, key, allowed)
                grad_p = matmul_last(grad_head, value)
                delta = jnp.sum(probs * grad_p, axis=-1, keepdims=True)
                grad_scores = (probs * (grad_p - delta)).astype(low)
                scale = HEAD ** (-0.5)
                gqkv[0, at, head] = (matmul(grad_scores, key) * scale).astype(low)
                gqkv[1, at, head] = (matmul_first(grad_scores, query) * scale).astype(low)
                gqkv[2, at, head] = matmul_first(probs.astype(low), grad_head).astype(low)

        def backward_at(distance):
            def side(i):
                chip = place.p + (1 - 2 * i) * distance

                @pl.when((chip >= 0) & (chip < place.chips))
                def _():
                    backward(chip)

            loop(2 if distance else 1, side)

        for step in range(1, chips):
            ga_line.step(step)
            if step < chips - 1:
                to_slot = travel * step // (chips - 1)
                mlp_scatter.run(at_slot, to_slot)
                at_slot = to_slot
            if step == 1:
                for fetch in fetches[1:]:
                    fetch.wait()
            backward_at(step - 1)
            if step == chips // 2:
                ups.step()
        backward_at(chips - 1)
        ga_line.drain()
        scatter = LineScatter(place, ga_g, grad_h1, sems[2])
        qkvs = GridScatter(place, gqkv_w, grad_qkv_own, tile_qkv, sems[4])
        outs = GridScatter(place, gout_w, grad_out_own, tile_out, sems[5])

        def out_tile(i):
            d, r = i // row_tiles, lax.rem(i, row_tiles)
            left = ga_g[:, :, span(i, COLUMN_STEP)].reshape(tokens, COLUMN_STEP)
            gout_w[0, d, span(r, COLUMN_STEP), :] = matmul_first(left, att[...]).astype(low)

        loop(n_dp * row_tiles, out_tile)
        outs.start()

        def compute(chip):
            at = span(chip, pair)
            for d in range(n_dp):
                total = matmul_last(gqkv[0, at, :], qkv_w[0, d])
                for w in range(1, which):
                    total = total + matmul_last(gqkv[w, at, :], qkv_w[w, d])
                piece = total.astype(low).reshape(2, rows, weight_rows)
                ga_g[span(chip, 2), :, d * weight_rows : (d + 1) * weight_rows] = piece

        def grad_tile(i):
            d, r = i // row_tiles, lax.rem(i, row_tiles)
            left = hid_g[:, :, span(i, COLUMN_STEP)].reshape(tokens, COLUMN_STEP)
            for w in range(which):
                gqkv_w[w, d, span(r, COLUMN_STEP), :] = matmul_first(left, gqkv[w]).astype(low)

        def then(k):
            @pl.when(k == 0)
            def _():
                loop(n_dp * row_tiles, grad_tile)
                qkvs.start()

            @pl.when(k == 1)
            def _():
                mlp_scatter.run(at_slot, travel)

        slot = scatter.paced(compute, 3, then)
        outs.step()
        slot = scatter.run_to(slot, scatter.slots // 2)
        qkvs.step()
        slot = scatter.run_to(slot, scatter.slots * 5 // 8)
        ups.step_own()
        mlp_scatter.finish()
        ups.finish()
        own = Rows(place, cod, mods_ref, micro, rows, own_images // micro)
        sums_own[...] = jnp.zeros_like(sums_own)

        def branch_out(m, at):
            slot_of, alive = own.slot_live(m, at)
            branch = mlp_own[at, :]
            block_out[at, :] = (mid_ref[at, :] + own.pick(5, m, slot_of) * branch).astype(low)
            own.add_up(sums_own, 2, m, slot_of, cot[at, :].astype(f32) * alive * branch)

        own.tiles(branch_out)
        scatter.run_to(slot, scatter.slots)
        outs.step_own()
        qkvs.step_own()
        scatter.finish()

        def norm_grad(m, at):
            slot_of, _ = own.slot_live(m, at)
            normed, inv_std = normalize(tok[at, :].astype(f32))
            grad = grad_h1[at, :]
            before = normalize_back(grad * (1.0 + own.pick(1, m, slot_of)), normed, inv_std)
            input_grad[at, :] = gmid[at, :] + before
            own.add_up(sums_own, 0, m, slot_of, grad)
            own.add_up(sums_own, 1, m, slot_of, grad * normed)

        own.tiles(norm_grad)
        outs.finish()
        qkvs.finish()
        squares[...] = tile_up[...] + tile_qkv[...] + tile_out[...]

    return pl.pallas_call(
        kernel,
        out_shape=[
            jax.ShapeDtypeStruct((rows, width), low),
            jax.ShapeDtypeStruct((rows, width), f32),
            jax.ShapeDtypeStruct((3, own_images, width), f32),
            jax.ShapeDtypeStruct(up_shape, f32),
            jax.ShapeDtypeStruct((which, weight_rows, head_columns), f32),
            jax.ShapeDtypeStruct((1, weight_rows, head_columns), f32),
            jax.ShapeDtypeStruct(TILE, f32),
        ],
        in_specs=[WHOLE] * 8 + [HBM] * 7,
        out_specs=[WHOLE] * 7,
        scratch_shapes=[
            pltpu.VMEM((n_fsdp, rows, width), low),
            pltpu.VMEM((which, tokens, head_columns), low),
            pltpu.VMEM((which, n_dp, weight_rows, head_columns), low),
            pltpu.VMEM((1, n_dp, weight_rows, head_columns), low),
            pltpu.VMEM((rows, width), f32),
            pltpu.VMEM((rows, width), f32),
            pltpu.VMEM(TILE, f32),
            pltpu.VMEM(TILE, f32),
            pltpu.VMEM(TILE, f32),
            pltpu.VMEM((chips, rows, width), low),
            *[pltpu.VMEM(a.shape, low) for a in (grad_up, qkv_g, out_g, qkv_low, attended, hidden_g)],
            pltpu.SemaphoreType.DMA((6,)),
            pltpu.SemaphoreType.DMA((chips,)),
            *line, *scatter_got, *scatter_got, *up_got, *qkv_got, *out_got,
        ],
        compiler_params=parameters(3),
    )(
        grad_attn, tokens_own, mid, grad_mid, cotangent, codes, mods, codes_g, mlp_part, grad_up, qkv_g, out_g, qkv_low,
        attended, hidden_g,
    )


def norm_kernel(n_dp, n_fsdp, micro, sums_first, sums_second, condition, products, squares, states):
    own_images, width = sums_first.shape[1:]
    wide = width // n_fsdp
    images, deep = condition.shape[1:]
    lanes = wide // 128
    slots_here = own_images // micro
    source = [(0, 0), (0, 1), (1, 0), (1, 1), (1, 2), (0, 2)]

    def kernel(sums_a, sums_b, cond, product, squares_ref, *refs):
        states_in, refs = refs[: len(states)], refs[len(states) :]
        grad, norm, refs = refs[0], refs[1], refs[2:]
        states_out, refs = refs[: len(states)], refs[len(states) :]
        mail, boxes, mine, all_mods, columns, tile, tiles, moves, *sems = refs
        place = Place(n_dp, n_fsdp)
        fetches = [
            pltpu.make_async_copy(src, dst, moves.at[i]) for i, (src, dst) in enumerate(zip(states_in, states_out))
        ]
        for fetch in fetches:
            fetch.start()
        barrier = pltpu.get_barrier_semaphore()
        for i in range(1, n_dp):
            pl.semaphore_signal(
                barrier, inc=1, device_id=place.at_dp((place.dp + i) % n_dp), device_id_type=MESH
            )
        for i in range(1, n_fsdp):
            pl.semaphore_signal(
                barrier, inc=1, device_id=(place.dp, (place.f + i) % n_fsdp), device_id_type=MESH
            )
        for j, (which, row) in enumerate(source):
            values = (sums_a, sums_b)[which][row].astype(jnp.bfloat16).astype(jnp.float32)
            for f in range(n_fsdp):
                for g in range(lanes):
                    at = (j * lanes + g) * own_images
                    mail[f, at : at + own_images, :] = values[:, f * wide + g * 128 : f * wide + (g + 1) * 128]
        pl.semaphore_wait(barrier, n_dp + n_fsdp - 2)
        inner = Direct(place, mail, boxes, sems[0:2], "fsdp", block=lambda ref, d: ref.at[d])
        inner.start()
        boxes[place.f] = mail[place.f]
        inner.finish()
        for j in range(MODS):
            for g in range(lanes):
                pieces = []
                for m in range(micro):
                    at = (j * lanes + g) * own_images + m * slots_here
                    pieces += [boxes[f, at : at + slots_here, :] for f in range(n_fsdp)]
                mine[j, :, g * 128 : (g + 1) * 128] = jnp.concatenate(pieces, axis=0).astype(jnp.bfloat16)
        outer = Direct(place, mine, all_mods, sems[2:4])
        beside = Direct(place, squares_ref, columns, sems[4:6])
        outer.start()
        beside.start()
        all_mods[place.dp] = mine[...]
        columns[place.dp] = squares_ref[...]
        high = product[...].astype(jnp.bfloat16)
        rest = (product[...] - high.astype(jnp.float32)).astype(jnp.bfloat16)
        outer.finish()
        beside.finish()
        total = columns[0]
        for d in range(1, n_dp):
            total = total + columns[d]
        for j in range(MODS):
            values = all_mods[:, j].reshape(n_dp * images, wide)
            both = (matmul(high, values) + matmul(rest, values)) * values.astype(jnp.float32)
            for at in range(0, n_dp * images, ROW_STEP):
                for lane in range(0, wide, 128):
                    total = total + both[at : at + ROW_STEP, lane : lane + 128]
        tile[...] = total
        first = Direct(place, tile, tiles, sems[6:8], "fsdp")
        first.start()
        tiles[place.f] = tile[...]
        every = cond[...].reshape(n_dp * images, deep)
        for j in range(MODS):
            grad[j] = matmul_first(every, all_mods[:, j].reshape(n_dp * images, wide))
        first.finish()
        total = tiles[0]
        for f in range(1, n_fsdp):
            total = total + tiles[f]
        norm[0, 0] = jnp.sqrt(jnp.sum(total))
        for fetch in fetches:
            fetch.wait()

    return pl.pallas_call(
        kernel,
        out_shape=[
            jax.ShapeDtypeStruct((MODS, deep, wide), jnp.float32),
            jax.ShapeDtypeStruct((1, 1), jnp.float32),
            *[pltpu.VMEM(state.shape, state.dtype) for state in states],
        ],
        in_specs=[WHOLE] * 5 + [HBM] * len(states),
        out_specs=[WHOLE, pl.BlockSpec(memory_space=pltpu.SMEM)] + [HBM] * len(states),
        scratch_shapes=[
            pltpu.VMEM((n_fsdp, MODS * lanes * own_images, 128), jnp.float32),
            pltpu.VMEM((n_fsdp, MODS * lanes * own_images, 128), jnp.float32),
            pltpu.VMEM((MODS, images, wide), jnp.bfloat16),
            pltpu.VMEM((n_dp, MODS, images, wide), jnp.bfloat16),
            pltpu.VMEM((n_dp, *TILE), jnp.float32),
            pltpu.VMEM(TILE, jnp.float32),
            pltpu.VMEM((n_fsdp, *TILE), jnp.float32),
            pltpu.SemaphoreType.DMA((len(states),)),
            *Direct.scratch(n_fsdp), *Direct.scratch(n_dp), *Direct.scratch(n_dp), *Direct.scratch(n_fsdp),
        ],
        compiler_params=parameters(1, NORM_LIMIT),
    )(sums_first, sums_second, condition, products, squares, *states)


def adam_kernel(factor, grad, master, first, second):
    which, rows, columns = master.shape
    step = min(rows, max(64, 131072 // columns))
    block = pl.BlockSpec((1, step, columns), lambda w, r: (w, r, 0))
    root = (1.0 - BETA_TWO**STEP) ** 0.5
    rate = LEARN_RATE * root / (1.0 - BETA_ONE**STEP)

    def kernel(factor_ref, grad_ref, master_ref, first_ref, second_ref, new_ref, copy_ref, moment_ref, square_ref):
        scale = factor_ref[0, 0]
        grad = grad_ref[...]
        moment = BETA_ONE * first_ref[...] + ((1.0 - BETA_ONE) * scale) * grad
        square = BETA_TWO * second_ref[...] + ((1.0 - BETA_TWO) * scale * scale) * (grad * grad)
        moment_ref[...] = moment
        square_ref[...] = square
        below = jnp.sqrt(square) + ADAM_EPS * root
        new = (1.0 - LEARN_RATE * WEIGHT_DECAY) * master_ref[...] - (rate * moment) / below
        new_ref[...] = new
        copy_ref[...] = new.astype(jnp.bfloat16)

    shape = jax.ShapeDtypeStruct(master.shape, jnp.float32)
    return pl.pallas_call(
        kernel,
        grid=(which, rows // step),
        out_shape=[shape, jax.ShapeDtypeStruct(master.shape, jnp.bfloat16), shape, shape],
        in_specs=[pl.BlockSpec(memory_space=pltpu.SMEM)] + [block] * 4,
        out_specs=[block] * 4,
        compiler_params=pltpu.CompilerParams(vmem_limit_bytes=SMALL_LIMIT),
    )(factor, grad, master, first, second)


def normalize(values):
    average = jnp.mean(values, axis=-1, keepdims=True)
    centred = values - average
    inv_std = lax.rsqrt(jnp.mean(centred * centred, axis=-1, keepdims=True) + NORM_EPS)
    return (centred * inv_std, inv_std)


def normalize_back(grad, normed, inv_std):
    return inv_std * (
        grad
        - jnp.mean(grad, axis=-1, keepdims=True)
        - normed * jnp.mean(grad * normed, axis=-1, keepdims=True)
    )


def body(n_dp, n_fsdp, *arguments):
    tokens, embedding, image_slot, token_mask, cotangent = arguments[:5]
    weights = [w if w.ndim == 3 else w[:, None] for w in arguments[5:]]
    weights = [w.transpose(1, 0, 2) for w in weights]
    masters, firsts, seconds = weights[:5], weights[5:10], weights[10:]
    qkv_w, out_w, up_w, down_w, ada_w = masters
    micro, tok_rows, width = tokens.shape
    own_rows = micro * tok_rows
    image_count = embedding.shape[1] // n_fsdp
    images = micro * n_fsdp * image_count
    images_of = jnp.arange(micro, dtype=jnp.int32)[:, None] * image_count
    codes = jnp.stack([(images_of + image_slot).reshape(own_rows), token_mask.reshape(own_rows)])
    codes = jnp.pad(codes.astype(jnp.float32), ((0, 6), (0, 0)))
    own_tokens = tokens.reshape(own_rows, width)
    own_cot = cotangent.reshape(own_rows, width)

    (
        attn_own, mid, hidden2, mods, cond_all, products, codes, codes_g, qkv_low, attended, down_low,
        hidden1_g, qkv_g, out_g, up_g, grad_mlp_g,
    ) = attention_kernel(
        n_dp, n_fsdp, micro, own_tokens, own_cot, codes, embedding.reshape(images, -1), ada_w, qkv_w, out_w, up_w, down_w
    )
    grad_mid, grad_attn, sums_second, grad_down, squares_down, mlp_part, grad_up = feed_forward_kernel(
        n_dp, n_fsdp, micro, hidden2, mid, attn_own, own_cot, codes, mods, grad_mlp_g, up_g, down_low
    )
    block_out, input_grad, sums_first, grad_up, grad_qkv_w, grad_out, squares = attention_grad_kernel(
        n_dp, n_fsdp, micro, grad_attn, own_tokens, mid, grad_mid, own_cot, codes, mods, codes_g, mlp_part, grad_up,
        qkv_g, out_g, qkv_low, attended, hidden1_g,
    )
    block_out = block_out.reshape(tokens.shape)
    input_grad = input_grad.reshape(tokens.shape)
    grad_ada, grad_norm, *states = norm_kernel(
        n_dp, n_fsdp, micro, sums_first, sums_second, cond_all, products, squares_down + squares,
        (*masters, *firsts, *seconds),
    )
    masters, firsts, seconds = states[:5], states[5:10], states[10:]

    factor = jnp.minimum(1.0, CLIP_AT / grad_norm)
    results = []
    grads = (grad_qkv_w, grad_out, grad_up, grad_down, grad_ada)
    for given, grad, master, first, second in zip(arguments[5:], grads, masters, firsts, seconds):
        for updated in adam_kernel(factor, grad, master, first, second):
            results.append(updated.transpose(1, 0, 2).reshape(given.shape))
    return (block_out, input_grad, *results, grad_norm[0, 0])


def solution(mesh):
    n_dp, n_fsdp = mesh.shape["dp"], mesh.shape["fsdp"]
    rows = P(None, ("dp", "fsdp"), None)
    slots = P(None, ("dp", "fsdp"))
    thick = P("dp", None, "fsdp")
    flat = P("dp", "fsdp")
    weights = (thick, flat, flat, flat, thick)
    updated = tuple(spec for spec in weights for _ in range(4))
    return jax.shard_map(
        functools.partial(body, n_dp, n_fsdp),
        mesh=mesh,
        in_specs=(rows, P(None, "dp", None), slots, slots, rows, *weights, *weights, *weights),
        out_specs=(rows, rows, *updated, P()),
        check_vma=False,
    )
```

```python
import functools

import jax
import jax.numpy as jnp
from jax import lax
from jax.experimental import pallas as pl
from jax.experimental.pallas import tpu as pltpu
from jax.sharding import PartitionSpec as P

HEAD = 128
STEP = 10
MODS = 6
FIRST_KINDS = (0, 1, 5)
OTHER_KINDS = (2, 3, 4)

NORM_EPS = 1e-06
CLIP_AT = 1.0
BETA_ONE = 0.9
BETA_TWO = 0.999
LEARN_RATE = 0.05
WEIGHT_DECAY = 0.1
ADAM_EPS = 1e-08

MESH = pl.DeviceIdType.MESH
VMEM_LIMIT = 62 * 1024 * 1024
SMALL_LIMIT = 16 * 1024 * 1024
NORM_LIMIT = 27 * 1024 * 1024
ROW_STEP = 16


class Place:
    def __init__(self, n_dp, n_fsdp):
        self.n_dp, self.n_fsdp = n_dp, n_fsdp
        self.chips = n_fsdp // 2
        self.grid_a = 2
        self.grid_b = n_dp // 2
        self.dp = lax.axis_index("dp")
        self.f = lax.axis_index("fsdp")
        self.p = self.f // 2
        self.c = self.f % 2
        self.a = self.dp // self.grid_b
        self.b = self.dp % self.grid_b

    def at_chip(self, chip):
        return (self.dp, chip * 2 + self.c)

    def sibling(self):
        return (self.dp, self.p * 2 + 1 - self.c)

    def at_dp(self, dp):
        return (dp, self.f)

    def b_peer(self, i):
        return (self.b + i) % self.grid_b

    def a_peer(self, i):
        return (self.a + i) % self.grid_a


def announce(place, line=False, grid=False, group=False):
    barrier = pltpu.get_barrier_semaphore()
    devices = []
    if group:
        for i in range(1, place.n_fsdp):
            devices.append((place.dp, (place.f + i) % place.n_fsdp))
    elif line:
        devices.append(place.at_chip((place.p + 1) % place.chips))
        devices.append(place.at_chip((place.p + place.chips - 1) % place.chips))
        devices.append(place.sibling())
    if grid:
        for i in range(1, place.n_dp):
            devices.append(place.at_dp((place.dp + i) % place.n_dp))
    for device in devices:
        pl.semaphore_signal(barrier, inc=1, device_id=device, device_id_type=MESH)
    return len(devices)


def enter(place, line=False, grid=False, group=False):
    count = announce(place, line, grid, group)
    pl.semaphore_wait(pltpu.get_barrier_semaphore(), count)


def remote(src, dst, send, recv, device):
    return pltpu.make_async_remote_copy(
        src_ref=src, dst_ref=dst, send_sem=send, recv_sem=recv, device_id=device, device_id_type=MESH
    )


class LineGather:
    @staticmethod
    def scratch(n_fsdp):
        chips = n_fsdp // 2
        return [
            pltpu.SemaphoreType.DMA((2, chips)),
            pltpu.SemaphoreType.DMA((2, chips)),
            pltpu.SemaphoreType.DMA((chips,)),
            pltpu.SemaphoreType.DMA((chips,)),
            pltpu.SemaphoreType.DMA,
        ]

    def __init__(self, place, src, out, sems, block=None):
        self.place, self.src, self.out = place, src, out
        self.send, self.recv, self.csend, self.crecv, self.local = sems
        self.of = block or (lambda ref, d: ref.at[d])

    def _block(self, chip):
        return self.of(self.out, chip * 2 + self.place.c)

    def _hop(self, way, step, first):
        pc = self.place
        chip = pc.p - step if way == 0 else pc.p + step
        target = pc.p + 1 if way == 0 else pc.p - 1
        src = self.src if first else self._block(chip)
        return remote(src, self._block(chip), self.send.at[way, step], self.recv.at[way, step], pc.at_chip(target))

    def _side(self, chip, first=False):
        src = self.src if first else self._block(chip)
        return remote(src, self._block(chip), self.csend.at[chip], self.crecv.at[chip], self.place.sibling())

    def _sends(self, way, step):
        pc = self.place
        if way == 0:
            return (pc.p < pc.chips - 1) & (pc.p >= step)
        return (pc.p > 0) & (pc.p + step <= pc.chips - 1)

    def start_way(self, way):
        @pl.when(self._sends(way, 0))
        def _():
            self._hop(way, 0, True).start()

    def start_here(self):
        pc = self.place
        self._side(pc.p, True).start()
        pltpu.make_async_copy(self.src, self._block(pc.p), self.local).start()

    def start(self):
        self.start_way(0)
        self.start_way(1)
        self.start_here()

    def step(self, step):
        pc = self.place
        for way in range(2):
            chip = pc.p - step if way == 0 else pc.p + step
            here = (chip >= 0) if way == 0 else (chip <= pc.chips - 1)

            @pl.when(here)
            def _():
                remote(
                    self._block(chip), self._block(chip), self.send.at[way, step - 1], self.recv.at[way, step - 1],
                    pc.sibling(),
                ).wait_recv()
                if step < pc.chips - 1:
                    @pl.when(self._sends(way, step))
                    def _():
                        self._hop(way, step, False).start()
                self._side(chip).start()

    def ready(self, chip):
        pc = self.place
        other = self.of(self.out, chip * 2 + 1 - pc.c)
        remote(other, other, self.csend.at[chip], self.crecv.at[chip], pc.sibling()).wait_recv()

        @pl.when(chip == pc.p)
        def _():
            pltpu.make_async_copy(self.src, self._block(pc.p), self.local).wait()

    def drain(self):
        pc = self.place
        for chip in range(pc.chips):
            self._side(chip).wait_send()
        for way in range(2):
            for step in range(pc.chips - 1):
                @pl.when(self._sends(way, step))
                def _():
                    self._hop(way, step, False).wait_send()

    def finish(self):
        for chip in range(self.place.chips):
            self.ready(chip)
        self.drain()


class LineCast:
    @staticmethod
    def scratch(n_fsdp):
        return [pltpu.SemaphoreType.DMA((n_fsdp // 2,)) for _ in range(4)] + [pltpu.SemaphoreType.DMA]

    def __init__(self, place, src, out, sems, block):
        self.place, self.src, self.out, self.of = place, src, out, block
        self.send, self.recv, self.csend, self.crecv, self.local = sems

    def _copy(self, i, coming=False):
        pc = self.place
        chip = (pc.p + pc.chips - i) % pc.chips if coming else pc.p
        return remote(
            self.src, self.of(self.out, chip * 2 + pc.c), self.send.at[i], self.recv.at[i],
            pc.at_chip((pc.p + i) % pc.chips),
        )

    def _side(self, i, coming=False):
        pc = self.place
        chip = (pc.p + pc.chips - i) % pc.chips
        block = self.of(self.out, chip * 2 + (1 - pc.c if coming else pc.c))
        return remote(block if i else self.src, block, self.csend.at[i], self.crecv.at[i], pc.sibling())

    def start(self):
        pc = self.place
        for i in range(1, pc.chips):
            self._copy(i).start()
        self._side(0).start()
        pltpu.make_async_copy(self.src, self.of(self.out, pc.f), self.local).start()

    def step(self):
        for i in range(1, self.place.chips):
            self._copy(i, True).wait_recv()
            self._side(i).start()

    def finish(self):
        pc = self.place
        pltpu.make_async_copy(self.src, self.of(self.out, pc.f), self.local).wait()
        for i in range(pc.chips):
            self._side(i, True).wait_recv()
            self._side(i).wait_send()
        for i in range(1, pc.chips):
            self._copy(i).wait_send()


def row_loop(rows, body, first=0):
    def run(i, carry):
        body(pl.ds(pl.multiple_of(first + i * ROW_STEP, ROW_STEP), ROW_STEP))
        return carry

    lax.fori_loop(0, rows // ROW_STEP, run, 0)


class LineScatter:
    pieces = 4

    @classmethod
    def scratch(cls, n_fsdp, rows, width):
        chips = n_fsdp // 2
        return [
            pltpu.VMEM((chips, rows, width), jnp.bfloat16),
            pltpu.VMEM((chips + 1, rows, width), jnp.bfloat16),
            pltpu.SemaphoreType.DMA((chips,)),
            pltpu.SemaphoreType.DMA((chips,)),
            pltpu.SemaphoreType.DMA((2, chips, cls.pieces)),
            pltpu.SemaphoreType.DMA((2, chips, cls.pieces)),
        ]

    def __init__(self, place, part, out, scratch, mine=None, lag=2):
        self.place, self.part, self.out, self.mine = place, part, out, mine
        self.side, self.inbox, self.csend, self.crecv, self.send, self.recv = scratch
        self.rows = out.shape[0]
        self.piece = self.rows // self.pieces
        self.lag = lag
        self.slots = (place.chips - 1) * self.lag + place.chips * self.pieces

    def _side(self, chip):
        pc = self.place
        return remote(
            self.part.at[chip * 2 + 1 - pc.c], self.side.at[chip], self.csend.at[chip], self.crecv.at[chip], pc.sibling()
        )

    def _hop(self, way, chip, s):
        pc = self.place
        target = pc.p + 1 if way == 0 else pc.p - 1
        rows = pl.ds(pl.multiple_of(s * self.piece, self.piece), self.piece)
        return remote(
            self.side.at[chip, rows], self.inbox.at[chip + 1 - way, rows], self.send.at[way, chip, s],
            self.recv.at[way, chip, s], pc.at_chip(target),
        )

    def start(self):
        def one(k, carry):
            self.offer(self.order(k))
            return carry

        lax.fori_loop(0, self.place.chips, one, 0)

    def offer(self, chip):
        self._side(chip).start()

    def order(self, k):
        pc = self.place
        chips = pc.chips
        after, before = chips - 1 - pc.p, pc.p
        short = jnp.minimum(after, before)
        lone = jnp.maximum(after, before) - short
        rest = jnp.maximum(k - lone, 0)
        near = short - rest // 2
        pair = jnp.where(lax.rem(rest, 2) == 0, pc.p + near, pc.p - near)
        return jnp.where(k < lone, jnp.where(after > before, chips - 1 - k, k), pair)

    def first_slot(self, k):
        pc = self.place
        chips = pc.chips
        chip = self.order(k)
        after = pc.p * self.lag + (chips - 1 - chip) * self.pieces
        before = (chips - 1 - pc.p) * self.lag + chip * self.pieces
        slot = jnp.where(chip > pc.p, after, before)
        return jnp.where((k >= chips - 1) | (chip == pc.p), self.slots, slot)

    def paced(self, compute, pace, then):
        def one(k, slot):
            chip = self.order(k)
            compute(chip)
            self.offer(chip)
            until = jnp.minimum(self.first_slot(k + 1), self.first_slot(k + 2))
            until = jnp.maximum(jnp.minimum(until, (k + 1) * pace), slot)
            self.run(slot, until)
            then(k)
            return until

        return lax.fori_loop(0, self.place.chips, one, jnp.int32(0))

    def beside(self, slot, count, work, every=1):
        def one(i, carry):
            work(i)

            @pl.when(lax.rem(i, every) == every - 1)
            def _():
                self.step(slot + i // every)

            return carry

        lax.fori_loop(0, count, one, 0)
        return slot + count // every

    def run_to(self, slot, end):
        end = jnp.maximum(slot, end)
        self.run(slot, end)
        return end

    def _add(self, chip, s, inboxes, store):
        pc = self.place

        def add(rows):
            if self.mine is None:
                total = self.part[chip * 2 + pc.c, rows, :].astype(jnp.float32)
            else:
                total = self.mine[chip, rows, :].astype(jnp.float32)
            total = total + self.side[chip, rows, :].astype(jnp.float32)
            for way in inboxes:
                total = total + self.inbox[chip + 1 - way, rows, :].astype(jnp.float32)
            store(rows, total)

        row_loop(self.piece, add, s * self.piece)

    def _travel(self, way, t):
        pc = self.place
        chips = pc.chips
        i = t - (pc.p if way == 0 else chips - 1 - pc.p) * self.lag
        k = jnp.clip(i // self.pieces, 0, chips - 1)
        s = lax.rem(jnp.maximum(i, 0), self.pieces)
        chip = chips - 1 - k if way == 0 else k
        going = (i >= 0) & (i < chips * self.pieces) & ((chip > pc.p) if way == 0 else (chip < pc.p))
        first = (pc.p == 0) if way == 0 else (pc.p == chips - 1)

        def store(rows, total):
            self.side[chip, rows, :] = total.astype(jnp.bfloat16)

        @pl.when(going)
        def _():
            @pl.when(s == 0)
            def _():
                self._side(chip).wait_recv()

            @pl.when(first)
            def _():
                self._add(chip, s, (), store)

            @pl.when(jnp.logical_not(first))
            def _():
                self._hop(way, chip, s).wait_recv()
                self._add(chip, s, (way,), store)

            self._hop(way, chip, s).start()

    def step(self, t):
        self._travel(0, t)
        self._travel(1, t)

    def run(self, begin, end):
        def one(t, carry):
            self.step(t)
            return carry

        lax.fori_loop(begin, end, one, 0)

    def finish(self):
        pc = self.place
        chips = pc.chips
        self._side(pc.p).wait_recv()

        def store(rows, total):
            self.out[rows, :] = total

        def piece(s, carry):
            @pl.when(pc.p == 0)
            def _():
                self._hop(1, pc.p, s).wait_recv()
                self._add(pc.p, s, (1,), store)

            @pl.when(pc.p == chips - 1)
            def _():
                self._hop(0, pc.p, s).wait_recv()
                self._add(pc.p, s, (0,), store)

            @pl.when((pc.p > 0) & (pc.p < chips - 1))
            def _():
                self._hop(0, pc.p, s).wait_recv()
                self._hop(1, pc.p, s).wait_recv()
                self._add(pc.p, s, (0, 1), store)

            return carry

        lax.fori_loop(0, self.pieces, piece, 0)
        for chip in range(chips):
            self._side(chip).wait_send()

            def sent(s, carry):
                @pl.when(chip > pc.p)
                def _():
                    self._hop(0, chip, s).wait_send()

                @pl.when(chip < pc.p)
                def _():
                    self._hop(1, chip, s).wait_send()

                return carry

            lax.fori_loop(0, self.pieces, sent, 0)


class GridGather:
    @staticmethod
    def scratch(n_dp):
        na, nb = 2, n_dp // 2
        return [
            pltpu.SemaphoreType.DMA((2, max(nb - 1, 1))),
            pltpu.SemaphoreType.DMA((2, max(nb - 1, 1))),
            pltpu.SemaphoreType.DMA((2, na - 1)),
            pltpu.SemaphoreType.DMA((2, na - 1)),
            pltpu.SemaphoreType.DMA((2, max(nb - 1, 1), na - 1)),
            pltpu.SemaphoreType.DMA((2, max(nb - 1, 1), na - 1)),
            pltpu.SemaphoreType.DMA,
        ]

    def __init__(self, place, src, out, sems):
        self.place, self.src, self.out = place, src, out
        self.bsend, self.brecv, self.asend, self.arecv, self.fsend, self.frecv, self.local = sems
        self.half = src.shape[1] // 2

    def _own(self, h):
        return self.src.at[:, pl.ds(h * self.half, self.half)]

    def _block(self, a, b, h):
        return self.out.at[:, a * self.place.grid_b + b, pl.ds(h * self.half, self.half)]

    def _b_copy(self, i, h, coming):
        pc = self.place
        b = pc.b_peer(pc.grid_b - i) if coming else pc.b
        return remote(
            self._own(h), self._block(pc.a, b, h), self.bsend.at[h, i - 1], self.brecv.at[h, i - 1],
            pc.at_dp(pc.a * pc.grid_b + pc.b_peer(i)),
        )

    def _a_copy(self, i, h, coming):
        pc = self.place
        a = pc.a_peer(pc.grid_a - i) if coming else pc.a
        return remote(
            self._own(h), self._block(a, pc.b, h), self.asend.at[h, i - 1], self.arecv.at[h, i - 1],
            pc.at_dp(pc.a_peer(i) * pc.grid_b + pc.b),
        )

    def _on(self, h, ib, ia, coming):
        pc = self.place
        if h == 0:
            b = pc.b_peer(pc.grid_b - ib)
            a = pc.a_peer(pc.grid_a - ia) if coming else pc.a
            target = pc.at_dp(pc.a_peer(ia) * pc.grid_b + pc.b)
        else:
            a = pc.a_peer(pc.grid_a - ia)
            b = pc.b_peer(pc.grid_b - ib) if coming else pc.b
            target = pc.at_dp(pc.a * pc.grid_b + pc.b_peer(ib))
        block = self._block(a, b, h)
        return remote(block, block, self.fsend.at[h, ib - 1, ia - 1], self.frecv.at[h, ib - 1, ia - 1], target)

    def start(self):
        pc = self.place
        for h in range(2):
            for i in range(1, pc.grid_b):
                self._b_copy(i, h, False).start()
            for i in range(1, pc.grid_a):
                self._a_copy(i, 1 - h, False).start()
        pltpu.make_async_copy(self.src, self.out.at[:, pc.dp], self.local).start()

    def step(self):
        pc = self.place
        for ib in range(1, pc.grid_b):
            self._b_copy(ib, 0, True).wait_recv()
            for ia in range(1, pc.grid_a):
                self._on(0, ib, ia, False).start()
        for ia in range(1, pc.grid_a):
            self._a_copy(ia, 1, True).wait_recv()
            for ib in range(1, pc.grid_b):
                self._on(1, ib, ia, False).start()

    def finish(self):
        pc = self.place
        pltpu.make_async_copy(self.src, self.out.at[:, pc.dp], self.local).wait()
        for ib in range(1, pc.grid_b):
            self._b_copy(ib, 1, True).wait_recv()
        for ia in range(1, pc.grid_a):
            self._a_copy(ia, 0, True).wait_recv()
        for h in range(2):
            for ib in range(1, pc.grid_b):
                for ia in range(1, pc.grid_a):
                    self._on(h, ib, ia, True).wait_recv()
                    self._on(h, ib, ia, False).wait_send()
        for h in range(2):
            for ib in range(1, pc.grid_b):
                self._b_copy(ib, h, False).wait_send()
            for ia in range(1, pc.grid_a):
                self._a_copy(ia, h, False).wait_send()


class GridScatter:
    @staticmethod
    def scratch(n_dp, which, rows, width):
        na, nb = 2, n_dp // 2
        half = rows // 2
        most = max(nb - 1, 1)
        return [
            pltpu.VMEM((most, na, which, half, width), jnp.bfloat16),
            pltpu.VMEM((na - 1, nb, which, half, width), jnp.bfloat16),
            pltpu.VMEM((na - 1, which, half, width), jnp.bfloat16),
            pltpu.VMEM((most, which, half, width), jnp.bfloat16),
            pltpu.VMEM((na - 1, which, half, width), jnp.bfloat16),
            pltpu.VMEM((most, which, half, width), jnp.bfloat16),
            pltpu.SemaphoreType.DMA((most, na)),
            pltpu.SemaphoreType.DMA((most, na)),
            pltpu.SemaphoreType.DMA((na - 1, nb)),
            pltpu.SemaphoreType.DMA((na - 1, nb)),
            pltpu.SemaphoreType.DMA((na - 1,)),
            pltpu.SemaphoreType.DMA((na - 1,)),
            pltpu.SemaphoreType.DMA((most,)),
            pltpu.SemaphoreType.DMA((most,)),
        ]

    def __init__(self, place, part, out, squares, scratch):
        self.place, self.part, self.out, self.squares = place, part, out, squares
        self.box_b, self.box_a, self.sum_b, self.sum_a, self.end_a, self.end_b = scratch[:6]
        self.bs, self.br, self.as_, self.ar, self.eas, self.ear, self.ebs, self.ebr = scratch[6:]
        self.which = out.shape[0]
        self.half = out.shape[1] // 2

    def _part(self, a, b, h):
        return self.part.at[:, a * self.place.grid_b + b, pl.ds(h * self.half, self.half)]

    def _first_b(self, i, j):
        pc = self.place
        return remote(
            self._part(pc.a_peer(j), pc.b_peer(i), 0), self.box_b.at[i - 1, j], self.bs.at[i - 1, j],
            self.br.at[i - 1, j], pc.at_dp(pc.a * pc.grid_b + pc.b_peer(i)),
        )

    def _first_a(self, i, j):
        pc = self.place
        return remote(
            self._part(pc.a_peer(i), pc.b_peer(j), 1), self.box_a.at[i - 1, j], self.as_.at[i - 1, j],
            self.ar.at[i - 1, j], pc.at_dp(pc.a_peer(i) * pc.grid_b + pc.b),
        )

    def _second_a(self, i):
        pc = self.place
        return remote(
            self.sum_b.at[i - 1], self.end_a.at[i - 1], self.eas.at[i - 1], self.ear.at[i - 1],
            pc.at_dp(pc.a_peer(i) * pc.grid_b + pc.b),
        )

    def _second_b(self, i):
        pc = self.place
        return remote(
            self.sum_a.at[i - 1], self.end_b.at[i - 1], self.ebs.at[i - 1], self.ebr.at[i - 1],
            pc.at_dp(pc.a * pc.grid_b + pc.b_peer(i)),
        )

    def _firsts_b(self):
        pc = self.place
        return [(i, j) for j in list(range(1, pc.grid_a)) + [0] for i in range(1, pc.grid_b)]

    def _firsts_a(self):
        pc = self.place
        return [(i, j) for j in list(range(1, pc.grid_b)) + [0] for i in range(1, pc.grid_a)]

    def start(self):
        for (ib, jb), (ia, ja) in zip(self._firsts_b(), self._firsts_a(), strict=False):
            self._first_b(ib, jb).start()
            self._first_a(ia, ja).start()
        shared = min(len(self._firsts_b()), len(self._firsts_a()))
        for i, j in self._firsts_b()[shared:]:
            self._first_b(i, j).start()
        for i, j in self._firsts_a()[shared:]:
            self._first_a(i, j).start()

    def _low(self, rows):
        return pl.ds(pl.multiple_of(self.half + rows.start, ROW_STEP), ROW_STEP)

    def _sum_b(self, j):
        pc = self.place
        for i in range(1, pc.grid_b):
            self._first_b(i, j).wait_recv()
        mine = pc.a_peer(j) * pc.grid_b + pc.b

        def add(rows):
            for w in range(self.which):
                total = self.part[w, mine, rows, :].astype(jnp.float32)
                for i in range(1, pc.grid_b):
                    total = total + self.box_b[i - 1, j, w, rows, :].astype(jnp.float32)
                if j == 0:
                    self.out[w, rows, :] = total
                else:
                    self.sum_b[j - 1, w, rows, :] = total.astype(jnp.bfloat16)

        row_loop(self.half, add)
        if j:
            self._second_a(j).start()

    def _sum_a(self, j):
        pc = self.place
        for i in range(1, pc.grid_a):
            self._first_a(i, j).wait_recv()
        mine = pc.a * pc.grid_b + pc.b_peer(j)

        def add(rows):
            for w in range(self.which):
                total = self.part[w, mine, self._low(rows), :].astype(jnp.float32)
                for i in range(1, pc.grid_a):
                    total = total + self.box_a[i - 1, j, w, rows, :].astype(jnp.float32)
                if j == 0:
                    self.out[w, self._low(rows), :] = total
                else:
                    self.sum_a[j - 1, w, rows, :] = total.astype(jnp.bfloat16)

        row_loop(self.half, add)
        if j:
            self._second_b(j).start()

    def step(self):
        pc = self.place
        for j in range(1, max(pc.grid_a, pc.grid_b)):
            if j < pc.grid_a:
                self._sum_b(j)
            if j < pc.grid_b:
                self._sum_a(j)

    def step_own(self):
        self._sum_b(0)
        self._sum_a(0)

    def finish(self):
        pc = self.place
        for i in range(1, pc.grid_a):
            self._second_a(i).wait_recv()
        for i in range(1, pc.grid_b):
            self._second_b(i).wait_recv()
        self.squares[...] = jnp.zeros_like(self.squares)

        def tile(total):
            total = total * total
            folded = total[:, :128]
            for at in range(128, total.shape[1], 128):
                folded = folded + total[:, at : at + 128]
            return folded

        def add(rows):
            low = self._low(rows)
            for w in range(self.which):
                total = self.out[w, rows, :]
                for i in range(1, pc.grid_a):
                    total = total + self.end_a[i - 1, w, rows, :].astype(jnp.float32)
                self.out[w, rows, :] = total
                self.squares[...] += tile(total)
                total = self.out[w, low, :]
                for i in range(1, pc.grid_b):
                    total = total + self.end_b[i - 1, w, rows, :].astype(jnp.float32)
                self.out[w, low, :] = total
                self.squares[...] += tile(total)

        row_loop(self.half, add)
        for i, j in self._firsts_b():
            self._first_b(i, j).wait_send()
        for i, j in self._firsts_a():
            self._first_a(i, j).wait_send()
        for i in range(1, pc.grid_a):
            self._second_a(i).wait_send()
        for i in range(1, pc.grid_b):
            self._second_b(i).wait_send()


class Direct:
    @staticmethod
    def scratch(n):
        return [pltpu.SemaphoreType.DMA((n - 1,)), pltpu.SemaphoreType.DMA((n - 1,))]

    def __init__(self, place, src, out, sems, axis="dp", block=None, to=None):
        self.place, self.src, self.out = place, src, out
        self.send, self.recv = sems
        self.n = place.n_dp if axis == "dp" else place.n_fsdp
        self.me = place.dp if axis == "dp" else place.f
        self.axis = axis
        self.of = block or (lambda ref, d: ref)
        self.to = to or (lambda ref, d: ref.at[d])

    def _device(self, other):
        return self.place.at_dp(other) if self.axis == "dp" else (self.place.dp, other)

    def _copy(self, i, coming=False):
        other = (self.me + i) % self.n
        origin = (self.me + self.n - i) % self.n if coming else self.me
        return remote(
            self.of(self.src, other), self.to(self.out, origin), self.send.at[i - 1], self.recv.at[i - 1], self._device(other)
        )

    def start(self):
        for i in range(1, self.n):
            self._copy(i).start()

    def finish(self):
        for i in range(1, self.n):
            self._copy(i, True).wait_recv()
            self._copy(i).wait_send()


def split_refs(refs, counts):
    out, at = [], 0
    for count in counts:
        out.append(refs[at : at + count])
        at += count
    return out


HBM = pl.BlockSpec(memory_space=pl.ANY)
WHOLE = pl.BlockSpec(memory_space=pltpu.VMEM)
TILE = (ROW_STEP, 128)


def parameters(collective_id, limit=VMEM_LIMIT):
    return pltpu.CompilerParams(collective_id=collective_id, has_side_effects=True, vmem_limit_bytes=limit)


def matmul(left, right):
    return jnp.dot(left, right, preferred_element_type=jnp.float32)


def matmul_last(left, right):
    return lax.dot_general(left, right, (((1,), (1,)), ((), ())), preferred_element_type=jnp.float32)


def matmul_first(left, right):
    return lax.dot_general(left, right, (((0,), (0,)), ((), ())), preferred_element_type=jnp.float32)


def loop(count, work):
    def one(i, carry):
        work(i)
        return carry

    lax.fori_loop(0, count, one, 0)


def span(i, size):
    return pl.ds(pl.multiple_of(i * size, size), size)


def chip_rows(ref, chip):
    pair = ref[span(chip, 2)]
    return pair.reshape(-1, pair.shape[-1])


def pair_mask(codes_ref, chip, rows):
    pair = [codes_ref[chip * 2 + i] for i in range(2)]
    query = jnp.floor(jnp.concatenate([block[:rows] for block in pair], axis=0))
    query = jnp.concatenate([query] * (2 * rows // 128), axis=1)
    key = jnp.concatenate([block[rows : rows + 1] for block in pair], axis=1)
    shape = (2 * rows, 2 * rows)
    same = lax.broadcasted_iota(jnp.int32, shape, 0) == lax.broadcasted_iota(jnp.int32, shape, 1)
    return (query == key) | same


class Rows:
    def __init__(self, place, codes, mods, micro, rows, slots_here):
        self.place, self.codes, self.mods = place, codes, mods
        self.micro, self.tok_rows, self.slots_here = micro, rows // micro, slots_here

    def tiles(self, work):
        for m in range(self.micro):
            row_loop(self.tok_rows, functools.partial(work, m), m * self.tok_rows)

    def slot_live(self, m, rows):
        column = self.codes[rows, :][:, :1]
        number = jnp.floor(column)
        first = ((self.place.f * self.micro + m) * self.slots_here).astype(jnp.float32)
        return number - first, jnp.where(column == number, 1.0, 0.0)

    def pick(self, j, m, slot):
        at = m * self.slots_here
        picked = self.mods[j, at : at + 1, :]
        for i in range(1, self.slots_here):
            picked = jnp.where(slot == i, self.mods[j, at + i : at + i + 1, :], picked)
        return picked

    def add_up(self, out, j, m, slot, values):
        for i in range(self.slots_here):
            at = m * self.slots_here + i
            chosen = jnp.where(slot == i, values, 0.0)
            out[j, at : at + 1, :] += jnp.sum(chosen, axis=0, keepdims=True)


def cast_rows(src, dst):
    for w in range(src.shape[0]):
        def tile(rows):
            dst[w, rows, :] = src[w, rows, :].astype(dst.dtype)

        row_loop(src.shape[1], tile)


def attention_probs(query, key, allowed):
    scores = jnp.where(allowed, matmul_last(query, key) * HEAD ** (-0.5), -1e30)
    raw = jnp.exp(scores - jnp.max(scores, axis=-1, keepdims=True))
    return raw / jnp.sum(raw, axis=-1, keepdims=True)


def attention_kernel(n_dp, n_fsdp, micro, tokens, cotangent, image_slot, token_mask, embedding, ada, qkv, out_w, up, down):
    low, f32 = jnp.bfloat16, jnp.float32
    images = embedding.shape[0]
    rows, width = tokens.shape
    deep, wide = ada.shape[1:]
    which, _, head_columns = qkv.shape
    slots_here = images // (micro * n_fsdp)
    own_images = micro * slots_here
    line = LineGather.scratch(n_fsdp)
    grid = GridGather.scratch(n_dp)
    direct = Direct.scratch(n_dp)
    scatter_got = LineScatter.scratch(n_fsdp, rows, width)
    counts = [len(line)] * 3 + [len(grid)] * 3 + [len(direct)] * 5 + [len(LineCast.scratch(n_fsdp)), len(scatter_got)]
    weights = (qkv, out_w, up, down, ada)
    pair = 2 * rows

    def kernel(
        tok, cot, slot_ref, mask_ref, emb, ada_f, qkv_f, out_f, up_f, down_f,
        attn_own, mid, hidden2, mods_own, cond_g, products, cod, cod_g, qkv_low, attended, down_low,
        hidden_out, qkv_out, out_out, up_g, gmlp_g,
        cond, parts, boxes, mail_first, mail, inbox, mods_g, averages, inv_stds, product, products_g, gmlp, part, hidden_g, qkv_g, out_g,
        qkv_s, out_s, up_s, down_s, ada_s, qkv_l, out_l, up_l, moves, *rest,
    ):
        sems = split_refs(rest, counts)
        place = Place(n_dp, n_fsdp)
        fetches = [
            pltpu.make_async_copy(ref, stage, moves.at[i])
            for i, (ref, stage) in enumerate(
                ((qkv_f, qkv_s), (out_f, out_s), (up_f, up_s), (down_f, down_s), (ada_f, ada_s))
            )
        ]
        for i in (0, 1, 4, 2, 3):
            fetches[i].start()
        present = announce(place, True, True, True)
        level = emb[...].astype(f32)
        level = (level / (1.0 + jnp.exp(-level))).astype(low)
        for d in range(n_dp):
            cond[d] = level[:, d * deep : (d + 1) * deep]
        number = jnp.concatenate(
            [slot_ref[m : m + 1, :].astype(f32) + (m * slots_here) for m in range(micro)], axis=1
        )
        number = number + ((place.f * micro) * slots_here).astype(f32)
        live = jnp.concatenate([mask_ref[m : m + 1, :].astype(f32) for m in range(micro)], axis=1)
        cod[:rows, :] = jnp.transpose(jnp.broadcast_to(jnp.where(live > 0.5, number, number + 0.25), (rows, rows)))
        cod[rows:, :] = jnp.broadcast_to(jnp.where(live > 0.5, number, -1.0), (8, rows))
        own = Rows(place, cod, mods_own, micro, rows, slots_here)
        fetches[0].wait()
        cast_rows(qkv_s, qkv_l)
        fetches[1].wait()
        cast_rows(out_s, out_l)
        pl.semaphore_wait(pltpu.get_barrier_semaphore(), present)
        conds = Direct(place, cond, cond_g, sems[6], block=lambda ref, d: ref.at[d])
        conds.start()
        token_line = LineGather(place, tok, hidden_g, sems[1])
        code_line = LineGather(place, cod, cod_g, sems[0])
        token_line.start()
        code_line.start()
        grids = [GridGather(place, qkv_l, qkv_g, sems[3]), GridGather(place, out_l, out_g, sems[4])]
        cond_g[place.dp] = cond[place.dp]
        fetches[4].wait()
        conds.finish()
        every = cond_g[...].reshape(n_dp * images, deep)

        def project(kinds):
            for j, kind in kinds:
                parts[:, j] = matmul(every, ada_s[kind].astype(low)).reshape(n_dp, images, wide)

        def add_parts(kinds, letter):
            for j in kinds:
                total = parts[place.dp, j]
                for i in range(1, n_dp):
                    total = total + boxes[(place.dp + i) % n_dp, j]
                for f in range(n_fsdp):
                    for m in range(micro):
                        at = (m * n_fsdp + f) * slots_here
                        letter[f, j - kinds[0], m * slots_here : (m + 1) * slots_here, :] = total[at : at + slots_here]

        first_sums = Direct(
            place, parts, boxes, sems[7], block=lambda ref, d: ref.at[d, 0:3], to=lambda ref, d: ref.at[d, 0:3]
        )
        other_sums = Direct(
            place, parts, boxes, sems[8], block=lambda ref, d: ref.at[d, 3:MODS], to=lambda ref, d: ref.at[d, 3:MODS]
        )
        project(list(enumerate(FIRST_KINDS)))
        first_sums.start()
        for gather in grids:
            gather.start()
        project(list(enumerate(OTHER_KINDS, 3)))
        product[...] = matmul_last(every, every)

        def statistics(chip):
            token_line.ready(chip)
            for i in range(2):
                device = chip * 2 + i

                def tile(at):
                    values = hidden_g[device, at, :].astype(f32)
                    average = jnp.mean(values, axis=-1, keepdims=True)
                    centred = values - average
                    inv_std = lax.rsqrt(jnp.mean(centred * centred, axis=-1, keepdims=True) + NORM_EPS)
                    averages[device, at, :] = jnp.broadcast_to(average, (ROW_STEP, 128))
                    inv_stds[device, at, :] = jnp.broadcast_to(inv_std, (ROW_STEP, 128))

                row_loop(rows, tile)

        def statistics_at(distance):
            def side(i):
                chip = place.p + (1 - 2 * i) * distance

                @pl.when((chip >= 0) & (chip < place.chips))
                def _():
                    statistics(chip)

            loop(2 if distance else 1, side)

        statistics_at(0)
        first_sums.finish()
        add_parts((0, 1, 2), mail_first)
        mods_line = LineCast(
            place, mail_first, mods_g, sems[11],
            block=lambda ref, d: ref.at[:, :, :, pl.ds(pl.multiple_of(d * wide, wide), wide)],
        )
        mods_line.start()
        token_line.step(1)
        code_line.step(1)
        fetches[2].wait()
        cast_rows(up_s, up_l)
        fetches[3].wait()
        cast_rows(down_s, down_low)
        crosses = Direct(place, product, products_g, sems[10])
        products_g[place.dp] = product[...]
        mods_line.step()
        ups = GridGather(place, up_l, up_g, sems[5])
        letters = Direct(place, mail, inbox, sems[9], "fsdp", block=lambda ref, d: ref.at[d])
        gmlp_line = LineGather(place, gmlp, gmlp_g, sems[2])

        def branch_grad(m, at):
            slot, alive = own.slot_live(m, at)
            gmlp[at, :] = (cot[at, :].astype(f32) * alive * own.pick(5, m, slot)).astype(low)

        mods_line.finish()
        for j, kind in enumerate(FIRST_KINDS):
            mods_own[kind] = mods_g[place.f, j]
        own.tiles(branch_grad)
        gmlp_line.start_here()
        for step in range(2, place.chips + 1):
            if step < place.chips:
                token_line.step(step)
                code_line.step(step)
            if step == 2:
                for gather in grids:
                    gather.step()
            statistics_at(step - 1)

            @pl.when((place.p + 1 == step) | ((place.p + 1 < step) & (step == 2)))
            def _():
                gmlp_line.start_way(0)

            @pl.when((place.chips - place.p == step) | ((place.chips - place.p < step) & (step == 2)))
            def _():
                gmlp_line.start_way(1)

        for gather in grids:
            gather.finish()
        other_sums.start()
        crosses.start()
        ups.start()
        token_line.drain()
        code_line.finish()
        leaves = [
            pltpu.make_async_copy(ref, out, moves.at[len(weights) + i])
            for i, (ref, out) in enumerate(((qkv_g, qkv_out), (out_g, out_out), (hidden_g, hidden_out)))
        ]
        for leave in leaves[:2]:
            leave.start()
        scatter = LineScatter(place, part, attn_own, sems[12])

        def norm_block(chip):
            for i in range(2):
                device = chip * 2 + i
                for m in range(micro):
                    first = ((device * micro + m) * slots_here).astype(f32)

                    def table(j, slot):
                        at = m * slots_here
                        picked = mods_g[device, j, at : at + 1, :]
                        for k in range(1, slots_here):
                            picked = jnp.where(slot == k, mods_g[device, j, at + k : at + k + 1, :], picked)
                        return picked

                    def tile(at):
                        slot = jnp.floor(cod_g[device, at, :][:, :1]) - first
                        centred = hidden_g[device, at, :].astype(f32) - averages[device, at, :][:, :1]
                        normed = centred * inv_stds[device, at, :][:, :1]
                        hidden_g[device, at, :] = (normed * (1.0 + table(1, slot)) + table(0, slot)).astype(low)

                    row_loop(rows // micro, tile, m * (rows // micro))

        def compute(chip):
            at = span(chip, pair)
            norm_block(chip)
            values = chip_rows(hidden_g, chip)
            for w in range(which):
                weight = qkv_g[w].reshape(width, head_columns)
                qkv_low[w, at, :] = matmul(values, weight).astype(low)
            allowed = pair_mask(cod_g, chip, rows)
            for h in range(head_columns // HEAD):
                head = slice(h * HEAD, (h + 1) * HEAD)
                probs = attention_probs(qkv_low[0, at, head], qkv_low[1, at, head], allowed)
                attended[at, head] = matmul(probs.astype(low), qkv_low[2, at, head]).astype(low)
            heads = attended[at, :]
            weight_rows = out_g.shape[2]
            for d in range(n_dp):
                piece = matmul_last(heads, out_g[0, d]).astype(low).reshape(2, rows, weight_rows)
                part[span(chip, 2), :, d * weight_rows : (d + 1) * weight_rows] = piece

        def then(k):
            @pl.when(k == 1)
            def _():
                gmlp_line.step(1)

        slot = scatter.paced(compute, 1, then)
        leaves[2].start()
        for step in range(2, place.chips):
            gmlp_line.step(step)
            slot = scatter.run_to(slot, scatter.slots * (step + 1) // (place.chips + 1))
            if step == place.chips // 2:
                other_sums.finish()
                add_parts((3, 4, 5), mail)
                letters.start()
                inbox[place.f] = mail[place.f]
                ups.step()
                crosses.finish()
                total = products_g[0]
                for d in range(1, n_dp):
                    total = total + products_g[d]
                products[...] = total
        scatter.run_to(slot, scatter.slots)
        scatter.finish()
        letters.finish()
        for f in range(n_fsdp):
            for j, kind in enumerate(OTHER_KINDS):
                mods_own[kind, :, f * wide : (f + 1) * wide] = inbox[f, j]

        def second_norm(m, at):
            slot, _ = own.slot_live(m, at)
            values = tok[at, :].astype(f32) + own.pick(2, m, slot) * attn_own[at, :]
            mid[at, :] = values
            normed, _ = normalize(values)
            hidden2[at, :] = (normed * (1.0 + own.pick(4, m, slot)) + own.pick(3, m, slot)).astype(low)

        own.tiles(second_norm)
        gmlp_line.finish()
        ups.finish()
        for leave in leaves:
            leave.wait()

    def gathered(w):
        return jax.ShapeDtypeStruct((w.shape[0], n_dp, *w.shape[1:]), low)

    return pl.pallas_call(
        kernel,
        out_shape=[
            jax.ShapeDtypeStruct((rows, width), f32),
            jax.ShapeDtypeStruct((rows, width), f32),
            jax.ShapeDtypeStruct((rows, width), low),
            jax.ShapeDtypeStruct((MODS, own_images, width), f32),
            jax.ShapeDtypeStruct((n_dp, images, deep), low),
            jax.ShapeDtypeStruct((n_dp * images, n_dp * images), f32),
            jax.ShapeDtypeStruct((rows + 8, rows), f32),
            jax.ShapeDtypeStruct((n_fsdp, rows + 8, rows), f32),
            jax.ShapeDtypeStruct((which, n_fsdp * rows, head_columns), low),
            jax.ShapeDtypeStruct((n_fsdp * rows, head_columns), low),
            jax.ShapeDtypeStruct(down.shape, low),
            jax.ShapeDtypeStruct((n_fsdp, rows, width), low),
            gathered(qkv),
            gathered(out_w),
            gathered(up),
            jax.ShapeDtypeStruct((n_fsdp, rows, width), low),
        ],
        in_specs=[WHOLE] * 5 + [HBM] * 5,
        out_specs=[WHOLE] * 11 + [HBM] * 5,
        scratch_shapes=[
            pltpu.VMEM((n_dp, images, deep), low),
            pltpu.VMEM((n_dp, MODS, images, wide), f32),
            pltpu.VMEM((n_dp, MODS, images, wide), f32),
            pltpu.VMEM((n_fsdp, 3, own_images, wide), f32),
            pltpu.VMEM((n_fsdp, 3, own_images, wide), f32),
            pltpu.VMEM((n_fsdp, 3, own_images, wide), f32),
            pltpu.VMEM((n_fsdp, 3, own_images, width), f32),
            pltpu.VMEM((n_fsdp, rows, 128), f32),
            pltpu.VMEM((n_fsdp, rows, 128), f32),
            pltpu.VMEM((n_dp * images, n_dp * images), f32),
            pltpu.VMEM((n_dp, n_dp * images, n_dp * images), f32),
            pltpu.VMEM((rows, width), low),
            pltpu.VMEM((n_fsdp, rows, width), low),
            pltpu.VMEM((n_fsdp, rows, width), low),
            pltpu.VMEM((which, n_dp, *qkv.shape[1:]), low),
            pltpu.VMEM((1, n_dp, *out_w.shape[1:]), low),
            *[pltpu.VMEM(w.shape, f32) for w in weights],
            *[pltpu.VMEM(w.shape, low) for w in weights[:3]],
            pltpu.SemaphoreType.DMA((len(weights) + 3,)),
            *line, *line, *line, *grid, *grid, *grid, *direct, *direct, *direct,
            *Direct.scratch(n_fsdp), *direct, *LineCast.scratch(n_fsdp), *scatter_got,
        ],
        compiler_params=parameters(0),
    )(tokens, cotangent, image_slot, token_mask, embedding, ada, qkv, out_w, up, down)


def gelu_parts(v):
    root = 0.7978845608028654
    square = v * v
    bent = jnp.tanh(root * (v + 0.044715 * v * square))
    value = 0.5 * v * (1.0 + bent)
    slope = 0.5 * (1.0 + bent) + (0.5 * root) * v * (1.0 - bent * bent) * (1.0 + (3.0 * 0.044715) * square)
    return value, slope


COLUMN_STEP = 256


def feed_forward_kernel(n_dp, n_fsdp, micro, hidden, mid, attn_own, cotangent, codes, mods, grad_mlp, up_g, down):
    low, f32 = jnp.bfloat16, jnp.float32
    rows, width = hidden.shape
    _, weight_rows, columns = down.shape
    tokens = n_fsdp * rows
    pair = 2 * rows
    own_images = mods.shape[1]
    line = LineGather.scratch(n_fsdp)
    grid = GridGather.scratch(n_dp)
    scatter_got = LineScatter.scratch(n_fsdp, rows, width)
    grads_got = GridScatter.scratch(n_dp, 1, weight_rows, columns)
    counts = [len(line), len(grid), len(scatter_got), len(grads_got)]
    tiles = columns // COLUMN_STEP
    row_tiles = weight_rows // COLUMN_STEP

    def kernel(
        hid, mid_ref, attn_ref, cot, cod, mods_ref, down_ref, gmlp_ref, up_ref,
        grad_mid, grad_attn, sums_own, grad_down, squares, mlp_part, grad_up,
        gmlp, up, hidden_g, down_g, upper, activ, grad_upper, part, gdown, grad_h2, stage, stage_up,
        moves, out_sem, up_sem, *rest,
    ):
        sems = split_refs(rest, counts)
        place = Place(n_dp, n_fsdp)
        fetch_up = pltpu.make_async_copy(up_ref, up, moves.at[0])
        fetch_gmlp = pltpu.make_async_copy(gmlp_ref, gmlp, moves.at[1])
        fetch_up.start()
        fetch_gmlp.start()
        enter(place, True, True)
        hidden_line = LineGather(place, hid, hidden_g, sems[0])
        downs = GridGather(place, down_ref, down_g, sems[1])
        hidden_line.start()
        downs.start()
        fetch_up.wait()

        def forward(chip):
            at = span(chip, pair)
            hidden_line.ready(chip)

            def tile(i):
                to = span(i, COLUMN_STEP)
                values = chip_rows(hidden_g, chip)
                total = jnp.zeros((pair, COLUMN_STEP), f32)
                for d in range(n_dp):
                    total = total + matmul(values[:, d * weight_rows : (d + 1) * weight_rows], up[0, d, :, to])
                upper[at, to] = total
                activ[at, to] = gelu_parts(total)[0].astype(low)

            loop(tiles, tile)

        def forward_at(distance):
            def side(i):
                chip = place.p + (1 - 2 * i) * distance

                @pl.when((chip >= 0) & (chip < place.chips))
                def _():
                    forward(chip)

            loop(2 if distance else 1, side)

        for step in range(1, place.chips):
            hidden_line.step(step)
            if step == place.chips // 2:
                downs.step()
            forward_at(step - 1)
        forward_at(place.chips - 1)
        fetch_gmlp.wait()
        downs.finish()
        scatter = LineScatter(place, part, grad_h2, sems[2])
        grads = GridScatter(place, gdown, grad_down, squares, sems[3])

        def backward(chip):
            at = span(chip, pair)

            def tile(i):
                to = span(i, COLUMN_STEP)
                values = chip_rows(gmlp, chip)
                total = jnp.zeros((pair, COLUMN_STEP), f32)
                for d in range(n_dp):
                    total = total + matmul(values[:, d * weight_rows : (d + 1) * weight_rows], down_g[0, d, :, to])
                grad_upper[at, to] = (total * gelu_parts(upper[at, to])[1]).astype(low)

            loop(tiles, tile)
            values = grad_upper[at, :]
            for d in range(n_dp):
                piece = matmul_last(values, up[0, d]).astype(low).reshape(2, rows, weight_rows)
                part[span(chip, 2), :, d * weight_rows : (d + 1) * weight_rows] = piece

        def down_tile(i):
            d, r = i // row_tiles, lax.rem(i, row_tiles)
            left = gmlp[:, :, span(i, COLUMN_STEP)].reshape(tokens, COLUMN_STEP)
            gdown[0, d, span(r, COLUMN_STEP), :] = matmul_first(left, activ[...]).astype(low)

        def then(k):
            @pl.when(k == 0)
            def _():
                loop(n_dp * row_tiles, down_tile)
                grads.start()

        slot = scatter.paced(backward, 2, then)

        def up_copy(i, d, r):
            return pltpu.make_async_copy(
                stage_up.at[lax.rem(i, 2)], grad_up.at[0, d, span(r, COLUMN_STEP)], up_sem.at[lax.rem(i, 2)]
            )

        def up_tile(i):
            d, r = i // row_tiles, lax.rem(i, row_tiles)

            @pl.when(i >= 2)
            def _():
                up_copy(i, 0, 0).wait()

            left = hidden_g[:, :, span(i, COLUMN_STEP)].reshape(tokens, COLUMN_STEP)
            stage_up[lax.rem(i, 2)] = matmul_first(left, grad_upper[...]).astype(low)
            up_copy(i, d, r).start()

        slot = scatter.beside(slot, n_dp * row_tiles, up_tile, 2)
        up_copy(0, 0, 0).wait()
        up_copy(1, 0, 0).wait()
        grads.step()

        def mlp_copy(chip):
            to = lax.rem(chip, 2)
            return pltpu.make_async_copy(stage.at[to], mlp_part.at[span(chip, 2)], out_sem.at[to])

        def mlp_tile(chip):
            @pl.when(chip >= 2)
            def _():
                mlp_copy(chip).wait()

            values = activ[span(chip, pair), :]
            for d in range(n_dp):
                piece = matmul_last(values, down_g[0, d]).astype(low).reshape(2, rows, weight_rows)
                stage[lax.rem(chip, 2), :, :, d * weight_rows : (d + 1) * weight_rows] = piece
            mlp_copy(chip).start()

        slot = scatter.beside(slot, place.chips, mlp_tile)
        mlp_copy(0).wait()
        mlp_copy(1).wait()
        scatter.run_to(slot, scatter.slots)
        grads.step_own()
        scatter.finish()
        own = Rows(place, cod, mods_ref, micro, rows, own_images // micro)
        sums_own[...] = jnp.zeros_like(sums_own)

        def norm_grad(m, at):
            slot, alive = own.slot_live(m, at)
            normed, inv_std = normalize(mid_ref[at, :])
            grad = grad_h2[at, :]
            before = normalize_back(grad * (1.0 + own.pick(4, m, slot)), normed, inv_std)
            total = cot[at, :].astype(f32) * alive + before
            grad_mid[at, :] = total
            grad_attn[at, :] = (total * own.pick(2, m, slot)).astype(low)
            own.add_up(sums_own, 0, m, slot, total * attn_ref[at, :])
            own.add_up(sums_own, 1, m, slot, grad)
            own.add_up(sums_own, 2, m, slot, grad * normed)

        own.tiles(norm_grad)
        grads.finish()
        hidden_line.drain()

    return pl.pallas_call(
        kernel,
        out_shape=[
            jax.ShapeDtypeStruct((rows, width), f32),
            jax.ShapeDtypeStruct((rows, width), low),
            jax.ShapeDtypeStruct((3, own_images, width), f32),
            jax.ShapeDtypeStruct((1, weight_rows, columns), f32),
            jax.ShapeDtypeStruct(TILE, f32),
            jax.ShapeDtypeStruct((n_fsdp, rows, width), low),
            jax.ShapeDtypeStruct((1, n_dp, weight_rows, columns), low),
        ],
        in_specs=[WHOLE] * 6 + [HBM] * 3,
        out_specs=[WHOLE] * 5 + [HBM] * 2,
        scratch_shapes=[
            pltpu.VMEM((n_fsdp, rows, width), low),
            pltpu.VMEM((1, n_dp, weight_rows, columns), low),
            pltpu.VMEM((n_fsdp, rows, width), low),
            pltpu.VMEM((1, n_dp, weight_rows, columns), low),
            pltpu.VMEM((tokens, columns), f32),
            pltpu.VMEM((tokens, columns), low),
            pltpu.VMEM((tokens, columns), low),
            pltpu.VMEM((n_fsdp, rows, width), low),
            pltpu.VMEM((1, n_dp, weight_rows, columns), low),
            pltpu.VMEM((rows, width), f32),
            pltpu.VMEM((2, 2, rows, width), low),
            pltpu.VMEM((2, COLUMN_STEP, columns), low),
            pltpu.SemaphoreType.DMA((2,)),
            pltpu.SemaphoreType.DMA((2,)),
            pltpu.SemaphoreType.DMA((2,)),
            *line, *grid, *scatter_got, *grads_got,
        ],
        compiler_params=parameters(2),
    )(hidden, mid, attn_own, cotangent, codes, mods, down, grad_mlp, up_g)


def attention_grad_kernel(
    n_dp, n_fsdp, micro, grad_attn, tokens_own, mid, grad_mid, cotangent, codes, mods, codes_g, mlp_part, grad_up, qkv_g,
    out_g, qkv_low, attended, hidden_g,
):
    low, f32 = jnp.bfloat16, jnp.float32
    rows, width = grad_attn.shape
    which, _, weight_rows, head_columns = qkv_g.shape
    tokens = n_fsdp * rows
    pair = 2 * rows
    chips = n_fsdp // 2
    own_images = mods.shape[1]
    line = LineGather.scratch(n_fsdp)
    scatter_got = LineScatter.scratch(n_fsdp, rows, width)
    up_shape = (1, *grad_up.shape[2:])
    up_got = GridScatter.scratch(n_dp, *up_shape)
    qkv_got = GridScatter.scratch(n_dp, which, weight_rows, head_columns)
    out_got = GridScatter.scratch(n_dp, 1, weight_rows, head_columns)
    counts = [len(line), len(scatter_got), len(scatter_got), len(up_got), len(qkv_got), len(out_got)]
    row_tiles = weight_rows // COLUMN_STEP

    def kernel(
        ga, tok, mid_ref, gmid, cot, cod, mods_ref, cod_g, mlp_ref, gup_ref, qkv_wr, out_wr, qkv_lr, att_r, hid_r,
        block_out, input_grad, sums_own, grad_up_own, grad_qkv_own, grad_out_own, squares,
        ga_g, gqkv, gqkv_w, gout_w, mlp_own, grad_h1, tile_up, tile_qkv, tile_out,
        mine, gup, qkv_w, out_w, qkv_ref, att, hid_g, moves, mine_sem, *rest,
    ):
        sems = split_refs(rest, counts)
        place = Place(n_dp, n_fsdp)
        fetches = [
            pltpu.make_async_copy(ref, to, moves.at[i])
            for i, (ref, to) in enumerate(
                ((gup_ref, gup), (att_r, att), (out_wr, out_w), (qkv_lr, qkv_ref), (qkv_wr, qkv_w), (hid_r, hid_g))
            )
        ]
        terms = [
            pltpu.make_async_copy(mlp_ref.at[chip * 2 + place.c], mine.at[chip], mine_sem.at[chip])
            for chip in range(chips)
        ]
        fetches[0].start()
        for term in terms:
            term.start()
        for fetch in fetches[1:]:
            fetch.start()
        enter(place, True, True)
        ga_line = LineGather(place, ga, ga_g, sems[0])
        mlp_scatter = LineScatter(place, mlp_ref, mlp_own, sems[1], mine, LineScatter.pieces)
        ups = GridScatter(place, gup, grad_up_own, tile_up, sems[3])
        ga_line.start()
        fetches[0].wait()
        ups.start()
        mlp_scatter.start()
        for term in terms:
            term.wait()
        travel = LineScatter.pieces * (chips - 1)
        at_slot = 0

        def backward(chip):
            at = span(chip, pair)
            ga_line.ready(chip)
            values = chip_rows(ga_g, chip)
            grad_heads = matmul(values, out_w[0].reshape(width, head_columns)).astype(low)
            allowed = pair_mask(cod_g, chip, rows)
            for h in range(head_columns // HEAD):
                head = slice(h * HEAD, (h + 1) * HEAD)
                query, key, value = [qkv_ref[w, at, head] for w in range(which)]
                grad_head = grad_heads[:, head]
                probs = attention_probs(query, key, allowed)
                grad_p = matmul_last(grad_head, value)
                delta = jnp.sum(probs * grad_p, axis=-1, keepdims=True)
                grad_scores = (probs * (grad_p - delta)).astype(low)
                scale = HEAD ** (-0.5)
                gqkv[0, at, head] = (matmul(grad_scores, key) * scale).astype(low)
                gqkv[1, at, head] = (matmul_first(grad_scores, query) * scale).astype(low)
                gqkv[2, at, head] = matmul_first(probs.astype(low), grad_head).astype(low)

        def backward_at(distance):
            def side(i):
                chip = place.p + (1 - 2 * i) * distance

                @pl.when((chip >= 0) & (chip < place.chips))
                def _():
                    backward(chip)

            loop(2 if distance else 1, side)

        for step in range(1, chips):
            ga_line.step(step)
            if step < chips - 1:
                to_slot = travel * step // (chips - 1)
                mlp_scatter.run(at_slot, to_slot)
                at_slot = to_slot
            if step == 1:
                for fetch in fetches[1:]:
                    fetch.wait()
            backward_at(step - 1)
            if step == chips // 2:
                ups.step()
        backward_at(chips - 1)
        ga_line.drain()
        scatter = LineScatter(place, ga_g, grad_h1, sems[2])
        qkvs = GridScatter(place, gqkv_w, grad_qkv_own, tile_qkv, sems[4])
        outs = GridScatter(place, gout_w, grad_out_own, tile_out, sems[5])

        def out_tile(i):
            d, r = i // row_tiles, lax.rem(i, row_tiles)
            left = ga_g[:, :, span(i, COLUMN_STEP)].reshape(tokens, COLUMN_STEP)
            gout_w[0, d, span(r, COLUMN_STEP), :] = matmul_first(left, att[...]).astype(low)

        loop(n_dp * row_tiles, out_tile)
        outs.start()

        def compute(chip):
            at = span(chip, pair)
            for d in range(n_dp):
                total = matmul_last(gqkv[0, at, :], qkv_w[0, d])
                for w in range(1, which):
                    total = total + matmul_last(gqkv[w, at, :], qkv_w[w, d])
                piece = total.astype(low).reshape(2, rows, weight_rows)
                ga_g[span(chip, 2), :, d * weight_rows : (d + 1) * weight_rows] = piece

        def grad_tile(i):
            d, r = i // row_tiles, lax.rem(i, row_tiles)
            left = hid_g[:, :, span(i, COLUMN_STEP)].reshape(tokens, COLUMN_STEP)
            for w in range(which):
                gqkv_w[w, d, span(r, COLUMN_STEP), :] = matmul_first(left, gqkv[w]).astype(low)

        def then(k):
            @pl.when(k == 0)
            def _():
                loop(n_dp * row_tiles, grad_tile)
                qkvs.start()

            @pl.when(k == 1)
            def _():
                mlp_scatter.run(at_slot, travel)

        slot = scatter.paced(compute, 3, then)
        outs.step()
        slot = scatter.run_to(slot, scatter.slots // 2)
        qkvs.step()
        slot = scatter.run_to(slot, scatter.slots * 5 // 8)
        ups.step_own()
        mlp_scatter.finish()
        ups.finish()
        own = Rows(place, cod, mods_ref, micro, rows, own_images // micro)
        sums_own[...] = jnp.zeros_like(sums_own)

        def branch_out(m, at):
            slot_of, alive = own.slot_live(m, at)
            branch = mlp_own[at, :]
            block_out[at, :] = (mid_ref[at, :] + own.pick(5, m, slot_of) * branch).astype(low)
            own.add_up(sums_own, 2, m, slot_of, cot[at, :].astype(f32) * alive * branch)

        own.tiles(branch_out)
        scatter.run_to(slot, scatter.slots)
        outs.step_own()
        qkvs.step_own()
        scatter.finish()

        def norm_grad(m, at):
            slot_of, _ = own.slot_live(m, at)
            normed, inv_std = normalize(tok[at, :].astype(f32))
            grad = grad_h1[at, :]
            before = normalize_back(grad * (1.0 + own.pick(1, m, slot_of)), normed, inv_std)
            input_grad[at, :] = gmid[at, :] + before
            own.add_up(sums_own, 0, m, slot_of, grad)
            own.add_up(sums_own, 1, m, slot_of, grad * normed)

        own.tiles(norm_grad)
        outs.finish()
        qkvs.finish()
        squares[...] = tile_up[...] + tile_qkv[...] + tile_out[...]

    return pl.pallas_call(
        kernel,
        out_shape=[
            jax.ShapeDtypeStruct((rows, width), low),
            jax.ShapeDtypeStruct((rows, width), f32),
            jax.ShapeDtypeStruct((3, own_images, width), f32),
            jax.ShapeDtypeStruct(up_shape, f32),
            jax.ShapeDtypeStruct((which, weight_rows, head_columns), f32),
            jax.ShapeDtypeStruct((1, weight_rows, head_columns), f32),
            jax.ShapeDtypeStruct(TILE, f32),
        ],
        in_specs=[WHOLE] * 8 + [HBM] * 7,
        out_specs=[WHOLE] * 7,
        scratch_shapes=[
            pltpu.VMEM((n_fsdp, rows, width), low),
            pltpu.VMEM((which, tokens, head_columns), low),
            pltpu.VMEM((which, n_dp, weight_rows, head_columns), low),
            pltpu.VMEM((1, n_dp, weight_rows, head_columns), low),
            pltpu.VMEM((rows, width), f32),
            pltpu.VMEM((rows, width), f32),
            pltpu.VMEM(TILE, f32),
            pltpu.VMEM(TILE, f32),
            pltpu.VMEM(TILE, f32),
            pltpu.VMEM((chips, rows, width), low),
            *[pltpu.VMEM(a.shape, low) for a in (grad_up, qkv_g, out_g, qkv_low, attended, hidden_g)],
            pltpu.SemaphoreType.DMA((6,)),
            pltpu.SemaphoreType.DMA((chips,)),
            *line, *scatter_got, *scatter_got, *up_got, *qkv_got, *out_got,
        ],
        compiler_params=parameters(3),
    )(
        grad_attn, tokens_own, mid, grad_mid, cotangent, codes, mods, codes_g, mlp_part, grad_up, qkv_g, out_g, qkv_low,
        attended, hidden_g,
    )


def norm_kernel(n_dp, n_fsdp, micro, sums_first, sums_second, condition, products, squares, more_squares, states):
    own_images, width = sums_first.shape[1:]
    wide = width // n_fsdp
    images, deep = condition.shape[1:]
    lanes = wide // 128
    slots_here = own_images // micro
    source = [(0, 0), (0, 1), (1, 0), (1, 1), (1, 2), (0, 2)]

    def kernel(sums_a, sums_b, cond, product, squares_ref, more_ref, *refs):
        states_in, refs = refs[: len(states)], refs[len(states) :]
        grad, norm, refs = refs[0], refs[1], refs[2:]
        states_out, refs = refs[: len(states)], refs[len(states) :]
        mail, boxes, mine, all_mods, columns, tile, tiles, moves, *sems = refs
        place = Place(n_dp, n_fsdp)
        fetches = [
            pltpu.make_async_copy(src, dst, moves.at[i]) for i, (src, dst) in enumerate(zip(states_in, states_out))
        ]
        for fetch in fetches:
            fetch.start()
        barrier = pltpu.get_barrier_semaphore()
        for i in range(1, n_dp):
            pl.semaphore_signal(
                barrier, inc=1, device_id=place.at_dp((place.dp + i) % n_dp), device_id_type=MESH
            )
        for i in range(1, n_fsdp):
            pl.semaphore_signal(
                barrier, inc=1, device_id=(place.dp, (place.f + i) % n_fsdp), device_id_type=MESH
            )
        for j, (which, row) in enumerate(source):
            values = (sums_a, sums_b)[which][row].astype(jnp.bfloat16).astype(jnp.float32)
            for f in range(n_fsdp):
                for g in range(lanes):
                    at = (j * lanes + g) * own_images
                    mail[f, at : at + own_images, :] = values[:, f * wide + g * 128 : f * wide + (g + 1) * 128]
        pl.semaphore_wait(barrier, n_dp + n_fsdp - 2)
        inner = Direct(place, mail, boxes, sems[0:2], "fsdp", block=lambda ref, d: ref.at[d])
        inner.start()
        boxes[place.f] = mail[place.f]
        inner.finish()
        for j in range(MODS):
            for g in range(lanes):
                pieces = []
                for m in range(micro):
                    at = (j * lanes + g) * own_images + m * slots_here
                    pieces += [boxes[f, at : at + slots_here, :] for f in range(n_fsdp)]
                mine[j, :, g * 128 : (g + 1) * 128] = jnp.concatenate(pieces, axis=0).astype(jnp.bfloat16)
        outer = Direct(place, mine, all_mods, sems[2:4])
        tile[...] = squares_ref[...] + more_ref[...]
        beside = Direct(place, tile, columns, sems[4:6])
        outer.start()
        beside.start()
        all_mods[place.dp] = mine[...]
        columns[place.dp] = tile[...]
        high = product[...].astype(jnp.bfloat16)
        rest = (product[...] - high.astype(jnp.float32)).astype(jnp.bfloat16)
        outer.finish()
        beside.finish()
        total = columns[0]
        for d in range(1, n_dp):
            total = total + columns[d]
        for j in range(MODS):
            values = all_mods[:, j].reshape(n_dp * images, wide)
            both = (matmul(high, values) + matmul(rest, values)) * values.astype(jnp.float32)
            for at in range(0, n_dp * images, ROW_STEP):
                for lane in range(0, wide, 128):
                    total = total + both[at : at + ROW_STEP, lane : lane + 128]
        tile[...] = total
        first = Direct(place, tile, tiles, sems[6:8], "fsdp")
        first.start()
        tiles[place.f] = tile[...]
        every = cond[...].reshape(n_dp * images, deep)
        for j in range(MODS):
            grad[j] = matmul_first(every, all_mods[:, j].reshape(n_dp * images, wide))
        first.finish()
        total = tiles[0]
        for f in range(1, n_fsdp):
            total = total + tiles[f]
        norm[0, 0] = jnp.sqrt(jnp.sum(total))
        for fetch in fetches:
            fetch.wait()

    return pl.pallas_call(
        kernel,
        out_shape=[
            jax.ShapeDtypeStruct((MODS, deep, wide), jnp.float32),
            jax.ShapeDtypeStruct((1, 1), jnp.float32),
            *[pltpu.VMEM(state.shape, state.dtype) for state in states],
        ],
        in_specs=[WHOLE] * 6 + [HBM] * len(states),
        out_specs=[WHOLE, pl.BlockSpec(memory_space=pltpu.SMEM)] + [HBM] * len(states),
        scratch_shapes=[
            pltpu.VMEM((n_fsdp, MODS * lanes * own_images, 128), jnp.float32),
            pltpu.VMEM((n_fsdp, MODS * lanes * own_images, 128), jnp.float32),
            pltpu.VMEM((MODS, images, wide), jnp.bfloat16),
            pltpu.VMEM((n_dp, MODS, images, wide), jnp.bfloat16),
            pltpu.VMEM((n_dp, *TILE), jnp.float32),
            pltpu.VMEM(TILE, jnp.float32),
            pltpu.VMEM((n_fsdp, *TILE), jnp.float32),
            pltpu.SemaphoreType.DMA((len(states),)),
            *Direct.scratch(n_fsdp), *Direct.scratch(n_dp), *Direct.scratch(n_dp), *Direct.scratch(n_fsdp),
        ],
        compiler_params=parameters(1, NORM_LIMIT),
    )(sums_first, sums_second, condition, products, squares, more_squares, *states)


def adam_kernel(factor, grad, master, first, second):
    which, rows, columns = master.shape
    step = min(rows, max(64, 131072 // columns))
    block = pl.BlockSpec((1, step, columns), lambda w, r: (w, r, 0))
    root = (1.0 - BETA_TWO**STEP) ** 0.5
    rate = LEARN_RATE * root / (1.0 - BETA_ONE**STEP)

    def kernel(factor_ref, grad_ref, master_ref, first_ref, second_ref, new_ref, copy_ref, moment_ref, square_ref):
        scale = factor_ref[0, 0]
        at = (pl.ds(pl.program_id(0), 1), span(pl.program_id(1), step))
        grad = grad_ref[at]
        moment = BETA_ONE * first_ref[at] + ((1.0 - BETA_ONE) * scale) * grad
        square = BETA_TWO * second_ref[at] + ((1.0 - BETA_TWO) * scale * scale) * (grad * grad)
        moment_ref[...] = moment
        square_ref[...] = square
        below = jnp.sqrt(square) + ADAM_EPS * root
        new = (1.0 - LEARN_RATE * WEIGHT_DECAY) * master_ref[at] - (rate * moment) / below
        new_ref[...] = new
        copy_ref[...] = new.astype(jnp.bfloat16)

    shape = jax.ShapeDtypeStruct(master.shape, jnp.float32)
    return pl.pallas_call(
        kernel,
        grid=(which, rows // step),
        out_shape=[shape, jax.ShapeDtypeStruct(master.shape, jnp.bfloat16), shape, shape],
        in_specs=[pl.BlockSpec(memory_space=pltpu.SMEM)] + [WHOLE] * 4,
        out_specs=[block] * 4,
        compiler_params=pltpu.CompilerParams(vmem_limit_bytes=SMALL_LIMIT),
    )(factor, grad, master, first, second)


def normalize(values):
    average = jnp.mean(values, axis=-1, keepdims=True)
    centred = values - average
    inv_std = lax.rsqrt(jnp.mean(centred * centred, axis=-1, keepdims=True) + NORM_EPS)
    return (centred * inv_std, inv_std)


def normalize_back(grad, normed, inv_std):
    return inv_std * (
        grad
        - jnp.mean(grad, axis=-1, keepdims=True)
        - normed * jnp.mean(grad * normed, axis=-1, keepdims=True)
    )


def body(n_dp, n_fsdp, *arguments):
    tokens, embedding, image_slot, token_mask, cotangent = arguments[:5]
    weights = [w if w.ndim == 3 else w[:, None] for w in arguments[5:]]
    weights = [w.transpose(1, 0, 2) for w in weights]
    masters, firsts, seconds = weights[:5], weights[5:10], weights[10:]
    qkv_w, out_w, up_w, down_w, ada_w = masters
    micro, tok_rows, width = tokens.shape
    own_rows = micro * tok_rows
    image_count = embedding.shape[1] // n_fsdp
    images = micro * n_fsdp * image_count
    own_tokens = tokens.reshape(own_rows, width)
    own_cot = cotangent.reshape(own_rows, width)

    (
        attn_own, mid, hidden2, mods, cond_all, products, codes, codes_g, qkv_low, attended, down_low,
        hidden1_g, qkv_g, out_g, up_g, grad_mlp_g,
    ) = attention_kernel(
        n_dp, n_fsdp, micro, own_tokens, own_cot, image_slot, token_mask, embedding.reshape(images, -1), ada_w, qkv_w, out_w,
        up_w, down_w,
    )
    grad_mid, grad_attn, sums_second, grad_down, squares_down, mlp_part, grad_up = feed_forward_kernel(
        n_dp, n_fsdp, micro, hidden2, mid, attn_own, own_cot, codes, mods, grad_mlp_g, up_g, down_low
    )
    block_out, input_grad, sums_first, grad_up, grad_qkv_w, grad_out, squares = attention_grad_kernel(
        n_dp, n_fsdp, micro, grad_attn, own_tokens, mid, grad_mid, own_cot, codes, mods, codes_g, mlp_part, grad_up,
        qkv_g, out_g, qkv_low, attended, hidden1_g,
    )
    block_out = block_out.reshape(tokens.shape)
    input_grad = input_grad.reshape(tokens.shape)
    grad_ada, grad_norm, *states = norm_kernel(
        n_dp, n_fsdp, micro, sums_first, sums_second, cond_all, products, squares_down, squares,
        (*masters, *firsts, *seconds),
    )
    masters, firsts, seconds = states[:5], states[5:10], states[10:]

    factor = jnp.minimum(1.0, CLIP_AT / grad_norm)
    results = []
    grads = (grad_qkv_w, grad_out, grad_up, grad_down, grad_ada)
    for given, grad, master, first, second in zip(arguments[5:], grads, masters, firsts, seconds):
        for updated in adam_kernel(factor, grad, master, first, second):
            results.append(updated.transpose(1, 0, 2).reshape(given.shape))
    return (block_out, input_grad, *results, grad_norm[0, 0])


def solution(mesh):
    n_dp, n_fsdp = mesh.shape["dp"], mesh.shape["fsdp"]
    rows = P(None, ("dp", "fsdp"), None)
    slots = P(None, ("dp", "fsdp"))
    thick = P("dp", None, "fsdp")
    flat = P("dp", "fsdp")
    weights = (thick, flat, flat, flat, thick)
    updated = tuple(spec for spec in weights for _ in range(4))
    return jax.shard_map(
        functools.partial(body, n_dp, n_fsdp),
        mesh=mesh,
        in_specs=(rows, P(None, "dp", None), slots, slots, rows, *weights, *weights, *weights),
        out_specs=(rows, rows, *updated, P()),
        check_vma=False,
    )
```

```python
import functools

import jax
import jax.numpy as jnp
from jax import lax
from jax.experimental import pallas as pl
from jax.experimental.pallas import tpu as pltpu
from jax.sharding import PartitionSpec as P

HEAD = 128
STEP = 10
MODS = 6
FIRST_KINDS = (0, 1, 5)
OTHER_KINDS = (2, 3, 4)

NORM_EPS = 1e-06
CLIP_AT = 1.0
BETA_ONE = 0.9
BETA_TWO = 0.999
LEARN_RATE = 0.05
WEIGHT_DECAY = 0.1
ADAM_EPS = 1e-08

MESH = pl.DeviceIdType.MESH
VMEM_LIMIT = 62 * 1024 * 1024
SMALL_LIMIT = 16 * 1024 * 1024
NORM_LIMIT = 27 * 1024 * 1024
ROW_STEP = 16


class Place:
    def __init__(self, n_dp, n_fsdp):
        self.n_dp, self.n_fsdp = n_dp, n_fsdp
        self.chips = n_fsdp // 2
        self.grid_a = 2
        self.grid_b = n_dp // 2
        self.dp = lax.axis_index("dp")
        self.f = lax.axis_index("fsdp")
        self.p = self.f // 2
        self.c = self.f % 2
        self.a = self.dp // self.grid_b
        self.b = self.dp % self.grid_b

    def at_chip(self, chip):
        return (self.dp, chip * 2 + self.c)

    def sibling(self):
        return (self.dp, self.p * 2 + 1 - self.c)

    def at_dp(self, dp):
        return (dp, self.f)

    def b_peer(self, i):
        return (self.b + i) % self.grid_b

    def a_peer(self, i):
        return (self.a + i) % self.grid_a


def announce(place, line=False, grid=False, group=False):
    barrier = pltpu.get_barrier_semaphore()
    devices = []
    if group:
        for i in range(1, place.n_fsdp):
            devices.append((place.dp, (place.f + i) % place.n_fsdp))
    elif line:
        devices.append(place.at_chip((place.p + 1) % place.chips))
        devices.append(place.at_chip((place.p + place.chips - 1) % place.chips))
        devices.append(place.sibling())
    if grid:
        for i in range(1, place.n_dp):
            devices.append(place.at_dp((place.dp + i) % place.n_dp))
    for device in devices:
        pl.semaphore_signal(barrier, inc=1, device_id=device, device_id_type=MESH)
    return len(devices)


def enter(place, line=False, grid=False, group=False):
    count = announce(place, line, grid, group)
    pl.semaphore_wait(pltpu.get_barrier_semaphore(), count)


def remote(src, dst, send, recv, device):
    return pltpu.make_async_remote_copy(
        src_ref=src, dst_ref=dst, send_sem=send, recv_sem=recv, device_id=device, device_id_type=MESH
    )


class LineGather:
    @staticmethod
    def scratch(n_fsdp):
        chips = n_fsdp // 2
        return [
            pltpu.SemaphoreType.DMA((2, chips)),
            pltpu.SemaphoreType.DMA((2, chips)),
            pltpu.SemaphoreType.DMA((chips,)),
            pltpu.SemaphoreType.DMA((chips,)),
            pltpu.SemaphoreType.DMA,
        ]

    def __init__(self, place, src, out, sems, block=None):
        self.place, self.src, self.out = place, src, out
        self.send, self.recv, self.csend, self.crecv, self.local = sems
        self.of = block or (lambda ref, d: ref.at[d])

    def _block(self, chip):
        return self.of(self.out, chip * 2 + self.place.c)

    def _hop(self, way, step, first):
        pc = self.place
        chip = pc.p - step if way == 0 else pc.p + step
        target = pc.p + 1 if way == 0 else pc.p - 1
        src = self.src if first else self._block(chip)
        return remote(src, self._block(chip), self.send.at[way, step], self.recv.at[way, step], pc.at_chip(target))

    def _side(self, chip, first=False):
        src = self.src if first else self._block(chip)
        return remote(src, self._block(chip), self.csend.at[chip], self.crecv.at[chip], self.place.sibling())

    def _sends(self, way, step):
        pc = self.place
        if way == 0:
            return (pc.p < pc.chips - 1) & (pc.p >= step)
        return (pc.p > 0) & (pc.p + step <= pc.chips - 1)

    def start_way(self, way):
        @pl.when(self._sends(way, 0))
        def _():
            self._hop(way, 0, True).start()

    def start_here(self):
        pc = self.place
        self._side(pc.p, True).start()
        pltpu.make_async_copy(self.src, self._block(pc.p), self.local).start()

    def start(self):
        self.start_way(0)
        self.start_way(1)
        self.start_here()

    def step(self, step):
        pc = self.place
        for way in range(2):
            chip = pc.p - step if way == 0 else pc.p + step
            here = (chip >= 0) if way == 0 else (chip <= pc.chips - 1)

            @pl.when(here)
            def _():
                remote(
                    self._block(chip), self._block(chip), self.send.at[way, step - 1], self.recv.at[way, step - 1],
                    pc.sibling(),
                ).wait_recv()
                if step < pc.chips - 1:
                    @pl.when(self._sends(way, step))
                    def _():
                        self._hop(way, step, False).start()
                self._side(chip).start()

    def ready(self, chip):
        pc = self.place
        other = self.of(self.out, chip * 2 + 1 - pc.c)
        remote(other, other, self.csend.at[chip], self.crecv.at[chip], pc.sibling()).wait_recv()

        @pl.when(chip == pc.p)
        def _():
            pltpu.make_async_copy(self.src, self._block(pc.p), self.local).wait()

    def drain(self):
        pc = self.place
        for chip in range(pc.chips):
            self._side(chip).wait_send()
        for way in range(2):
            for step in range(pc.chips - 1):
                @pl.when(self._sends(way, step))
                def _():
                    self._hop(way, step, False).wait_send()

    def finish(self):
        for chip in range(self.place.chips):
            self.ready(chip)
        self.drain()


class LineCast:
    @staticmethod
    def scratch(n_fsdp):
        return [pltpu.SemaphoreType.DMA((n_fsdp // 2,)) for _ in range(4)] + [pltpu.SemaphoreType.DMA]

    def __init__(self, place, src, out, sems, block):
        self.place, self.src, self.out, self.of = place, src, out, block
        self.send, self.recv, self.csend, self.crecv, self.local = sems

    def _copy(self, i, coming=False):
        pc = self.place
        chip = (pc.p + pc.chips - i) % pc.chips if coming else pc.p
        return remote(
            self.src, self.of(self.out, chip * 2 + pc.c), self.send.at[i], self.recv.at[i],
            pc.at_chip((pc.p + i) % pc.chips),
        )

    def _side(self, i, coming=False):
        pc = self.place
        chip = (pc.p + pc.chips - i) % pc.chips
        block = self.of(self.out, chip * 2 + (1 - pc.c if coming else pc.c))
        return remote(block if i else self.src, block, self.csend.at[i], self.crecv.at[i], pc.sibling())

    def start(self):
        pc = self.place
        for i in range(1, pc.chips):
            self._copy(i).start()
        self._side(0).start()
        pltpu.make_async_copy(self.src, self.of(self.out, pc.f), self.local).start()

    def step(self):
        for i in range(1, self.place.chips):
            self._copy(i, True).wait_recv()
            self._side(i).start()

    def finish(self):
        pc = self.place
        pltpu.make_async_copy(self.src, self.of(self.out, pc.f), self.local).wait()
        for i in range(pc.chips):
            self._side(i, True).wait_recv()
            self._side(i).wait_send()
        for i in range(1, pc.chips):
            self._copy(i).wait_send()


def row_loop(rows, body, first=0):
    def run(i, carry):
        body(pl.ds(pl.multiple_of(first + i * ROW_STEP, ROW_STEP), ROW_STEP))
        return carry

    lax.fori_loop(0, rows // ROW_STEP, run, 0)


class LineScatter:
    pieces = 4

    @classmethod
    def scratch(cls, n_fsdp, rows, width):
        chips = n_fsdp // 2
        return [
            pltpu.VMEM((chips, rows, width), jnp.bfloat16),
            pltpu.VMEM((chips + 1, rows, width), jnp.bfloat16),
            pltpu.SemaphoreType.DMA((chips,)),
            pltpu.SemaphoreType.DMA((chips,)),
            pltpu.SemaphoreType.DMA((2, chips, cls.pieces)),
            pltpu.SemaphoreType.DMA((2, chips, cls.pieces)),
        ]

    def __init__(self, place, part, out, scratch, mine=None, lag=2):
        self.place, self.part, self.out, self.mine = place, part, out, mine
        self.side, self.inbox, self.csend, self.crecv, self.send, self.recv = scratch
        self.rows = out.shape[0]
        self.piece = self.rows // self.pieces
        self.lag = lag
        self.slots = (place.chips - 1) * self.lag + place.chips * self.pieces

    def _side(self, chip):
        pc = self.place
        return remote(
            self.part.at[chip * 2 + 1 - pc.c], self.side.at[chip], self.csend.at[chip], self.crecv.at[chip], pc.sibling()
        )

    def _hop(self, way, chip, s):
        pc = self.place
        target = pc.p + 1 if way == 0 else pc.p - 1
        rows = pl.ds(pl.multiple_of(s * self.piece, self.piece), self.piece)
        return remote(
            self.side.at[chip, rows], self.inbox.at[chip + 1 - way, rows], self.send.at[way, chip, s],
            self.recv.at[way, chip, s], pc.at_chip(target),
        )

    def start(self):
        def one(k, carry):
            self.offer(self.order(k))
            return carry

        lax.fori_loop(0, self.place.chips, one, 0)

    def offer(self, chip):
        self._side(chip).start()

    def order(self, k):
        pc = self.place
        chips = pc.chips
        after, before = chips - 1 - pc.p, pc.p
        short = jnp.minimum(after, before)
        lone = jnp.maximum(after, before) - short
        rest = jnp.maximum(k - lone, 0)
        near = short - rest // 2
        pair = jnp.where(lax.rem(rest, 2) == 0, pc.p + near, pc.p - near)
        return jnp.where(k < lone, jnp.where(after > before, chips - 1 - k, k), pair)

    def first_slot(self, k):
        pc = self.place
        chips = pc.chips
        chip = self.order(k)
        after = pc.p * self.lag + (chips - 1 - chip) * self.pieces
        before = (chips - 1 - pc.p) * self.lag + chip * self.pieces
        slot = jnp.where(chip > pc.p, after, before)
        return jnp.where((k >= chips - 1) | (chip == pc.p), self.slots, slot)

    def paced(self, compute, pace, then):
        def one(k, slot):
            chip = self.order(k)
            compute(chip)
            self.offer(chip)
            until = jnp.minimum(self.first_slot(k + 1), self.first_slot(k + 2))
            until = jnp.maximum(jnp.minimum(until, (k + 1) * pace), slot)
            self.run(slot, until)
            then(k)
            return until

        return lax.fori_loop(0, self.place.chips, one, jnp.int32(0))

    def beside(self, slot, count, work, every=1):
        def one(i, carry):
            work(i)

            @pl.when(lax.rem(i, every) == every - 1)
            def _():
                self.step(slot + i // every)

            return carry

        lax.fori_loop(0, count, one, 0)
        return slot + count // every

    def run_to(self, slot, end):
        end = jnp.maximum(slot, end)
        self.run(slot, end)
        return end

    def _add(self, chip, s, inboxes, store):
        pc = self.place

        def add(rows):
            if self.mine is None:
                total = self.part[chip * 2 + pc.c, rows, :].astype(jnp.float32)
            else:
                total = self.mine[chip, rows, :].astype(jnp.float32)
            total = total + self.side[chip, rows, :].astype(jnp.float32)
            for way in inboxes:
                total = total + self.inbox[chip + 1 - way, rows, :].astype(jnp.float32)
            store(rows, total)

        row_loop(self.piece, add, s * self.piece)

    def _travel(self, way, t):
        pc = self.place
        chips = pc.chips
        i = t - (pc.p if way == 0 else chips - 1 - pc.p) * self.lag
        k = jnp.clip(i // self.pieces, 0, chips - 1)
        s = lax.rem(jnp.maximum(i, 0), self.pieces)
        chip = chips - 1 - k if way == 0 else k
        going = (i >= 0) & (i < chips * self.pieces) & ((chip > pc.p) if way == 0 else (chip < pc.p))
        first = (pc.p == 0) if way == 0 else (pc.p == chips - 1)

        def store(rows, total):
            self.side[chip, rows, :] = total.astype(jnp.bfloat16)

        @pl.when(going)
        def _():
            @pl.when(s == 0)
            def _():
                self._side(chip).wait_recv()

            @pl.when(first)
            def _():
                self._add(chip, s, (), store)

            @pl.when(jnp.logical_not(first))
            def _():
                self._hop(way, chip, s).wait_recv()
                self._add(chip, s, (way,), store)

            self._hop(way, chip, s).start()

    def step(self, t):
        self._travel(0, t)
        self._travel(1, t)

    def run(self, begin, end):
        def one(t, carry):
            self.step(t)
            return carry

        lax.fori_loop(begin, end, one, 0)

    def finish(self):
        pc = self.place
        chips = pc.chips
        self._side(pc.p).wait_recv()

        def store(rows, total):
            self.out[rows, :] = total

        def piece(s, carry):
            @pl.when(pc.p == 0)
            def _():
                self._hop(1, pc.p, s).wait_recv()
                self._add(pc.p, s, (1,), store)

            @pl.when(pc.p == chips - 1)
            def _():
                self._hop(0, pc.p, s).wait_recv()
                self._add(pc.p, s, (0,), store)

            @pl.when((pc.p > 0) & (pc.p < chips - 1))
            def _():
                self._hop(0, pc.p, s).wait_recv()
                self._hop(1, pc.p, s).wait_recv()
                self._add(pc.p, s, (0, 1), store)

            return carry

        lax.fori_loop(0, self.pieces, piece, 0)
        for chip in range(chips):
            self._side(chip).wait_send()

            def sent(s, carry):
                @pl.when(chip > pc.p)
                def _():
                    self._hop(0, chip, s).wait_send()

                @pl.when(chip < pc.p)
                def _():
                    self._hop(1, chip, s).wait_send()

                return carry

            lax.fori_loop(0, self.pieces, sent, 0)


class GridGather:
    @staticmethod
    def scratch(n_dp):
        na, nb = 2, n_dp // 2
        return [
            pltpu.SemaphoreType.DMA((2, max(nb - 1, 1))),
            pltpu.SemaphoreType.DMA((2, max(nb - 1, 1))),
            pltpu.SemaphoreType.DMA((2, na - 1)),
            pltpu.SemaphoreType.DMA((2, na - 1)),
            pltpu.SemaphoreType.DMA((2, max(nb - 1, 1), na - 1)),
            pltpu.SemaphoreType.DMA((2, max(nb - 1, 1), na - 1)),
            pltpu.SemaphoreType.DMA,
        ]

    def __init__(self, place, src, out, sems):
        self.place, self.src, self.out = place, src, out
        self.bsend, self.brecv, self.asend, self.arecv, self.fsend, self.frecv, self.local = sems
        self.half = src.shape[1] // 2

    def _own(self, h):
        return self.src.at[:, pl.ds(h * self.half, self.half)]

    def _block(self, a, b, h):
        return self.out.at[:, a * self.place.grid_b + b, pl.ds(h * self.half, self.half)]

    def _b_copy(self, i, h, coming):
        pc = self.place
        b = pc.b_peer(pc.grid_b - i) if coming else pc.b
        return remote(
            self._own(h), self._block(pc.a, b, h), self.bsend.at[h, i - 1], self.brecv.at[h, i - 1],
            pc.at_dp(pc.a * pc.grid_b + pc.b_peer(i)),
        )

    def _a_copy(self, i, h, coming):
        pc = self.place
        a = pc.a_peer(pc.grid_a - i) if coming else pc.a
        return remote(
            self._own(h), self._block(a, pc.b, h), self.asend.at[h, i - 1], self.arecv.at[h, i - 1],
            pc.at_dp(pc.a_peer(i) * pc.grid_b + pc.b),
        )

    def _on(self, h, ib, ia, coming):
        pc = self.place
        if h == 0:
            b = pc.b_peer(pc.grid_b - ib)
            a = pc.a_peer(pc.grid_a - ia) if coming else pc.a
            target = pc.at_dp(pc.a_peer(ia) * pc.grid_b + pc.b)
        else:
            a = pc.a_peer(pc.grid_a - ia)
            b = pc.b_peer(pc.grid_b - ib) if coming else pc.b
            target = pc.at_dp(pc.a * pc.grid_b + pc.b_peer(ib))
        block = self._block(a, b, h)
        return remote(block, block, self.fsend.at[h, ib - 1, ia - 1], self.frecv.at[h, ib - 1, ia - 1], target)

    def start(self):
        pc = self.place
        for h in range(2):
            for i in range(1, pc.grid_b):
                self._b_copy(i, h, False).start()
            for i in range(1, pc.grid_a):
                self._a_copy(i, 1 - h, False).start()
        pltpu.make_async_copy(self.src, self.out.at[:, pc.dp], self.local).start()

    def step(self):
        pc = self.place
        for ib in range(1, pc.grid_b):
            self._b_copy(ib, 0, True).wait_recv()
            for ia in range(1, pc.grid_a):
                self._on(0, ib, ia, False).start()
        for ia in range(1, pc.grid_a):
            self._a_copy(ia, 1, True).wait_recv()
            for ib in range(1, pc.grid_b):
                self._on(1, ib, ia, False).start()

    def finish(self):
        pc = self.place
        pltpu.make_async_copy(self.src, self.out.at[:, pc.dp], self.local).wait()
        for ib in range(1, pc.grid_b):
            self._b_copy(ib, 1, True).wait_recv()
        for ia in range(1, pc.grid_a):
            self._a_copy(ia, 0, True).wait_recv()
        for h in range(2):
            for ib in range(1, pc.grid_b):
                for ia in range(1, pc.grid_a):
                    self._on(h, ib, ia, True).wait_recv()
                    self._on(h, ib, ia, False).wait_send()
        for h in range(2):
            for ib in range(1, pc.grid_b):
                self._b_copy(ib, h, False).wait_send()
            for ia in range(1, pc.grid_a):
                self._a_copy(ia, h, False).wait_send()


class GridScatter:
    @staticmethod
    def scratch(n_dp, which, rows, width):
        na, nb = 2, n_dp // 2
        half = rows // 2
        most = max(nb - 1, 1)
        return [
            pltpu.VMEM((most, na, which, half, width), jnp.bfloat16),
            pltpu.VMEM((na - 1, nb, which, half, width), jnp.bfloat16),
            pltpu.VMEM((na - 1, which, half, width), jnp.bfloat16),
            pltpu.VMEM((most, which, half, width), jnp.bfloat16),
            pltpu.VMEM((na - 1, which, half, width), jnp.bfloat16),
            pltpu.VMEM((most, which, half, width), jnp.bfloat16),
            pltpu.SemaphoreType.DMA((most, na)),
            pltpu.SemaphoreType.DMA((most, na)),
            pltpu.SemaphoreType.DMA((na - 1, nb)),
            pltpu.SemaphoreType.DMA((na - 1, nb)),
            pltpu.SemaphoreType.DMA((na - 1,)),
            pltpu.SemaphoreType.DMA((na - 1,)),
            pltpu.SemaphoreType.DMA((most,)),
            pltpu.SemaphoreType.DMA((most,)),
        ]

    def __init__(self, place, part, out, squares, scratch):
        self.place, self.part, self.out, self.squares = place, part, out, squares
        self.box_b, self.box_a, self.sum_b, self.sum_a, self.end_a, self.end_b = scratch[:6]
        self.bs, self.br, self.as_, self.ar, self.eas, self.ear, self.ebs, self.ebr = scratch[6:]
        self.which = out.shape[0]
        self.half = out.shape[1] // 2

    def _part(self, a, b, h):
        return self.part.at[:, a * self.place.grid_b + b, pl.ds(h * self.half, self.half)]

    def _first_b(self, i, j):
        pc = self.place
        return remote(
            self._part(pc.a_peer(j), pc.b_peer(i), 0), self.box_b.at[i - 1, j], self.bs.at[i - 1, j],
            self.br.at[i - 1, j], pc.at_dp(pc.a * pc.grid_b + pc.b_peer(i)),
        )

    def _first_a(self, i, j):
        pc = self.place
        return remote(
            self._part(pc.a_peer(i), pc.b_peer(j), 1), self.box_a.at[i - 1, j], self.as_.at[i - 1, j],
            self.ar.at[i - 1, j], pc.at_dp(pc.a_peer(i) * pc.grid_b + pc.b),
        )

    def _second_a(self, i):
        pc = self.place
        return remote(
            self.sum_b.at[i - 1], self.end_a.at[i - 1], self.eas.at[i - 1], self.ear.at[i - 1],
            pc.at_dp(pc.a_peer(i) * pc.grid_b + pc.b),
        )

    def _second_b(self, i):
        pc = self.place
        return remote(
            self.sum_a.at[i - 1], self.end_b.at[i - 1], self.ebs.at[i - 1], self.ebr.at[i - 1],
            pc.at_dp(pc.a * pc.grid_b + pc.b_peer(i)),
        )

    def _firsts_b(self):
        pc = self.place
        return [(i, j) for j in list(range(1, pc.grid_a)) + [0] for i in range(1, pc.grid_b)]

    def _firsts_a(self):
        pc = self.place
        return [(i, j) for j in list(range(1, pc.grid_b)) + [0] for i in range(1, pc.grid_a)]

    def start(self):
        for (ib, jb), (ia, ja) in zip(self._firsts_b(), self._firsts_a(), strict=False):
            self._first_b(ib, jb).start()
            self._first_a(ia, ja).start()
        shared = min(len(self._firsts_b()), len(self._firsts_a()))
        for i, j in self._firsts_b()[shared:]:
            self._first_b(i, j).start()
        for i, j in self._firsts_a()[shared:]:
            self._first_a(i, j).start()

    def _low(self, rows):
        return pl.ds(pl.multiple_of(self.half + rows.start, ROW_STEP), ROW_STEP)

    def _sum_b(self, j):
        pc = self.place
        for i in range(1, pc.grid_b):
            self._first_b(i, j).wait_recv()
        mine = pc.a_peer(j) * pc.grid_b + pc.b

        def add(rows):
            for w in range(self.which):
                total = self.part[w, mine, rows, :].astype(jnp.float32)
                for i in range(1, pc.grid_b):
                    total = total + self.box_b[i - 1, j, w, rows, :].astype(jnp.float32)
                if j == 0:
                    self.out[w, rows, :] = total
                else:
                    self.sum_b[j - 1, w, rows, :] = total.astype(jnp.bfloat16)

        row_loop(self.half, add)
        if j:
            self._second_a(j).start()

    def _sum_a(self, j):
        pc = self.place
        for i in range(1, pc.grid_a):
            self._first_a(i, j).wait_recv()
        mine = pc.a * pc.grid_b + pc.b_peer(j)

        def add(rows):
            for w in range(self.which):
                total = self.part[w, mine, self._low(rows), :].astype(jnp.float32)
                for i in range(1, pc.grid_a):
                    total = total + self.box_a[i - 1, j, w, rows, :].astype(jnp.float32)
                if j == 0:
                    self.out[w, self._low(rows), :] = total
                else:
                    self.sum_a[j - 1, w, rows, :] = total.astype(jnp.bfloat16)

        row_loop(self.half, add)
        if j:
            self._second_b(j).start()

    def step(self):
        pc = self.place
        for j in range(1, max(pc.grid_a, pc.grid_b)):
            if j < pc.grid_a:
                self._sum_b(j)
            if j < pc.grid_b:
                self._sum_a(j)

    def step_own(self):
        self._sum_b(0)
        self._sum_a(0)

    def finish(self):
        pc = self.place
        for i in range(1, pc.grid_a):
            self._second_a(i).wait_recv()
        for i in range(1, pc.grid_b):
            self._second_b(i).wait_recv()
        self.squares[...] = jnp.zeros_like(self.squares)

        def tile(total):
            total = total * total
            folded = total[:, :128]
            for at in range(128, total.shape[1], 128):
                folded = folded + total[:, at : at + 128]
            return folded

        def add(rows):
            low = self._low(rows)
            for w in range(self.which):
                total = self.out[w, rows, :]
                for i in range(1, pc.grid_a):
                    total = total + self.end_a[i - 1, w, rows, :].astype(jnp.float32)
                self.out[w, rows, :] = total
                self.squares[...] += tile(total)
                total = self.out[w, low, :]
                for i in range(1, pc.grid_b):
                    total = total + self.end_b[i - 1, w, rows, :].astype(jnp.float32)
                self.out[w, low, :] = total
                self.squares[...] += tile(total)

        row_loop(self.half, add)
        for i, j in self._firsts_b():
            self._first_b(i, j).wait_send()
        for i, j in self._firsts_a():
            self._first_a(i, j).wait_send()
        for i in range(1, pc.grid_a):
            self._second_a(i).wait_send()
        for i in range(1, pc.grid_b):
            self._second_b(i).wait_send()


class Direct:
    @staticmethod
    def scratch(n):
        return [pltpu.SemaphoreType.DMA((n - 1,)), pltpu.SemaphoreType.DMA((n - 1,))]

    def __init__(self, place, src, out, sems, axis="dp", block=None, to=None):
        self.place, self.src, self.out = place, src, out
        self.send, self.recv = sems
        self.n = place.n_dp if axis == "dp" else place.n_fsdp
        self.me = place.dp if axis == "dp" else place.f
        self.axis = axis
        self.of = block or (lambda ref, d: ref)
        self.to = to or (lambda ref, d: ref.at[d])

    def _device(self, other):
        return self.place.at_dp(other) if self.axis == "dp" else (self.place.dp, other)

    def _copy(self, i, coming=False):
        other = (self.me + i) % self.n
        origin = (self.me + self.n - i) % self.n if coming else self.me
        return remote(
            self.of(self.src, other), self.to(self.out, origin), self.send.at[i - 1], self.recv.at[i - 1], self._device(other)
        )

    def start(self):
        for i in range(1, self.n):
            self._copy(i).start()

    def finish(self):
        for i in range(1, self.n):
            self._copy(i, True).wait_recv()
            self._copy(i).wait_send()


def split_refs(refs, counts):
    out, at = [], 0
    for count in counts:
        out.append(refs[at : at + count])
        at += count
    return out


HBM = pl.BlockSpec(memory_space=pl.ANY)
WHOLE = pl.BlockSpec(memory_space=pltpu.VMEM)
TILE = (ROW_STEP, 128)


def parameters(collective_id, limit=VMEM_LIMIT):
    return pltpu.CompilerParams(collective_id=collective_id, has_side_effects=True, vmem_limit_bytes=limit)


def matmul(left, right):
    return jnp.dot(left, right, preferred_element_type=jnp.float32)


def matmul_last(left, right):
    return lax.dot_general(left, right, (((1,), (1,)), ((), ())), preferred_element_type=jnp.float32)


def matmul_first(left, right):
    return lax.dot_general(left, right, (((0,), (0,)), ((), ())), preferred_element_type=jnp.float32)


def loop(count, work):
    def one(i, carry):
        work(i)
        return carry

    lax.fori_loop(0, count, one, 0)


def span(i, size):
    return pl.ds(pl.multiple_of(i * size, size), size)


def chip_rows(ref, chip):
    pair = ref[span(chip, 2)]
    return pair.reshape(-1, pair.shape[-1])


def pair_mask(codes_ref, chip, rows):
    pair = [codes_ref[chip * 2 + i] for i in range(2)]
    query = jnp.floor(jnp.concatenate([block[:rows] for block in pair], axis=0))
    query = jnp.concatenate([query] * (2 * rows // 128), axis=1)
    key = jnp.concatenate([block[rows : rows + 1] for block in pair], axis=1)
    shape = (2 * rows, 2 * rows)
    same = lax.broadcasted_iota(jnp.int32, shape, 0) == lax.broadcasted_iota(jnp.int32, shape, 1)
    return (query == key) | same


class Rows:
    def __init__(self, place, codes, mods, micro, rows, slots_here):
        self.place, self.codes, self.mods = place, codes, mods
        self.micro, self.tok_rows, self.slots_here = micro, rows // micro, slots_here

    def tiles(self, work):
        for m in range(self.micro):
            row_loop(self.tok_rows, functools.partial(work, m), m * self.tok_rows)

    def slot_live(self, m, rows):
        column = self.codes[rows, :][:, :1]
        number = jnp.floor(column)
        first = ((self.place.f * self.micro + m) * self.slots_here).astype(jnp.float32)
        return number - first, jnp.where(column == number, 1.0, 0.0)

    def pick(self, j, m, slot):
        at = m * self.slots_here
        picked = self.mods[j, at : at + 1, :]
        for i in range(1, self.slots_here):
            picked = jnp.where(slot == i, self.mods[j, at + i : at + i + 1, :], picked)
        return picked

    def add_up(self, out, j, m, slot, values):
        for i in range(self.slots_here):
            at = m * self.slots_here + i
            chosen = jnp.where(slot == i, values, 0.0)
            out[j, at : at + 1, :] += jnp.sum(chosen, axis=0, keepdims=True)


def cast_rows(src, dst):
    for w in range(src.shape[0]):
        def tile(rows):
            dst[w, rows, :] = src[w, rows, :].astype(dst.dtype)

        row_loop(src.shape[1], tile)


def attention_probs(query, key, allowed):
    scores = jnp.where(allowed, matmul_last(query, key) * HEAD ** (-0.5), -1e30)
    raw = jnp.exp(scores - jnp.max(scores, axis=-1, keepdims=True))
    return raw / jnp.sum(raw, axis=-1, keepdims=True)


def attention_kernel(n_dp, n_fsdp, micro, tokens, cotangent, image_slot, token_mask, embedding, ada, qkv, out_w, up, down):
    low, f32 = jnp.bfloat16, jnp.float32
    images = embedding.shape[0]
    rows, width = tokens.shape
    deep, wide = ada.shape[1:]
    which, _, head_columns = qkv.shape
    slots_here = images // (micro * n_fsdp)
    own_images = micro * slots_here
    line = LineGather.scratch(n_fsdp)
    grid = GridGather.scratch(n_dp)
    direct = Direct.scratch(n_dp)
    scatter_got = LineScatter.scratch(n_fsdp, rows, width)
    counts = [len(line)] * 3 + [len(grid)] * 3 + [len(direct)] * 5 + [len(LineCast.scratch(n_fsdp)), len(scatter_got)]
    weights = (qkv, out_w, up, down, ada)
    pair = 2 * rows

    def kernel(
        tok, cot, slot_ref, mask_ref, emb, ada_f, qkv_f, out_f, up_f, down_f,
        attn_own, mid, hidden2, mods_own, cond_g, products, cod, cod_g, qkv_low, attended, down_low,
        hidden_out, qkv_out, out_out, up_g, gmlp_g,
        cond, parts, boxes, mail_first, mail, inbox, mods_g, averages, inv_stds, product, products_g, gmlp, part, hidden_g, qkv_g, out_g,
        qkv_s, out_s, up_s, down_s, ada_s, qkv_l, out_l, up_l, moves, *rest,
    ):
        sems = split_refs(rest, counts)
        place = Place(n_dp, n_fsdp)
        fetches = [
            pltpu.make_async_copy(ref, stage, moves.at[i])
            for i, (ref, stage) in enumerate(
                ((qkv_f, qkv_s), (out_f, out_s), (up_f, up_s), (down_f, down_s), (ada_f, ada_s))
            )
        ]
        for i in (0, 1, 4, 2, 3):
            fetches[i].start()
        present = announce(place, True, True, True)
        level = emb[...].astype(f32)
        level = (level / (1.0 + jnp.exp(-level))).astype(low)
        for d in range(n_dp):
            cond[d] = level[:, d * deep : (d + 1) * deep]
        number = jnp.concatenate(
            [slot_ref[m : m + 1, :].astype(f32) + (m * slots_here) for m in range(micro)], axis=1
        )
        number = number + ((place.f * micro) * slots_here).astype(f32)
        live = jnp.concatenate([mask_ref[m : m + 1, :].astype(f32) for m in range(micro)], axis=1)
        cod[:rows, :] = jnp.transpose(jnp.broadcast_to(jnp.where(live > 0.5, number, number + 0.25), (rows, rows)))
        cod[rows:, :] = jnp.broadcast_to(jnp.where(live > 0.5, number, -1.0), (8, rows))
        own = Rows(place, cod, mods_own, micro, rows, slots_here)
        fetches[0].wait()
        cast_rows(qkv_s, qkv_l)
        fetches[1].wait()
        cast_rows(out_s, out_l)
        pl.semaphore_wait(pltpu.get_barrier_semaphore(), present)
        conds = Direct(place, cond, cond_g, sems[6], block=lambda ref, d: ref.at[d])
        conds.start()
        token_line = LineGather(place, tok, hidden_g, sems[1])
        code_line = LineGather(place, cod, cod_g, sems[0])
        token_line.start()
        code_line.start()
        grids = [GridGather(place, qkv_l, qkv_g, sems[3]), GridGather(place, out_l, out_g, sems[4])]
        cond_g[place.dp] = cond[place.dp]
        fetches[4].wait()
        conds.finish()
        every = cond_g[...].reshape(n_dp * images, deep)

        def project(kinds):
            for j, kind in kinds:
                parts[:, j] = matmul(every, ada_s[kind].astype(low)).reshape(n_dp, images, wide)

        def add_parts(kinds, letter):
            for j in kinds:
                total = parts[place.dp, j]
                for i in range(1, n_dp):
                    total = total + boxes[(place.dp + i) % n_dp, j]
                for f in range(n_fsdp):
                    for m in range(micro):
                        at = (m * n_fsdp + f) * slots_here
                        letter[f, j - kinds[0], m * slots_here : (m + 1) * slots_here, :] = total[at : at + slots_here]

        first_sums = Direct(
            place, parts, boxes, sems[7], block=lambda ref, d: ref.at[d, 0:3], to=lambda ref, d: ref.at[d, 0:3]
        )
        other_sums = Direct(
            place, parts, boxes, sems[8], block=lambda ref, d: ref.at[d, 3:MODS], to=lambda ref, d: ref.at[d, 3:MODS]
        )
        project(list(enumerate(FIRST_KINDS)))
        first_sums.start()
        for gather in grids:
            gather.start()
        project(list(enumerate(OTHER_KINDS, 3)))
        product[...] = matmul_last(every, every)

        def statistics(chip):
            token_line.ready(chip)
            for i in range(2):
                device = chip * 2 + i

                def tile(at):
                    values = hidden_g[device, at, :].astype(f32)
                    average = jnp.mean(values, axis=-1, keepdims=True)
                    centred = values - average
                    inv_std = lax.rsqrt(jnp.mean(centred * centred, axis=-1, keepdims=True) + NORM_EPS)
                    averages[device, at, :] = jnp.broadcast_to(average, (ROW_STEP, 128))
                    inv_stds[device, at, :] = jnp.broadcast_to(inv_std, (ROW_STEP, 128))

                row_loop(rows, tile)

        def statistics_at(distance):
            def side(i):
                chip = place.p + (1 - 2 * i) * distance

                @pl.when((chip >= 0) & (chip < place.chips))
                def _():
                    statistics(chip)

            loop(2 if distance else 1, side)

        statistics_at(0)
        first_sums.finish()
        add_parts((0, 1, 2), mail_first)
        mods_line = LineCast(
            place, mail_first, mods_g, sems[11],
            block=lambda ref, d: ref.at[:, :, :, pl.ds(pl.multiple_of(d * wide, wide), wide)],
        )
        mods_line.start()
        token_line.step(1)
        code_line.step(1)
        fetches[2].wait()
        cast_rows(up_s, up_l)
        fetches[3].wait()
        cast_rows(down_s, down_low)
        crosses = Direct(place, product, products_g, sems[10])
        products_g[place.dp] = product[...]
        mods_line.step()
        ups = GridGather(place, up_l, up_g, sems[5])
        letters = Direct(place, mail, inbox, sems[9], "fsdp", block=lambda ref, d: ref.at[d])
        gmlp_line = LineGather(place, gmlp, gmlp_g, sems[2])

        def branch_grad(m, at):
            slot, alive = own.slot_live(m, at)
            gmlp[at, :] = (cot[at, :].astype(f32) * alive * own.pick(5, m, slot)).astype(low)

        mods_line.finish()
        for j, kind in enumerate(FIRST_KINDS):
            mods_own[kind] = mods_g[place.f, j]
        own.tiles(branch_grad)
        gmlp_line.start_here()
        for step in range(2, place.chips + 1):
            if step < place.chips:
                token_line.step(step)
                code_line.step(step)
            if step == 2:
                for gather in grids:
                    gather.step()
            statistics_at(step - 1)

            @pl.when((place.p + 1 == step) | ((place.p + 1 < step) & (step == 2)))
            def _():
                gmlp_line.start_way(0)

            @pl.when((place.chips - place.p == step) | ((place.chips - place.p < step) & (step == 2)))
            def _():
                gmlp_line.start_way(1)

        for gather in grids:
            gather.finish()
        other_sums.start()
        crosses.start()
        ups.start()
        token_line.drain()
        code_line.finish()
        leaves = [
            pltpu.make_async_copy(ref, out, moves.at[len(weights) + i])
            for i, (ref, out) in enumerate(((qkv_g, qkv_out), (out_g, out_out), (hidden_g, hidden_out)))
        ]
        for leave in leaves[:2]:
            leave.start()
        scatter = LineScatter(place, part, attn_own, sems[12])

        def norm_block(chip):
            for i in range(2):
                device = chip * 2 + i
                for m in range(micro):
                    first = ((device * micro + m) * slots_here).astype(f32)

                    def table(j, slot):
                        at = m * slots_here
                        picked = mods_g[device, j, at : at + 1, :]
                        for k in range(1, slots_here):
                            picked = jnp.where(slot == k, mods_g[device, j, at + k : at + k + 1, :], picked)
                        return picked

                    def tile(at):
                        slot = jnp.floor(cod_g[device, at, :][:, :1]) - first
                        centred = hidden_g[device, at, :].astype(f32) - averages[device, at, :][:, :1]
                        normed = centred * inv_stds[device, at, :][:, :1]
                        hidden_g[device, at, :] = (normed * (1.0 + table(1, slot)) + table(0, slot)).astype(low)

                    row_loop(rows // micro, tile, m * (rows // micro))

        def compute(chip):
            at = span(chip, pair)
            norm_block(chip)
            values = chip_rows(hidden_g, chip)
            for w in range(which):
                weight = qkv_g[w].reshape(width, head_columns)
                qkv_low[w, at, :] = matmul(values, weight).astype(low)
            allowed = pair_mask(cod_g, chip, rows)
            for h in range(head_columns // HEAD):
                head = slice(h * HEAD, (h + 1) * HEAD)
                probs = attention_probs(qkv_low[0, at, head], qkv_low[1, at, head], allowed)
                attended[at, head] = matmul(probs.astype(low), qkv_low[2, at, head]).astype(low)
            heads = attended[at, :]
            weight_rows = out_g.shape[2]
            for d in range(n_dp):
                piece = matmul_last(heads, out_g[0, d]).astype(low).reshape(2, rows, weight_rows)
                part[span(chip, 2), :, d * weight_rows : (d + 1) * weight_rows] = piece

        def then(k):
            @pl.when(k == 1)
            def _():
                gmlp_line.step(1)

        slot = scatter.paced(compute, 1, then)
        leaves[2].start()
        for step in range(2, place.chips):
            gmlp_line.step(step)
            slot = scatter.run_to(slot, scatter.slots * step // (place.chips + 1))
            if step == place.chips // 2:
                other_sums.finish()
                add_parts((3, 4, 5), mail)
                letters.start()
                inbox[place.f] = mail[place.f]
                ups.step()
                crosses.finish()
                total = products_g[0]
                for d in range(1, n_dp):
                    total = total + products_g[d]
                products[...] = total
        scatter.run_to(slot, scatter.slots)
        scatter.finish()
        letters.finish()
        for f in range(n_fsdp):
            for j, kind in enumerate(OTHER_KINDS):
                mods_own[kind, :, f * wide : (f + 1) * wide] = inbox[f, j]

        def second_norm(m, at):
            slot, _ = own.slot_live(m, at)
            values = tok[at, :].astype(f32) + own.pick(2, m, slot) * attn_own[at, :]
            mid[at, :] = values
            normed, _ = normalize(values)
            hidden2[at, :] = (normed * (1.0 + own.pick(4, m, slot)) + own.pick(3, m, slot)).astype(low)

        own.tiles(second_norm)
        gmlp_line.finish()
        ups.finish()
        for leave in leaves:
            leave.wait()

    def gathered(w):
        return jax.ShapeDtypeStruct((w.shape[0], n_dp, *w.shape[1:]), low)

    return pl.pallas_call(
        kernel,
        out_shape=[
            jax.ShapeDtypeStruct((rows, width), f32),
            jax.ShapeDtypeStruct((rows, width), f32),
            jax.ShapeDtypeStruct((rows, width), low),
            jax.ShapeDtypeStruct((MODS, own_images, width), f32),
            jax.ShapeDtypeStruct((n_dp, images, deep), low),
            jax.ShapeDtypeStruct((n_dp * images, n_dp * images), f32),
            jax.ShapeDtypeStruct((rows + 8, rows), f32),
            jax.ShapeDtypeStruct((n_fsdp, rows + 8, rows), f32),
            jax.ShapeDtypeStruct((which, n_fsdp * rows, head_columns), low),
            jax.ShapeDtypeStruct((n_fsdp * rows, head_columns), low),
            jax.ShapeDtypeStruct(down.shape, low),
            jax.ShapeDtypeStruct((n_fsdp, rows, width), low),
            gathered(qkv),
            gathered(out_w),
            gathered(up),
            jax.ShapeDtypeStruct((n_fsdp, rows, width), low),
        ],
        in_specs=[WHOLE] * 5 + [HBM] * 5,
        out_specs=[WHOLE] * 11 + [HBM] * 5,
        scratch_shapes=[
            pltpu.VMEM((n_dp, images, deep), low),
            pltpu.VMEM((n_dp, MODS, images, wide), f32),
            pltpu.VMEM((n_dp, MODS, images, wide), f32),
            pltpu.VMEM((n_fsdp, 3, own_images, wide), f32),
            pltpu.VMEM((n_fsdp, 3, own_images, wide), f32),
            pltpu.VMEM((n_fsdp, 3, own_images, wide), f32),
            pltpu.VMEM((n_fsdp, 3, own_images, width), f32),
            pltpu.VMEM((n_fsdp, rows, 128), f32),
            pltpu.VMEM((n_fsdp, rows, 128), f32),
            pltpu.VMEM((n_dp * images, n_dp * images), f32),
            pltpu.VMEM((n_dp, n_dp * images, n_dp * images), f32),
            pltpu.VMEM((rows, width), low),
            pltpu.VMEM((n_fsdp, rows, width), low),
            pltpu.VMEM((n_fsdp, rows, width), low),
            pltpu.VMEM((which, n_dp, *qkv.shape[1:]), low),
            pltpu.VMEM((1, n_dp, *out_w.shape[1:]), low),
            *[pltpu.VMEM(w.shape, f32) for w in weights],
            *[pltpu.VMEM(w.shape, low) for w in weights[:3]],
            pltpu.SemaphoreType.DMA((len(weights) + 3,)),
            *line, *line, *line, *grid, *grid, *grid, *direct, *direct, *direct,
            *Direct.scratch(n_fsdp), *direct, *LineCast.scratch(n_fsdp), *scatter_got,
        ],
        compiler_params=parameters(0),
    )(tokens, cotangent, image_slot, token_mask, embedding, ada, qkv, out_w, up, down)


def gelu_parts(v):
    root = 0.7978845608028654
    square = v * v
    bent = jnp.tanh(root * (v + 0.044715 * v * square))
    value = 0.5 * v * (1.0 + bent)
    slope = 0.5 * (1.0 + bent) + (0.5 * root) * v * (1.0 - bent * bent) * (1.0 + (3.0 * 0.044715) * square)
    return value, slope


COLUMN_STEP = 256


def feed_forward_kernel(n_dp, n_fsdp, micro, hidden, mid, attn_own, cotangent, codes, mods, grad_mlp, up_g, down):
    low, f32 = jnp.bfloat16, jnp.float32
    rows, width = hidden.shape
    _, weight_rows, columns = down.shape
    tokens = n_fsdp * rows
    pair = 2 * rows
    own_images = mods.shape[1]
    line = LineGather.scratch(n_fsdp)
    grid = GridGather.scratch(n_dp)
    scatter_got = LineScatter.scratch(n_fsdp, rows, width)
    grads_got = GridScatter.scratch(n_dp, 1, weight_rows, columns)
    counts = [len(line), len(grid), len(scatter_got), len(grads_got)]
    tiles = columns // COLUMN_STEP
    row_tiles = weight_rows // COLUMN_STEP

    def kernel(
        hid, mid_ref, attn_ref, cot, cod, mods_ref, down_ref, gmlp_ref, up_ref,
        grad_mid, grad_attn, sums_own, grad_down, squares, mlp_part, grad_up,
        gmlp, up, hidden_g, down_g, upper, activ, grad_upper, part, gdown, grad_h2, stage, stage_up,
        moves, out_sem, up_sem, *rest,
    ):
        sems = split_refs(rest, counts)
        place = Place(n_dp, n_fsdp)
        fetch_up = pltpu.make_async_copy(up_ref, up, moves.at[0])
        fetch_gmlp = pltpu.make_async_copy(gmlp_ref, gmlp, moves.at[1])
        fetch_up.start()
        fetch_gmlp.start()
        enter(place, True, True)
        hidden_line = LineGather(place, hid, hidden_g, sems[0])
        downs = GridGather(place, down_ref, down_g, sems[1])
        hidden_line.start()
        downs.start()
        fetch_up.wait()

        def forward(chip):
            at = span(chip, pair)
            hidden_line.ready(chip)

            def tile(i):
                to = span(i, COLUMN_STEP)
                values = chip_rows(hidden_g, chip)
                total = jnp.zeros((pair, COLUMN_STEP), f32)
                for d in range(n_dp):
                    total = total + matmul(values[:, d * weight_rows : (d + 1) * weight_rows], up[0, d, :, to])
                upper[at, to] = total
                activ[at, to] = gelu_parts(total)[0].astype(low)

            loop(tiles, tile)

        def forward_at(distance):
            def side(i):
                chip = place.p + (1 - 2 * i) * distance

                @pl.when((chip >= 0) & (chip < place.chips))
                def _():
                    forward(chip)

            loop(2 if distance else 1, side)

        for step in range(1, place.chips):
            hidden_line.step(step)
            if step == place.chips // 2:
                downs.step()
            forward_at(step - 1)
        forward_at(place.chips - 1)
        fetch_gmlp.wait()
        downs.finish()
        scatter = LineScatter(place, part, grad_h2, sems[2])
        grads = GridScatter(place, gdown, grad_down, squares, sems[3])

        def backward(chip):
            at = span(chip, pair)

            def tile(i):
                to = span(i, COLUMN_STEP)
                values = chip_rows(gmlp, chip)
                total = jnp.zeros((pair, COLUMN_STEP), f32)
                for d in range(n_dp):
                    total = total + matmul(values[:, d * weight_rows : (d + 1) * weight_rows], down_g[0, d, :, to])
                grad_upper[at, to] = (total * gelu_parts(upper[at, to])[1]).astype(low)

            loop(tiles, tile)
            values = grad_upper[at, :]
            for d in range(n_dp):
                piece = matmul_last(values, up[0, d]).astype(low).reshape(2, rows, weight_rows)
                part[span(chip, 2), :, d * weight_rows : (d + 1) * weight_rows] = piece

        def down_tile(i):
            d, r = i // row_tiles, lax.rem(i, row_tiles)
            left = gmlp[:, :, span(i, COLUMN_STEP)].reshape(tokens, COLUMN_STEP)
            gdown[0, d, span(r, COLUMN_STEP), :] = matmul_first(left, activ[...]).astype(low)

        def then(k):
            @pl.when(k == 0)
            def _():
                loop(n_dp * row_tiles, down_tile)
                grads.start()

        slot = scatter.paced(backward, 2, then)

        def up_copy(i, d, r):
            return pltpu.make_async_copy(
                stage_up.at[lax.rem(i, 2)], grad_up.at[0, d, span(r, COLUMN_STEP)], up_sem.at[lax.rem(i, 2)]
            )

        def up_tile(i):
            d, r = i // row_tiles, lax.rem(i, row_tiles)

            @pl.when(i >= 2)
            def _():
                up_copy(i, 0, 0).wait()

            left = hidden_g[:, :, span(i, COLUMN_STEP)].reshape(tokens, COLUMN_STEP)
            stage_up[lax.rem(i, 2)] = matmul_first(left, grad_upper[...]).astype(low)
            up_copy(i, d, r).start()

        slot = scatter.beside(slot, n_dp * row_tiles, up_tile, 4)
        up_copy(0, 0, 0).wait()
        up_copy(1, 0, 0).wait()
        grads.step()

        def mlp_copy(chip):
            to = lax.rem(chip, 2)
            return pltpu.make_async_copy(stage.at[to], mlp_part.at[span(chip, 2)], out_sem.at[to])

        def mlp_tile(chip):
            @pl.when(chip >= 2)
            def _():
                mlp_copy(chip).wait()

            values = activ[span(chip, pair), :]
            for d in range(n_dp):
                piece = matmul_last(values, down_g[0, d]).astype(low).reshape(2, rows, weight_rows)
                stage[lax.rem(chip, 2), :, :, d * weight_rows : (d + 1) * weight_rows] = piece
            mlp_copy(chip).start()

        slot = scatter.beside(slot, place.chips, mlp_tile)
        mlp_copy(0).wait()
        mlp_copy(1).wait()
        scatter.run_to(slot, scatter.slots)
        grads.step_own()
        scatter.finish()
        own = Rows(place, cod, mods_ref, micro, rows, own_images // micro)
        sums_own[...] = jnp.zeros_like(sums_own)

        def norm_grad(m, at):
            slot, alive = own.slot_live(m, at)
            normed, inv_std = normalize(mid_ref[at, :])
            grad = grad_h2[at, :]
            before = normalize_back(grad * (1.0 + own.pick(4, m, slot)), normed, inv_std)
            total = cot[at, :].astype(f32) * alive + before
            grad_mid[at, :] = total
            grad_attn[at, :] = (total * own.pick(2, m, slot)).astype(low)
            own.add_up(sums_own, 0, m, slot, total * attn_ref[at, :])
            own.add_up(sums_own, 1, m, slot, grad)
            own.add_up(sums_own, 2, m, slot, grad * normed)

        own.tiles(norm_grad)
        grads.finish()
        hidden_line.drain()

    return pl.pallas_call(
        kernel,
        out_shape=[
            jax.ShapeDtypeStruct((rows, width), f32),
            jax.ShapeDtypeStruct((rows, width), low),
            jax.ShapeDtypeStruct((3, own_images, width), f32),
            jax.ShapeDtypeStruct((1, weight_rows, columns), f32),
            jax.ShapeDtypeStruct(TILE, f32),
            jax.ShapeDtypeStruct((n_fsdp, rows, width), low),
            jax.ShapeDtypeStruct((1, n_dp, weight_rows, columns), low),
        ],
        in_specs=[WHOLE] * 6 + [HBM] * 3,
        out_specs=[WHOLE] * 5 + [HBM] * 2,
        scratch_shapes=[
            pltpu.VMEM((n_fsdp, rows, width), low),
            pltpu.VMEM((1, n_dp, weight_rows, columns), low),
            pltpu.VMEM((n_fsdp, rows, width), low),
            pltpu.VMEM((1, n_dp, weight_rows, columns), low),
            pltpu.VMEM((tokens, columns), f32),
            pltpu.VMEM((tokens, columns), low),
            pltpu.VMEM((tokens, columns), low),
            pltpu.VMEM((n_fsdp, rows, width), low),
            pltpu.VMEM((1, n_dp, weight_rows, columns), low),
            pltpu.VMEM((rows, width), f32),
            pltpu.VMEM((2, 2, rows, width), low),
            pltpu.VMEM((2, COLUMN_STEP, columns), low),
            pltpu.SemaphoreType.DMA((2,)),
            pltpu.SemaphoreType.DMA((2,)),
            pltpu.SemaphoreType.DMA((2,)),
            *line, *grid, *scatter_got, *grads_got,
        ],
        compiler_params=parameters(2),
    )(hidden, mid, attn_own, cotangent, codes, mods, down, grad_mlp, up_g)


def attention_grad_kernel(
    n_dp, n_fsdp, micro, grad_attn, tokens_own, mid, grad_mid, cotangent, codes, mods, codes_g, mlp_part, grad_up, qkv_g,
    out_g, qkv_low, attended, hidden_g,
):
    low, f32 = jnp.bfloat16, jnp.float32
    rows, width = grad_attn.shape
    which, _, weight_rows, head_columns = qkv_g.shape
    tokens = n_fsdp * rows
    pair = 2 * rows
    chips = n_fsdp // 2
    own_images = mods.shape[1]
    line = LineGather.scratch(n_fsdp)
    scatter_got = LineScatter.scratch(n_fsdp, rows, width)
    up_shape = (1, *grad_up.shape[2:])
    up_got = GridScatter.scratch(n_dp, *up_shape)
    qkv_got = GridScatter.scratch(n_dp, which, weight_rows, head_columns)
    out_got = GridScatter.scratch(n_dp, 1, weight_rows, head_columns)
    counts = [len(line), len(scatter_got), len(scatter_got), len(up_got), len(qkv_got), len(out_got)]
    row_tiles = weight_rows // COLUMN_STEP

    def kernel(
        ga, tok, mid_ref, gmid, cot, cod, mods_ref, cod_g, mlp_ref, gup_ref, qkv_wr, out_wr, qkv_lr, att_r, hid_r,
        block_out, input_grad, sums_own, grad_up_own, grad_qkv_own, grad_out_own, squares,
        ga_g, gqkv, gqkv_w, gout_w, mlp_own, grad_h1, tile_up, tile_qkv, tile_out,
        mine, gup, qkv_w, out_w, qkv_ref, att, hid_g, moves, mine_sem, *rest,
    ):
        sems = split_refs(rest, counts)
        place = Place(n_dp, n_fsdp)
        fetches = [
            pltpu.make_async_copy(ref, to, moves.at[i])
            for i, (ref, to) in enumerate(
                ((gup_ref, gup), (att_r, att), (out_wr, out_w), (qkv_lr, qkv_ref), (qkv_wr, qkv_w), (hid_r, hid_g))
            )
        ]
        terms = [
            pltpu.make_async_copy(mlp_ref.at[chip * 2 + place.c], mine.at[chip], mine_sem.at[chip])
            for chip in range(chips)
        ]
        fetches[0].start()
        for term in terms:
            term.start()
        for fetch in fetches[1:]:
            fetch.start()
        enter(place, True, True)
        ga_line = LineGather(place, ga, ga_g, sems[0])
        mlp_scatter = LineScatter(place, mlp_ref, mlp_own, sems[1], mine, LineScatter.pieces)
        ups = GridScatter(place, gup, grad_up_own, tile_up, sems[3])
        ga_line.start()
        fetches[0].wait()
        ups.start()
        mlp_scatter.start()
        for term in terms:
            term.wait()
        travel = LineScatter.pieces * (chips - 1)
        at_slot = 0

        def backward(chip):
            at = span(chip, pair)
            ga_line.ready(chip)
            values = chip_rows(ga_g, chip)
            grad_heads = matmul(values, out_w[0].reshape(width, head_columns)).astype(low)
            allowed = pair_mask(cod_g, chip, rows)
            for h in range(head_columns // HEAD):
                head = slice(h * HEAD, (h + 1) * HEAD)
                query, key, value = [qkv_ref[w, at, head] for w in range(which)]
                grad_head = grad_heads[:, head]
                probs = attention_probs(query, key, allowed)
                grad_p = matmul_last(grad_head, value)
                delta = jnp.sum(probs * grad_p, axis=-1, keepdims=True)
                grad_scores = (probs * (grad_p - delta)).astype(low)
                scale = HEAD ** (-0.5)
                gqkv[0, at, head] = (matmul(grad_scores, key) * scale).astype(low)
                gqkv[1, at, head] = (matmul_first(grad_scores, query) * scale).astype(low)
                gqkv[2, at, head] = matmul_first(probs.astype(low), grad_head).astype(low)

        def backward_at(distance):
            def side(i):
                chip = place.p + (1 - 2 * i) * distance

                @pl.when((chip >= 0) & (chip < place.chips))
                def _():
                    backward(chip)

            loop(2 if distance else 1, side)

        for step in range(1, chips):
            ga_line.step(step)
            if step < chips - 1:
                to_slot = travel * step // (chips - 1)
                mlp_scatter.run(at_slot, to_slot)
                at_slot = to_slot
            if step == 1:
                for fetch in fetches[1:]:
                    fetch.wait()
            backward_at(step - 1)
            if step == chips // 2:
                ups.step()
        backward_at(chips - 1)
        ga_line.drain()
        scatter = LineScatter(place, ga_g, grad_h1, sems[2])
        qkvs = GridScatter(place, gqkv_w, grad_qkv_own, tile_qkv, sems[4])
        outs = GridScatter(place, gout_w, grad_out_own, tile_out, sems[5])

        def out_tile(i):
            d, r = i // row_tiles, lax.rem(i, row_tiles)
            left = ga_g[:, :, span(i, COLUMN_STEP)].reshape(tokens, COLUMN_STEP)
            gout_w[0, d, span(r, COLUMN_STEP), :] = matmul_first(left, att[...]).astype(low)

        loop(n_dp * row_tiles, out_tile)
        outs.start()

        def compute(chip):
            at = span(chip, pair)
            for d in range(n_dp):
                total = matmul_last(gqkv[0, at, :], qkv_w[0, d])
                for w in range(1, which):
                    total = total + matmul_last(gqkv[w, at, :], qkv_w[w, d])
                piece = total.astype(low).reshape(2, rows, weight_rows)
                ga_g[span(chip, 2), :, d * weight_rows : (d + 1) * weight_rows] = piece

        def grad_tile(i):
            d, r = i // row_tiles, lax.rem(i, row_tiles)
            left = hid_g[:, :, span(i, COLUMN_STEP)].reshape(tokens, COLUMN_STEP)
            for w in range(which):
                gqkv_w[w, d, span(r, COLUMN_STEP), :] = matmul_first(left, gqkv[w]).astype(low)

        def then(k):
            @pl.when(k == 0)
            def _():
                loop(n_dp * row_tiles, grad_tile)
                qkvs.start()

            @pl.when(k == 1)
            def _():
                mlp_scatter.run(at_slot, travel)

        slot = scatter.paced(compute, 3, then)
        outs.step()
        slot = scatter.run_to(slot, scatter.slots // 2)
        qkvs.step()
        slot = scatter.run_to(slot, scatter.slots * 5 // 8)
        ups.step_own()
        mlp_scatter.finish()
        ups.finish()
        own = Rows(place, cod, mods_ref, micro, rows, own_images // micro)
        sums_own[...] = jnp.zeros_like(sums_own)

        def branch_out(m, at):
            slot_of, alive = own.slot_live(m, at)
            branch = mlp_own[at, :]
            block_out[at, :] = (mid_ref[at, :] + own.pick(5, m, slot_of) * branch).astype(low)
            own.add_up(sums_own, 2, m, slot_of, cot[at, :].astype(f32) * alive * branch)

        own.tiles(branch_out)
        scatter.run_to(slot, scatter.slots)
        outs.step_own()
        qkvs.step_own()
        scatter.finish()

        def norm_grad(m, at):
            slot_of, _ = own.slot_live(m, at)
            normed, inv_std = normalize(tok[at, :].astype(f32))
            grad = grad_h1[at, :]
            before = normalize_back(grad * (1.0 + own.pick(1, m, slot_of)), normed, inv_std)
            input_grad[at, :] = gmid[at, :] + before
            own.add_up(sums_own, 0, m, slot_of, grad)
            own.add_up(sums_own, 1, m, slot_of, grad * normed)

        own.tiles(norm_grad)
        outs.finish()
        qkvs.finish()
        squares[...] = tile_up[...] + tile_qkv[...] + tile_out[...]

    return pl.pallas_call(
        kernel,
        out_shape=[
            jax.ShapeDtypeStruct((rows, width), low),
            jax.ShapeDtypeStruct((rows, width), f32),
            jax.ShapeDtypeStruct((3, own_images, width), f32),
            jax.ShapeDtypeStruct(up_shape, f32),
            jax.ShapeDtypeStruct((which, weight_rows, head_columns), f32),
            jax.ShapeDtypeStruct((1, weight_rows, head_columns), f32),
            jax.ShapeDtypeStruct(TILE, f32),
        ],
        in_specs=[WHOLE] * 8 + [HBM] * 7,
        out_specs=[WHOLE] * 7,
        scratch_shapes=[
            pltpu.VMEM((n_fsdp, rows, width), low),
            pltpu.VMEM((which, tokens, head_columns), low),
            pltpu.VMEM((which, n_dp, weight_rows, head_columns), low),
            pltpu.VMEM((1, n_dp, weight_rows, head_columns), low),
            pltpu.VMEM((rows, width), f32),
            pltpu.VMEM((rows, width), f32),
            pltpu.VMEM(TILE, f32),
            pltpu.VMEM(TILE, f32),
            pltpu.VMEM(TILE, f32),
            pltpu.VMEM((chips, rows, width), low),
            *[pltpu.VMEM(a.shape, low) for a in (grad_up, qkv_g, out_g, qkv_low, attended, hidden_g)],
            pltpu.SemaphoreType.DMA((6,)),
            pltpu.SemaphoreType.DMA((chips,)),
            *line, *scatter_got, *scatter_got, *up_got, *qkv_got, *out_got,
        ],
        compiler_params=parameters(3),
    )(
        grad_attn, tokens_own, mid, grad_mid, cotangent, codes, mods, codes_g, mlp_part, grad_up, qkv_g, out_g, qkv_low,
        attended, hidden_g,
    )


def norm_kernel(n_dp, n_fsdp, micro, sums_first, sums_second, condition, products, squares, more_squares, states):
    own_images, width = sums_first.shape[1:]
    wide = width // n_fsdp
    images, deep = condition.shape[1:]
    lanes = wide // 128
    slots_here = own_images // micro
    source = [(0, 0), (0, 1), (1, 0), (1, 1), (1, 2), (0, 2)]

    def kernel(sums_a, sums_b, cond, product, squares_ref, more_ref, *refs):
        states_in, refs = refs[: len(states)], refs[len(states) :]
        grad, norm, refs = refs[0], refs[1], refs[2:]
        states_out, refs = refs[: len(states)], refs[len(states) :]
        mail, boxes, mine, all_mods, columns, tile, tiles, moves, *sems = refs
        place = Place(n_dp, n_fsdp)
        fetches = [
            pltpu.make_async_copy(src, dst, moves.at[i]) for i, (src, dst) in enumerate(zip(states_in, states_out))
        ]
        for fetch in fetches:
            fetch.start()
        barrier = pltpu.get_barrier_semaphore()
        for i in range(1, n_dp):
            pl.semaphore_signal(
                barrier, inc=1, device_id=place.at_dp((place.dp + i) % n_dp), device_id_type=MESH
            )
        for i in range(1, n_fsdp):
            pl.semaphore_signal(
                barrier, inc=1, device_id=(place.dp, (place.f + i) % n_fsdp), device_id_type=MESH
            )
        for j, (which, row) in enumerate(source):
            values = (sums_a, sums_b)[which][row].astype(jnp.bfloat16).astype(jnp.float32)
            for f in range(n_fsdp):
                for g in range(lanes):
                    at = (j * lanes + g) * own_images
                    mail[f, at : at + own_images, :] = values[:, f * wide + g * 128 : f * wide + (g + 1) * 128]
        pl.semaphore_wait(barrier, n_dp + n_fsdp - 2)
        inner = Direct(place, mail, boxes, sems[0:2], "fsdp", block=lambda ref, d: ref.at[d])
        inner.start()
        boxes[place.f] = mail[place.f]
        inner.finish()
        for j in range(MODS):
            for g in range(lanes):
                pieces = []
                for m in range(micro):
                    at = (j * lanes + g) * own_images + m * slots_here
                    pieces += [boxes[f, at : at + slots_here, :] for f in range(n_fsdp)]
                mine[j, :, g * 128 : (g + 1) * 128] = jnp.concatenate(pieces, axis=0).astype(jnp.bfloat16)
        outer = Direct(place, mine, all_mods, sems[2:4])
        tile[...] = squares_ref[...] + more_ref[...]
        beside = Direct(place, tile, columns, sems[4:6])
        outer.start()
        beside.start()
        all_mods[place.dp] = mine[...]
        columns[place.dp] = tile[...]
        high = product[...].astype(jnp.bfloat16)
        rest = (product[...] - high.astype(jnp.float32)).astype(jnp.bfloat16)
        outer.finish()
        beside.finish()
        total = columns[0]
        for d in range(1, n_dp):
            total = total + columns[d]
        for j in range(MODS):
            values = all_mods[:, j].reshape(n_dp * images, wide)
            both = (matmul(high, values) + matmul(rest, values)) * values.astype(jnp.float32)
            for at in range(0, n_dp * images, ROW_STEP):
                for lane in range(0, wide, 128):
                    total = total + both[at : at + ROW_STEP, lane : lane + 128]
        tile[...] = total
        first = Direct(place, tile, tiles, sems[6:8], "fsdp")
        first.start()
        tiles[place.f] = tile[...]
        every = cond[...].reshape(n_dp * images, deep)
        for j in range(MODS):
            grad[j] = matmul_first(every, all_mods[:, j].reshape(n_dp * images, wide))
        first.finish()
        total = tiles[0]
        for f in range(1, n_fsdp):
            total = total + tiles[f]
        norm[0, 0] = jnp.sqrt(jnp.sum(total))
        for fetch in fetches:
            fetch.wait()

    return pl.pallas_call(
        kernel,
        out_shape=[
            jax.ShapeDtypeStruct((MODS, deep, wide), jnp.float32),
            jax.ShapeDtypeStruct((1, 1), jnp.float32),
            *[pltpu.VMEM(state.shape, state.dtype) for state in states],
        ],
        in_specs=[WHOLE] * 6 + [HBM] * len(states),
        out_specs=[WHOLE, pl.BlockSpec(memory_space=pltpu.SMEM)] + [HBM] * len(states),
        scratch_shapes=[
            pltpu.VMEM((n_fsdp, MODS * lanes * own_images, 128), jnp.float32),
            pltpu.VMEM((n_fsdp, MODS * lanes * own_images, 128), jnp.float32),
            pltpu.VMEM((MODS, images, wide), jnp.bfloat16),
            pltpu.VMEM((n_dp, MODS, images, wide), jnp.bfloat16),
            pltpu.VMEM((n_dp, *TILE), jnp.float32),
            pltpu.VMEM(TILE, jnp.float32),
            pltpu.VMEM((n_fsdp, *TILE), jnp.float32),
            pltpu.SemaphoreType.DMA((len(states),)),
            *Direct.scratch(n_fsdp), *Direct.scratch(n_dp), *Direct.scratch(n_dp), *Direct.scratch(n_fsdp),
        ],
        compiler_params=parameters(1, NORM_LIMIT),
    )(sums_first, sums_second, condition, products, squares, more_squares, *states)


def adam_kernel(factor, grad, master, first, second):
    which, rows, columns = master.shape
    step = min(rows, max(64, 131072 // columns))
    block = pl.BlockSpec((1, step, columns), lambda w, r: (w, r, 0))
    root = (1.0 - BETA_TWO**STEP) ** 0.5
    rate = LEARN_RATE * root / (1.0 - BETA_ONE**STEP)

    def kernel(factor_ref, grad_ref, master_ref, first_ref, second_ref, new_ref, copy_ref, moment_ref, square_ref):
        scale = factor_ref[0, 0]
        at = (pl.ds(pl.program_id(0), 1), span(pl.program_id(1), step))
        grad = grad_ref[at]
        moment = BETA_ONE * first_ref[at] + ((1.0 - BETA_ONE) * scale) * grad
        square = BETA_TWO * second_ref[at] + ((1.0 - BETA_TWO) * scale * scale) * (grad * grad)
        moment_ref[...] = moment
        square_ref[...] = square
        below = jnp.sqrt(square) + ADAM_EPS * root
        new = (1.0 - LEARN_RATE * WEIGHT_DECAY) * master_ref[at] - (rate * moment) / below
        new_ref[...] = new
        copy_ref[...] = new.astype(jnp.bfloat16)

    shape = jax.ShapeDtypeStruct(master.shape, jnp.float32)
    return pl.pallas_call(
        kernel,
        grid=(which, rows // step),
        out_shape=[shape, jax.ShapeDtypeStruct(master.shape, jnp.bfloat16), shape, shape],
        in_specs=[pl.BlockSpec(memory_space=pltpu.SMEM)] + [WHOLE] * 4,
        out_specs=[block] * 4,
        compiler_params=pltpu.CompilerParams(vmem_limit_bytes=SMALL_LIMIT),
    )(factor, grad, master, first, second)


def normalize(values):
    average = jnp.mean(values, axis=-1, keepdims=True)
    centred = values - average
    inv_std = lax.rsqrt(jnp.mean(centred * centred, axis=-1, keepdims=True) + NORM_EPS)
    return (centred * inv_std, inv_std)


def normalize_back(grad, normed, inv_std):
    return inv_std * (
        grad
        - jnp.mean(grad, axis=-1, keepdims=True)
        - normed * jnp.mean(grad * normed, axis=-1, keepdims=True)
    )


def body(n_dp, n_fsdp, *arguments):
    tokens, embedding, image_slot, token_mask, cotangent = arguments[:5]
    weights = [w if w.ndim == 3 else w[:, None] for w in arguments[5:]]
    weights = [w.transpose(1, 0, 2) for w in weights]
    masters, firsts, seconds = weights[:5], weights[5:10], weights[10:]
    qkv_w, out_w, up_w, down_w, ada_w = masters
    micro, tok_rows, width = tokens.shape
    own_rows = micro * tok_rows
    image_count = embedding.shape[1] // n_fsdp
    images = micro * n_fsdp * image_count
    own_tokens = tokens.reshape(own_rows, width)
    own_cot = cotangent.reshape(own_rows, width)

    (
        attn_own, mid, hidden2, mods, cond_all, products, codes, codes_g, qkv_low, attended, down_low,
        hidden1_g, qkv_g, out_g, up_g, grad_mlp_g,
    ) = attention_kernel(
        n_dp, n_fsdp, micro, own_tokens, own_cot, image_slot, token_mask, embedding.reshape(images, -1), ada_w, qkv_w, out_w,
        up_w, down_w,
    )
    grad_mid, grad_attn, sums_second, grad_down, squares_down, mlp_part, grad_up = feed_forward_kernel(
        n_dp, n_fsdp, micro, hidden2, mid, attn_own, own_cot, codes, mods, grad_mlp_g, up_g, down_low
    )
    block_out, input_grad, sums_first, grad_up, grad_qkv_w, grad_out, squares = attention_grad_kernel(
        n_dp, n_fsdp, micro, grad_attn, own_tokens, mid, grad_mid, own_cot, codes, mods, codes_g, mlp_part, grad_up,
        qkv_g, out_g, qkv_low, attended, hidden1_g,
    )
    block_out = block_out.reshape(tokens.shape)
    input_grad = input_grad.reshape(tokens.shape)
    grad_ada, grad_norm, *states = norm_kernel(
        n_dp, n_fsdp, micro, sums_first, sums_second, cond_all, products, squares_down, squares,
        (*masters, *firsts, *seconds),
    )
    masters, firsts, seconds = states[:5], states[5:10], states[10:]

    factor = jnp.minimum(1.0, CLIP_AT / grad_norm)
    results = []
    grads = (grad_qkv_w, grad_out, grad_up, grad_down, grad_ada)
    for given, grad, master, first, second in zip(arguments[5:], grads, masters, firsts, seconds):
        for updated in adam_kernel(factor, grad, master, first, second):
            results.append(updated.transpose(1, 0, 2).reshape(given.shape))
    return (block_out, input_grad, *results, grad_norm[0, 0])


def solution(mesh):
    n_dp, n_fsdp = mesh.shape["dp"], mesh.shape["fsdp"]
    rows = P(None, ("dp", "fsdp"), None)
    slots = P(None, ("dp", "fsdp"))
    thick = P("dp", None, "fsdp")
    flat = P("dp", "fsdp")
    weights = (thick, flat, flat, flat, thick)
    updated = tuple(spec for spec in weights for _ in range(4))
    return jax.shard_map(
        functools.partial(body, n_dp, n_fsdp),
        mesh=mesh,
        in_specs=(rows, P(None, "dp", None), slots, slots, rows, *weights, *weights, *weights),
        out_specs=(rows, rows, *updated, P()),
        check_vma=False,
    )
```
